32 devices in a mesh: dp: 4 (over y, x), expert: 8 (over z, core).
Axes of the slice: x: 2, y: 2, z: 4, core: 2. Of those that a mesh axis runs over, the one named last changes fastest.
Arguments:
- tokens: bfloat16 [4, 1024, 2048], P('dp', 'expert'), may hold values from -6 to 6
- routes: int32 [4, 1024, 8], P('dp', 'expert'), may hold values from 0 to 15, all different within a row; in each aligned block of 128 rows (0 to 127, 128 to 255, ..., all dimensions but the last counted through in order) at most 128 rows name the same one
- grad_output: bfloat16 [4, 1024, 2048], P('dp', 'expert'), may hold values from -6 to 6
- w_query: bfloat16 [2048, 2048], P(('dp', 'expert')), may hold values from -0.125 to 0.125
- w_key: bfloat16 [2048, 2048], P(('dp', 'expert')), may hold values from -0.125 to 0.125
- w_value: bfloat16 [2048, 2048], P(('dp', 'expert')), may hold values from -0.125 to 0.125
- w_out: bfloat16 [2048, 2048], P(('dp', 'expert')), may hold values from -1 to 1
- w_router: bfloat16 [2048, 16], P(('dp', 'expert')), may hold values from -0.0625 to 0.0625
- gain_attn: bfloat16 [2048], P(('dp', 'expert')), may hold values from 0.5 to 1.5
- gain_query: bfloat16 [2048], P(('dp', 'expert')), may hold values from 0.5 to 1.5
- gain_key: bfloat16 [2048], P(('dp', 'expert')), may hold values from 0.5 to 1.5
- gain_ffn: bfloat16 [2048], P(('dp', 'expert')), may hold values from 0.5 to 1.5
- w_gate: bfloat16 [16, 2048, 1024], P('expert', 'dp'), may hold values from -0.125 to 0.125
- w_up: bfloat16 [16, 2048, 1024], P('expert', 'dp'), may hold values from -0.125 to 0.125
- w_down: bfloat16 [16, 1024, 2048], P('expert', 'dp'), may hold values from -1.5 to 1.5
Outputs:
- output: float32 [4, 1024, 2048], P('dp', 'expert')
- input_grad: float32 [4, 1024, 2048], P('dp', 'expert')
- grad_query: float32 [2048, 2048], P(('dp', 'expert'))
- grad_key: float32 [2048, 2048], P(('dp', 'expert'))
- grad_value: float32 [2048, 2048], P(('dp', 'expert'))
- grad_out: float32 [2048, 2048], P(('dp', 'expert'))
- grad_router: float32 [2048, 16], P(('dp', 'expert'))
- grad_gain_attn: float32 [2048], P(('dp', 'expert'))
- grad_gain_query: float32 [2048], P(('dp', 'expert'))
- grad_gain_key: float32 [2048], P(('dp', 'expert'))
- grad_gain_ffn: float32 [2048], P(('dp', 'expert'))
- grad_gate: float32 [16, 2048, 1024], P('expert', 'dp')
- grad_up: float32 [16, 2048, 1024], P('expert', 'dp')
- grad_down: float32 [16, 1024, 2048], P('expert', 'dp')
The draws below stay inside these ranges and needn't reach their ends.
Inputs may be any that keep to these rules, and one draw needn't show every extreme that they name: `routes`: each token names 8 different experts; in the rows of one device no expert is named more than 128 times, a bound that some block reaches.
All inputs are finite; a program needn't handle non-finite values.
Results may differ from the reference program's by a relative error of at most 0.02.
Values may be sent and summed in bfloat16 or wider, within the bound.
A program may use at most 384 MiB of HBM per device.

```python
import math
import jax
import jax.numpy as jnp
import numpy as np
from jax import lax

D = 2048
HEADS = 16
HEAD_DIM = 128
FF = 1024
TOPK = 8
TOK_DEV = 128
EXPERTS = 16
SEQS = 4
LENGTH = 1024
CAP = 128
N_EXPERT = 8


def level_of(rng, shape, cuts, least, top_value):
    def one(axis_at, blocks):
        heights = jax.random.uniform(jax.random.fold_in(jax.random.fold_in(rng, 6), axis_at), (blocks,), jnp.float32, least / len(cuts), top_value / len(cuts))
        return jnp.repeat(jnp.exp(heights), shape[axis_at] // blocks).reshape((-1,) + (1,) * (len(shape) - axis_at - 1))

    loudness = one(*cuts[0])
    for cut in cuts[1:]:
        loudness = loudness * one(*cut)
    return loudness


def assign_block(own_key, own, number, rows, count, top, limit, slope):
    ranking = jax.random.permutation(own_key, count)
    packed, usual = shares(count, rows * top, limit, slope, True), shares(count, rows * top, limit, slope, False)
    places = jnp.arange(count)

    def named(sizes, offset_by):
        used = int((sizes > 0).sum())
        fixed = max(1, used // 4)
        passed = fixed + (places - fixed + offset_by * (used - fixed)) % max(1, count - fixed)
        return jnp.zeros((count,), jnp.int32).at[ranking[jnp.where(places < fixed, places, passed)]].set(jnp.asarray(sizes, jnp.int32))

    sizes = jnp.where(number % 4 == 0, named(packed, number // 4), named(usual, number - number // 4 - 1))
    mixed = jax.random.permutation(jax.random.fold_in(own, 3), count)
    giver, sink = mixed[0:count // 2 * 2:2], mixed[1:count // 2 * 2:2]
    margin = jnp.minimum(sizes[giver] - 1, limit - sizes[sink]) // 2
    margin = jnp.where((giver == ranking[0]) | (sink == ranking[0]) | (sizes[sink] == 0), 0, jnp.maximum(margin, 0))
    passed = jax.random.randint(jax.random.fold_in(own, 4), (count // 2,), 0, 1 << 20) % (margin + 1)
    sizes = sizes.at[giver].add(-passed).at[sink].add(passed)
    members = jnp.searchsorted(jnp.cumsum(sizes), jnp.arange(rows * top), side="right").astype(jnp.int32)
    grid = members.reshape(top, rows).T
    grid = grid[jax.random.permutation(jax.random.fold_in(own, 1), rows)]
    offset_by = jax.random.randint(jax.random.fold_in(own, 2), (rows, 1), 0, top)
    return jnp.take_along_axis(grid, (jnp.arange(top)[None, :] + offset_by) % top, axis=1)


def shares(number_of, total, reach, lean, full):
    weights = [(1 << 20) // math.isqrt(standing ** lean) + 1 for standing in range(1, number_of + 1)]
    largest = reach if full else min(reach, max(-(-total // number_of), total * weights[0] // sum(weights)))
    least = 1 if total - largest >= number_of - 1 else 0
    holding, spare = [largest] + [least] * (number_of - 1), total - largest - least * (number_of - 1)
    while spare > 0:
        movable = [i for i in range(1, number_of) if holding[i] < largest] or [i for i in range(1, number_of) if holding[i] < reach]
        whole, remaining = sum([weights[i] for i in movable]), spare
        for i in movable:
            more = min(reach - holding[i], max(1, remaining * weights[i] // whole), spare)
            holding[i] = holding[i] + more
            spare = spare - more
    return np.array(holding)


def bell_draw(rng, dims, spread, limit, shards=(), held_as=jnp.bfloat16):
    drawn = jax.random.normal(rng, dims, jnp.float32) * spread
    if len(shards) > 0:
        drawn = level_of(rng, dims, shards, -0.22, 0.18) * drawn
    return jnp.clip(drawn, min=-limit, max=limit).astype(held_as)


def setup_inputs(seed: int = 0) -> dict:
    seeds = jax.random.split(jax.random.key(seed), 16)
    tokens = bell_draw(seeds[0], (SEQS, LENGTH, D), 1.0, 6.0, ((0, 4), (1, 8)))
    routes_keys = jax.random.split(jax.random.fold_in(seeds[1], 1), SEQS * LENGTH // TOK_DEV)
    routes_turns = jax.random.permutation(jax.random.fold_in(seeds[1], 3), SEQS * LENGTH // TOK_DEV)
    routes = jax.vmap(lambda own, number: assign_block(jax.random.fold_in(seeds[1], 2), own, number, TOK_DEV, EXPERTS, TOPK, CAP, 2))(routes_keys, routes_turns).reshape((SEQS, LENGTH, TOPK))
    grad_output = bell_draw(seeds[2], (SEQS, LENGTH, D), 1.0, 6.0, ((0, 4), (1, 8)))
    w_query = bell_draw(seeds[3], (D, D), D ** -0.5, 0.125, ((0, 32),))
    w_key = bell_draw(seeds[4], (D, D), D ** -0.5, 0.125, ((0, 32),))
    w_value = bell_draw(seeds[5], (D, D), D ** -0.5, 0.125, ((0, 32),))
    w_out = bell_draw(seeds[6], (D, D), (D // 64) ** -0.5, 1.0, ((0, 32),))
    w_router = bell_draw(seeds[7], (D, EXPERTS), (4 * D) ** -0.5, 0.0625, ((0, 32),))
    gain_attn = jnp.clip(1.0 + 0.1 * jax.random.normal(seeds[8], (D,), jnp.float32), 0.5, 1.5).astype(jnp.bfloat16)
    gain_query = jnp.clip(1.0 + 0.1 * jax.random.normal(seeds[9], (D,), jnp.float32), 0.5, 1.5).astype(jnp.bfloat16)
    gain_key = jnp.clip(1.0 + 0.1 * jax.random.normal(seeds[10], (D,), jnp.float32), 0.5, 1.5).astype(jnp.bfloat16)
    gain_ffn = jnp.clip(1.0 + 0.1 * jax.random.normal(seeds[11], (D,), jnp.float32), 0.5, 1.5).astype(jnp.bfloat16)
    w_gate = bell_draw(seeds[12], (EXPERTS, D, FF), D ** -0.5, 0.125, ((0, 8), (1, 4)))
    w_up = bell_draw(seeds[13], (EXPERTS, D, FF), D ** -0.5, 0.125, ((0, 8), (1, 4)))
    w_down = bell_draw(seeds[14], (EXPERTS, FF, D), (0.5 * EXPERTS * FF ** -0.5), 1.5, ((0, 8), (1, 4)))
    return {"tokens": tokens, "routes": routes, "grad_output": grad_output, "w_query": w_query, "w_key": w_key, "w_value": w_value, "w_out": w_out, "w_router": w_router, "gain_attn": gain_attn, "gain_query": gain_query, "gain_key": gain_key, "gain_ffn": gain_ffn, "w_gate": w_gate, "w_up": w_up, "w_down": w_down}


EPS = 1e-05
THETA = 10000.0
NEG = -1e+30
HIGH = lax.Precision.HIGHEST

@jax.custom_vjp
def low(v):
    return lax.optimization_barrier(v.astype(jnp.bfloat16)).astype(jnp.float32)

@jax.custom_vjp
def low_back(v):
    return v

def low_keep(v):
    return (low(v), None)

def low_pass(kept, grad):
    return (grad,)

def back_keep(v):
    return (v, None)

def back_low(kept, grad):
    return (low(grad),)
low.defvjp(low_keep, low_pass)
low_back.defvjp(back_keep, back_low)

def norm_rows(values, gain_vec):
    return values * lax.rsqrt(lax.optimization_barrier(jnp.mean(values * values, axis=-1, keepdims=True)) + EPS) * gain_vec

def rotary(values, positions):
    half_dim = values.shape[-1] // 2
    inv_freq = jnp.exp(jnp.arange(half_dim, dtype=jnp.float32) * (-2.0 * math.log(THETA) / values.shape[-1]))
    angles = positions.astype(jnp.float32)[:, None] * inv_freq[None, :]
    cosine = jnp.cos(angles)[:, None, :]
    sine_val = jnp.sin(angles)[:, None, :]
    front_half = values[..., :half_dim]
    back_half = values[..., half_dim:]
    return jnp.concatenate([front_half * cosine - back_half * sine_val, back_half * cosine + front_half * sine_val], axis=-1)

def project_heads(raw_proj, gain_vec, positions):
    normed = norm_rows(raw_proj, gain_vec).reshape(raw_proj.shape[0], HEADS, HEAD_DIM)
    return rotary(normed, positions)

def matmul(left, right):
    return jnp.dot(left, right, precision=HIGH, preferred_element_type=jnp.float32)

def attend_sequence(sequence, w_q, w_k, w_v, w_o, g_attn, g_query, g_key):
    positions = jnp.arange(LENGTH, dtype=jnp.int32)
    normed_in = low(norm_rows(sequence, g_attn))
    queries = low(project_heads(low_back(matmul(normed_in, w_q)), g_query, positions))
    key_rows = low(project_heads(low_back(matmul(normed_in, w_k)), g_key, positions))
    value_rows = low(low_back(matmul(normed_in, w_v))).reshape(LENGTH, HEADS, HEAD_DIM)
    scores = low_back(jnp.einsum('qhd,khd->hqk', queries, key_rows, precision=HIGH)) * HEAD_DIM ** (-0.5)
    allowed = positions[None, :] <= positions[:, None]
    scores = jnp.where(allowed[None], scores, NEG)
    prob_low = low(jax.nn.softmax(scores, axis=-1))
    attn_mix = jnp.einsum('hqk,khd->qhd', prob_low, value_rows, precision=HIGH).reshape(LENGTH, D)
    attn_mix = low_back(low(attn_mix))
    return sequence + low_back(matmul(attn_mix, w_o))

def reference(tokens, routes, grad_output, w_query, w_key, w_value, w_out, w_router, gain_attn, gain_query, gain_key, gain_ffn, w_gate, w_up, w_down):
    route_rows = routes.reshape(SEQS * LENGTH, TOPK).astype(jnp.int32)
    flat_ids = route_rows.reshape(SEQS * LENGTH * TOPK)
    span_rows = SEQS * N_EXPERT * CAP
    sorted_ids = jnp.argsort(flat_ids, stable=True).astype(jnp.int32)
    sorted_ids = jnp.concatenate([sorted_ids, jnp.zeros((span_rows,), jnp.int32)])
    counts = lax.optimization_barrier(jnp.sum((flat_ids[:, None] == jnp.arange(EXPERTS, dtype=jnp.int32)[None, :]).astype(jnp.int32), axis=0))
    starts = (jnp.cumsum(counts) - counts).astype(jnp.int32)

    def layer_fwd(x_in, w_q, w_k, w_v, w_o, w_r, g_attn, g_query, g_key, g_ffn, wg_all, wu_all, wd_all):

        def attend_one(sequence):
            return attend_sequence(sequence, w_q, w_k, w_v, w_o, g_attn, g_query, g_key)
        after_attn = lax.map(jax.checkpoint(attend_one), x_in)
        flat_rows = after_attn.reshape(SEQS * LENGTH, D)
        normed_ffn = low(norm_rows(flat_rows, g_ffn))
        router_prob = jax.nn.softmax(low_back(matmul(normed_ffn, w_r)), axis=-1)
        route_weight = jnp.take_along_axis(router_prob, route_rows, axis=1).reshape(SEQS * LENGTH * TOPK)

        def expert_step(summed, expert_id):
            picked = lax.dynamic_slice_in_dim(sorted_ids, starts[expert_id], span_rows)
            live_rows = (jnp.arange(span_rows, dtype=jnp.int32) < counts[expert_id]).astype(jnp.float32)
            token_ids = picked // TOPK
            row_weight = route_weight[picked] * live_rows
            inputs = normed_ffn[token_ids]
            gate_proj = low_back(matmul(inputs, wg_all[expert_id]))
            up_proj = low_back(matmul(inputs, wu_all[expert_id]))
            hidden = low(jax.nn.silu(gate_proj) * up_proj)
            result = low_back(low(matmul(hidden, wd_all[expert_id])))
            return (summed.at[token_ids].add(result * row_weight[:, None]), None)
        summed, _ = lax.scan(jax.checkpoint(expert_step), jnp.zeros_like(flat_rows), jnp.arange(EXPERTS, dtype=jnp.int32))
        return (flat_rows + summed).reshape(SEQS, LENGTH, D)
    f32 = jnp.float32
    output, pull = jax.vjp(layer_fwd, tokens.astype(f32), w_query.astype(f32), w_key.astype(f32), w_value.astype(f32), w_out.astype(f32), w_router.astype(f32), gain_attn.astype(f32), gain_query.astype(f32), gain_key.astype(f32), gain_ffn.astype(f32), w_gate.astype(f32), w_up.astype(f32), w_down.astype(f32))
    grads = pull(grad_output.astype(f32))
    return (output, grads[0], grads[1], grads[2], grads[3], grads[4], grads[5], grads[6], grads[7], grads[8], grads[9], grads[10], grads[11], grads[12])
```

```python
import math

import jax
import jax.numpy as jnp
from jax import lax
from jax.sharding import PartitionSpec as P

HEADS = 16
HEAD_DIM = 128

EPS = 1e-05
THETA = 10000.0
NEG = -1e30

F32 = jnp.float32
BF16 = jnp.bfloat16


def dot(left, right):
    return jnp.dot(left, right, preferred_element_type=F32)


def dot_tn(left, right):
    return lax.dot_general(left, right, (((0,), (0,)), ((), ())), preferred_element_type=F32)


def dot_nt(left, right):
    return lax.dot_general(left, right, (((1,), (1,)), ((), ())), preferred_element_type=F32)


def inv_rms(values):
    return lax.rsqrt(jnp.mean(values * values, axis=-1, keepdims=True) + EPS)


def norm_back(values, inv, gain_vec, grad):
    scaled = grad * gain_vec
    mean_dot = jnp.mean(scaled * values, axis=-1, keepdims=True)
    d_values = inv * scaled - values * (inv * inv * inv * mean_dot)
    d_gain = jnp.sum(grad * values * inv, axis=0)
    return d_values, d_gain


def rope_tables(length):
    half_dim = HEAD_DIM // 2
    inv_freq = jnp.exp(
        jnp.arange(half_dim, dtype=F32) * (-2.0 * math.log(THETA) / HEAD_DIM)
    )
    angles = jnp.arange(length, dtype=jnp.int32).astype(F32)[:, None] * inv_freq[None, :]
    cosine, sine = jnp.cos(angles), jnp.sin(angles)
    return (
        jnp.concatenate([cosine, cosine], axis=1)[:, None, :],
        jnp.concatenate([-sine, sine], axis=1)[:, None, :],
    )


def swap_halves(values):
    half_dim = HEAD_DIM // 2
    return jnp.concatenate([values[..., half_dim:], values[..., :half_dim]], axis=-1)


def rotary(values, tables):
    return values * tables[0] + swap_halves(values) * tables[1]


def rotary_back(grad, tables):
    return grad * tables[0] - swap_halves(grad) * tables[1]


def gather_expert(block, axis=0):
    return lax.all_gather(block, "expert", axis=axis, tiled=True)


def scatter_expert(partial):
    return lax.psum_scatter(partial.astype(BF16), "expert", scatter_dimension=0, tiled=True).astype(F32)


def shards(
    tokens, routes, grad_output, w_query, w_key, w_value, w_out, w_router,
    gain_attn, gain_query, gain_key, gain_ffn, w_gate, w_up, w_down,
):
    rows = tokens.shape[1]
    width = tokens.shape[2]
    groups = lax.axis_size("expert")
    seqs = lax.axis_size("dp")
    me = lax.axis_index("expert")
    length = rows * groups
    local_experts = w_gate.shape[0]
    all_experts = local_experts * groups
    block = w_query.shape[0]
    own = width // groups
    slab = max(own, HEAD_DIM)
    copies = slab // own
    heads = slab // HEAD_DIM
    share = 1.0 / copies
    offset = (me % copies) * own

    x_low = tokens.reshape(rows, width)
    g_low = grad_output.reshape(rows, width)

    small = jnp.concatenate(
        [w_router] + [g[:, None] for g in (gain_attn, gain_query, gain_key, gain_ffn)], axis=1
    )
    small_all = lax.all_gather(small, ("dp", "expert"), axis=0, tiled=True)
    w_r = small_all[:, :all_experts]
    gains = small_all[:, all_experts:].astype(F32)
    g_attn, g_ffn = gains[:, 0], gains[:, 3]
    slab_start = (me // copies) * slab
    g_query = lax.dynamic_slice(gains[:, 1], (slab_start,), (slab,))
    g_key = lax.dynamic_slice(gains[:, 2], (slab_start,), (slab,))

    qkv_send = jnp.stack([w_query, w_key, w_value], axis=1).reshape(block, 3, width // slab, slab)
    qkv_send = qkv_send.transpose(2, 0, 1, 3).reshape(width // slab, block, 3 * slab)
    qkv_send = jnp.repeat(qkv_send, copies, axis=0)
    qkv_got = lax.all_to_all(qkv_send, "expert", split_axis=0, concat_axis=0, tiled=True)
    w_qkv = lax.all_gather(qkv_got.reshape(groups * block, 3 * slab), "dp", axis=0, tiled=True)
    total = seqs * groups
    moves = [(b, (b % seqs) * groups + b // seqs) for b in range(total)]
    w_o = lax.ppermute(w_out, ("dp", "expert"), moves)
    w_o = lax.all_gather(w_o, "dp", axis=0, tiled=True)
    if copies > 1:
        sets = [[c * copies + i for i in range(copies)] for c in range(groups // copies)]
        w_o = lax.all_gather(w_o, "expert", axis_index_groups=sets, axis=0, tiled=True)

    x_in = x_low.astype(F32)
    inv_attn = inv_rms(x_in)
    normed_low = (x_in * inv_attn * g_attn).astype(BF16)
    normed_all = gather_expert(normed_low)
    g_all = gather_expert(g_low)

    raw = dot(normed_all, w_qkv)
    q_raw, k_raw, v_raw = raw[:, :slab], raw[:, slab : 2 * slab], raw[:, 2 * slab :]
    squares = jnp.stack([jnp.sum(q_raw * q_raw, axis=1), jnp.sum(k_raw * k_raw, axis=1)], axis=0)
    squares = lax.psum(squares * share, "expert")
    inv_qk = lax.rsqrt(squares / width + EPS)
    inv_q, inv_k = inv_qk[0][:, None], inv_qk[1][:, None]
    tables = rope_tables(length)

    def to_heads(values):
        return values.reshape(length, heads, HEAD_DIM)

    queries = rotary(to_heads(q_raw * inv_q * g_query), tables).astype(BF16).transpose(1, 0, 2)
    keys = rotary(to_heads(k_raw * inv_k * g_key), tables).astype(BF16).transpose(1, 0, 2)
    values = to_heads(v_raw).astype(BF16).transpose(1, 0, 2)
    positions = jnp.arange(length, dtype=jnp.int32)
    scale = HEAD_DIM ** (-0.5)

    def head_probs(q, k):
        scores = dot_nt(q, k) * scale
        scores = jnp.where(positions[None, :] <= positions[:, None], scores, NEG)
        exp_terms = jnp.exp(scores - jnp.max(scores, axis=-1, keepdims=True))
        return exp_terms / jnp.sum(exp_terms, axis=-1, keepdims=True)

    mixes = []
    for h in range(heads):
        mixes.append(dot(head_probs(queries[h], keys[h]).astype(BF16), values[h]).astype(BF16))
    mix = jnp.concatenate(mixes, axis=1)
    after_attn = x_in + scatter_expert(dot(mix, w_o) * share)

    inv_ffn = inv_rms(after_attn)
    ffn_low = (after_attn * inv_ffn * g_ffn).astype(BF16)
    ffn_all = gather_expert(ffn_low)
    router_prob = jax.nn.softmax(dot(ffn_low, w_r), axis=-1)
    chosen = routes.reshape(rows, routes.shape[2])
    chosen_mask = jnp.sum(
        (chosen[:, :, None] == jnp.arange(all_experts, dtype=jnp.int32)[None, None, :]).astype(F32),
        axis=1,
    )
    route_dense = router_prob * chosen_mask
    route_all = gather_expert(route_dense)
    route_mine = lax.dynamic_slice(route_all, (0, me * local_experts), (length, local_experts))

    wg, wu, wd = (
        lax.all_gather(w_gate, "dp", axis=1, tiled=True),
        lax.all_gather(w_up, "dp", axis=1, tiled=True),
        lax.all_gather(w_down, "dp", axis=1, tiled=True),
    )
    y_part = 0.0
    dx_part = 0.0
    d_down, d_gate_w, d_up_w, d_weights = [], [], [], []
    for i in range(local_experts):
        weight = route_mine[:, i : i + 1]
        gate = dot(ffn_all, wg[i])
        up = dot(ffn_all, wu[i])
        d_hid = dot_nt(g_all, wd[i])
        sig = jax.nn.sigmoid(gate)
        silu = gate * sig
        hidden = silu * up
        d_weights.append(jnp.sum(hidden * d_hid, axis=1))
        hidden_w = (hidden * weight).astype(BF16)
        d_hid = d_hid * weight
        d_gate = (d_hid * up * sig * (1.0 + gate * (1.0 - sig))).astype(BF16)
        d_up = (d_hid * silu).astype(BF16)
        y_part = y_part + dot(hidden_w, wd[i])
        d_down.append(dot_tn(hidden_w, g_all).astype(BF16))
        d_gate_w.append(dot_tn(ffn_all, d_gate).astype(BF16))
        d_up_w.append(dot_tn(ffn_all, d_up).astype(BF16))
        dx_part = dx_part + dot_nt(d_gate, wg[i]) + dot_nt(d_up, wu[i])
    d_down, d_gate_w, d_up_w = jnp.stack(d_down), jnp.stack(d_gate_w), jnp.stack(d_up_w)

    output = after_attn + scatter_expert(y_part)
    d_rows = scatter_expert(dx_part)
    d_weight = lax.all_to_all(
        jnp.stack(d_weights, axis=0).reshape(local_experts, groups, rows).transpose(1, 0, 2),
        "expert", split_axis=0, concat_axis=0, tiled=True,
    )
    d_router_prob = d_weight.reshape(all_experts, rows).T * chosen_mask

    d_logits = (
        router_prob * (d_router_prob - jnp.sum(d_router_prob * router_prob, axis=-1, keepdims=True))
    ).astype(BF16)
    d_router_w = dot_tn(ffn_low, d_logits)
    d_normed_ffn = d_rows + dot_nt(d_logits, w_r)
    d_after_norm, d_gain_ffn = norm_back(after_attn, inv_ffn, g_ffn, d_normed_ffn)
    d_after = g_low.astype(F32) + d_after_norm
    d_after_all = gather_expert(d_after.astype(BF16))

    d_out_w = dot_tn(mix, d_after_all)
    d_mix = dot_nt(d_after_all, w_o).astype(BF16)
    dqs, dks, dvs = [], [], []
    for h in range(heads):
        prob = head_probs(queries[h], keys[h])
        d_m = d_mix[:, h * HEAD_DIM : (h + 1) * HEAD_DIM]
        d_prob = dot_nt(d_m, values[h])
        row_delta = jnp.sum(d_prob * prob, axis=-1, keepdims=True)
        d_score = (prob * (d_prob - row_delta) * scale).astype(BF16)
        dqs.append(dot(d_score, keys[h]))
        dks.append(dot_tn(d_score, queries[h]))
        dvs.append(dot_tn(prob.astype(BF16), d_m))
    dq_n = rotary_back(jnp.stack(dqs, axis=1), tables).reshape(length, slab)
    dk_n = rotary_back(jnp.stack(dks, axis=1), tables).reshape(length, slab)
    dv_low = jnp.concatenate(dvs, axis=1).astype(BF16)
    dots = jnp.stack(
        [jnp.sum(dq_n * g_query * q_raw, axis=1), jnp.sum(dk_n * g_key * k_raw, axis=1)], axis=0
    )
    dots = lax.psum(dots * share, "expert") / width
    d_gain_query = jnp.sum(dq_n * q_raw * inv_q, axis=0)
    d_gain_key = jnp.sum(dk_n * k_raw * inv_k, axis=0)
    dq_low = (inv_q * dq_n * g_query - q_raw * (inv_q**3 * dots[0][:, None])).astype(BF16)
    dk_low = (inv_k * dk_n * g_key - k_raw * (inv_k**3 * dots[1][:, None])).astype(BF16)
    d_raw = jnp.concatenate([dq_low, dk_low, dv_low], axis=1)
    d_qkv_w = dot_tn(normed_all, d_raw).astype(BF16)
    d_normed_in = scatter_expert(dot_nt(d_raw, w_qkv) * share)
    d_in_norm, d_gain_attn = norm_back(x_in, inv_attn, g_attn, d_normed_in)
    input_grad = d_after + d_in_norm

    d_qkv_w = d_qkv_w.reshape(width, 3, slab)
    d_qkv_w = lax.dynamic_slice(d_qkv_w, (0, 0, offset), (width, 3, own))
    d_qkv_w = lax.psum_scatter(
        d_qkv_w.reshape(width, 3 * own), "dp", scatter_dimension=0, tiled=True
    )
    d_qkv_w = lax.all_to_all(
        d_qkv_w.reshape(groups, block, 3 * own), "expert", split_axis=0, concat_axis=0, tiled=True
    ).reshape(groups, block, 3, own)
    d_qkv_w = d_qkv_w.transpose(2, 1, 0, 3).reshape(3, block, width).astype(F32)
    d_out_w = lax.dynamic_slice(d_out_w.astype(BF16), (offset, 0), (own, width))
    d_out_w = lax.psum_scatter(d_out_w, "dp", scatter_dimension=0, tiled=True)
    d_out_w = lax.ppermute(d_out_w, ("dp", "expert"), [(b, a) for a, b in moves]).astype(F32)

    spread = jnp.zeros((2, width), F32)
    spread = lax.dynamic_update_slice(
        spread, jnp.stack([d_gain_query, d_gain_key]) * share, (0, slab_start)
    )
    small_grad = jnp.concatenate(
        [d_router_w, d_gain_attn[:, None], spread.T, d_gain_ffn[:, None]], axis=1
    )
    small_grad = lax.psum_scatter(small_grad, ("dp", "expert"), scatter_dimension=0, tiled=True)

    expert_owned = [
        lax.psum_scatter(d, "dp", scatter_dimension=1, tiled=True).astype(F32)
        for d in (d_gate_w, d_up_w, d_down)
    ]
    return (
        output.reshape(1, rows, width),
        input_grad.reshape(1, rows, width),
        d_qkv_w[0],
        d_qkv_w[1],
        d_qkv_w[2],
        d_out_w,
        small_grad[:, :all_experts],
        small_grad[:, all_experts],
        small_grad[:, all_experts + 1],
        small_grad[:, all_experts + 2],
        small_grad[:, all_experts + 3],
        *expert_owned,
    )


def solution(mesh):
    tok = P("dp", "expert", None)
    mat = P(("dp", "expert"), None)
    vec = P(("dp", "expert"))
    exp = P("expert", "dp", None)
    return jax.shard_map(
        shards,
        mesh=mesh,
        in_specs=(tok, tok, tok, mat, mat, mat, mat, mat, vec, vec, vec, vec, exp, exp, exp),
        out_specs=(tok, tok, mat, mat, mat, mat, mat, vec, vec, vec, vec, exp, exp, exp),
        check_vma=False,
    )
```

```python
import functools
import math

import jax
import jax.numpy as jnp
from jax import lax
from jax.experimental import pallas as pl
from jax.experimental.pallas import tpu as pltpu
from jax.sharding import PartitionSpec as P

HEADS = 16
HEAD_DIM = 128

EPS = 1e-05
THETA = 10000.0
NEG = -1e30

F32 = jnp.float32
BF16 = jnp.bfloat16


def dot(left, right):
    return jnp.dot(left, right, preferred_element_type=F32)


def dot_tn(left, right):
    return lax.dot_general(left, right, (((0,), (0,)), ((), ())), preferred_element_type=F32)


def dot_nt(left, right):
    return lax.dot_general(left, right, (((1,), (1,)), ((), ())), preferred_element_type=F32)


def inv_rms(values):
    return lax.rsqrt(jnp.mean(values * values, axis=-1, keepdims=True) + EPS)


def norm_back(values, inv, gain_vec, grad):
    scaled = grad * gain_vec
    mean_dot = jnp.mean(scaled * values, axis=-1, keepdims=True)
    d_values = inv * scaled - values * (inv * inv * inv * mean_dot)
    d_gain = jnp.sum(grad * values * inv, axis=0)
    return d_values, d_gain


def rope_tables(length):
    half_dim = HEAD_DIM // 2
    inv_freq = jnp.exp(
        jnp.arange(half_dim, dtype=F32) * (-2.0 * math.log(THETA) / HEAD_DIM)
    )
    angles = jnp.arange(length, dtype=jnp.int32).astype(F32)[:, None] * inv_freq[None, :]
    cosine, sine = jnp.cos(angles), jnp.sin(angles)
    return (
        jnp.concatenate([cosine, cosine], axis=1)[:, None, :],
        jnp.concatenate([-sine, sine], axis=1)[:, None, :],
    )


def swap_halves(values):
    half_dim = HEAD_DIM // 2
    return jnp.concatenate([values[..., half_dim:], values[..., :half_dim]], axis=-1)


def rotary(values, tables):
    return values * tables[0] + swap_halves(values) * tables[1]


def rotary_back(grad, tables):
    return grad * tables[0] - swap_halves(grad) * tables[1]


MESH = pl.DeviceIdType.MESH
VMEM_LIMIT = 56 * 1024 * 1024


def cost_of(micros):
    return pl.CostEstimate(flops=0, bytes_accessed=int(micros * 3.0e6), transcendentals=0)


def flipped(dp, flip):
    return dp + flip - 2 * flip * ((dp // flip) % 2)


class Plane:
    def __init__(self, sends, later, sources, targets, send, recv):
        self.me, self.dp = lax.axis_index("expert"), lax.axis_index("dp")
        self.sends, self.later = sends, later
        self.sources, self.targets, self.send, self.recv = sources, targets, send, recv

    def busy(self):
        return len(self.sends) > 0

    def greet(self, barrier):
        if self.busy():
            for flip in (1, 2):
                pl.semaphore_signal(
                    barrier, inc=1, device_id=(flipped(self.dp, flip), self.me), device_id_type=MESH
                )

    def copy(self, i):
        first = len(self.sends)
        if i < first:
            source, start, size, flip = self.sends[i]
            ref = self.sources[source]
        else:
            source, start, size, flip = self.later[i - first]
            ref = self.targets[source]
        return pltpu.make_async_remote_copy(
            src_ref=ref.at[pl.ds(start, size)],
            dst_ref=self.targets[i],
            send_sem=self.send.at[i],
            recv_sem=self.recv.at[i],
            device_id=(flipped(self.dp, flip), self.me),
            device_id_type=MESH,
        )

    def start(self):
        for i in range(len(self.sends)):
            self.copy(i).start()

    def start_later(self):
        first = len(self.sends)
        for source in sorted({l[0] for l in self.later}):
            self.copy(source).wait_recv()
        for i in range(len(self.later)):
            self.copy(first + i).start()

    def finish(self):
        waited = {l[0] for l in self.later}
        for i in range(len(self.sends) + len(self.later)):
            self.copy(i).wait_send()
            if i not in waited:
                self.copy(i).wait_recv()


def line_greet(me, dp, chip, chips, plane):
    barrier = pltpu.get_barrier_semaphore()
    sibling = chip * 2 + 1 - me % 2
    extra = 2 if plane.busy() else 0
    pl.semaphore_signal(barrier, inc=1, device_id=(dp, sibling), device_id_type=MESH)
    plane.greet(barrier)

    @pl.when(chip > 0)
    def _():
        pl.semaphore_signal(barrier, inc=1, device_id=(dp, me - 2), device_id_type=MESH)

    @pl.when(chip < chips - 1)
    def _():
        pl.semaphore_signal(barrier, inc=1, device_id=(dp, me + 2), device_id_type=MESH)

    @pl.when((chip > 0) & (chip < chips - 1))
    def _():
        pl.semaphore_wait(barrier, 3 + extra)

    @pl.when((chip == 0) | (chip == chips - 1))
    def _():
        pl.semaphore_wait(barrier, 2 + extra)


def gather_body(groups, rows, parts, plane, x_ref, o_ref, own_sem, send, recv, pair_send, pair_recv):
    chips = groups // 2
    me, dp = lax.axis_index("expert"), lax.axis_index("dp")
    chip = me // 2
    sibling = chip * 2 + 1 - me % 2
    part = rows // parts
    line_greet(me, dp, chip, chips, plane)
    keep = pltpu.make_async_copy(x_ref, o_ref.at[pl.ds(pl.multiple_of(me * rows, rows), rows)], own_sem)

    def copy(origin, u, target, send_sem, recv_sem, first):
        place = pl.ds(pl.multiple_of(origin * rows + u * part, part), part)
        return pltpu.make_async_remote_copy(
            src_ref=x_ref.at[pl.ds(u * part, part)] if first else o_ref.at[place],
            dst_ref=o_ref.at[place],
            send_sem=send_sem,
            recv_sem=recv_sem,
            device_id=(dp, target),
            device_id_type=MESH,
        )

    def right(k, u):
        return copy(me - 2 * k, u, me + 2, send.at[0, k, u], recv.at[0, k, u], k == 0)

    def left(k, u):
        return copy(me + 2 * k, u, me - 2, send.at[1, k, u], recv.at[1, k, u], k == 0)

    def pair(side, k, u):
        origin = me - 2 * k if side == 0 else me + 2 * k
        return copy(origin, u, sibling, pair_send.at[side, k, u], pair_recv.at[side, k, u], k == 0)

    sides = lambda k: (
        (0, chip - k >= 0, chip < chips - 1),
        (1, chip + k <= chips - 1, chip > 0),
    )
    for k in range(chips):
        if k == chips - 1:
            plane.start_later()
        for u in range(parts):
            for side, has, send_on in sides(k):
                step = right if side == 0 else left

                @pl.when(has)
                def _(k=k, u=u, side=side, send_on=send_on, step=step):
                    if k > 0:
                        step(k - 1, u).wait_recv()
                    if k < chips - 1:

                        @pl.when(send_on)
                        def _():
                            step(k, u).start()

                    if k > 0:
                        pair(side, k, u).start()

            if k == 0:
                pair(0, 0, u).start()
        if k == 0:
            plane.start()
            keep.start()

    keep.wait()
    for k in range(chips):
        for u in range(parts):
            if k == 0:
                pair(0, 0, u).wait()
            for side, has, send_on in sides(k):
                step = right if side == 0 else left

                @pl.when(has)
                def _(k=k, u=u, side=side, send_on=send_on, step=step):
                    if k < chips - 1:

                        @pl.when(send_on)
                        def _():
                            step(k, u).wait_send()

                    if k > 0:
                        pair(side, k, u).wait()

    plane.finish()


def reduce_body(
    groups, rows, parts, plane, p_ref, o_ref, own, pair, inbox, load_sem, pair_send, pair_recv, send, recv
):
    chips = groups // 2
    me, dp = lax.axis_index("expert"), lax.axis_index("dp")
    chip, core = me // 2, me % 2
    sibling = chip * 2 + 1 - core
    part = rows // parts
    step_rows = 16
    line_greet(me, dp, chip, chips, plane)

    def pair_copy(d):
        place = pl.ds(pl.multiple_of((2 * d + 1 - core) * rows, rows), rows)
        return pltpu.make_async_remote_copy(
            src_ref=p_ref.at[place],
            dst_ref=pair.at[d],
            send_sem=pair_send.at[d],
            recv_sem=pair_recv.at[d],
            device_id=(dp, sibling),
            device_id_type=MESH,
        )

    def own_copy(d):
        place = pl.ds(pl.multiple_of((2 * d + core) * rows, rows), rows)
        return pltpu.make_async_copy(p_ref.at[place], own.at[d], load_sem.at[d])

    order = []
    for j in range((chips + 1) // 2):
        order += [chips - 1 - j] + ([j] if j != chips - 1 - j else [])
    for d in order:
        pair_copy(d).start()
        own_copy(d).start()
    plane.start()

    def hop(d, u, side):
        place = pl.ds(u * part, part)
        target = me + 2 if side == 0 else me - 2
        slot = d if side == 0 else chips + d
        return pltpu.make_async_remote_copy(
            src_ref=own.at[d, place],
            dst_ref=inbox.at[slot, place],
            send_sem=send.at[d, u],
            recv_sem=recv.at[slot, u],
            device_id=(dp, target),
            device_id_type=MESH,
        )

    def add(d, u, slots, store):
        def body(i, carry):
            at = pl.ds(pl.multiple_of(u * part + i * step_rows, step_rows), step_rows)
            value = own[d, at].astype(F32) + pair[d, at].astype(F32)
            for slot in slots:
                value = value + inbox[slot, at].astype(F32)
            store(at, value)
            return carry

        lax.fori_loop(0, part // step_rows, body, 0)

    def forward(d, side):
        pair_copy(d).wait_recv()
        own_copy(d).wait()

        def store(at, value):
            own[d, at] = value.astype(BF16)

        end = chip == (0 if side == 0 else chips - 1)
        for u in range(parts):

            @pl.when(end)
            def _(u=u):
                add(d, u, (), store)

            @pl.when(jnp.logical_not(end))
            def _(u=u):
                hop(d, u, side).wait_recv()
                add(d, u, (d if side == 0 else chips + d,), store)

            hop(d, u, side).start()

    for j in range(chips - 1):
        far, near = chips - 1 - j, j

        @pl.when(far > chip)
        def _(far=far):
            forward(far, 0)

        @pl.when(near < chip)
        def _(near=near):
            forward(near, 1)

        if j == chips - 2:
            plane.start_later()

    pair_copy(chip).wait_recv()
    own_copy(chip).wait()

    def finish(at, value):
        o_ref[at] = value

    for u in range(parts):

        @pl.when(chip == 0)
        def _(u=u):
            hop(chip, u, 1).wait_recv()
            add(chip, u, (chips + chip,), finish)

        @pl.when(chip == chips - 1)
        def _(u=u):
            hop(chip, u, 0).wait_recv()
            add(chip, u, (chip,), finish)

        @pl.when((chip > 0) & (chip < chips - 1))
        def _(u=u):
            hop(chip, u, 0).wait_recv()
            hop(chip, u, 1).wait_recv()
            add(chip, u, (chip, chips + chip), finish)

    for d in range(chips):
        pair_copy(d).wait_send()
        for u in range(parts):

            @pl.when(d > chip)
            def _(d=d, u=u):
                hop(d, u, 0).wait_send()

            @pl.when(d < chip)
            def _(d=d, u=u):
                hop(d, u, 1).wait_send()

    plane.finish()


def exchange_body(count, spread, same, reduce, plane, x_ref, o_ref, box, send, recv):
    me, dp = lax.axis_index("expert"), lax.axis_index("dp")
    groups = lax.axis_size("expert")
    mine = dp * groups + me if spread else me

    def device(index):
        return (index // groups, index % groups) if spread else (dp, index)

    barrier = pltpu.get_barrier_semaphore()

    def hello(s, carry):
        pl.semaphore_signal(
            barrier, inc=1, device_id=device((mine + s) % count), device_id_type=MESH
        )
        return carry

    lax.fori_loop(1, count, hello, 0)
    plane.greet(barrier)
    pl.semaphore_wait(barrier, count - 1 + (2 if plane.busy() else 0))

    def copy(s):
        target = (mine + s) % count
        return pltpu.make_async_remote_copy(
            src_ref=x_ref.at[0] if same else x_ref.at[target],
            dst_ref=box.at[mine],
            send_sem=send.at[s],
            recv_sem=recv.at[s],
            device_id=device(target),
            device_id_type=MESH,
        )

    def start(s, carry):
        copy(s).start()
        return carry

    def wait(s, carry):
        copy(s).wait()
        return carry

    lax.fori_loop(1, count, start, 0)
    plane.start()
    box[mine] = x_ref[0] if same else x_ref[mine]
    lax.fori_loop(1, count, wait, 0)
    if reduce:

        def add(s, total):
            return total + box[s]

        o_ref[...] = lax.fori_loop(1, count, add, box[0])
    else:
        o_ref[...] = box[...]
    plane.start_later()
    plane.finish()


def run(body, name, micros, collective_id, x, x_space, out, out_space, scratch, sends, later):
    arrays, specs = [], []
    for array, start, size, flip in sends:
        found = [i for i, a in enumerate(arrays) if a is array]
        if not found:
            arrays.append(array)
            found = [len(arrays) - 1]
        specs.append((found[0], start, size, flip))
    targets = [jax.ShapeDtypeStruct((s[2],) + s[0].shape[1:], s[0].dtype) for s in sends]
    for source, start, size, flip in later:
        targets.append(jax.ShapeDtypeStruct((size,) + targets[source].shape[1:], targets[source].dtype))
    n_in, n_out = len(arrays), len(targets)

    def kernel(*refs):
        x_ref, sources = refs[0], refs[1 : 1 + n_in]
        o_ref, dests = refs[1 + n_in], refs[2 + n_in : 2 + n_in + n_out]
        rest = refs[2 + n_in + n_out :]
        plane = Plane(specs, later, sources, dests, *rest[:2])
        body(plane, x_ref, o_ref, *rest[2:])

    anywhere = pl.BlockSpec(memory_space=pl.ANY)
    got = pl.pallas_call(
        kernel,
        out_shape=[out] + targets,
        in_specs=[pl.BlockSpec(memory_space=x_space)] + [anywhere] * n_in,
        out_specs=[pl.BlockSpec(memory_space=out_space)] + [anywhere] * n_out,
        scratch_shapes=[pltpu.SemaphoreType.DMA((max(n_out, 1),))] * 2 + scratch,
        compiler_params=pltpu.CompilerParams(
            collective_id=collective_id, has_side_effects=True, vmem_limit_bytes=VMEM_LIMIT
        ),
        cost_estimate=cost_of(micros),
        name=name,
    )(x, *arrays)
    return got if n_out else got[0]


def line_gather(x, collective_id, sends=(), later=(), parts=2):
    rows, width = x.shape
    groups = lax.axis_size("expert")
    shape = (2, groups // 2, parts)
    return run(
        functools.partial(gather_body, groups, rows, parts), "line_gather", 40, collective_id,
        x, pl.ANY, jax.ShapeDtypeStruct((groups * rows, width), x.dtype), pl.ANY,
        [pltpu.SemaphoreType.DMA] + [pltpu.SemaphoreType.DMA(shape)] * 4, sends, later,
    )


def line_reduce(partial, collective_id, sends=(), later=(), parts=2):
    groups = lax.axis_size("expert")
    chips = groups // 2
    rows, width = partial.shape[0] // groups, partial.shape[1]
    return run(
        functools.partial(reduce_body, groups, rows, parts), "line_reduce", 40, collective_id,
        partial.astype(BF16), pl.ANY, jax.ShapeDtypeStruct((rows, width), F32), pltpu.VMEM,
        [
            pltpu.VMEM((chips, rows, width), BF16),
            pltpu.VMEM((chips, rows, width), BF16),
            pltpu.VMEM((2 * chips, rows, width), BF16),
            pltpu.SemaphoreType.DMA((chips,)),
            pltpu.SemaphoreType.DMA((chips,)),
            pltpu.SemaphoreType.DMA((chips,)),
            pltpu.SemaphoreType.DMA((chips, parts)),
            pltpu.SemaphoreType.DMA((2 * chips, parts)),
        ],
        sends, later,
    )


def exchange(x, collective_id, spread=False, same=False, reduce=False, sends=(), later=()):
    count = lax.axis_size("expert") * (lax.axis_size("dp") if spread else 1)
    block = x.shape[1:]
    return run(
        functools.partial(exchange_body, count, spread, same, reduce), "exchange", 8, collective_id,
        x, pltpu.VMEM, jax.ShapeDtypeStruct(block if reduce else (count,) + block, x.dtype), pltpu.VMEM,
        [
            pltpu.VMEM((count,) + block, x.dtype),
            pltpu.SemaphoreType.DMA((count,)),
            pltpu.SemaphoreType.DMA((count,)),
        ],
        sends, later,
    )


def both(array, start=0, size=None):
    size = array.shape[0] if size is None else size
    return [(array, start, size, 1), (array, start, size, 2)]


def swap_dp(block, flip):
    seqs = lax.axis_size("dp")
    return lax.ppermute(block, "dp", [(i, i ^ flip) for i in range(seqs)])


def tie(value, *deps):
    return lax.optimization_barrier((value,) + deps)[0]


def near_dp(block):
    return block, swap_dp(block, 1), swap_dp(block, 2)


def far_dp(near, *deps):
    block, near_x, near_y = near
    half = block.shape[0] // 2
    via_x, via_y = lax.optimization_barrier((near_y[:half], near_x[half:]) + deps)[:2]
    far = jnp.concatenate([swap_dp(via_x, 1), swap_dp(via_y, 2)], axis=0)
    return [block, near_x, near_y, far]


def halves(block):
    half = block.shape[0] // 2
    return [(block, 0, half, 1), (block, half, half, 2)]


def relay(blocks, from_x, from_y):
    _, to_x, to_y, _ = blocks
    half = to_x.shape[0] // 2
    to_x = jnp.concatenate(
        [to_x[:half], (to_x[half:].astype(F32) + from_y.astype(F32)).astype(BF16)], axis=0
    )
    to_y = jnp.concatenate(
        [(to_y[:half].astype(F32) + from_x.astype(F32)).astype(BF16), to_y[half:]], axis=0
    )
    return to_x, to_y


def settle(blocks, from_x, from_y):
    return blocks[0].astype(F32) + from_x.astype(F32) + from_y.astype(F32)


def send_halves(blocks):
    half = blocks[3].shape[0] // 2
    return swap_dp(blocks[3][:half], 1), swap_dp(blocks[3][half:], 2)


def in_order(pieces, index, axis):
    low = (index % 2) == 1
    high = (index // 2) == 1
    a, b, c, d = pieces
    a, b, c, d = (
        jnp.where(low, b, a), jnp.where(low, a, b), jnp.where(low, d, c), jnp.where(low, c, d)
    )
    return jnp.concatenate(
        [jnp.where(high, c, a), jnp.where(high, d, b), jnp.where(high, a, c), jnp.where(high, b, d)],
        axis=axis,
    )


def own_order(array, index, axis):
    return in_order(jnp.split(array, 4, axis=axis), index, axis)


def shards(
    tokens, routes, grad_output, w_query, w_key, w_value, w_out, w_router,
    gain_attn, gain_query, gain_key, gain_ffn, w_gate, w_up, w_down,
):
    rows = tokens.shape[1]
    width = tokens.shape[2]
    groups = lax.axis_size("expert")
    seqs = lax.axis_size("dp")
    me = lax.axis_index("expert")
    length = rows * groups
    local_experts = w_gate.shape[0]
    all_experts = local_experts * groups
    block = w_query.shape[0]
    own = width // groups
    slab = max(own, HEAD_DIM)
    copies = slab // own
    heads = slab // HEAD_DIM
    share = 1.0 / copies
    offset = (me % copies) * own

    x_low = tokens.reshape(rows, width)
    g_low = grad_output.reshape(rows, width)

    my_dp = lax.axis_index("dp")
    small_size = block * (all_experts + 4)
    small_rows = -(-small_size // (16 * 128)) * 16
    small = jnp.concatenate(
        [w_router.reshape(-1), gain_attn, gain_query, gain_key, gain_ffn,
         jnp.zeros((small_rows * 128 - small_size,), BF16)]
    )
    small_all = exchange(small.reshape(1, small_rows, 128), 1, spread=True, same=True)
    small_all = small_all.reshape(seqs * groups, small_rows * 128)
    split = block * all_experts
    w_r = small_all[:, :split].reshape(width, all_experts)
    gains = [
        small_all[:, split + i * block : split + (i + 1) * block].reshape(width).astype(F32)
        for i in range(4)
    ]
    g_attn, g_ffn = gains[0], gains[3]
    slab_start = (me // copies) * slab
    g_query = lax.dynamic_slice(gains[1], (slab_start,), (slab,))
    g_key = lax.dynamic_slice(gains[2], (slab_start,), (slab,))

    qkv_send = jnp.stack([w_query, w_key, w_value], axis=1).reshape(block, 3, width // slab, slab)
    qkv_send = qkv_send.transpose(2, 0, 1, 3).reshape(width // slab, block, 3 * slab)
    qkv_send = jnp.repeat(qkv_send, copies, axis=0)
    qkv_got, gate0_x, gate0_y = exchange(
        tie(qkv_send, small_all), 2, sends=both(w_gate, 0, 1)
    )
    qkv_got = qkv_got.reshape(groups * block, 3 * slab)
    total = seqs * groups
    moves = [(b, (b % seqs) * groups + b // seqs) for b in range(total)]
    o_own = lax.ppermute(tie(w_out, small_all), ("dp", "expert"), moves)

    x_in = x_low.astype(F32)
    inv_attn = inv_rms(x_in)
    normed_low = (x_in * inv_attn * g_attn).astype(BF16)
    half_q, half_o = qkv_got.shape[0] // 2, block // 2
    normed_all, q_x, q_y, o_x, o_y, q_f0, q_f1, o_f0, o_f1 = line_gather(
        tie(normed_low, qkv_got), 3,
        sends=both(qkv_got) + both(o_own),
        later=[(1, 0, half_q, 1), (0, half_q, half_q, 2), (3, 0, half_o, 1), (2, half_o, half_o, 2)],
    )
    w_qkv = in_order([qkv_got, q_x, q_y, jnp.concatenate([q_f0, q_f1], axis=0)], my_dp, 0)
    w_o = in_order([o_own, o_x, o_y, jnp.concatenate([o_f0, o_f1], axis=0)], my_dp, 0)
    if copies > 1:
        sets = [[c * copies + i for i in range(copies)] for c in range(groups // copies)]
        w_o = lax.all_gather(w_o, "expert", axis_index_groups=sets, axis=0, tiled=True)

    gate1 = tie(w_gate[1:2], normed_all)
    gate1_x, gate1_y = swap_dp(gate1, 1), swap_dp(gate1, 2)
    g_all = lax.all_gather(tie(g_low, normed_all), "expert", axis=0, tiled=True)

    raw = dot(normed_all, w_qkv)
    q_raw, k_raw, v_raw = raw[:, :slab], raw[:, slab : 2 * slab], raw[:, 2 * slab :]
    squares = jnp.stack([jnp.sum(q_raw * q_raw, axis=1), jnp.sum(k_raw * k_raw, axis=1)], axis=0)
    squares = exchange(
        (squares * share).reshape(1, 2 * length // 128, 128), 4, same=True, reduce=True
    ).reshape(2, length)
    inv_qk = lax.rsqrt(squares / width + EPS)
    inv_q, inv_k = inv_qk[0][:, None], inv_qk[1][:, None]
    tables = rope_tables(length)

    def to_heads(values):
        return values.reshape(length, heads, HEAD_DIM)

    queries = rotary(to_heads(q_raw * inv_q * g_query), tables).astype(BF16).transpose(1, 0, 2)
    keys = rotary(to_heads(k_raw * inv_k * g_key), tables).astype(BF16).transpose(1, 0, 2)
    values = to_heads(v_raw).astype(BF16).transpose(1, 0, 2)
    positions = jnp.arange(length, dtype=jnp.int32)
    scale = HEAD_DIM ** (-0.5)

    def head_probs(q, k):
        scores = dot_nt(q, k) * scale
        scores = jnp.where(positions[None, :] <= positions[:, None], scores, NEG)
        exp_terms = jnp.exp(scores - jnp.max(scores, axis=-1, keepdims=True))
        return exp_terms / jnp.sum(exp_terms, axis=-1, keepdims=True)

    mixes = []
    for h in range(heads):
        mixes.append(dot(head_probs(queries[h], keys[h]).astype(BF16), values[h]).astype(BF16))
    mix = jnp.concatenate(mixes, axis=1)
    o_sum, gate0_f, gate1_f, up0_x, up0_y = line_reduce(
        dot(mix, w_o) * share, 5,
        sends=[(gate0_y, 0, 1, 1), (gate1_x, 0, 1, 2)] + both(w_up, 0, 1),
    )
    after_attn = x_in + o_sum

    inv_ffn = inv_rms(after_attn)
    ffn_low = (after_attn * inv_ffn * g_ffn).astype(BF16)
    ffn_all, up1_x, up1_y, up0_f, up1_f = line_gather(
        own_order(ffn_low, my_dp, 1), 9,
        sends=both(w_up, 1, 1) + [(up0_y, 0, 1, 1)], later=[(0, 0, 1, 2)],
    )
    router_prob = jax.nn.softmax(dot(ffn_low, w_r), axis=-1)
    chosen = routes.reshape(rows, routes.shape[2])
    chosen_mask = jnp.sum(
        (chosen[:, :, None] == jnp.arange(all_experts, dtype=jnp.int32)[None, None, :]).astype(F32),
        axis=1,
    )
    route_dense = router_prob * chosen_mask
    pad = -local_experts % 8
    route_send = route_dense.T.reshape(groups, local_experts, rows)
    route_send = jnp.pad(route_send, ((0, 0), (0, pad), (0, 0)))
    route_mine = exchange(route_send, 6)[:, :local_experts].transpose(0, 2, 1)
    route_mine = route_mine.reshape(length, local_experts)

    near_down = near_dp(tie(w_down, ffn_all))
    wd = in_order(far_dp(near_down), my_dp, 1)
    wg = [
        jnp.concatenate([own[0], x[0], y[0], f[0]], axis=0)
        for own, x, y, f in (
            (w_gate[0:1], gate0_x, gate0_y, gate0_f), (w_gate[1:2], gate1_x, gate1_y, gate1_f)
        )
    ]
    wu = [
        jnp.concatenate([own[0], x[0], y[0], f[0]], axis=0)
        for own, x, y, f in ((w_up[0:1], up0_x, up0_y, up0_f), (w_up[1:2], up1_x, up1_y, up1_f))
    ]
    cols = jnp.split(ffn_all, 4, axis=1)
    gates, ups, hidden_ws, d_weights, d_gates, d_ups = [], [], [], [], [], []
    d_down, d_gate_w, d_up_w = [], [], []
    for i in range(local_experts):
        gate, up = dot(ffn_all, wg[i]), dot(ffn_all, wu[i])
        gates.append(gate)
        ups.append(up)
        hidden = gate * jax.nn.sigmoid(gate) * up
        hidden_ws.append((hidden * route_mine[:, i : i + 1]).astype(BF16))
        mine = own_order(hidden_ws[i], my_dp, 1)
        d_down.append([dot_tn(h, g_all).astype(BF16) for h in jnp.split(mine, 4, axis=1)])
    d_down = [jnp.stack(b) for b in zip(*d_down)]
    down_x, down_y = send_halves(d_down)
    for i in range(local_experts):
        gate, up = gates[i], ups[i]
        d_hid = dot_nt(g_all, tie(wd, *d_down)[i])
        sig = jax.nn.sigmoid(gate)
        silu = gate * sig
        d_weights.append(jnp.sum(silu * up * d_hid, axis=1))
        d_hid = d_hid * route_mine[:, i : i + 1]
        d_gates.append((d_hid * up * sig * (1.0 + gate * (1.0 - sig))).astype(BF16))
        d_ups.append((d_hid * silu).astype(BF16))
        d_gate_w.append([dot_tn(f, d_gates[i]).astype(BF16) for f in cols])
    d_gate_w = [jnp.stack(b) for b in zip(*d_gate_w)]
    gate_x, gate_y = send_halves(d_gate_w)
    d_gates = [tie(d, *d_gate_w) for d in d_gates]
    dx_part = 0.0
    for i in range(local_experts):
        dx_part = dx_part + dot_nt(d_gates[i], wg[i]) + dot_nt(d_ups[i], wu[i])
    dx_part = dx_part.astype(BF16)
    down_to_x, down_to_y = relay(d_down, down_x, down_y)
    down_fx, down_fy = swap_dp(down_to_x, 1), swap_dp(down_to_y, 2)
    gate_to_x, gate_to_y = relay(d_gate_w, gate_x, gate_y)
    d_rows, gate_fx, gate_fy = line_reduce(
        tie(dx_part, down_to_x, down_to_y), 10,
        sends=[(gate_to_x, 0, 2, 1), (gate_to_y, 0, 2, 2)],
    )
    d_rows = own_order(d_rows, my_dp, 1)
    d_ups = [tie(d, d_rows) for d in d_ups]
    for i in range(local_experts):
        d_up_w.append([dot_tn(f, d_ups[i]).astype(BF16) for f in cols])
    d_up_w = [jnp.stack(b) for b in zip(*d_up_w)]
    y_part = 0.0
    for i in range(local_experts):
        y_part = y_part + dot(tie(hidden_ws[i], d_rows), wd[i])
    y_sum = lax.psum_scatter(y_part.astype(BF16), "expert", scatter_dimension=0, tiled=True)
    output = after_attn + y_sum.astype(F32)
    d_weight = jnp.stack(d_weights, axis=0).reshape(local_experts, groups, rows).transpose(1, 0, 2)
    d_weight = exchange(jnp.pad(d_weight, ((0, 0), (0, pad), (0, 0))), 6)[:, :local_experts]
    d_router_prob = d_weight.reshape(all_experts, rows).T * chosen_mask

    d_logits = (
        router_prob * (d_router_prob - jnp.sum(d_router_prob * router_prob, axis=-1, keepdims=True))
    ).astype(BF16)
    d_router_w = dot_tn(ffn_low, d_logits)
    d_normed_ffn = d_rows + dot_nt(d_logits, w_r)
    d_after_norm, d_gain_ffn = norm_back(after_attn, inv_ffn, g_ffn, d_normed_ffn)
    d_after = g_low.astype(F32) + d_after_norm
    d_after_all, up_x, up_y = line_gather(
        d_after.astype(BF16), 11, sends=halves(d_up_w[3])
    )
    up_to_x, up_to_y = relay(d_up_w, up_x, up_y)
    up_fx, up_fy = swap_dp(up_to_x, 1), swap_dp(up_to_y, 2)

    d_out_w = dot_tn(mix, d_after_all)
    d_mix = dot_nt(d_after_all, w_o).astype(BF16)
    dqs, dks, dvs = [], [], []
    for h in range(heads):
        prob = head_probs(queries[h], keys[h])
        d_m = d_mix[:, h * HEAD_DIM : (h + 1) * HEAD_DIM]
        d_prob = dot_nt(d_m, values[h])
        row_delta = jnp.sum(d_prob * prob, axis=-1, keepdims=True)
        d_score = (prob * (d_prob - row_delta) * scale).astype(BF16)
        dqs.append(dot(d_score, keys[h]))
        dks.append(dot_tn(d_score, queries[h]))
        dvs.append(dot_tn(prob.astype(BF16), d_m))
    dq_n = rotary_back(jnp.stack(dqs, axis=1), tables).reshape(length, slab)
    dk_n = rotary_back(jnp.stack(dks, axis=1), tables).reshape(length, slab)
    dv_low = jnp.concatenate(dvs, axis=1).astype(BF16)
    dots = jnp.stack(
        [jnp.sum(dq_n * g_query * q_raw, axis=1), jnp.sum(dk_n * g_key * k_raw, axis=1)], axis=0
    )
    dots = exchange(
        (dots * share).reshape(1, 2 * length // 128, 128), 4, same=True, reduce=True
    ).reshape(2, length) / width
    d_gain_query = jnp.sum(dq_n * q_raw * inv_q, axis=0)
    d_gain_key = jnp.sum(dk_n * k_raw * inv_k, axis=0)
    dq_low = (inv_q * dq_n * g_query - q_raw * (inv_q**3 * dots[0][:, None])).astype(BF16)
    dk_low = (inv_k * dk_n * g_key - k_raw * (inv_k**3 * dots[1][:, None])).astype(BF16)
    d_raw = jnp.concatenate([dq_low, dk_low, dv_low], axis=1)
    d_qkv_w = dot_tn(normed_all, d_raw).astype(BF16)
    d_qkv_w = d_qkv_w.reshape(width, 3, slab)
    d_qkv_w = lax.dynamic_slice(d_qkv_w, (0, 0, offset), (width, 3, own))
    d_qkv_w = jnp.split(own_order(d_qkv_w.reshape(width, 3 * own), my_dp, 0), 4, axis=0)
    d_out_w = lax.dynamic_slice(d_out_w.astype(BF16), (offset, 0), (own, width))
    d_out_w = jnp.split(own_order(d_out_w, my_dp, 0), 4, axis=0)
    d_normed_in, qkv_x, qkv_y, out_x, out_y = line_reduce(
        dot_nt(d_raw, w_qkv) * share, 12, sends=halves(d_qkv_w[3]) + halves(d_out_w[3])
    )
    d_in_norm, d_gain_attn = norm_back(x_in, inv_attn, g_attn, d_normed_in)
    input_grad = d_after + d_in_norm

    spread = jnp.zeros((2, width), F32)
    spread = lax.dynamic_update_slice(
        spread, jnp.stack([d_gain_query, d_gain_key]) * share, (0, slab_start)
    )
    total = seqs * groups
    small_grad = jnp.concatenate(
        [d_router_w.reshape(total, split)]
        + [v.reshape(total, block) for v in (d_gain_attn, spread[0], spread[1], d_gain_ffn)]
        + [jnp.zeros((total, small_rows * 128 - small_size), F32)],
        axis=1,
    )
    qkv_to_x, qkv_to_y = relay(d_qkv_w, qkv_x, qkv_y)
    out_to_x, out_to_y = relay(d_out_w, out_x, out_y)
    small_grad, qkv_x, qkv_y, out_x, out_y = exchange(
        small_grad.reshape(total, small_rows, 128), 8, spread=True, reduce=True,
        sends=[
            (qkv_to_x, 0, qkv_to_x.shape[0], 1), (qkv_to_y, 0, qkv_to_y.shape[0], 2),
            (out_to_x, 0, out_to_x.shape[0], 1), (out_to_y, 0, out_to_y.shape[0], 2),
        ],
    )
    small_grad = small_grad.reshape(-1)
    d_qkv_w = settle(d_qkv_w, qkv_x, qkv_y).astype(BF16)
    d_qkv_w = exchange(d_qkv_w.reshape(groups, block, 3 * own), 7).reshape(groups, block, 3, own)
    d_qkv_w = d_qkv_w.transpose(2, 1, 0, 3).reshape(3, block, width).astype(F32)
    d_out_w = settle(d_out_w, out_x, out_y).astype(BF16)
    d_out_w = lax.ppermute(d_out_w, ("dp", "expert"), [(b, a) for a, b in moves]).astype(F32)
    expert_owned = [
        settle(d_gate_w, gate_fx, gate_fy),
        settle(d_up_w, up_fx, up_fy),
        settle(d_down, down_fx, down_fy),
    ]

    return (
        output.reshape(1, rows, width),
        input_grad.reshape(1, rows, width),
        d_qkv_w[0],
        d_qkv_w[1],
        d_qkv_w[2],
        d_out_w,
        small_grad[:split].reshape(block, all_experts),
        small_grad[split : split + block],
        small_grad[split + block : split + 2 * block],
        small_grad[split + 2 * block : split + 3 * block],
        small_grad[split + 3 * block : split + 4 * block],
        *expert_owned,
    )


def solution(mesh):
    tok = P("dp", "expert", None)
    mat = P(("dp", "expert"), None)
    vec = P(("dp", "expert"))
    exp = P("expert", "dp", None)
    return jax.shard_map(
        shards,
        mesh=mesh,
        in_specs=(tok, tok, tok, mat, mat, mat, mat, mat, vec, vec, vec, vec, exp, exp, exp),
        out_specs=(tok, tok, mat, mat, mat, mat, mat, vec, vec, vec, vec, exp, exp, exp),
        check_vma=False,
    )
```

```python
import functools
import math

import jax
import jax.numpy as jnp
from jax import lax
from jax.experimental import pallas as pl
from jax.experimental.pallas import tpu as pltpu
from jax.sharding import PartitionSpec as P

HEADS = 16
HEAD_DIM = 128

EPS = 1e-05
THETA = 10000.0
NEG = -1e30

F32 = jnp.float32
BF16 = jnp.bfloat16


def dot(left, right):
    return jnp.dot(left, right, preferred_element_type=F32)


def dot_tn(left, right):
    return lax.dot_general(left, right, (((0,), (0,)), ((), ())), preferred_element_type=F32)


def dot_nt(left, right):
    return lax.dot_general(left, right, (((1,), (1,)), ((), ())), preferred_element_type=F32)


def inv_rms(values):
    return lax.rsqrt(jnp.mean(values * values, axis=-1, keepdims=True) + EPS)


def norm_back(values, inv, gain_vec, grad):
    scaled = grad * gain_vec
    mean_dot = jnp.mean(scaled * values, axis=-1, keepdims=True)
    d_values = inv * scaled - values * (inv * inv * inv * mean_dot)
    d_gain = jnp.sum(grad * values * inv, axis=0)
    return d_values, d_gain


def rope_tables(length):
    half_dim = HEAD_DIM // 2
    inv_freq = jnp.exp(
        jnp.arange(half_dim, dtype=F32) * (-2.0 * math.log(THETA) / HEAD_DIM)
    )
    angles = jnp.arange(length, dtype=jnp.int32).astype(F32)[:, None] * inv_freq[None, :]
    cosine, sine = jnp.cos(angles), jnp.sin(angles)
    return (
        jnp.concatenate([cosine, cosine], axis=1)[:, None, :],
        jnp.concatenate([-sine, sine], axis=1)[:, None, :],
    )


def swap_halves(values):
    half_dim = HEAD_DIM // 2
    return jnp.concatenate([values[..., half_dim:], values[..., :half_dim]], axis=-1)


def rotary(values, tables):
    return values * tables[0] + swap_halves(values) * tables[1]


def rotary_back(grad, tables):
    return grad * tables[0] - swap_halves(grad) * tables[1]


MESH = pl.DeviceIdType.MESH
VMEM_LIMIT = 56 * 1024 * 1024


def cost_of(micros):
    return pl.CostEstimate(flops=0, bytes_accessed=int(micros * 3.0e6), transcendentals=0)


def flipped(dp, flip):
    return dp + flip - 2 * flip * ((dp // flip) % 2)


class Plane:
    def __init__(self, sends, later, sources, targets, send, recv):
        self.me, self.dp = lax.axis_index("expert"), lax.axis_index("dp")
        self.sends, self.later = sends, later
        self.sources, self.targets, self.send, self.recv = sources, targets, send, recv

    def busy(self):
        return len(self.sends) > 0

    def greet(self, barrier):
        if self.busy():
            for flip in (1, 2):
                pl.semaphore_signal(
                    barrier, inc=1, device_id=(flipped(self.dp, flip), self.me), device_id_type=MESH
                )

    def copy(self, i):
        first = len(self.sends)
        if i < first:
            source, start, size, flip = self.sends[i]
            ref = self.sources[source]
        else:
            source, start, size, flip = self.later[i - first]
            ref = self.targets[source]
        return pltpu.make_async_remote_copy(
            src_ref=ref.at[pl.ds(start, size)],
            dst_ref=self.targets[i],
            send_sem=self.send.at[i],
            recv_sem=self.recv.at[i],
            device_id=(flipped(self.dp, flip), self.me),
            device_id_type=MESH,
        )

    def start(self):
        for i in range(len(self.sends)):
            self.copy(i).start()

    def start_later(self):
        first = len(self.sends)
        for source in sorted({l[0] for l in self.later}):
            self.copy(source).wait_recv()
        for i in range(len(self.later)):
            self.copy(first + i).start()

    def finish(self):
        waited = {l[0] for l in self.later}
        for i in range(len(self.sends) + len(self.later)):
            self.copy(i).wait_send()
            if i not in waited:
                self.copy(i).wait_recv()


def line_greet(me, dp, chip, chips, plane):
    barrier = pltpu.get_barrier_semaphore()
    sibling = chip * 2 + 1 - me % 2
    extra = 2 if plane.busy() else 0
    pl.semaphore_signal(barrier, inc=1, device_id=(dp, sibling), device_id_type=MESH)
    plane.greet(barrier)

    @pl.when(chip > 0)
    def _():
        pl.semaphore_signal(barrier, inc=1, device_id=(dp, me - 2), device_id_type=MESH)

    @pl.when(chip < chips - 1)
    def _():
        pl.semaphore_signal(barrier, inc=1, device_id=(dp, me + 2), device_id_type=MESH)

    @pl.when((chip > 0) & (chip < chips - 1))
    def _():
        pl.semaphore_wait(barrier, 3 + extra)

    @pl.when((chip == 0) | (chip == chips - 1))
    def _():
        pl.semaphore_wait(barrier, 2 + extra)


def gather_body(groups, rows, parts, plane, x_ref, o_ref, own_sem, send, recv, pair_send, pair_recv):
    chips = groups // 2
    me, dp = lax.axis_index("expert"), lax.axis_index("dp")
    chip = me // 2
    sibling = chip * 2 + 1 - me % 2
    part = rows // parts
    line_greet(me, dp, chip, chips, plane)
    keep = pltpu.make_async_copy(x_ref, o_ref.at[pl.ds(pl.multiple_of(me * rows, rows), rows)], own_sem)

    def copy(origin, u, target, send_sem, recv_sem, first):
        place = pl.ds(pl.multiple_of(origin * rows + u * part, part), part)
        return pltpu.make_async_remote_copy(
            src_ref=x_ref.at[pl.ds(u * part, part)] if first else o_ref.at[place],
            dst_ref=o_ref.at[place],
            send_sem=send_sem,
            recv_sem=recv_sem,
            device_id=(dp, target),
            device_id_type=MESH,
        )

    def right(k, u):
        return copy(me - 2 * k, u, me + 2, send.at[0, k, u], recv.at[0, k, u], k == 0)

    def left(k, u):
        return copy(me + 2 * k, u, me - 2, send.at[1, k, u], recv.at[1, k, u], k == 0)

    def pair(side, k, u):
        origin = me - 2 * k if side == 0 else me + 2 * k
        return copy(origin, u, sibling, pair_send.at[side, k, u], pair_recv.at[side, k, u], k == 0)

    sides = lambda k: (
        (0, chip - k >= 0, chip < chips - 1),
        (1, chip + k <= chips - 1, chip > 0),
    )
    for k in range(chips):
        if k == chips - 1:
            plane.start_later()
        for u in range(parts):
            for side, has, send_on in sides(k):
                step = right if side == 0 else left

                @pl.when(has)
                def _(k=k, u=u, side=side, send_on=send_on, step=step):
                    if k > 0:
                        step(k - 1, u).wait_recv()
                    if k < chips - 1:

                        @pl.when(send_on)
                        def _():
                            step(k, u).start()

                    if k > 0:
                        pair(side, k, u).start()

            if k == 0:
                pair(0, 0, u).start()
        if k == 0:
            plane.start()
            keep.start()

    keep.wait()
    for k in range(chips):
        for u in range(parts):
            if k == 0:
                pair(0, 0, u).wait()
            for side, has, send_on in sides(k):
                step = right if side == 0 else left

                @pl.when(has)
                def _(k=k, u=u, side=side, send_on=send_on, step=step):
                    if k < chips - 1:

                        @pl.when(send_on)
                        def _():
                            step(k, u).wait_send()

                    if k > 0:
                        pair(side, k, u).wait()

    plane.finish()


def reduce_body(
    groups, rows, parts, plane, p_ref, o_ref, own, pair, inbox, load_sem, pair_send, pair_recv, send, recv
):
    chips = groups // 2
    me, dp = lax.axis_index("expert"), lax.axis_index("dp")
    chip, core = me // 2, me % 2
    sibling = chip * 2 + 1 - core
    part = rows // parts
    step_rows = 16
    line_greet(me, dp, chip, chips, plane)

    def pair_copy(d):
        place = pl.ds(pl.multiple_of((2 * d + 1 - core) * rows, rows), rows)
        return pltpu.make_async_remote_copy(
            src_ref=p_ref.at[place],
            dst_ref=pair.at[d],
            send_sem=pair_send.at[d],
            recv_sem=pair_recv.at[d],
            device_id=(dp, sibling),
            device_id_type=MESH,
        )

    def own_copy(d):
        place = pl.ds(pl.multiple_of((2 * d + core) * rows, rows), rows)
        return pltpu.make_async_copy(p_ref.at[place], own.at[d], load_sem.at[d])

    order = []
    for j in range((chips + 1) // 2):
        order += [chips - 1 - j] + ([j] if j != chips - 1 - j else [])
    for d in order:
        pair_copy(d).start()
        own_copy(d).start()
    plane.start()

    def hop(d, u, side):
        place = pl.ds(u * part, part)
        target = me + 2 if side == 0 else me - 2
        slot = d if side == 0 else chips + d
        return pltpu.make_async_remote_copy(
            src_ref=own.at[d, place],
            dst_ref=inbox.at[slot, place],
            send_sem=send.at[d, u],
            recv_sem=recv.at[slot, u],
            device_id=(dp, target),
            device_id_type=MESH,
        )

    def add(d, u, slots, store):
        def body(i, carry):
            at = pl.ds(pl.multiple_of(u * part + i * step_rows, step_rows), step_rows)
            value = own[d, at].astype(F32) + pair[d, at].astype(F32)
            for slot in slots:
                value = value + inbox[slot, at].astype(F32)
            store(at, value)
            return carry

        lax.fori_loop(0, part // step_rows, body, 0)

    def forward(d, side):
        pair_copy(d).wait_recv()
        own_copy(d).wait()

        def store(at, value):
            own[d, at] = value.astype(BF16)

        end = chip == (0 if side == 0 else chips - 1)
        for u in range(parts):

            @pl.when(end)
            def _(u=u):
                add(d, u, (), store)

            @pl.when(jnp.logical_not(end))
            def _(u=u):
                hop(d, u, side).wait_recv()
                add(d, u, (d if side == 0 else chips + d,), store)

            hop(d, u, side).start()

    for j in range(chips - 1):
        far, near = chips - 1 - j, j

        @pl.when(far > chip)
        def _(far=far):
            forward(far, 0)

        @pl.when(near < chip)
        def _(near=near):
            forward(near, 1)

        if j == chips - 2:
            plane.start_later()

    pair_copy(chip).wait_recv()
    own_copy(chip).wait()

    def finish(at, value):
        o_ref[at] = value

    for u in range(parts):

        @pl.when(chip == 0)
        def _(u=u):
            hop(chip, u, 1).wait_recv()
            add(chip, u, (chips + chip,), finish)

        @pl.when(chip == chips - 1)
        def _(u=u):
            hop(chip, u, 0).wait_recv()
            add(chip, u, (chip,), finish)

        @pl.when((chip > 0) & (chip < chips - 1))
        def _(u=u):
            hop(chip, u, 0).wait_recv()
            hop(chip, u, 1).wait_recv()
            add(chip, u, (chip, chips + chip), finish)

    for d in range(chips):
        pair_copy(d).wait_send()
        for u in range(parts):

            @pl.when(d > chip)
            def _(d=d, u=u):
                hop(d, u, 0).wait_send()

            @pl.when(d < chip)
            def _(d=d, u=u):
                hop(d, u, 1).wait_send()

    plane.finish()


def exchange_body(count, spread, same, reduce, plane, x_ref, o_ref, box, send, recv):
    me, dp = lax.axis_index("expert"), lax.axis_index("dp")
    groups = lax.axis_size("expert")
    mine = dp * groups + me if spread else me

    def device(index):
        return (index // groups, index % groups) if spread else (dp, index)

    barrier = pltpu.get_barrier_semaphore()

    def hello(s, carry):
        pl.semaphore_signal(
            barrier, inc=1, device_id=device((mine + s) % count), device_id_type=MESH
        )
        return carry

    lax.fori_loop(1, count, hello, 0)
    plane.greet(barrier)
    pl.semaphore_wait(barrier, count - 1 + (2 if plane.busy() else 0))

    def copy(s):
        target = (mine + s) % count
        return pltpu.make_async_remote_copy(
            src_ref=x_ref.at[0] if same else x_ref.at[target],
            dst_ref=box.at[mine],
            send_sem=send.at[s],
            recv_sem=recv.at[s],
            device_id=device(target),
            device_id_type=MESH,
        )

    def start(s, carry):
        copy(s).start()
        return carry

    def wait(s, carry):
        copy(s).wait()
        return carry

    lax.fori_loop(1, count, start, 0)
    plane.start()
    box[mine] = x_ref[0] if same else x_ref[mine]
    lax.fori_loop(1, count, wait, 0)
    if reduce:

        def add(s, total):
            return total + box[s]

        o_ref[...] = lax.fori_loop(1, count, add, box[0])
    else:
        o_ref[...] = box[...]
    plane.start_later()
    plane.finish()


def run(
    body, name, micros, collective_id, x, x_space, out, out_space, scratch, sends, later, carry=(), after=()
):
    arrays, specs = [], []
    for array, start, size, flip in sends:
        found = [i for i, a in enumerate(arrays) if a is array]
        if not found:
            arrays.append(array)
            found = [len(arrays) - 1]
        specs.append((found[0], start, size, flip))
    targets = [jax.ShapeDtypeStruct((s[2],) + s[0].shape[1:], s[0].dtype) for s in sends]
    for source, start, size, flip in later:
        targets.append(jax.ShapeDtypeStruct((size,) + targets[source].shape[1:], targets[source].dtype))
    n_in, n_out, held = len(arrays), len(targets), len(carry)

    def kernel(*refs):
        x_ref, sources = refs[0], refs[1 : 1 + n_in]
        refs = refs[1 + n_in + held + len(after) :]
        o_ref, dests = refs[0], refs[1 : 1 + n_out]
        rest = refs[1 + n_out + held :]
        plane = Plane(specs, later, sources, dests, *rest[:2])
        body(plane, x_ref, o_ref, *rest[2:])

    anywhere = pl.BlockSpec(memory_space=pl.ANY)
    got = pl.pallas_call(
        kernel,
        out_shape=[out] + targets + [jax.ShapeDtypeStruct(c.shape, c.dtype) for c in carry],
        in_specs=[pl.BlockSpec(memory_space=x_space)] + [anywhere] * (n_in + held + len(after)),
        out_specs=[pl.BlockSpec(memory_space=out_space)] + [anywhere] * (n_out + held),
        input_output_aliases={1 + n_in + i: 1 + n_out + i for i in range(held)},
        scratch_shapes=[pltpu.SemaphoreType.DMA((max(n_out, 1),))] * 2 + scratch,
        compiler_params=pltpu.CompilerParams(
            collective_id=collective_id, has_side_effects=True, vmem_limit_bytes=VMEM_LIMIT
        ),
        cost_estimate=cost_of(micros),
        name=name,
    )(x, *arrays, *carry, *after)
    return got if n_out + held else got[0]


def line_gather(x, collective_id, sends=(), later=(), after=(), parts=2):
    rows, width = x.shape
    groups = lax.axis_size("expert")
    shape = (2, groups // 2, parts)
    return run(
        functools.partial(gather_body, groups, rows, parts), "line_gather", 40, collective_id,
        x, pl.ANY, jax.ShapeDtypeStruct((groups * rows, width), x.dtype), pl.ANY,
        [pltpu.SemaphoreType.DMA] + [pltpu.SemaphoreType.DMA(shape)] * 4, sends, later, (), after,
    )


def line_reduce(partial, collective_id, sends=(), later=(), after=(), parts=2):
    groups = lax.axis_size("expert")
    chips = groups // 2
    rows, width = partial.shape[0] // groups, partial.shape[1]
    return run(
        functools.partial(reduce_body, groups, rows, parts), "line_reduce", 40, collective_id,
        partial.astype(BF16), pl.ANY, jax.ShapeDtypeStruct((rows, width), F32), pltpu.VMEM,
        [
            pltpu.VMEM((chips, rows, width), BF16),
            pltpu.VMEM((chips, rows, width), BF16),
            pltpu.VMEM((2 * chips, rows, width), BF16),
            pltpu.SemaphoreType.DMA((chips,)),
            pltpu.SemaphoreType.DMA((chips,)),
            pltpu.SemaphoreType.DMA((chips,)),
            pltpu.SemaphoreType.DMA((chips, parts)),
            pltpu.SemaphoreType.DMA((2 * chips, parts)),
        ],
        sends, later, (), after,
    )


def exchange(
    x, collective_id, spread=False, same=False, reduce=False, sends=(), later=(), carry=()
):
    count = lax.axis_size("expert") * (lax.axis_size("dp") if spread else 1)
    block = x.shape[1:]
    return run(
        functools.partial(exchange_body, count, spread, same, reduce), "exchange", 8, collective_id,
        x, pltpu.VMEM, jax.ShapeDtypeStruct(block if reduce else (count,) + block, x.dtype), pltpu.VMEM,
        [
            pltpu.VMEM((count,) + block, x.dtype),
            pltpu.SemaphoreType.DMA((count,)),
            pltpu.SemaphoreType.DMA((count,)),
        ],
        sends, later, carry,
    )


LANES = 128
TILE = 512


def expert_first_body(
    groups, seqs, rows, width, ff, experts, parts,
    x_ref, g_ref, gate_ref, up_ref, down_ref, near_refs,
    f_out, hid_out, sg_out, su_out, tail_out, down_out,
    f_buf, g_buf, wg, wu, wd, hid, sg, su, tail_buf, tail_sum,
    line_send, line_recv, side_send, side_recv, own_sem, f_sem, w_sem, d_sem, g_sem, out_sem, tail_sem,
    plane_send, plane_recv,
):
    chips = groups // 2
    me, dp = lax.axis_index("expert"), lax.axis_index("dp")
    chip, core = me // 2, me % 2
    sibling = chip * 2 + 1 - core
    chunk = 2 * rows
    part = rows // parts
    depth, wide_ff = width // seqs, ff // seqs

    def remote(src, dst, send_sem, recv_sem, device):
        return pltpu.make_async_remote_copy(
            src_ref=src, dst_ref=dst, send_sem=send_sem, recv_sem=recv_sem,
            device_id=device, device_id_type=MESH,
        )

    def at(index, size):
        return pl.ds(pl.multiple_of(index * size, size), size)

    def neighbour(flip):
        return (flipped(dp, flip), me)

    barrier = pltpu.get_barrier_semaphore()
    pl.semaphore_signal(barrier, inc=1, device_id=(dp, sibling), device_id_type=MESH)
    for flip in (1, 2):
        pl.semaphore_signal(barrier, inc=1, device_id=neighbour(flip), device_id_type=MESH)

    @pl.when(chip > 0)
    def _():
        pl.semaphore_signal(barrier, inc=1, device_id=(dp, me - 2), device_id_type=MESH)

    @pl.when(chip < chips - 1)
    def _():
        pl.semaphore_signal(barrier, inc=1, device_id=(dp, me + 2), device_id_type=MESH)

    @pl.when((chip > 0) & (chip < chips - 1))
    def _():
        pl.semaphore_wait(barrier, 5)

    @pl.when((chip == 0) | (chip == chips - 1))
    def _():
        pl.semaphore_wait(barrier, 4)

    def row_copy(origin, u, target, send_sem, recv_sem, first):
        place = pl.ds(pl.multiple_of(origin * rows + u * part, part), part)
        return remote(
            x_ref.at[pl.ds(u * part, part)] if first else f_buf.at[place], f_buf.at[place],
            send_sem, recv_sem, (dp, target),
        )

    def step(side, k, u):
        origin, target = (me - 2 * k, me + 2) if side == 0 else (me + 2 * k, me - 2)
        return row_copy(origin, u, target, line_send.at[side, k, u], line_recv.at[side, k, u], k == 0)

    def aside(side, k, u):
        origin = me - 2 * k if side == 0 else me + 2 * k
        return row_copy(origin, u, sibling, side_send.at[side, k, u], side_recv.at[side, k, u], k == 0)

    def sides(k):
        return (
            (0, chip - k >= 0, chip < chips - 1),
            (1, chip + k <= chips - 1, chip > 0),
        )

    keep = pltpu.make_async_copy(x_ref, f_buf.at[at(me, rows)], own_sem)

    def rows_out(c):
        return pltpu.make_async_copy(
            f_buf.at[at(c, chunk), pl.ds(0, width)], f_out.at[at(c, chunk)], f_sem.at[c]
        )

    def plane_copy(i):
        e, flip = (i // 2, i % 2 + 1) if i < 4 else (i - 4, i - 3)
        if i < 4:
            src, dst = down_ref.at[e], wd.at[e, at(dp, wide_ff)]
        else:
            src = wd.at[e, at(flipped(dp, 3 - flip), wide_ff)]
            dst = src
        return remote(src, dst, plane_send.at[i], plane_recv.at[i], neighbour(flip))

    owners = (dp, flipped(dp, 1), flipped(dp, 2), flipped(flipped(dp, 1), 2))

    def weight_copies():
        copies = []
        for m, (own, buf) in enumerate(((gate_ref, wg), (up_ref, wu))):
            for e in range(experts):
                near = near_refs[4 * m : 4 * m + 4]
                pieces = [own.at[e], near[0].at[e], near[1].at[e], near[2 + e].at[0]]
                for q, piece in enumerate(pieces):
                    copies.append(
                        pltpu.make_async_copy(
                            piece, buf.at[at(owners[q], depth), pl.ds(e * ff, ff)],
                            w_sem.at[m, e, q],
                        )
                    )
        return copies

    def down_copies():
        return [
            pltpu.make_async_copy(down_ref.at[e], wd.at[e, at(dp, wide_ff)], d_sem.at[e])
            for e in range(experts)
        ]

    def grad_rows(r):
        return pltpu.make_async_copy(
            g_ref.at[pl.ds((r % chips) * chunk, chunk)], g_buf.at[r % 2], g_sem.at[r % 2]
        )

    def first_layer(c):
        place = at(c, chunk)

        def tile(t, carry):
            cols = at(t, TILE)
            gate = dot(f_buf[place, pl.ds(0, width)], wg[:, cols])
            up = dot(f_buf[place, pl.ds(0, width)], wu[:, cols])
            sig = 1.0 / (1.0 + jnp.exp(-gate))
            silu = gate * sig
            hid[place, cols] = (silu * up).astype(BF16)
            sg[place, cols] = (up * sig * (1.0 + gate * (1.0 - sig))).astype(BF16)
            su[place, cols] = silu.astype(BF16)
            return carry

        lax.fori_loop(0, experts * ff // TILE, tile, 0)

    def ready(k):
        for u in range(parts):
            if k == 0:
                aside(0, 0, u).wait_recv()
            else:
                for side, has, _ in sides(k):

                    @pl.when(has)
                    def _(side=side, u=u):
                        aside(side, k, u).wait_recv()

        if k == 0:
            rows_out(chip).start()
            first_layer(chip)
        else:
            for side, has, _ in sides(k):
                c = chip - k if side == 0 else chip + k

                @pl.when(has)
                def _(c=c):
                    rows_out(c).start()
                    first_layer(c)

    for k in range(chips):
        for u in range(parts):
            for side, has, send_on in sides(k):

                @pl.when(has)
                def _(k=k, u=u, side=side, send_on=send_on):
                    if k > 0:
                        step(side, k - 1, u).wait_recv()
                    if k < chips - 1:

                        @pl.when(send_on)
                        def _():
                            step(side, k, u).start()

                    if k > 0:
                        aside(side, k, u).start()

            if k == 0:
                aside(0, 0, u).start()
        if k == 0:
            for i in range(4):
                plane_copy(i).start()
            keep.start()
            for copy in weight_copies():
                copy.start()
            for copy in down_copies():
                copy.start()
            grad_rows(0).start()
            keep.wait()
            for copy in weight_copies():
                copy.wait()
        if k > 0:
            ready(k - 1)
    plane_copy(1).wait_recv()
    plane_copy(4).start()
    ready(chips - 1)
    plane_copy(2).wait_recv()
    plane_copy(5).start()

    for copy in down_copies():
        copy.wait()
    for i in (0, 3):
        plane_copy(i).wait_recv()

    def outs(r):
        place = pl.ds(r * chunk, chunk)
        return [
            pltpu.make_async_copy(buf.at[place], out.at[place], out_sem.at[i, r])
            for i, (buf, out) in enumerate(((hid, hid_out), (sg, sg_out), (su, su_out)))
        ]

    lane = lax.broadcasted_iota(jnp.int32, (chunk, LANES), 1)

    def back(r, first, last):
        place = pl.ds(r * chunk, chunk)
        extra = f_buf[place, pl.ds(width, LANES)].astype(F32)
        tail = jnp.zeros((chunk, LANES), F32) if first == 0 else tail_sum[place, :]
        for e in range(experts):
            which = me * experts + e
            low = which + LANES // 2
            weight = jnp.sum(
                jnp.where((lane == which) | (lane == low), extra, 0.0), axis=1, keepdims=True
            )
            for owner in owners[first:last]:
                d_hid = dot_nt(g_buf[r % 2], wd[e, at(owner, wide_ff), :])
                cols = pl.ds(pl.multiple_of(e * ff + owner * wide_ff, wide_ff), wide_ff)
                hidden = hid[place, cols].astype(F32)
                d_weight = jnp.sum(hidden * d_hid, axis=1, keepdims=True)
                tail = tail + jnp.where(lane == which, d_weight, 0.0)
                d_hid = d_hid * weight
                hid[place, cols] = (hidden * weight).astype(BF16)
                sg[place, cols] = (d_hid * sg[place, cols].astype(F32)).astype(BF16)
                su[place, cols] = (d_hid * su[place, cols].astype(F32)).astype(BF16)
        if last < len(owners):
            tail_sum[place, :] = tail
        else:
            high = tail.astype(BF16).astype(F32)
            tail_buf[place, :] = (high + pltpu.roll(tail - high, LANES // 2, 1)).astype(BF16)

    for r in range(chips):
        grad_rows(r + 1 if r + 1 < chips else chips).start()
        grad_rows(r).wait()
        back(r, 0, 3)
    for i in (4, 5):
        plane_copy(i).wait_recv()
    keep_down = pltpu.make_async_copy(wd, down_out, d_sem.at[experts])
    keep_down.start()
    for r in range(chips):
        if r + 1 < chips:
            grad_rows(chips + r + 1).start()
        grad_rows(chips + r).wait()
        back(r, 3, 4)
        for copy in outs(r):
            copy.start()
    keep_tail = pltpu.make_async_copy(tail_buf, tail_out, tail_sem)
    keep_tail.start()
    keep_tail.wait()
    keep_down.wait()
    for k in range(chips):
        for u in range(parts):
            if k == 0:
                aside(0, 0, u).wait_send()
            for side, has, send_on in sides(k):

                @pl.when(has)
                def _(k=k, u=u, side=side, send_on=send_on):
                    if k < chips - 1:

                        @pl.when(send_on)
                        def _():
                            step(side, k, u).wait_send()

                    if k > 0:
                        aside(side, k, u).wait_send()

    for i in range(6):
        plane_copy(i).wait_send()
    for d in range(chips):
        rows_out(d).wait()
        for copy in outs(d):
            copy.wait()


def expert_first(x, g_all, w_gate, w_up, w_down, near, collective_id, parts=2):
    groups, seqs = lax.axis_size("expert"), lax.axis_size("dp")
    chips = groups // 2
    rows, wide = x.shape
    length, width = g_all.shape
    experts, _, ff = w_gate.shape
    n = len(near)

    def kernel(*refs):
        expert_first_body(
            groups, seqs, rows, width, ff, experts, parts, *refs[:5], refs[5 : 5 + n], *refs[5 + n :]
        )

    anywhere = pl.BlockSpec(memory_space=pl.ANY)
    dma = pltpu.SemaphoreType.DMA
    flat = jax.ShapeDtypeStruct((length, experts * ff), BF16)
    return pl.pallas_call(
        kernel,
        out_shape=[
            jax.ShapeDtypeStruct((length, width), BF16), flat, flat, flat,
            jax.ShapeDtypeStruct((length, LANES), BF16),
            jax.ShapeDtypeStruct((experts, ff, width), BF16),
        ],
        in_specs=[anywhere] * (5 + n),
        out_specs=[anywhere] * 6,
        scratch_shapes=[
            pltpu.VMEM((length, wide), BF16),
            pltpu.VMEM((2, 2 * rows, width), BF16),
            pltpu.VMEM((width, experts * ff), BF16),
            pltpu.VMEM((width, experts * ff), BF16),
            pltpu.VMEM((experts, ff, width), BF16),
            pltpu.VMEM((length, experts * ff), BF16),
            pltpu.VMEM((length, experts * ff), BF16),
            pltpu.VMEM((length, experts * ff), BF16),
            pltpu.VMEM((length, LANES), BF16),
            pltpu.VMEM((length, LANES), F32),
            dma((2, chips, parts)), dma((2, chips, parts)), dma((2, chips, parts)), dma((2, chips, parts)),
            dma, dma((chips,)), dma((2, experts, 4)), dma((experts + 1,)), dma((2,)), dma((3, chips)), dma,
            dma((6,)), dma((6,)),
        ],
        compiler_params=pltpu.CompilerParams(
            collective_id=collective_id, has_side_effects=True, vmem_limit_bytes=VMEM_LIMIT
        ),
        cost_estimate=cost_of(70),
        name="expert_first",
    )(x, g_all, w_gate, w_up, w_down, *near)


def expert_second_body(
    groups, seqs, rows, width, ff, experts, parts,
    hid_ref, sg_ref, su_ref, tail_ref, down_ref, gate_ref, up_ref, near_refs, y_out, o_ref,
    wg, wu, wd, hid, sg, su, tail_buf, acc, pair_in, inbox, last, y_buf,
    in_sem, w_sem, y_sem, pair_send, pair_recv, hop_send, hop_recv, last_recv,
):
    chips = groups // 2
    me, dp = lax.axis_index("expert"), lax.axis_index("dp")
    chip, core = me // 2, me % 2
    sibling = chip * 2 + 1 - core
    chunk = 2 * rows
    part = rows // parts
    depth = width // seqs

    def remote(src, dst, send_sem, recv_sem, device):
        return pltpu.make_async_remote_copy(
            src_ref=src, dst_ref=dst, send_sem=send_sem, recv_sem=recv_sem,
            device_id=device, device_id_type=MESH,
        )

    def at(index, size):
        return pl.ds(pl.multiple_of(index * size, size), size)

    owners = (dp, flipped(dp, 1), flipped(dp, 2), flipped(flipped(dp, 1), 2))
    loads = [
        pltpu.make_async_copy(src, dst, in_sem.at[i])
        for i, (src, dst) in enumerate(
            ((sg_ref, sg), (su_ref, su), (tail_ref, tail_buf), (hid_ref, hid), (down_ref, wd))
        )
    ]
    weights = []
    for m, (own, buf) in enumerate(((gate_ref, wg), (up_ref, wu))):
        for e in range(experts):
            near = near_refs[4 * m : 4 * m + 4]
            pieces = [own.at[e], near[0].at[e], near[1].at[e], near[2 + e].at[0]]
            for q, piece in enumerate(pieces):
                weights.append(
                    pltpu.make_async_copy(
                        piece, buf.at[at(owners[q], depth), pl.ds(e * ff, ff)], w_sem.at[m, e, q]
                    )
                )
    for copy in loads[:3] + weights + loads[3:]:
        copy.start()
    line_greet(me, dp, chip, chips, Plane((), (), (), (), None, None))
    for copy in loads[:3] + weights:
        copy.wait()
    for r in range(chips):
        for half in range(2):
            acc[r, half, :, pl.ds(width, LANES)] = tail_buf[pl.ds(r * chunk + half * rows, rows), :]

    out_tile = 256

    def row_grads(d):
        place = at(d, chunk)

        def tile(t, carry):
            cols = at(t, out_tile)
            value = dot_nt(sg[place, :], wg[cols, :]) + dot_nt(su[place, :], wu[cols, :])
            value = value.astype(BF16)
            acc[d, 0, :, cols] = value[:rows]
            acc[d, 1, :, cols] = value[rows:]
            return carry

        lax.fori_loop(0, width // out_tile, tile, 0)

    def pair_copy(d):
        return remote(acc.at[d, 1 - core], pair_in.at[d], pair_send.at[d], pair_recv.at[d], (dp, sibling))

    def hop(d, u, kind):
        place = pl.ds(u * part, part)
        if kind == 0:
            return remote(
                acc.at[d, core, place], inbox.at[d, place], hop_send.at[d, u], hop_recv.at[d, u],
                (dp, me + 2),
            )
        if kind == 1:
            return remote(
                acc.at[d, core, place], inbox.at[d, place], hop_send.at[d, u], hop_recv.at[d, u],
                (dp, me - 2),
            )
        return remote(
            acc.at[d, core, place], last.at[place], hop_send.at[d, u], last_recv.at[u], (dp, me - 2)
        )

    step_rows = 16

    def add(d, u, more, store):
        def body(i, carry):
            here = pl.ds(pl.multiple_of(u * part + i * step_rows, step_rows), step_rows)
            value = acc[d, core, here].astype(F32) + pair_in[d, here].astype(F32)
            for ref in more:
                value = value + ref[here].astype(F32)
            store(here, value)
            return carry

        lax.fori_loop(0, part // step_rows, body, 0)

    def forward(d):
        pair_copy(d).wait_recv()

        def store(here, value):
            acc[d, core, here] = value.astype(BF16)

        source = ((d > chip) & (chip == 0)) | ((d < chip) & (chip == chips - 1))
        for u in range(parts):

            @pl.when(source)
            def _(u=u):
                add(d, u, (), store)

            @pl.when(jnp.logical_not(source))
            def _(u=u):
                hop(d, u, 0).wait_recv()
                add(d, u, (inbox.at[d],), store)

            @pl.when(d > chip)
            def _(u=u):
                hop(d, u, 0).start()

            @pl.when((d < chip) & (d != chip - 1))
            def _(u=u):
                hop(d, u, 1).start()

            @pl.when((d < chip) & (d == chip - 1))
            def _(u=u):
                hop(d, u, 2).start()

    upper = chip // (chips // 2)
    mirrored = chip + upper * (chips - 1 - 2 * chip)

    def goal(j):
        turn = (j + mirrored) // (chips - 1)
        d = (1 - turn) * (chips - 1 - j) + turn * (j + mirrored - (chips - 1))
        return d + upper * (chips - 1 - 2 * d)

    edge = (chip == 0) | (chip == chips - 1)

    def mix_copy(r):
        return pltpu.make_async_copy(y_buf.at[r % 2], y_out.at[pl.ds(r * chunk, chunk)], y_sem.at[r % 2])

    def mix(r):
        if r >= 2:
            mix_copy(r - 2).wait()

        def tile(t, carry):
            cols = at(t, TILE)
            value = jnp.zeros((chunk, TILE), F32)
            for e in range(experts):
                value = value + dot(hid[pl.ds(r * chunk, chunk), pl.ds(e * ff, ff)], wd[e, :, cols])
            y_buf[r % 2, :, cols] = value.astype(BF16)
            return carry

        lax.fori_loop(0, width // TILE, tile, 0)
        mix_copy(r).start()

    for j in range(chips):
        row_grads(goal(j))
        pair_copy(goal(j)).start()
        if j > 0:

            @pl.when(edge)
            def _(j=j):
                forward(goal(j - 1))

    for copy in loads[3:]:
        copy.wait()
    for j in range(chips):
        if j < chips - 1:

            @pl.when(jnp.logical_not(edge))
            def _(j=j):
                forward(goal(j))

        mix(j)

    pair_copy(chip).wait_recv()

    def finish(here, value):
        o_ref[here] = value

    for u in range(parts):

        @pl.when(chip == 0)
        def _(u=u):
            hop(chip, u, 2).wait_recv()
            add(chip, u, (last,), finish)

        @pl.when(chip == chips - 1)
        def _(u=u):
            hop(chip, u, 0).wait_recv()
            add(chip, u, (inbox.at[chip],), finish)

        @pl.when((chip > 0) & (chip < chips - 1))
        def _(u=u):
            hop(chip, u, 0).wait_recv()
            hop(chip, u, 2).wait_recv()
            add(chip, u, (inbox.at[chip], last), finish)

    for d in range(chips):
        pair_copy(d).wait_send()
        for u in range(parts):

            @pl.when(d != chip)
            def _(d=d, u=u):
                hop(d, u, 0).wait_send()

    for r in range(max(chips - 2, 0), chips):
        mix_copy(r).wait()


def expert_second(hid, sg, su, tail, w_down, w_gate, w_up, near, before, collective_id, parts=2):
    groups, seqs = lax.axis_size("expert"), lax.axis_size("dp")
    chips = groups // 2
    length = hid.shape[0]
    rows = length // groups
    experts, ff, width = w_down.shape
    wide = width + LANES
    n = len(near)

    def kernel(*refs):
        expert_second_body(
            groups, seqs, rows, width, ff, experts, parts, *refs[:7], refs[7 : 7 + n],
            *refs[8 + n : 10 + n], *refs[11 + n :],
        )

    anywhere = pl.BlockSpec(memory_space=pl.ANY)
    dma = pltpu.SemaphoreType.DMA
    return pl.pallas_call(
        kernel,
        out_shape=[
            jax.ShapeDtypeStruct((length, width), BF16),
            jax.ShapeDtypeStruct((rows, wide), F32),
            jax.ShapeDtypeStruct(sg.shape, BF16),
        ],
        in_specs=[anywhere] * (8 + n),
        out_specs=[anywhere, pl.BlockSpec(memory_space=pltpu.VMEM), anywhere],
        input_output_aliases={1: 2},
        scratch_shapes=[
            pltpu.VMEM((width, experts * ff), BF16),
            pltpu.VMEM((width, experts * ff), BF16),
            pltpu.VMEM((experts, ff, width), BF16),
            pltpu.VMEM((length, experts * ff), BF16),
            pltpu.VMEM((length, experts * ff), BF16),
            pltpu.VMEM((length, experts * ff), BF16),
            pltpu.VMEM((length, LANES), BF16),
            pltpu.VMEM((chips, 2, rows, wide), BF16),
            pltpu.VMEM((chips, rows, wide), BF16),
            pltpu.VMEM((chips, rows, wide), BF16),
            pltpu.VMEM((rows, wide), BF16),
            pltpu.VMEM((2, 2 * rows, width), BF16),
            dma((5,)), dma((2, experts, 4)), dma((2,)), dma((chips,)), dma((chips,)),
            dma((chips, parts)), dma((chips, parts)), dma((parts,)),
        ],
        compiler_params=pltpu.CompilerParams(
            collective_id=collective_id, has_side_effects=True, vmem_limit_bytes=VMEM_LIMIT
        ),
        cost_estimate=cost_of(60),
        name="expert_second",
    )(hid, sg, su, tail, w_down, w_gate, w_up, *near, before)


def spread_body(groups, copies, slab, plane, q_ref, k_ref, v_ref, o_ref, own_sem, send, recv):
    me, dp = lax.axis_index("expert"), lax.axis_index("dp")
    block = q_ref.shape[0]
    barrier = pltpu.get_barrier_semaphore()
    for s in range(1, groups):
        pl.semaphore_signal(
            barrier, inc=1, device_id=(dp, (me + s) % groups), device_id_type=MESH
        )
    plane.greet(barrier)
    pl.semaphore_wait(barrier, groups - 1 + (2 if plane.busy() else 0))
    half = groups // 2
    place = pl.ds(pl.multiple_of((me % half) * block, block), block)
    copies_out = []
    for s in range(1, groups):
        peer = (me + s) % groups
        for m, ref in enumerate((q_ref, k_ref, v_ref)):
            cols = pl.ds(pl.multiple_of((peer // copies) * slab, slab), slab)
            copies_out.append(
                pltpu.make_async_remote_copy(
                    src_ref=ref.at[:, cols],
                    dst_ref=o_ref.at[me // half, m, place],
                    send_sem=send.at[s, m],
                    recv_sem=recv.at[s, m],
                    device_id=(dp, peer),
                    device_id_type=MESH,
                )
            )
    for copy in copies_out:
        copy.start()
    plane.start()
    own = []
    for m, ref in enumerate((q_ref, k_ref, v_ref)):
        cols = pl.ds(pl.multiple_of((me // copies) * slab, slab), slab)
        own.append(
            pltpu.make_async_copy(ref.at[:, cols], o_ref.at[me // half, m, place], own_sem.at[m])
        )
    for copy in own:
        copy.start()
    for copy in own + copies_out:
        copy.wait()
    plane.finish()


def spread_columns(w_query, w_key, w_value, copies, slab, collective_id, sends):
    groups = lax.axis_size("expert")
    block = w_query.shape[0]
    arrays, specs = [], []
    for array, start, size, flip in sends:
        arrays.append(array)
        specs.append((len(arrays) - 1, start, size, flip))
    targets = [jax.ShapeDtypeStruct((s[2],) + s[0].shape[1:], s[0].dtype) for s in sends]
    n = len(sends)

    def kernel(q_ref, k_ref, v_ref, *refs):
        plane = Plane(specs, (), refs[:n], refs[n + 1 : 2 * n + 1], *refs[2 * n + 1 : 2 * n + 3])
        spread_body(groups, copies, slab, plane, q_ref, k_ref, v_ref, refs[n], *refs[2 * n + 3 :])

    anywhere = pl.BlockSpec(memory_space=pl.ANY)
    dma = pltpu.SemaphoreType.DMA
    return pl.pallas_call(
        kernel,
        out_shape=[jax.ShapeDtypeStruct((2, 3, groups // 2 * block, slab), BF16)] + targets,
        in_specs=[anywhere] * (3 + n),
        out_specs=[anywhere] * (1 + n),
        scratch_shapes=[dma((max(n, 1),)), dma((max(n, 1),)), dma((3,)), dma((groups, 3)), dma((groups, 3))],
        compiler_params=pltpu.CompilerParams(collective_id=collective_id, has_side_effects=True),
        cost_estimate=cost_of(20),
        name="spread_columns",
    )(w_query, w_key, w_value, *arrays)


def both(array, start=0, size=None):
    size = array.shape[0] if size is None else size
    return [(array, start, size, 1), (array, start, size, 2)]


def swap_dp(block, flip):
    seqs = lax.axis_size("dp")
    return lax.ppermute(block, "dp", [(i, i ^ flip) for i in range(seqs)])


def tie(value, *deps):
    return lax.optimization_barrier((value,) + deps)[0]


def near_dp(block):
    return block, swap_dp(block, 1), swap_dp(block, 2)


def far_dp(near, *deps):
    block, near_x, near_y = near
    half = block.shape[0] // 2
    via_x, via_y = lax.optimization_barrier((near_y[:half], near_x[half:]) + deps)[:2]
    far = jnp.concatenate([swap_dp(via_x, 1), swap_dp(via_y, 2)], axis=0)
    return [block, near_x, near_y, far]


def halves(block):
    half = block.shape[0] // 2
    return [(block, 0, half, 1), (block, half, half, 2)]


def relay(blocks, from_x, from_y):
    _, to_x, to_y, _ = blocks
    half = to_x.shape[0] // 2
    to_x = jnp.concatenate(
        [to_x[:half], (to_x[half:].astype(F32) + from_y.astype(F32)).astype(BF16)], axis=0
    )
    to_y = jnp.concatenate(
        [(to_y[:half].astype(F32) + from_x.astype(F32)).astype(BF16), to_y[half:]], axis=0
    )
    return to_x, to_y


def settle(blocks, from_x, from_y):
    return blocks[0].astype(F32) + from_x.astype(F32) + from_y.astype(F32)


def send_halves(blocks):
    half = blocks[3].shape[0] // 2
    return swap_dp(blocks[3][:half], 1), swap_dp(blocks[3][half:], 2)


def in_order(pieces, index, axis):
    low = (index % 2) == 1
    high = (index // 2) == 1
    a, b, c, d = pieces
    a, b, c, d = (
        jnp.where(low, b, a), jnp.where(low, a, b), jnp.where(low, d, c), jnp.where(low, c, d)
    )
    return jnp.concatenate(
        [jnp.where(high, c, a), jnp.where(high, d, b), jnp.where(high, a, c), jnp.where(high, b, d)],
        axis=axis,
    )


def own_order(array, index, axis):
    return in_order(jnp.split(array, 4, axis=axis), index, axis)


def shards(
    tokens, routes, grad_output, w_query, w_key, w_value, w_out, w_router,
    gain_attn, gain_query, gain_key, gain_ffn, w_gate, w_up, w_down,
):
    rows = tokens.shape[1]
    width = tokens.shape[2]
    groups = lax.axis_size("expert")
    seqs = lax.axis_size("dp")
    me = lax.axis_index("expert")
    length = rows * groups
    local_experts = w_gate.shape[0]
    all_experts = local_experts * groups
    block = w_query.shape[0]
    own = width // groups
    slab = max(own, HEAD_DIM)
    copies = slab // own
    heads = slab // HEAD_DIM
    share = 1.0 / copies
    offset = (me % copies) * own

    x_low = tokens.reshape(rows, width)
    g_low = grad_output.reshape(rows, width)

    my_dp = lax.axis_index("dp")
    small_size = block * (all_experts + 4)
    small_rows = -(-small_size // (16 * 128)) * 16
    small = jnp.concatenate(
        [w_router.reshape(-1), gain_attn, gain_query, gain_key, gain_ffn,
         jnp.zeros((small_rows * 128 - small_size,), BF16)]
    )
    small_all = exchange(small.reshape(1, small_rows, 128), 1, spread=True, same=True)
    small_all = small_all.reshape(seqs * groups, small_rows * 128)
    split = block * all_experts
    w_r = small_all[:, :split].reshape(width, all_experts)
    gains = [
        small_all[:, split + i * block : split + (i + 1) * block].reshape(width).astype(F32)
        for i in range(4)
    ]
    g_attn, g_ffn = gains[0], gains[3]
    slab_start = (me // copies) * slab
    g_query = lax.dynamic_slice(gains[1], (slab_start,), (slab,))
    g_key = lax.dynamic_slice(gains[2], (slab_start,), (slab,))

    near_gate = tie(w_gate, small_all)
    gate_x, gate_y = swap_dp(near_gate, 1), swap_dp(near_gate, 2)
    (qkv_got,) = spread_columns(tie(w_query, small_all), w_key, w_value, copies, slab, 2, ())
    total = seqs * groups
    moves = [(b, (b % seqs) * groups + b // seqs) for b in range(total)]
    o_own = lax.ppermute(tie(w_out, small_all), ("dp", "expert"), moves)

    x_in = x_low.astype(F32)
    inv_attn = inv_rms(x_in)
    normed_low = (x_in * inv_attn * g_attn).astype(BF16)
    half_o = block // 2
    normed_all, q_x, q_y, o_x, o_y, q_f0, q_f1, o_f0, o_f1 = line_gather(
        tie(normed_low, qkv_got), 3,
        sends=both(qkv_got) + both(o_own),
        later=[(1, 0, 1, 1), (0, 1, 1, 2), (3, 0, half_o, 1), (2, half_o, half_o, 2)],
    )
    qkv_pieces = [qkv_got, q_x, q_y, jnp.concatenate([q_f0, q_f1], axis=0)]
    w_qkv = jnp.concatenate(
        [in_order([p[:, m].reshape(-1, slab) for p in qkv_pieces], my_dp, 0) for m in range(3)], axis=1
    )
    w_o = in_order([o_own, o_x, o_y, jnp.concatenate([o_f0, o_f1], axis=0)], my_dp, 0)
    if copies > 1:
        sets = [[c * copies + i for i in range(copies)] for c in range(groups // copies)]
        w_o = lax.all_gather(w_o, "expert", axis_index_groups=sets, axis=0, tiled=True)

    near_up = tie(w_up, normed_all)
    up_x, up_y = swap_dp(near_up, 1), swap_dp(near_up, 2)
    g_all = lax.all_gather(g_low, "expert", axis=0, tiled=True)

    raw = dot(normed_all, w_qkv)
    q_raw, k_raw, v_raw = raw[:, :slab], raw[:, slab : 2 * slab], raw[:, 2 * slab :]
    squares = jnp.stack([jnp.sum(q_raw * q_raw, axis=1), jnp.sum(k_raw * k_raw, axis=1)], axis=0)
    squares = exchange(
        (squares * share).reshape(1, 2 * length // 128, 128), 4, same=True, reduce=True
    ).reshape(2, length)
    inv_qk = lax.rsqrt(squares / width + EPS)
    inv_q, inv_k = inv_qk[0][:, None], inv_qk[1][:, None]
    tables = rope_tables(length)

    def to_heads(values):
        return values.reshape(length, heads, HEAD_DIM)

    queries = rotary(to_heads(q_raw * inv_q * g_query), tables).astype(BF16).transpose(1, 0, 2)
    keys = rotary(to_heads(k_raw * inv_k * g_key), tables).astype(BF16).transpose(1, 0, 2)
    values = to_heads(v_raw).astype(BF16).transpose(1, 0, 2)
    positions = jnp.arange(length, dtype=jnp.int32)
    scale = HEAD_DIM ** (-0.5)

    def head_probs(q, k):
        scores = dot_nt(q, k) * scale
        scores = jnp.where(positions[None, :] <= positions[:, None], scores, NEG)
        exp_terms = jnp.exp(scores - jnp.max(scores, axis=-1, keepdims=True))
        return exp_terms / jnp.sum(exp_terms, axis=-1, keepdims=True)

    mixes = []
    for h in range(heads):
        mixes.append(dot(head_probs(queries[h], keys[h]).astype(BF16), values[h]).astype(BF16))
    mix = jnp.concatenate(mixes, axis=1)
    o_sum, gate0_f, gate1_f, up0_f, up1_f = line_reduce(
        dot(mix, w_o) * share, 5,
        sends=[(gate_y, 0, 1, 1), (gate_x, 1, 1, 2), (up_y, 0, 1, 1), (up_x, 1, 1, 2)],
    )
    after_attn = x_in + o_sum

    inv_ffn = inv_rms(after_attn)
    ffn_low = (after_attn * inv_ffn * g_ffn).astype(BF16)
    router_prob = jax.nn.softmax(dot(ffn_low, w_r), axis=-1)
    chosen = routes.reshape(rows, routes.shape[2])
    chosen_mask = jnp.sum(
        (chosen[:, :, None] == jnp.arange(all_experts, dtype=jnp.int32)[None, None, :]).astype(F32),
        axis=1,
    )
    route_dense = router_prob * chosen_mask
    gate_near = [gate_x, gate_y, gate0_f, gate1_f]
    up_near = [up_x, up_y, up0_f, up1_f]
    ff = w_gate.shape[2]
    if copies == 1 and length * width <= 1 << 21:
        high = lax.reduce_precision(route_dense, 8, 7)
        space = jnp.zeros((rows, LANES // 2 - all_experts), F32)
        extra = jnp.concatenate([high, space, route_dense - high, space], axis=1).astype(BF16)
        ffn_all, hidden_w, d_gate, d_up, tail, wd = expert_first(
            jnp.concatenate([ffn_low, extra], axis=1), g_all, w_gate, w_up, w_down,
            gate_near + up_near, 9,
        )
        d_down = dot_tn(hidden_w, g_all).astype(BF16)
        y_part, d_rows, d_gate = expert_second(
            hidden_w, d_gate, d_up, tail, wd, w_gate, w_up, gate_near + up_near, d_down, 13
        )
        d_weight = d_rows[:, width : width + LANES]
        d_weight = d_weight[:, :all_experts] + d_weight[:, LANES // 2 : LANES // 2 + all_experts]
        d_rows = d_rows[:, :width]
    else:
        ffn_all = line_gather(ffn_low, 3)
        pad = -local_experts % 8
        route_send = route_dense.T.reshape(groups, local_experts, rows)
        route_send = jnp.pad(route_send, ((0, 0), (0, pad), (0, 0)))
        route_mine = exchange(route_send, 6)[:, :local_experts].transpose(0, 2, 1)
        route_mine = route_mine.reshape(length, local_experts)
        near_down = near_dp(tie(w_down, ffn_all))
        wd = in_order(far_dp(near_down), my_dp, 1)
        hidden_w, d_gate, d_up, d_weights = [], [], [], []
        y_part, dx_part = 0.0, 0.0
        for i in range(local_experts):
            wg, wu = (
                in_order([own[i], near[0][i], near[1][i], near[2 + i][0]], my_dp, 0)
                for own, near in ((w_gate, gate_near), (w_up, up_near))
            )
            weight = route_mine[:, i : i + 1]
            gate, up = dot(ffn_all, wg), dot(ffn_all, wu)
            d_hid = dot_nt(g_all, wd[i])
            sig = jax.nn.sigmoid(gate)
            silu = gate * sig
            d_weights.append(jnp.sum(silu * up * d_hid, axis=1))
            hidden_w.append((silu * up * weight).astype(BF16))
            d_hid = d_hid * weight
            d_gate.append((d_hid * up * sig * (1.0 + gate * (1.0 - sig))).astype(BF16))
            d_up.append((d_hid * silu).astype(BF16))
            y_part = y_part + dot(hidden_w[i], wd[i])
            dx_part = dx_part + dot_nt(d_gate[i], wg) + dot_nt(d_up[i], wu)
            (ffn_all, y_part, dx_part) = lax.optimization_barrier((ffn_all, y_part, dx_part))
        hidden_w, d_gate, d_up = (jnp.concatenate(a, axis=1) for a in (hidden_w, d_gate, d_up))
        y_part = y_part.astype(BF16)
        d_down = dot_tn(hidden_w, g_all).astype(BF16)
        d_rows = line_reduce(dx_part, 10)
        d_weight = jnp.stack(d_weights, axis=0).reshape(local_experts, groups, rows)
        d_weight = jnp.pad(d_weight.transpose(1, 0, 2), ((0, 0), (0, pad), (0, 0)))
        d_weight = exchange(d_weight, 6)[:, :local_experts].reshape(all_experts, rows).T

    own_down = lax.psum_scatter(
        d_down.reshape(local_experts, ff, width), "dp", scatter_dimension=1, tiled=True
    )

    def in_grad(grad):
        product = dot_tn(ffn_all, grad).astype(BF16)
        return product, lax.psum_scatter(product, "dp", scatter_dimension=0, tiled=True)

    def to_experts(own_grad):
        return jnp.stack([own_grad[:, i * ff : (i + 1) * ff] for i in range(local_experts)]).astype(F32)

    d_gate_w, own_gate = in_grad(d_gate)
    d_router_prob = d_weight * chosen_mask

    d_logits = (
        router_prob * (d_router_prob - jnp.sum(d_router_prob * router_prob, axis=-1, keepdims=True))
    ).astype(BF16)
    d_router_w = dot_tn(ffn_low, d_logits)
    d_normed_ffn = d_rows + dot_nt(d_logits, w_r)
    d_after_norm, d_gain_ffn = norm_back(after_attn, inv_ffn, g_ffn, d_normed_ffn)
    d_after = g_low.astype(F32) + d_after_norm
    d_after_all = line_gather(d_after.astype(BF16), 11, after=[own_down, d_gate_w])
    d_out_w = dot_tn(mix, d_after_all)
    d_mix = dot_nt(d_after_all, w_o).astype(BF16)
    dqs, dks, dvs = [], [], []
    for h in range(heads):
        prob = head_probs(queries[h], keys[h])
        d_m = d_mix[:, h * HEAD_DIM : (h + 1) * HEAD_DIM]
        d_prob = dot_nt(d_m, values[h])
        row_delta = jnp.sum(d_prob * prob, axis=-1, keepdims=True)
        d_score = (prob * (d_prob - row_delta) * scale).astype(BF16)
        dqs.append(dot(d_score, keys[h]))
        dks.append(dot_tn(d_score, queries[h]))
        dvs.append(dot_tn(prob.astype(BF16), d_m))
    dq_n = rotary_back(jnp.stack(dqs, axis=1), tables).reshape(length, slab)
    dk_n = rotary_back(jnp.stack(dks, axis=1), tables).reshape(length, slab)
    dv_low = jnp.concatenate(dvs, axis=1).astype(BF16)
    dots = jnp.stack(
        [jnp.sum(dq_n * g_query * q_raw, axis=1), jnp.sum(dk_n * g_key * k_raw, axis=1)], axis=0
    )
    dots, d_up = exchange(
        (dots * share).reshape(1, 2 * length // 128, 128), 14, same=True, reduce=True, carry=[d_up]
    )
    dots = dots.reshape(2, length) / width
    d_up_w, own_up = in_grad(d_up)
    d_gain_query = jnp.sum(dq_n * q_raw * inv_q, axis=0)
    d_gain_key = jnp.sum(dk_n * k_raw * inv_k, axis=0)
    dq_low = (inv_q * dq_n * g_query - q_raw * (inv_q**3 * dots[0][:, None])).astype(BF16)
    dk_low = (inv_k * dk_n * g_key - k_raw * (inv_k**3 * dots[1][:, None])).astype(BF16)
    d_raw = jnp.concatenate([dq_low, dk_low, dv_low], axis=1)
    d_qkv_w = dot_tn(normed_all, d_raw).astype(BF16)
    d_qkv_w = d_qkv_w.reshape(width, 3, slab)
    d_qkv_w = lax.dynamic_slice(d_qkv_w, (0, 0, offset), (width, 3, own))
    d_qkv_w = jnp.split(own_order(d_qkv_w.reshape(width, 3 * own), my_dp, 0), 4, axis=0)
    d_out_w = lax.dynamic_slice(d_out_w.astype(BF16), (offset, 0), (own, width))
    d_out_w = jnp.split(own_order(d_out_w, my_dp, 0), 4, axis=0)
    d_normed_in, qkv_x, qkv_y, out_x, out_y = line_reduce(
        dot_nt(d_raw, w_qkv) * share, 12, sends=halves(d_qkv_w[3]) + halves(d_out_w[3]),
        after=[own_gate, d_up_w],
    )
    d_in_norm, d_gain_attn = norm_back(x_in, inv_attn, g_attn, d_normed_in)
    input_grad = d_after + d_in_norm

    spread = jnp.zeros((2, width), F32)
    spread = lax.dynamic_update_slice(
        spread, jnp.stack([d_gain_query, d_gain_key]) * share, (0, slab_start)
    )
    total = seqs * groups
    small_grad = jnp.concatenate(
        [d_router_w.reshape(total, split)]
        + [v.reshape(total, block) for v in (d_gain_attn, spread[0], spread[1], d_gain_ffn)]
        + [jnp.zeros((total, small_rows * 128 - small_size), F32)],
        axis=1,
    )
    qkv_to_x, qkv_to_y = relay(d_qkv_w, qkv_x, qkv_y)
    out_to_x, out_to_y = relay(d_out_w, out_x, out_y)
    y_sum, qkv_x, qkv_y, out_x, out_y = line_reduce(
        tie(y_part, d_normed_in), 15,
        sends=[
            (qkv_to_x, 0, qkv_to_x.shape[0], 1), (qkv_to_y, 0, qkv_to_y.shape[0], 2),
            (out_to_x, 0, out_to_x.shape[0], 1), (out_to_y, 0, out_to_y.shape[0], 2),
        ],
    )
    output = after_attn + y_sum
    small_grad = exchange(small_grad.reshape(total, small_rows, 128), 8, spread=True, reduce=True)
    small_grad = small_grad.reshape(-1)
    d_qkv_w = settle(d_qkv_w, qkv_x, qkv_y).astype(BF16)
    d_qkv_w = exchange(d_qkv_w.reshape(groups, block, 3 * own), 7).reshape(groups, block, 3, own)
    d_qkv_w = d_qkv_w.transpose(2, 1, 0, 3).reshape(3, block, width).astype(F32)
    d_out_w = settle(d_out_w, out_x, out_y).astype(BF16)
    d_out_w = lax.ppermute(d_out_w, ("dp", "expert"), [(b, a) for a, b in moves]).astype(F32)
    expert_owned = [to_experts(own_gate), to_experts(own_up), own_down.astype(F32)]
    return (
        output.reshape(1, rows, width),
        input_grad.reshape(1, rows, width),
        d_qkv_w[0],
        d_qkv_w[1],
        d_qkv_w[2],
        d_out_w,
        small_grad[:split].reshape(block, all_experts),
        small_grad[split : split + block],
        small_grad[split + block : split + 2 * block],
        small_grad[split + 2 * block : split + 3 * block],
        small_grad[split + 3 * block : split + 4 * block],
        *expert_owned,
    )


def solution(mesh):
    tok = P("dp", "expert", None)
    mat = P(("dp", "expert"), None)
    vec = P(("dp", "expert"))
    exp = P("expert", "dp", None)
    return jax.shard_map(
        shards,
        mesh=mesh,
        in_specs=(tok, tok, tok, mat, mat, mat, mat, mat, vec, vec, vec, vec, exp, exp, exp),
        out_specs=(tok, tok, mat, mat, mat, mat, mat, vec, vec, vec, vec, exp, exp, exp),
        check_vma=False,
    )
```

```python
import functools
import math

import jax
import jax.numpy as jnp
from jax import lax
from jax.experimental import pallas as pl
from jax.experimental.pallas import tpu as pltpu
from jax.sharding import PartitionSpec as P

HEADS = 16
HEAD_DIM = 128

EPS = 1e-05
THETA = 10000.0
NEG = -1e30

F32 = jnp.float32
BF16 = jnp.bfloat16


def dot(left, right):
    return jnp.dot(left, right, preferred_element_type=F32)


def dot_tn(left, right):
    return lax.dot_general(left, right, (((0,), (0,)), ((), ())), preferred_element_type=F32)


def dot_nt(left, right):
    return lax.dot_general(left, right, (((1,), (1,)), ((), ())), preferred_element_type=F32)


def inv_rms(values):
    return lax.rsqrt(jnp.mean(values * values, axis=-1, keepdims=True) + EPS)


def norm_back(values, inv, gain_vec, grad):
    scaled = grad * gain_vec
    mean_dot = jnp.mean(scaled * values, axis=-1, keepdims=True)
    d_values = inv * scaled - values * (inv * inv * inv * mean_dot)
    d_gain = jnp.sum(grad * values * inv, axis=0)
    return d_values, d_gain


def rope_tables(length):
    half_dim = HEAD_DIM // 2
    inv_freq = jnp.exp(
        jnp.arange(half_dim, dtype=F32) * (-2.0 * math.log(THETA) / HEAD_DIM)
    )
    angles = jnp.arange(length, dtype=jnp.int32).astype(F32)[:, None] * inv_freq[None, :]
    cosine, sine = jnp.cos(angles), jnp.sin(angles)
    return (
        jnp.concatenate([cosine, cosine], axis=1)[:, None, :],
        jnp.concatenate([-sine, sine], axis=1)[:, None, :],
    )


def swap_halves(values):
    half_dim = HEAD_DIM // 2
    return jnp.concatenate([values[..., half_dim:], values[..., :half_dim]], axis=-1)


def rotary(values, tables):
    return values * tables[0] + swap_halves(values) * tables[1]


def rotary_back(grad, tables):
    return grad * tables[0] - swap_halves(grad) * tables[1]


MESH = pl.DeviceIdType.MESH
VMEM_LIMIT = 56 * 1024 * 1024


def cost_of(micros):
    return pl.CostEstimate(flops=0, bytes_accessed=int(micros * 3.0e6), transcendentals=0)


def flipped(dp, flip):
    return dp + flip - 2 * flip * ((dp // flip) % 2)


class Whole:
    def __init__(self, source, target, own_sem, send, recv):
        self.me, self.dp = lax.axis_index("expert"), lax.axis_index("dp")
        self.source, self.target = source, target
        self.own_sem, self.send, self.recv = own_sem, send, recv
        self.rows = source.shape[0]
        half = self.rows // 2
        self.split = (half, half) if half % 16 == 0 else (self.rows, 0)

    def place(self, owner, start, size):
        return self.target.at[pl.ds(pl.multiple_of(owner * self.rows, self.rows) + start, size)]

    def keep(self):
        return pltpu.make_async_copy(self.source, self.place(self.dp, 0, self.rows), self.own_sem)

    def copy(self, i):
        flip = i % 2 + 1
        if i < 2:
            src, dst = self.source, self.place(self.dp, 0, self.rows)
        else:
            start = 0 if i == 2 else self.split[0]
            src = dst = self.place(flipped(self.dp, 3 - flip), start, self.split[i - 2])
        return pltpu.make_async_remote_copy(
            src_ref=src, dst_ref=dst, send_sem=self.send.at[i], recv_sem=self.recv.at[i],
            device_id=(flipped(self.dp, flip), self.me), device_id_type=MESH,
        )

    def start(self):
        self.copy(0).start()
        self.copy(1).start()
        self.keep().start()

    def start_later(self):
        self.copy(1).wait_recv()
        self.copy(2).start()
        self.copy(0).wait_recv()
        if self.split[1]:
            self.copy(3).start()

    def finish(self):
        self.keep().wait()
        for i in range(4 if self.split[1] else 3):
            self.copy(i).wait_send()
            if i >= 2:
                self.copy(i).wait_recv()


class Plane:
    def __init__(self, sends, later, sources, targets, send, recv, wholes=()):
        self.me, self.dp = lax.axis_index("expert"), lax.axis_index("dp")
        self.sends, self.later, self.wholes = sends, later, wholes
        self.sources, self.targets, self.send, self.recv = sources, targets, send, recv

    def busy(self):
        return len(self.sends) + len(self.wholes) > 0

    def greet(self, barrier):
        if self.busy():
            for flip in (1, 2):
                pl.semaphore_signal(
                    barrier, inc=1, device_id=(flipped(self.dp, flip), self.me), device_id_type=MESH
                )

    def copy(self, i):
        first = len(self.sends)
        if i < first:
            source, start, size, flip = self.sends[i]
            ref = self.sources[source]
        else:
            source, start, size, flip = self.later[i - first]
            ref = self.targets[source]
        return pltpu.make_async_remote_copy(
            src_ref=ref.at[pl.ds(start, size)],
            dst_ref=self.targets[i],
            send_sem=self.send.at[i],
            recv_sem=self.recv.at[i],
            device_id=(flipped(self.dp, flip), self.me),
            device_id_type=MESH,
        )

    def start(self):
        for whole in self.wholes:
            whole.start()
        for i in range(len(self.sends)):
            self.copy(i).start()

    def start_later(self):
        first = len(self.sends)
        for source in sorted({l[0] for l in self.later}):
            self.copy(source).wait_recv()
        for i in range(len(self.later)):
            self.copy(first + i).start()
        for whole in self.wholes:
            whole.start_later()

    def finish(self):
        for whole in self.wholes:
            whole.finish()
        waited = {l[0] for l in self.later}
        for i in range(len(self.sends) + len(self.later)):
            self.copy(i).wait_send()
            if i not in waited:
                self.copy(i).wait_recv()


def line_greet(me, dp, chip, chips, plane):
    barrier = pltpu.get_barrier_semaphore()
    sibling = chip * 2 + 1 - me % 2
    extra = 2 if plane.busy() else 0
    pl.semaphore_signal(barrier, inc=1, device_id=(dp, sibling), device_id_type=MESH)
    plane.greet(barrier)

    @pl.when(chip > 0)
    def _():
        pl.semaphore_signal(barrier, inc=1, device_id=(dp, me - 2), device_id_type=MESH)

    @pl.when(chip < chips - 1)
    def _():
        pl.semaphore_signal(barrier, inc=1, device_id=(dp, me + 2), device_id_type=MESH)

    @pl.when((chip > 0) & (chip < chips - 1))
    def _():
        pl.semaphore_wait(barrier, 3 + extra)

    @pl.when((chip == 0) | (chip == chips - 1))
    def _():
        pl.semaphore_wait(barrier, 2 + extra)


def gather_body(
    groups, rows, parts, plane, x_ref, o_ref, own_sem, send, recv, pair_send, pair_recv,
    greet=True, work=None,
):
    chips = groups // 2
    me, dp = lax.axis_index("expert"), lax.axis_index("dp")
    chip = me // 2
    sibling = chip * 2 + 1 - me % 2
    part = rows // parts
    if greet:
        line_greet(me, dp, chip, chips, plane)
    keep = pltpu.make_async_copy(x_ref, o_ref.at[pl.ds(pl.multiple_of(me * rows, rows), rows)], own_sem)

    def copy(origin, u, target, send_sem, recv_sem, first):
        place = pl.ds(pl.multiple_of(origin * rows + u * part, part), part)
        return pltpu.make_async_remote_copy(
            src_ref=x_ref.at[pl.ds(u * part, part)] if first else o_ref.at[place],
            dst_ref=o_ref.at[place],
            send_sem=send_sem,
            recv_sem=recv_sem,
            device_id=(dp, target),
            device_id_type=MESH,
        )

    def right(k, u):
        return copy(me - 2 * k, u, me + 2, send.at[0, k, u], recv.at[0, k, u], k == 0)

    def left(k, u):
        return copy(me + 2 * k, u, me - 2, send.at[1, k, u], recv.at[1, k, u], k == 0)

    def pair(side, k, u):
        origin = me - 2 * k if side == 0 else me + 2 * k
        return copy(origin, u, sibling, pair_send.at[side, k, u], pair_recv.at[side, k, u], k == 0)

    sides = lambda k: (
        (0, chip - k >= 0, chip < chips - 1),
        (1, chip + k <= chips - 1, chip > 0),
    )
    for k in range(chips):
        if k == 1 and not greet:
            plane.start_mid()
        if k == chips - 1:
            plane.start_later()
        for u in range(parts):
            for side, has, send_on in sides(k):
                step = right if side == 0 else left

                @pl.when(has)
                def _(k=k, u=u, side=side, send_on=send_on, step=step):
                    if k > 0:
                        step(k - 1, u).wait_recv()
                    if k < chips - 1:

                        @pl.when(send_on)
                        def _():
                            step(k, u).start()

                    if k > 0:
                        pair(side, k, u).start()

            if k == 0:
                pair(0, 0, u).start()
        if k == 0:
            plane.start()
            keep.start()
        if work is not None:
            work(k)

    keep.wait()
    for k in range(chips):
        for u in range(parts):
            if k == 0:
                pair(0, 0, u).wait()
            for side, has, send_on in sides(k):
                step = right if side == 0 else left

                @pl.when(has)
                def _(k=k, u=u, side=side, send_on=send_on, step=step):
                    if k < chips - 1:

                        @pl.when(send_on)
                        def _():
                            step(k, u).wait_send()

                    if k > 0:
                        pair(side, k, u).wait()

    plane.finish()


def reduce_body(
    groups, rows, parts, plane, p_ref, o_ref, own, pair, inbox, load_sem, pair_send, pair_recv, send, recv
):
    chips = groups // 2
    me, dp = lax.axis_index("expert"), lax.axis_index("dp")
    chip, core = me // 2, me % 2
    sibling = chip * 2 + 1 - core
    part = rows // parts
    step_rows = 16
    line_greet(me, dp, chip, chips, plane)

    def pair_copy(d):
        place = pl.ds(pl.multiple_of((2 * d + 1 - core) * rows, rows), rows)
        return pltpu.make_async_remote_copy(
            src_ref=p_ref.at[place],
            dst_ref=pair.at[d],
            send_sem=pair_send.at[d],
            recv_sem=pair_recv.at[d],
            device_id=(dp, sibling),
            device_id_type=MESH,
        )

    def own_copy(d):
        place = pl.ds(pl.multiple_of((2 * d + core) * rows, rows), rows)
        return pltpu.make_async_copy(p_ref.at[place], own.at[d], load_sem.at[d])

    order = []
    for j in range((chips + 1) // 2):
        order += [chips - 1 - j] + ([j] if j != chips - 1 - j else [])
    for d in order:
        pair_copy(d).start()
        own_copy(d).start()
    plane.start()

    def hop(d, u, side):
        place = pl.ds(u * part, part)
        target = me + 2 if side == 0 else me - 2
        slot = d if side == 0 else chips + d
        return pltpu.make_async_remote_copy(
            src_ref=own.at[d, place],
            dst_ref=inbox.at[slot, place],
            send_sem=send.at[d, u],
            recv_sem=recv.at[slot, u],
            device_id=(dp, target),
            device_id_type=MESH,
        )

    def add(d, u, slots, store):
        def body(i, carry):
            at = pl.ds(pl.multiple_of(u * part + i * step_rows, step_rows), step_rows)
            value = own[d, at].astype(F32) + pair[d, at].astype(F32)
            for slot in slots:
                value = value + inbox[slot, at].astype(F32)
            store(at, value)
            return carry

        lax.fori_loop(0, part // step_rows, body, 0)

    def forward(d, side):
        pair_copy(d).wait_recv()
        own_copy(d).wait()

        def store(at, value):
            own[d, at] = value.astype(BF16)

        end = chip == (0 if side == 0 else chips - 1)
        for u in range(parts):

            @pl.when(end)
            def _(u=u):
                add(d, u, (), store)

            @pl.when(jnp.logical_not(end))
            def _(u=u):
                hop(d, u, side).wait_recv()
                add(d, u, (d if side == 0 else chips + d,), store)

            hop(d, u, side).start()

    for j in range(chips - 1):
        far, near = chips - 1 - j, j

        @pl.when(far > chip)
        def _(far=far):
            forward(far, 0)

        @pl.when(near < chip)
        def _(near=near):
            forward(near, 1)

        if j == chips - 2:
            plane.start_later()

    pair_copy(chip).wait_recv()
    own_copy(chip).wait()

    def finish(at, value):
        o_ref[at] = value

    for u in range(parts):

        @pl.when(chip == 0)
        def _(u=u):
            hop(chip, u, 1).wait_recv()
            add(chip, u, (chips + chip,), finish)

        @pl.when(chip == chips - 1)
        def _(u=u):
            hop(chip, u, 0).wait_recv()
            add(chip, u, (chip,), finish)

        @pl.when((chip > 0) & (chip < chips - 1))
        def _(u=u):
            hop(chip, u, 0).wait_recv()
            hop(chip, u, 1).wait_recv()
            add(chip, u, (chip, chips + chip), finish)

    for d in range(chips):
        pair_copy(d).wait_send()
        for u in range(parts):

            @pl.when(d > chip)
            def _(d=d, u=u):
                hop(d, u, 0).wait_send()

            @pl.when(d < chip)
            def _(d=d, u=u):
                hop(d, u, 1).wait_send()

    plane.finish()


def joint_body(
    groups, rows, parts, plane, p_refs, o_refs, own, pair, inbox, load_sem, pair_send, pair_recv, send, recv
):
    kinds = range(len(p_refs))
    chips = groups // 2
    me, dp = lax.axis_index("expert"), lax.axis_index("dp")
    chip, core = me // 2, me % 2
    sibling = chip * 2 + 1 - core
    part = rows // parts
    step_rows = 16
    line_greet(me, dp, chip, chips, plane)

    def pair_copy(a, d):
        place = pl.ds(pl.multiple_of((2 * d + 1 - core) * rows, rows), rows)
        return pltpu.make_async_remote_copy(
            src_ref=p_refs[a].at[place],
            dst_ref=pair.at[a, d],
            send_sem=pair_send.at[a, d],
            recv_sem=pair_recv.at[a, d],
            device_id=(dp, sibling),
            device_id_type=MESH,
        )

    def own_copy(a, d):
        place = pl.ds(pl.multiple_of((2 * d + core) * rows, rows), rows)
        return pltpu.make_async_copy(p_refs[a].at[place], own.at[a, d], load_sem.at[a, d])

    order = []
    for j in range((chips + 1) // 2):
        order += [chips - 1 - j] + ([j] if j != chips - 1 - j else [])
    for a in kinds:
        for d in order:
            pair_copy(a, d).start()
            own_copy(a, d).start()
    plane.start()

    def hop(a, d, u, side):
        place = pl.ds(u * part, part)
        target = me + 2 if side == 0 else me - 2
        slot = d if side == 0 else chips + d
        return pltpu.make_async_remote_copy(
            src_ref=own.at[a, d, place],
            dst_ref=inbox.at[a, slot, place],
            send_sem=send.at[a, d, u],
            recv_sem=recv.at[a, slot, u],
            device_id=(dp, target),
            device_id_type=MESH,
        )

    def add(a, d, u, slots, store):
        def body(i, carry):
            at = pl.ds(pl.multiple_of(u * part + i * step_rows, step_rows), step_rows)
            value = own[a, d, at].astype(F32) + pair[a, d, at].astype(F32)
            for slot in slots:
                value = value + inbox[a, slot, at].astype(F32)
            store(at, value)
            return carry

        lax.fori_loop(0, part // step_rows, body, 0)

    def forward(a, d, side):
        pair_copy(a, d).wait_recv()
        own_copy(a, d).wait()

        def store(at, value):
            own[a, d, at] = value.astype(BF16)

        end = chip == (0 if side == 0 else chips - 1)
        for u in range(parts):

            @pl.when(end)
            def _(u=u):
                add(a, d, u, (), store)

            @pl.when(jnp.logical_not(end))
            def _(u=u):
                hop(a, d, u, side).wait_recv()
                add(a, d, u, (d if side == 0 else chips + d,), store)

            hop(a, d, u, side).start()

    def finish(a):
        pair_copy(a, chip).wait_recv()
        own_copy(a, chip).wait()

        def store(at, value):
            o_refs[a][at] = value

        for u in range(parts):

            @pl.when(chip == 0)
            def _(u=u):
                hop(a, chip, u, 1).wait_recv()
                add(a, chip, u, (chips + chip,), store)

            @pl.when(chip == chips - 1)
            def _(u=u):
                hop(a, chip, u, 0).wait_recv()
                add(a, chip, u, (chip,), store)

            @pl.when((chip > 0) & (chip < chips - 1))
            def _(u=u):
                hop(a, chip, u, 0).wait_recv()
                hop(a, chip, u, 1).wait_recv()
                add(a, chip, u, (chip, chips + chip), store)

    for a in kinds:
        for j in range(chips - 1):
            far, near = chips - 1 - j, j

            @pl.when(far > chip)
            def _(a=a, far=far):
                forward(a, far, 0)

            @pl.when(near < chip)
            def _(a=a, near=near):
                forward(a, near, 1)

            if a == 0 and j == (chips - 1) // 2:
                plane.start_later()

        finish(a)

    for a in kinds:
        for d in range(chips):
            pair_copy(a, d).wait_send()
            for u in range(parts):

                @pl.when(d > chip)
                def _(a=a, d=d, u=u):
                    hop(a, d, u, 0).wait_send()

                @pl.when(d < chip)
                def _(a=a, d=d, u=u):
                    hop(a, d, u, 1).wait_send()

    plane.finish()


class PlaneSum:
    def __init__(self, parts):
        self.me, self.dp = lax.axis_index("expert"), lax.axis_index("dp")
        self.parts = parts
        self.owners = (
            self.dp, flipped(self.dp, 1), flipped(self.dp, 2), flipped(flipped(self.dp, 1), 2)
        )

    def busy(self):
        return True

    greet = Plane.greet

    def remote(self, src, dst, send, recv, flip):
        return pltpu.make_async_remote_copy(
            src_ref=src, dst_ref=dst, send_sem=send, recv_sem=recv,
            device_id=(flipped(self.dp, flip), self.me), device_id_type=MESH,
        )

    def sizes(self, p):
        rows = p["out"].shape[0]
        half = rows // 2
        return rows, ((half, half) if half % 16 == 0 else (rows, 0))

    def rows_of(self, p, q, start, size):
        rows, _ = self.sizes(p)
        return pl.ds(pl.multiple_of(self.owners[q] * rows, rows) + start, size)

    def load(self, p):
        return pltpu.make_async_copy(p["ref"], p["buf"], p["load"])

    def early(self, p, i):
        _, split = self.sizes(p)
        start = 0 if i == 0 else split[0]
        return self.remote(
            p["ref"].at[self.rows_of(p, 3, start, split[i])], p["first"].at[pl.ds(start, split[i])],
            p["send"].at[i], p["recv"].at[i], i + 1,
        )

    def late(self, p, i):
        rows, _ = self.sizes(p)
        return self.remote(
            p["buf"].at[self.rows_of(p, i + 1, 0, rows)], p["second"].at[i],
            p["send"].at[2 + i], p["recv"].at[2 + i], i + 1,
        )

    def counts(self, p):
        return 2 if self.sizes(p)[1][1] else 1

    def start(self):
        for p in self.parts:
            for i in range(self.counts(p)):
                self.early(p, i).start()
            self.load(p).start()

    def start_later(self):
        for p in self.parts:
            rows, split = self.sizes(p)
            self.load(p).wait()
            for i in range(self.counts(p)):
                self.early(p, i).wait_recv()
                start = 0 if i == 0 else split[0]
                step = 16
                base = pl.multiple_of(self.owners[2 - i] * rows, rows) + start

                def body(t, carry, p=p, start=start, base=base, step=step):
                    here = pl.ds(pl.multiple_of(base + t * step, step), step)
                    there = pl.ds(pl.multiple_of(start + t * step, step), step)
                    value = p["buf"][here].astype(F32) + p["first"][there].astype(F32)
                    p["buf"][here] = value.astype(BF16)
                    return carry

                lax.fori_loop(0, split[i] // step, body, 0)
            for i in range(2):
                self.late(p, i).start()

    def finish(self):
        for p in self.parts:
            rows, _ = self.sizes(p)
            for i in range(2):
                self.late(p, i).wait()
            for i in range(self.counts(p)):
                self.early(p, i).wait_send()
            step = 16
            base = pl.multiple_of(self.dp * rows, rows)

            def body(t, carry, p=p, base=base, step=step):
                here = pl.ds(pl.multiple_of(base + t * step, step), step)
                there = pl.ds(pl.multiple_of(t * step, step), step)
                value = p["buf"][here].astype(F32) + p["second"][0, there].astype(F32)
                value = value + p["second"][1, there].astype(F32)
                p["out"][there] = value.astype(BF16)
                return carry

            lax.fori_loop(0, rows // step, body, 0)


def joint_reduce(partials, sums, after, collective_id, parts=4):
    groups, seqs = lax.axis_size("expert"), lax.axis_size("dp")
    chips = groups // 2
    rows, width = partials[0].shape[0] // groups, partials[0].shape[1]
    n, m, extra = len(partials), len(sums), len(after)

    def kernel(*refs):
        p_refs, s_refs = refs[:n], refs[n : n + m]
        refs = refs[n + m + extra :]
        o_refs, outs, rest = refs[:n], refs[n : n + m], refs[n + m :]
        names = ("buf", "first", "second", "load", "send", "recv")
        made = [
            dict(zip(names, rest[len(names) * i : len(names) * (i + 1)]), ref=s_refs[i], out=outs[i])
            for i in range(m)
        ]
        joint_body(groups, rows, parts, PlaneSum(made), p_refs, o_refs, *rest[len(names) * m :])

    anywhere, vmem = pl.BlockSpec(memory_space=pl.ANY), pl.BlockSpec(memory_space=pltpu.VMEM)
    dma = pltpu.SemaphoreType.DMA
    scratch = []
    for s in sums:
        own_rows = s.shape[0] // seqs
        scratch += [
            pltpu.VMEM(s.shape, BF16), pltpu.VMEM((own_rows,) + s.shape[1:], BF16),
            pltpu.VMEM((2, own_rows) + s.shape[1:], BF16), dma, dma((4,)), dma((4,)),
        ]
    return pl.pallas_call(
        kernel,
        out_shape=[jax.ShapeDtypeStruct((rows, width), F32)] * n
        + [jax.ShapeDtypeStruct((s.shape[0] // seqs,) + s.shape[1:], BF16) for s in sums],
        in_specs=[anywhere] * (n + m + extra),
        out_specs=[vmem] * (n + m),
        scratch_shapes=scratch + [
            pltpu.VMEM((n, chips, rows, width), BF16),
            pltpu.VMEM((n, chips, rows, width), BF16),
            pltpu.VMEM((n, 2 * chips, rows, width), BF16),
            dma((n, chips)), dma((n, chips)), dma((n, chips)),
            dma((n, chips, parts)), dma((n, 2 * chips, parts)),
        ],
        compiler_params=pltpu.CompilerParams(
            collective_id=collective_id, has_side_effects=True, vmem_limit_bytes=VMEM_LIMIT
        ),
        cost_estimate=cost_of(70),
        name="joint_reduce",
    )(*partials, *sums, *after)


def last_body(
    groups, seqs, small_ref, qkv_ref, out_ref, small_to, q_to, k_to, v_to, o_to,
    box, qkv_box, out_box, send, recv, qkv_send, qkv_recv, out_sem,
):
    me, dp = lax.axis_index("expert"), lax.axis_index("dp")
    total = groups * seqs
    mine = dp * groups + me
    block, width = o_to.shape
    own = width // groups
    barrier = pltpu.get_barrier_semaphore()

    def device(index):
        return (index // groups, index % groups)

    def hello(s, carry):
        pl.semaphore_signal(
            barrier, inc=1, device_id=device((mine + s) % total), device_id_type=MESH
        )
        return carry

    lax.fori_loop(1, total, hello, 0)
    pl.semaphore_wait(barrier, total - 1)

    def qkv_copy(s):
        peer = (me + s) % groups
        return pltpu.make_async_remote_copy(
            src_ref=qkv_ref.at[pl.ds(pl.multiple_of(peer * block, block), block)],
            dst_ref=qkv_box.at[me],
            send_sem=qkv_send.at[s], recv_sem=qkv_recv.at[s],
            device_id=(dp, peer), device_id_type=MESH,
        )

    def small_copy(s):
        target = (mine + s) % total
        return pltpu.make_async_remote_copy(
            src_ref=small_ref.at[target], dst_ref=box.at[mine],
            send_sem=send.at[s], recv_sem=recv.at[s],
            device_id=device(target), device_id_type=MESH,
        )

    owner = me * seqs + dp
    out_copy = pltpu.make_async_remote_copy(
        src_ref=out_ref, dst_ref=out_box, send_sem=out_sem.at[0], recv_sem=out_sem.at[1],
        device_id=device(owner), device_id_type=MESH,
    )

    def start(s, carry):
        small_copy(s).start()
        return carry

    def wait(s, carry):
        small_copy(s).wait()
        return carry

    lax.fori_loop(1, total, start, 0)
    for s in range(1, groups):
        qkv_copy(s).start()

    @pl.when(owner != mine)
    def _():
        out_copy.start()

    box[mine] = small_ref[mine]
    qkv_box[me] = qkv_ref[pl.ds(pl.multiple_of(me * block, block), block)]
    lax.fori_loop(1, total, wait, 0)

    def add(s, value):
        return value + box[s]

    small_to[...] = lax.fori_loop(1, total, add, box[0])

    @pl.when(owner != mine)
    def _():
        out_copy.wait()
        o_to[...] = out_box[...].astype(F32)

    @pl.when(owner == mine)
    def _():
        o_to[...] = out_ref[...].astype(F32)

    for s in range(1, groups):
        qkv_copy(s).wait()
    for e in range(groups):
        for m, to in enumerate((q_to, k_to, v_to)):
            to[:, e * own : (e + 1) * own] = qkv_box[e, :, m * own : (m + 1) * own].astype(F32)


def last_exchange(small, qkv, out, collective_id):
    groups, seqs = lax.axis_size("expert"), lax.axis_size("dp")
    total = groups * seqs
    block, width = out.shape
    vmem = pl.BlockSpec(memory_space=pltpu.VMEM)
    dma = pltpu.SemaphoreType.DMA
    matrix = jax.ShapeDtypeStruct((block, width), F32)
    return pl.pallas_call(
        functools.partial(last_body, groups, seqs),
        out_shape=[jax.ShapeDtypeStruct(small.shape[1:], F32)] + [matrix] * 4,
        in_specs=[vmem] * 3,
        out_specs=[vmem] * 5,
        scratch_shapes=[
            pltpu.VMEM(small.shape, F32),
            pltpu.VMEM((groups, block, qkv.shape[1]), BF16),
            pltpu.VMEM((block, width), BF16),
            dma((total,)), dma((total,)), dma((groups,)), dma((groups,)), dma((2,)),
        ],
        compiler_params=pltpu.CompilerParams(
            collective_id=collective_id, has_side_effects=True, vmem_limit_bytes=VMEM_LIMIT
        ),
        cost_estimate=cost_of(25),
        name="last_exchange",
    )(small, qkv, out)


def exchange_body(count, spread, same, reduce, plane, x_ref, o_ref, box, send, recv):
    me, dp = lax.axis_index("expert"), lax.axis_index("dp")
    groups = lax.axis_size("expert")
    mine = dp * groups + me if spread else me

    def device(index):
        return (index // groups, index % groups) if spread else (dp, index)

    barrier = pltpu.get_barrier_semaphore()

    def hello(s, carry):
        pl.semaphore_signal(
            barrier, inc=1, device_id=device((mine + s) % count), device_id_type=MESH
        )
        return carry

    lax.fori_loop(1, count, hello, 0)
    plane.greet(barrier)
    pl.semaphore_wait(barrier, count - 1 + (2 if plane.busy() else 0))

    def copy(s):
        target = (mine + s) % count
        return pltpu.make_async_remote_copy(
            src_ref=x_ref.at[0] if same else x_ref.at[target],
            dst_ref=box.at[mine],
            send_sem=send.at[s],
            recv_sem=recv.at[s],
            device_id=device(target),
            device_id_type=MESH,
        )

    def start(s, carry):
        copy(s).start()
        return carry

    def wait(s, carry):
        copy(s).wait()
        return carry

    lax.fori_loop(1, count, start, 0)
    plane.start()
    box[mine] = x_ref[0] if same else x_ref[mine]
    lax.fori_loop(1, count, wait, 0)
    if reduce:

        def add(s, total):
            return total + box[s]

        o_ref[...] = lax.fori_loop(1, count, add, box[0])
    else:
        o_ref[...] = box[...]
    plane.start_later()
    plane.finish()


def run(
    body, name, micros, collective_id, x, x_space, out, out_space, scratch, sends, later,
    carry=(), after=(), wholes=(),
):
    arrays, specs = [], []
    for array, start, size, flip in sends:
        found = [i for i, a in enumerate(arrays) if a is array]
        if not found:
            arrays.append(array)
            found = [len(arrays) - 1]
        specs.append((found[0], start, size, flip))
    targets = [jax.ShapeDtypeStruct((s[2],) + s[0].shape[1:], s[0].dtype) for s in sends]
    for source, start, size, flip in later:
        targets.append(jax.ShapeDtypeStruct((size,) + targets[source].shape[1:], targets[source].dtype))
    seqs = lax.axis_size("dp")
    whole_out = [jax.ShapeDtypeStruct((seqs * w.shape[0],) + w.shape[1:], w.dtype) for w in wholes]
    n_in, n_out, held, n_whole = len(arrays), len(targets), len(carry), len(wholes)

    def kernel(*refs):
        x_ref, sources, whole_in = refs[0], refs[1 : 1 + n_in], refs[1 + n_in : 1 + n_in + n_whole]
        refs = refs[1 + n_in + n_whole + held + len(after) :]
        o_ref, dests, whole_to = refs[0], refs[1 : 1 + n_out], refs[1 + n_out : 1 + n_out + n_whole]
        rest = refs[1 + n_out + n_whole + held :]
        made = [
            Whole(a, b, rest[2].at[i], rest[3].at[i], rest[4].at[i])
            for i, (a, b) in enumerate(zip(whole_in, whole_to))
        ]
        plane = Plane(specs, later, sources, dests, *rest[:2], made)
        body(plane, x_ref, o_ref, *rest[5 if n_whole else 2 :])

    anywhere = pl.BlockSpec(memory_space=pl.ANY)
    dma = pltpu.SemaphoreType.DMA
    first, second = 1 + n_in + n_whole, 1 + n_out + n_whole
    got = pl.pallas_call(
        kernel,
        out_shape=[out] + targets + whole_out + [jax.ShapeDtypeStruct(c.shape, c.dtype) for c in carry],
        in_specs=[pl.BlockSpec(memory_space=x_space)] + [anywhere] * (n_in + n_whole + held + len(after)),
        out_specs=[pl.BlockSpec(memory_space=out_space)] + [anywhere] * (n_out + n_whole + held),
        input_output_aliases={first + i: second + i for i in range(held)},
        scratch_shapes=[dma((max(n_out, 1),))] * 2
        + ([dma((n_whole,)), dma((n_whole, 4)), dma((n_whole, 4))] if n_whole else [])
        + scratch,
        compiler_params=pltpu.CompilerParams(
            collective_id=collective_id, has_side_effects=True, vmem_limit_bytes=VMEM_LIMIT
        ),
        cost_estimate=cost_of(micros),
        name=name,
    )(x, *arrays, *wholes, *carry, *after)
    return got if n_out + n_whole + held else got[0]


def line_gather(x, collective_id, sends=(), later=(), carry=(), after=(), wholes=(), parts=4):
    rows, width = x.shape
    groups = lax.axis_size("expert")
    shape = (2, groups // 2, parts)
    return run(
        functools.partial(gather_body, groups, rows, parts), "line_gather", 40, collective_id,
        x, pl.ANY, jax.ShapeDtypeStruct((groups * rows, width), x.dtype), pl.ANY,
        [pltpu.SemaphoreType.DMA] + [pltpu.SemaphoreType.DMA(shape)] * 4,
        sends, later, carry, after, wholes,
    )


def line_reduce(partial, collective_id, sends=(), later=(), after=(), parts=4):
    groups = lax.axis_size("expert")
    chips = groups // 2
    rows, width = partial.shape[0] // groups, partial.shape[1]
    return run(
        functools.partial(reduce_body, groups, rows, parts), "line_reduce", 40, collective_id,
        partial.astype(BF16), pl.ANY, jax.ShapeDtypeStruct((rows, width), F32), pltpu.VMEM,
        [
            pltpu.VMEM((chips, rows, width), BF16),
            pltpu.VMEM((chips, rows, width), BF16),
            pltpu.VMEM((2 * chips, rows, width), BF16),
            pltpu.SemaphoreType.DMA((chips,)),
            pltpu.SemaphoreType.DMA((chips,)),
            pltpu.SemaphoreType.DMA((chips,)),
            pltpu.SemaphoreType.DMA((chips, parts)),
            pltpu.SemaphoreType.DMA((2 * chips, parts)),
        ],
        sends, later, (), after,
    )


def exchange(
    x, collective_id, spread=False, same=False, reduce=False, sends=(), later=(), carry=()
):
    count = lax.axis_size("expert") * (lax.axis_size("dp") if spread else 1)
    block = x.shape[1:]
    return run(
        functools.partial(exchange_body, count, spread, same, reduce), "exchange", 8, collective_id,
        x, pltpu.VMEM, jax.ShapeDtypeStruct(block if reduce else (count,) + block, x.dtype), pltpu.VMEM,
        [
            pltpu.VMEM((count,) + block, x.dtype),
            pltpu.SemaphoreType.DMA((count,)),
            pltpu.SemaphoreType.DMA((count,)),
        ],
        sends, later, carry,
    )


LANES = 128
TILE = 512


def expert_first_body(
    groups, seqs, rows, width, ff, experts, parts,
    x_ref, g_ref, gate_ref, up_ref, down_ref, near_refs,
    f_out, hid_out, sg_out, su_out, tail_out, down_out, grad_out,
    f_buf, g_buf, wg, wu, wd, hid, sg, su, tail_buf, tail_sum, stage,
    line_send, line_recv, side_send, side_recv, own_sem, f_sem, w_sem, d_sem, g_sem, out_sem, tail_sem,
    plane_send, plane_recv, stage_sem,
):
    chips = groups // 2
    me, dp = lax.axis_index("expert"), lax.axis_index("dp")
    chip, core = me // 2, me % 2
    sibling = chip * 2 + 1 - core
    chunk = 2 * rows
    part = rows // parts
    depth, wide_ff = width // seqs, ff // seqs

    def remote(src, dst, send_sem, recv_sem, device):
        return pltpu.make_async_remote_copy(
            src_ref=src, dst_ref=dst, send_sem=send_sem, recv_sem=recv_sem,
            device_id=device, device_id_type=MESH,
        )

    def at(index, size):
        return pl.ds(pl.multiple_of(index * size, size), size)

    def neighbour(flip):
        return (flipped(dp, flip), me)

    barrier = pltpu.get_barrier_semaphore()
    pl.semaphore_signal(barrier, inc=1, device_id=(dp, sibling), device_id_type=MESH)
    for flip in (1, 2):
        pl.semaphore_signal(barrier, inc=1, device_id=neighbour(flip), device_id_type=MESH)

    @pl.when(chip > 0)
    def _():
        pl.semaphore_signal(barrier, inc=1, device_id=(dp, me - 2), device_id_type=MESH)

    @pl.when(chip < chips - 1)
    def _():
        pl.semaphore_signal(barrier, inc=1, device_id=(dp, me + 2), device_id_type=MESH)

    @pl.when((chip > 0) & (chip < chips - 1))
    def _():
        pl.semaphore_wait(barrier, 5)

    @pl.when((chip == 0) | (chip == chips - 1))
    def _():
        pl.semaphore_wait(barrier, 4)

    def row_copy(origin, u, target, send_sem, recv_sem, first):
        place = pl.ds(pl.multiple_of(origin * rows + u * part, part), part)
        return remote(
            x_ref.at[pl.ds(u * part, part)] if first else f_buf.at[place], f_buf.at[place],
            send_sem, recv_sem, (dp, target),
        )

    def step(side, k, u):
        origin, target = (me - 2 * k, me + 2) if side == 0 else (me + 2 * k, me - 2)
        return row_copy(origin, u, target, line_send.at[side, k, u], line_recv.at[side, k, u], k == 0)

    def aside(side, k, u):
        origin = me - 2 * k if side == 0 else me + 2 * k
        return row_copy(origin, u, sibling, side_send.at[side, k, u], side_recv.at[side, k, u], k == 0)

    def sides(k):
        return (
            (0, chip - k >= 0, chip < chips - 1),
            (1, chip + k <= chips - 1, chip > 0),
        )

    keep = pltpu.make_async_copy(x_ref, f_buf.at[at(me, rows)], own_sem)

    def rows_out(c):
        return pltpu.make_async_copy(
            f_buf.at[at(c, chunk), pl.ds(0, width)], f_out.at[at(c, chunk)], f_sem.at[c]
        )

    def plane_copy(i):
        e, flip = (i // 2, i % 2 + 1) if i < 4 else (i - 4, i - 3)
        if i < 4:
            src, dst = down_ref.at[e], wd.at[e, at(dp, wide_ff)]
        else:
            src = wd.at[e, at(flipped(dp, 3 - flip), wide_ff)]
            dst = src
        return remote(src, dst, plane_send.at[i], plane_recv.at[i], neighbour(flip))

    owners = (dp, flipped(dp, 1), flipped(dp, 2), flipped(flipped(dp, 1), 2))

    def weight_copies():
        copies = []
        for m, (own, buf) in enumerate(((gate_ref, wg), (up_ref, wu))):
            for e in range(experts):
                near = [near_refs[6 * m + 2 * q + e] for q in range(3)]
                pieces = [own.at[e]] + [ref.at[index] for ref, index in near]
                for q, piece in enumerate(pieces):
                    copies.append(
                        pltpu.make_async_copy(
                            piece, buf.at[at(owners[q], depth), pl.ds(e * ff, ff)],
                            w_sem.at[m, e, q],
                        )
                    )
        return copies

    def down_copies():
        return [
            pltpu.make_async_copy(down_ref.at[e], wd.at[e, at(dp, wide_ff)], d_sem.at[e])
            for e in range(experts)
        ]

    grad_rows = [
        pltpu.make_async_copy(
            g_ref.at[pl.ds(r * chunk, chunk)], g_buf.at[pl.ds(r * chunk, chunk)], g_sem.at[r]
        )
        for r in range(chips)
    ]

    def first_layer(c):
        place = at(c, chunk)

        def tile(t, carry):
            cols = at(t, TILE)
            gate = dot(f_buf[place, pl.ds(0, width)], wg[:, cols])
            up = dot(f_buf[place, pl.ds(0, width)], wu[:, cols])
            sig = 1.0 / (1.0 + jnp.exp(-gate))
            silu = gate * sig
            hid[place, cols] = (silu * up).astype(BF16)
            sg[place, cols] = (up * sig * (1.0 + gate * (1.0 - sig))).astype(BF16)
            su[place, cols] = silu.astype(BF16)
            return carry

        lax.fori_loop(0, experts * ff // TILE, tile, 0)

    def ready(k):
        for u in range(parts):
            if k == 0:
                aside(0, 0, u).wait_recv()
            else:
                for side, has, _ in sides(k):

                    @pl.when(has)
                    def _(side=side, u=u):
                        aside(side, k, u).wait_recv()

        if k == 0:
            rows_out(chip).start()
            first_layer(chip)
        else:
            for side, has, _ in sides(k):
                c = chip - k if side == 0 else chip + k

                @pl.when(has)
                def _(c=c):
                    rows_out(c).start()
                    first_layer(c)

    for k in range(chips):
        for u in range(parts):
            for side, has, send_on in sides(k):

                @pl.when(has)
                def _(k=k, u=u, side=side, send_on=send_on):
                    if k > 0:
                        step(side, k - 1, u).wait_recv()
                    if k < chips - 1:

                        @pl.when(send_on)
                        def _():
                            step(side, k, u).start()

                    if k > 0:
                        aside(side, k, u).start()

            if k == 0:
                aside(0, 0, u).start()
        if k == 0:
            for i in range(4):
                plane_copy(i).start()
            keep.start()
            for copy in weight_copies():
                copy.start()
            for copy in down_copies():
                copy.start()
            for copy in grad_rows:
                copy.start()
            keep.wait()
            for copy in weight_copies():
                copy.wait()
        if k > 0:
            ready(k - 1)
    plane_copy(1).wait_recv()
    plane_copy(4).start()
    plane_copy(2).wait_recv()
    plane_copy(5).start()
    ready(chips - 1)

    for copy in down_copies():
        copy.wait()
    for i in (0, 3):
        plane_copy(i).wait_recv()

    def outs(r):
        place = pl.ds(r * chunk, chunk)
        return [
            pltpu.make_async_copy(buf.at[place], out.at[place], out_sem.at[i, r])
            for i, (buf, out) in enumerate(((hid, hid_out), (sg, sg_out), (su, su_out)))
        ]

    lane = lax.broadcasted_iota(jnp.int32, (chunk, LANES), 1)

    def back(r, first, last):
        place = pl.ds(r * chunk, chunk)
        extra = f_buf[place, pl.ds(width, LANES)].astype(F32)
        tail = jnp.zeros((chunk, LANES), F32) if first == 0 else tail_sum[place, :]
        for e in range(experts):
            which = me * experts + e
            low = which + LANES // 2
            weight = jnp.sum(
                jnp.where((lane == which) | (lane == low), extra, 0.0), axis=1, keepdims=True
            )
            for owner in owners[first:last]:
                d_hid = dot_nt(g_buf[place, :], wd[e, at(owner, wide_ff), :])
                cols = pl.ds(pl.multiple_of(e * ff + owner * wide_ff, wide_ff), wide_ff)
                hidden = hid[place, cols].astype(F32)
                d_weight = jnp.sum(hidden * d_hid, axis=1, keepdims=True)
                tail = tail + jnp.where(lane == which, d_weight, 0.0)
                d_hid = d_hid * weight
                hid[place, cols] = (hidden * weight).astype(BF16)
                sg[place, cols] = (d_hid * sg[place, cols].astype(F32)).astype(BF16)
                su[place, cols] = (d_hid * su[place, cols].astype(F32)).astype(BF16)
        if last < len(owners):
            tail_sum[place, :] = tail
        else:
            high = tail.astype(BF16).astype(F32)
            tail_buf[place, :] = (high + pltpu.roll(tail - high, LANES // 2, 1)).astype(BF16)

    tiles = [(e, q) for q in range(len(owners)) for e in range(experts)]

    def grad_place(t):
        e, q = tiles[t]
        return pl.ds(pl.multiple_of(e * ff + owners[q] * wide_ff, wide_ff), wide_ff)

    def grad_copy(t):
        return pltpu.make_async_copy(stage.at[t % 2], grad_out.at[grad_place(t)], stage_sem.at[t % 2])

    def grad_tile(t):
        if t >= 2:
            grad_copy(t - 2).wait()
        for n in range(width // (2 * TILE)):
            cols = pl.ds(n * 2 * TILE, 2 * TILE)
            stage[t % 2, :, cols] = dot_tn(hid[:, grad_place(t)], g_buf[:, cols]).astype(BF16)
        grad_copy(t).start()

    for copy in grad_rows:
        copy.wait()
    for r in range(chips):
        back(r, 0, 3)
    for t in range(3 * experts):
        grad_tile(t)
    for i in (4, 5):
        plane_copy(i).wait_recv()
    keep_down = pltpu.make_async_copy(wd, down_out, d_sem.at[experts])
    keep_down.start()
    for r in range(chips):
        back(r, 3, 4)
        for copy in outs(r):
            copy.start()
    for t in range(3 * experts, 4 * experts):
        grad_tile(t)
    for t in range(4 * experts - 2, 4 * experts):
        grad_copy(t).wait()
    keep_tail = pltpu.make_async_copy(tail_buf, tail_out, tail_sem)
    keep_tail.start()
    keep_tail.wait()
    keep_down.wait()
    for k in range(chips):
        for u in range(parts):
            if k == 0:
                aside(0, 0, u).wait_send()
            for side, has, send_on in sides(k):

                @pl.when(has)
                def _(k=k, u=u, side=side, send_on=send_on):
                    if k < chips - 1:

                        @pl.when(send_on)
                        def _():
                            step(side, k, u).wait_send()

                    if k > 0:
                        aside(side, k, u).wait_send()

    for i in range(6):
        plane_copy(i).wait_send()
    for d in range(chips):
        rows_out(d).wait()
        for copy in outs(d):
            copy.wait()


def expert_first(x, g_all, w_gate, w_up, w_down, near, collective_id, parts=4):
    groups, seqs = lax.axis_size("expert"), lax.axis_size("dp")
    chips = groups // 2
    rows, wide = x.shape
    length, width = g_all.shape
    experts, _, ff = w_gate.shape
    where = [index for _, index in near]
    near = [array for array, _ in near]
    n = len(near)

    def kernel(*refs):
        expert_first_body(
            groups, seqs, rows, width, ff, experts, parts, *refs[:5],
            list(zip(refs[5 : 5 + n], where)), *refs[5 + n :],
        )

    anywhere = pl.BlockSpec(memory_space=pl.ANY)
    dma = pltpu.SemaphoreType.DMA
    flat = jax.ShapeDtypeStruct((length, experts * ff), BF16)
    return pl.pallas_call(
        kernel,
        out_shape=[
            jax.ShapeDtypeStruct((length, width), BF16), flat, flat, flat,
            jax.ShapeDtypeStruct((length, LANES), BF16),
            jax.ShapeDtypeStruct((experts, ff, width), BF16),
            jax.ShapeDtypeStruct((experts * ff, width), BF16),
        ],
        in_specs=[anywhere] * (5 + n),
        out_specs=[anywhere] * 7,
        scratch_shapes=[
            pltpu.VMEM((length, wide), BF16),
            pltpu.VMEM((length, width), BF16),
            pltpu.VMEM((width, experts * ff), BF16),
            pltpu.VMEM((width, experts * ff), BF16),
            pltpu.VMEM((experts, ff, width), BF16),
            pltpu.VMEM((length, experts * ff), BF16),
            pltpu.VMEM((length, experts * ff), BF16),
            pltpu.VMEM((length, experts * ff), BF16),
            pltpu.VMEM((length, LANES), BF16),
            pltpu.VMEM((length, LANES), F32),
            pltpu.VMEM((2, ff // seqs, width), BF16),
            dma((2, chips, parts)), dma((2, chips, parts)), dma((2, chips, parts)), dma((2, chips, parts)),
            dma, dma((chips,)), dma((2, experts, 4)), dma((experts + 1,)), dma((chips,)), dma((3, chips)), dma,
            dma((6,)), dma((6,)), dma((2,)),
        ],
        compiler_params=pltpu.CompilerParams(
            collective_id=collective_id, has_side_effects=True, vmem_limit_bytes=VMEM_LIMIT
        ),
        cost_estimate=cost_of(70),
        name="expert_first",
    )(x, g_all, w_gate, w_up, w_down, *near)


class ExpertSum:
    def __init__(self, size, ref, out, first, mid, own, near, load, send, recv):
        self.me, self.dp = lax.axis_index("expert"), lax.axis_index("dp")
        self.size, self.ref, self.out = size, ref, out
        self.first, self.mid, self.own, self.near = first, mid, own, near
        self.load_sem, self.send, self.recv = load, send, recv
        x, y = flipped(self.dp, 1), flipped(self.dp, 2)
        self.owners = (self.dp, x, y, flipped(x, 2))
        self.stride = ref.shape[0] // 2

    def busy(self):
        return True

    greet = Plane.greet

    def piece(self, e, q):
        return self.ref.at[
            pl.ds(pl.multiple_of(e * self.stride + self.owners[q] * self.size, self.size), self.size)
        ]

    def copy(self, i):
        src, dst, flip = (
            (self.piece(0, 3), self.first.at[0], 1),
            (self.piece(1, 3), self.first.at[1], 2),
            (self.piece(0, 1), self.near.at[0, 0], 1),
            (self.piece(1, 2), self.near.at[1, 1], 2),
            (self.mid.at[1], self.near.at[0, 1], 1),
            (self.mid.at[0], self.near.at[1, 0], 2),
        )[i]
        return pltpu.make_async_remote_copy(
            src_ref=src, dst_ref=dst, send_sem=self.send.at[i], recv_sem=self.recv.at[i],
            device_id=(flipped(self.dp, flip), self.me), device_id_type=MESH,
        )

    def loads(self):
        return [
            pltpu.make_async_copy(src, dst, self.load_sem.at[i])
            for i, (src, dst) in enumerate(
                (
                    (self.piece(0, 2), self.mid.at[0]), (self.piece(1, 1), self.mid.at[1]),
                    (self.piece(0, 0), self.own.at[0]), (self.piece(1, 0), self.own.at[1]),
                )
            )
        ]

    def start(self):
        for i in range(4):
            self.copy(i).start()
        for copy in self.loads():
            copy.start()

    def relay(self):
        for copy in self.loads():
            copy.wait()
        for i in range(2):
            self.copy(i).wait_recv()

            def body(t, carry, i=i):
                here = pl.ds(pl.multiple_of(t * 16, 16), 16)
                value = self.mid[i, here].astype(F32) + self.first[i, here].astype(F32)
                self.mid[i, here] = value.astype(BF16)
                return carry

            lax.fori_loop(0, self.size // 16, body, 0)
        for i in (4, 5):
            self.copy(i).start()

    def finish(self):
        for i in range(2, 6):
            self.copy(i).wait_recv()
        for e in range(2):

            def body(t, carry, e=e):
                here = pl.ds(pl.multiple_of(t * 16, 16), 16)
                value = self.own[e, here].astype(F32)
                for side in range(2):
                    value = value + self.near[side, e, here].astype(F32)
                self.own[e, here] = value.astype(BF16)
                return carry

            lax.fori_loop(0, self.size // 16, body, 0)
        keep = pltpu.make_async_copy(self.own, self.out, self.load_sem.at[0])
        keep.start()
        for i in range(6):
            self.copy(i).wait_send()
        keep.wait()


def expert_second_body(
    groups, seqs, rows, width, ff, experts, parts,
    sg_ref, su_ref, tail_ref, f_ref, gate_ref, up_ref, down_ref, near_refs, grad_out, down_out, o_ref,
    wg, wu, sg, su, tail_buf, f_buf, stage, acc, pair_in, inbox, last,
    first, mid, own_block, near_buf,
    in_sem, w_sem, stage_sem, pair_send, pair_recv, hop_send, hop_recv, last_recv,
    sum_load, sum_send, sum_recv,
):
    chips = groups // 2
    me, dp = lax.axis_index("expert"), lax.axis_index("dp")
    chip, core = me // 2, me % 2
    sibling = chip * 2 + 1 - core
    chunk = 2 * rows
    part = rows // parts
    depth = width // seqs

    def remote(src, dst, send_sem, recv_sem, device):
        return pltpu.make_async_remote_copy(
            src_ref=src, dst_ref=dst, send_sem=send_sem, recv_sem=recv_sem,
            device_id=device, device_id_type=MESH,
        )

    def at(index, size):
        return pl.ds(pl.multiple_of(index * size, size), size)

    owners = (dp, flipped(dp, 1), flipped(dp, 2), flipped(flipped(dp, 1), 2))
    loads = [
        pltpu.make_async_copy(src, dst, in_sem.at[i])
        for i, (src, dst) in enumerate(
            ((sg_ref, sg), (su_ref, su), (tail_ref, tail_buf), (f_ref, f_buf))
        )
    ]
    weights = []
    for m, (own, buf) in enumerate(((gate_ref, wg), (up_ref, wu))):
        for e in range(experts):
            near = [near_refs[6 * m + 2 * q + e] for q in range(3)]
            pieces = [own.at[e]] + [ref.at[index] for ref, index in near]
            for q, piece in enumerate(pieces):
                weights.append(
                    pltpu.make_async_copy(
                        piece, buf.at[at(owners[q], depth), pl.ds(e * ff, ff)], w_sem.at[m, e, q]
                    )
                )
    for copy in loads[:3] + weights + loads[3:]:
        copy.start()
    total = ExpertSum(
        ff // seqs, down_ref, down_out, first, mid, own_block, near_buf, sum_load, sum_send, sum_recv
    )
    line_greet(me, dp, chip, chips, total)
    total.start()
    for copy in loads[:3]:
        copy.wait()
    for r in range(chips):
        for half in range(2):
            acc[r, half, :, pl.ds(width, LANES)] = tail_buf[pl.ds(r * chunk + half * rows, rows), :]

    out_tile = 256

    def row_grads(d, first=False):
        place = at(d, chunk)
        per = depth // out_tile

        def tile(t, carry):
            cols = at(t, out_tile)
            value = dot_nt(sg[place, :], wg[cols, :]) + dot_nt(su[place, :], wu[cols, :])
            value = value.astype(BF16)
            acc[d, 0, :, cols] = value[:rows]
            acc[d, 1, :, cols] = value[rows:]
            return carry

        if not first:
            lax.fori_loop(0, width // out_tile, tile, 0)
            return
        for q, owner in enumerate(owners):
            for copy in weights[q :: len(owners)]:
                copy.wait()
            lax.fori_loop(owner * per, owner * per + per, tile, 0)

    def pair_copy(d):
        return remote(acc.at[d, 1 - core], pair_in.at[d], pair_send.at[d], pair_recv.at[d], (dp, sibling))

    def hop(d, u, kind):
        place = pl.ds(u * part, part)
        if kind == 0:
            return remote(
                acc.at[d, core, place], inbox.at[d, place], hop_send.at[d, u], hop_recv.at[d, u],
                (dp, me + 2),
            )
        if kind == 1:
            return remote(
                acc.at[d, core, place], inbox.at[d, place], hop_send.at[d, u], hop_recv.at[d, u],
                (dp, me - 2),
            )
        return remote(
            acc.at[d, core, place], last.at[place], hop_send.at[d, u], last_recv.at[u], (dp, me - 2)
        )

    step_rows = 16

    def add(d, u, more, store):
        def body(i, carry):
            here = pl.ds(pl.multiple_of(u * part + i * step_rows, step_rows), step_rows)
            value = acc[d, core, here].astype(F32) + pair_in[d, here].astype(F32)
            for ref in more:
                value = value + ref[here].astype(F32)
            store(here, value)
            return carry

        lax.fori_loop(0, part // step_rows, body, 0)

    def forward(d):
        pair_copy(d).wait_recv()

        def store(here, value):
            acc[d, core, here] = value.astype(BF16)

        source = ((d > chip) & (chip == 0)) | ((d < chip) & (chip == chips - 1))
        for u in range(parts):

            @pl.when(source)
            def _(u=u):
                add(d, u, (), store)

            @pl.when(jnp.logical_not(source))
            def _(u=u):
                hop(d, u, 0).wait_recv()
                add(d, u, (inbox.at[d],), store)

            @pl.when(d > chip)
            def _(u=u):
                hop(d, u, 0).start()

            @pl.when((d < chip) & (d != chip - 1))
            def _(u=u):
                hop(d, u, 1).start()

            @pl.when((d < chip) & (d == chip - 1))
            def _(u=u):
                hop(d, u, 2).start()

    upper = chip // (chips // 2)
    mirrored = chip + upper * (chips - 1 - 2 * chip)

    def goal(j):
        turn = (j + mirrored) // (chips - 1)
        d = (1 - turn) * (chips - 1 - j) + turn * (j + mirrored - (chips - 1))
        return d + upper * (chips - 1 - 2 * d)

    edge = (chip == 0) | (chip == chips - 1)

    def grad_copy(t):
        return pltpu.make_async_copy(
            stage.at[t % 2], grad_out.at[pl.ds(t * out_tile, out_tile)], stage_sem.at[t % 2]
        )

    def grad_tile(t):
        if t >= 2:
            grad_copy(t - 2).wait()
        for n in range(experts * ff // (2 * TILE)):
            cols = pl.ds(n * 2 * TILE, 2 * TILE)
            stage[t % 2, :, cols] = dot_tn(
                f_buf[:, pl.ds(t * out_tile, out_tile)], sg[:, cols]
            ).astype(BF16)
        grad_copy(t).start()

    tiles = width // out_tile
    for j in range(chips):
        row_grads(goal(j), j == 0)
        pair_copy(goal(j)).start()
        if j > 0:

            @pl.when(edge)
            def _(j=j):
                forward(goal(j - 1))

    for copy in loads[3:]:
        copy.wait()
    for j in range(chips):
        if j < chips - 1:

            @pl.when(jnp.logical_not(edge))
            def _(j=j):
                forward(goal(j))

        if j == min(1, chips - 1):
            total.relay()
        for t in range(j * tiles // chips, (j + 1) * tiles // chips):
            grad_tile(t)

    pair_copy(chip).wait_recv()

    def finish(here, value):
        o_ref[here] = value

    for u in range(parts):

        @pl.when(chip == 0)
        def _(u=u):
            hop(chip, u, 2).wait_recv()
            add(chip, u, (last,), finish)

        @pl.when(chip == chips - 1)
        def _(u=u):
            hop(chip, u, 0).wait_recv()
            add(chip, u, (inbox.at[chip],), finish)

        @pl.when((chip > 0) & (chip < chips - 1))
        def _(u=u):
            hop(chip, u, 0).wait_recv()
            hop(chip, u, 2).wait_recv()
            add(chip, u, (inbox.at[chip], last), finish)

    for d in range(chips):
        pair_copy(d).wait_send()
        for u in range(parts):

            @pl.when(d != chip)
            def _(d=d, u=u):
                hop(d, u, 0).wait_send()

    for t in range(tiles - 2, tiles):
        grad_copy(t).wait()
    total.finish()


def expert_second(sg, su, tail, ffn_all, d_down, w_gate, w_up, near, collective_id, parts=4):
    groups, seqs = lax.axis_size("expert"), lax.axis_size("dp")
    chips = groups // 2
    length, width = ffn_all.shape
    rows = length // groups
    experts, _, ff = w_gate.shape
    wide = width + LANES
    size = ff // seqs
    where = [index for _, index in near]
    near = [array for array, _ in near]
    n = len(near)

    def kernel(*refs):
        expert_second_body(
            groups, seqs, rows, width, ff, experts, parts, *refs[:7], list(zip(refs[7 : 7 + n], where)),
            *refs[7 + n :],
        )

    anywhere = pl.BlockSpec(memory_space=pl.ANY)
    dma = pltpu.SemaphoreType.DMA
    flat = pltpu.VMEM((length, experts * ff), BF16)
    block = pltpu.VMEM((2, size, width), BF16)
    return pl.pallas_call(
        kernel,
        out_shape=[
            jax.ShapeDtypeStruct((width, experts * ff), BF16),
            jax.ShapeDtypeStruct((2, size, width), BF16),
            jax.ShapeDtypeStruct((rows, wide), F32),
        ],
        in_specs=[anywhere] * (7 + n),
        out_specs=[anywhere, anywhere, pl.BlockSpec(memory_space=pltpu.VMEM)],
        scratch_shapes=[
            pltpu.VMEM((width, experts * ff), BF16),
            pltpu.VMEM((width, experts * ff), BF16),
            flat, flat,
            pltpu.VMEM((length, LANES), BF16),
            pltpu.VMEM((length, width), BF16),
            pltpu.VMEM((2, 256, experts * ff), BF16),
            pltpu.VMEM((chips, 2, rows, wide), BF16),
            pltpu.VMEM((chips, rows, wide), BF16),
            pltpu.VMEM((chips, rows, wide), BF16),
            pltpu.VMEM((rows, wide), BF16),
            block, block, block, pltpu.VMEM((2, 2, size, width), BF16),
            dma((4,)), dma((2, experts, 4)), dma((2,)), dma((chips,)), dma((chips,)),
            dma((chips, parts)), dma((chips, parts)), dma((parts,)),
            dma((4,)), dma((6,)), dma((6,)),
        ],
        compiler_params=pltpu.CompilerParams(
            collective_id=collective_id, has_side_effects=True, vmem_limit_bytes=60 * 1024 * 1024
        ),
        cost_estimate=cost_of(65),
        name="expert_second",
    )(sg, su, tail, ffn_all, w_gate, w_up, d_down, *near)


def gather_fill_body(
    groups, rows, parts, x_ref, f_ref, su_ref, hid_ref, wd_ref, o_ref, grad_out, y_out,
    f_buf, su, hid, wd, stage, in_sem, stage_sem, own_sem, send, recv, pair_send, pair_recv,
):
    chips = groups // 2
    length, width = f_buf.shape
    hidden = su.shape[1]
    size = stage.shape[1]
    loads = [
        pltpu.make_async_copy(src, dst, in_sem.at[i])
        for i, (src, dst) in enumerate(((f_ref, f_buf), (su_ref, su), (hid_ref, hid), (wd_ref, wd)))
    ]
    for copy in loads:
        copy.start()
    grads, mixes = width // size, length // size
    total = grads + mixes

    def place(t):
        return pl.ds((t if t < grads else t - grads) * size, size)

    def out_copy(t):
        to = grad_out if t < grads else y_out
        return pltpu.make_async_copy(stage.at[t % 2], to.at[place(t)], stage_sem.at[t % 2])

    def tile(t):
        if t == 0:
            loads[0].wait()
            loads[1].wait()
        if t == grads:
            loads[2].wait()
            loads[3].wait()
        if t >= 2:
            out_copy(t - 2).wait()
        for n in range(hidden // (2 * TILE)):
            cols = pl.ds(n * 2 * TILE, 2 * TILE)
            if t < grads:
                value = dot_tn(f_buf[:, place(t)], su[:, cols])
            else:
                value = dot(hid[place(t), :], wd[:, cols])
            stage[t % 2, :, cols] = value.astype(BF16)
        out_copy(t).start()

    turns = max(chips - 1, 1)

    def work(k):
        if k < turns:
            for t in range(k * total // turns, (k + 1) * total // turns):
                tile(t)

    gather_body(
        groups, rows, parts, Plane((), (), (), (), None, None), x_ref, o_ref,
        own_sem, send, recv, pair_send, pair_recv, work=work,
    )
    for t in range(total - 2, total):
        out_copy(t).wait()


def gather_fill(x, ffn_all, su, hid, wd, collective_id, parts=4):
    groups = lax.axis_size("expert")
    rows, width = x.shape
    length, hidden = su.shape
    anywhere = pl.BlockSpec(memory_space=pl.ANY)
    dma = pltpu.SemaphoreType.DMA
    line = dma((2, groups // 2, parts))
    tokens = jax.ShapeDtypeStruct((length, width), BF16)
    return pl.pallas_call(
        functools.partial(gather_fill_body, groups, rows, parts),
        out_shape=[tokens, jax.ShapeDtypeStruct((width, hidden), BF16), tokens],
        in_specs=[anywhere] * 5,
        out_specs=[anywhere] * 3,
        scratch_shapes=[
            pltpu.VMEM((length, width), BF16),
            pltpu.VMEM((length, hidden), BF16),
            pltpu.VMEM((length, hidden), BF16),
            pltpu.VMEM((hidden, width), BF16),
            pltpu.VMEM((2, 256, max(hidden, width)), BF16),
            dma((4,)), dma((2,)), dma, line, line, line, line,
        ],
        compiler_params=pltpu.CompilerParams(
            collective_id=collective_id, has_side_effects=True, vmem_limit_bytes=VMEM_LIMIT
        ),
        cost_estimate=cost_of(45),
        name="gather_fill",
    )(x, ffn_all, su, hid, wd)


class Opening:
    def __init__(self, sends, arrived, wholes):
        self.sends, self.arrived, self.wholes = sends, arrived, wholes

    def start(self):
        for i in (0, 1):
            self.sends.copy(i).start()

    def start_mid(self):
        self.arrived()
        for whole in self.wholes:
            whole.start()
        for i in (2, 3):
            self.sends.copy(i).start()

    def start_later(self):
        for whole in self.wholes:
            whole.start_later()

    def finish(self):
        for whole in self.wholes:
            whole.finish()
        self.sends.finish()


def opening_body(
    groups, seqs, copies, slab, rows, parts, gate_refs, x_ref, small_ref, out_ref, q_ref, k_ref, v_ref, gate_ref,
    x_to, small_to, qkv_to, wo_to, out_to, spread_to,
    box, send, recv, out_sem, own_sem, qkv_send, qkv_recv, small_sem, plane_send, plane_recv,
    whole_own, whole_send, whole_recv, keep_sem, line_send, line_recv, pair_send, pair_recv,
):
    me, dp = lax.axis_index("expert"), lax.axis_index("dp")
    total = groups * seqs
    mine = dp * groups + me
    block = q_ref.shape[0]
    barrier = pltpu.get_barrier_semaphore()

    def device(index):
        return (index // groups, index % groups)

    def hello(s, carry):
        pl.semaphore_signal(
            barrier, inc=1, device_id=device((mine + s) % total), device_id_type=MESH
        )
        return carry

    lax.fori_loop(1, total, hello, 0)
    pl.semaphore_wait(barrier, total - 1)

    def small_copy(s):
        return pltpu.make_async_remote_copy(
            src_ref=small_ref, dst_ref=box.at[mine], send_sem=send.at[s], recv_sem=recv.at[s],
            device_id=device((mine + s) % total), device_id_type=MESH,
        )

    def start(s, carry):
        small_copy(s).start()
        return carry

    def wait(s, carry):
        small_copy(s).wait()
        return carry

    lax.fori_loop(1, total, start, 0)
    place = pl.ds(pl.multiple_of(me * block, block), block)
    spread, own = [], []
    for m, ref in enumerate((q_ref, k_ref, v_ref)):
        cols = pl.ds(pl.multiple_of((me // copies) * slab, slab), slab)
        dst = spread_to.at[place, pl.ds(m * slab, slab)]
        own.append(pltpu.make_async_copy(ref.at[:, cols], dst, own_sem.at[m]))
        for s in range(1, groups):
            peer = (me + s) % groups
            cols = pl.ds(pl.multiple_of((peer // copies) * slab, slab), slab)
            spread.append(
                pltpu.make_async_remote_copy(
                    src_ref=ref.at[:, cols], dst_ref=dst,
                    send_sem=qkv_send.at[s, m], recv_sem=qkv_recv.at[s, m],
                    device_id=(dp, peer), device_id_type=MESH,
                )
            )
    moved = (mine % seqs) * groups + mine // seqs
    away = pltpu.make_async_remote_copy(
        src_ref=out_ref, dst_ref=out_to, send_sem=out_sem.at[0], recv_sem=out_sem.at[1],
        device_id=device(moved), device_id_type=MESH,
    )
    stay = pltpu.make_async_copy(out_ref, out_to, out_sem.at[0])
    for copy in spread:
        copy.start()

    @pl.when(moved != mine)
    def _():
        away.start()

    @pl.when(moved == mine)
    def _():
        stay.start()

    for copy in own:
        copy.start()
    box[mine] = small_ref[...]
    out_small = pltpu.make_async_copy(box, small_to, small_sem)

    def arrived():
        lax.fori_loop(1, total, wait, 0)
        out_small.start()
        for copy in own + spread:
            copy.wait()

        @pl.when(moved != mine)
        def _():
            away.wait()

        @pl.when(moved == mine)
        def _():
            stay.wait()

    sends = Plane(
        [(0, 0, 1, 1), (0, 0, 1, 2), (0, 1, 1, 1), (0, 1, 1, 2)], (), [gate_ref], gate_refs,
        plane_send, plane_recv,
    )
    wholes = [
        Whole(a, b, whole_own.at[i], whole_send.at[i], whole_recv.at[i])
        for i, (a, b) in enumerate(((spread_to, qkv_to), (out_to, wo_to)))
    ]
    gather_body(
        groups, rows, parts, Opening(sends, arrived, wholes), x_ref, x_to,
        keep_sem, line_send, line_recv, pair_send, pair_recv, greet=False,
    )
    out_small.wait()


def opening(x, small, w_out, w_query, w_key, w_value, w_gate, copies, slab, carry, collective_id, parts=4):
    groups, seqs = lax.axis_size("expert"), lax.axis_size("dp")
    total = groups * seqs
    block, width = w_query.shape
    rows = x.shape[0]
    gate = jax.ShapeDtypeStruct((1,) + w_gate.shape[1:], BF16)

    def kernel(*refs):
        ins, refs = refs[:7], refs[8:]
        outs, gates, rest = refs[:6], refs[6:10], refs[11:]
        opening_body(groups, seqs, copies, slab, rows, parts, gates, *ins, *outs, *rest)

    vmem, anywhere = pl.BlockSpec(memory_space=pltpu.VMEM), pl.BlockSpec(memory_space=pl.ANY)
    dma = pltpu.SemaphoreType.DMA
    line = dma((2, groups // 2, parts))
    return pl.pallas_call(
        kernel,
        out_shape=[
            jax.ShapeDtypeStruct((groups * rows, width), x.dtype),
            jax.ShapeDtypeStruct((total,) + small.shape, small.dtype),
            jax.ShapeDtypeStruct((seqs * groups * block, 3 * slab), BF16),
            jax.ShapeDtypeStruct((seqs * block, width), BF16),
            jax.ShapeDtypeStruct((block, width), BF16),
            jax.ShapeDtypeStruct((groups * block, 3 * slab), BF16),
        ]
        + [gate] * 4
        + [jax.ShapeDtypeStruct(carry.shape, carry.dtype)],
        in_specs=[anywhere, vmem] + [anywhere] * 6,
        out_specs=[anywhere] * 11,
        input_output_aliases={7: 10},
        scratch_shapes=[pltpu.VMEM((total,) + small.shape, small.dtype)]
        + [dma((total,)), dma((total,)), dma((2,)), dma((3,)), dma((groups, 3)), dma((groups, 3)), dma]
        + [dma((4,)), dma((4,)), dma((2,)), dma((2, 4)), dma((2, 4))]
        + [dma] + [line] * 4,
        compiler_params=pltpu.CompilerParams(collective_id=collective_id, has_side_effects=True),
        cost_estimate=cost_of(80),
        name="opening",
    )(x, small, w_out, w_query, w_key, w_value, w_gate, carry)


def both(array, start=0, size=None):
    size = array.shape[0] if size is None else size
    return [(array, start, size, 1), (array, start, size, 2)]


def swap_dp(block, flip):
    seqs = lax.axis_size("dp")
    return lax.ppermute(block, "dp", [(i, i ^ flip) for i in range(seqs)])


def tie(value, *deps):
    return lax.optimization_barrier((value,) + deps)[0]


def near_dp(block):
    return block, swap_dp(block, 1), swap_dp(block, 2)


def far_dp(near, *deps):
    block, near_x, near_y = near
    half = block.shape[0] // 2
    via_x, via_y = lax.optimization_barrier((near_y[:half], near_x[half:]) + deps)[:2]
    far = jnp.concatenate([swap_dp(via_x, 1), swap_dp(via_y, 2)], axis=0)
    return [block, near_x, near_y, far]


def halves(block):
    half = block.shape[0] // 2
    return [(block, 0, half, 1), (block, half, half, 2)]


def relay(blocks, from_x, from_y):
    _, to_x, to_y, _ = blocks
    half = to_x.shape[0] // 2
    to_x = jnp.concatenate(
        [to_x[:half], (to_x[half:].astype(F32) + from_y.astype(F32)).astype(BF16)], axis=0
    )
    to_y = jnp.concatenate(
        [(to_y[:half].astype(F32) + from_x.astype(F32)).astype(BF16), to_y[half:]], axis=0
    )
    return to_x, to_y


def settle(blocks, from_x, from_y):
    return blocks[0].astype(F32) + from_x.astype(F32) + from_y.astype(F32)


def send_halves(blocks):
    half = blocks[3].shape[0] // 2
    return swap_dp(blocks[3][:half], 1), swap_dp(blocks[3][half:], 2)


def in_order(pieces, index, axis):
    low = (index % 2) == 1
    high = (index // 2) == 1
    a, b, c, d = pieces
    a, b, c, d = (
        jnp.where(low, b, a), jnp.where(low, a, b), jnp.where(low, d, c), jnp.where(low, c, d)
    )
    return jnp.concatenate(
        [jnp.where(high, c, a), jnp.where(high, d, b), jnp.where(high, a, c), jnp.where(high, b, d)],
        axis=axis,
    )


def own_order(array, index, axis):
    return in_order(jnp.split(array, 4, axis=axis), index, axis)


def shards(
    tokens, routes, grad_output, w_query, w_key, w_value, w_out, w_router,
    gain_attn, gain_query, gain_key, gain_ffn, w_gate, w_up, w_down,
):
    rows = tokens.shape[1]
    width = tokens.shape[2]
    groups = lax.axis_size("expert")
    seqs = lax.axis_size("dp")
    me = lax.axis_index("expert")
    length = rows * groups
    local_experts = w_gate.shape[0]
    all_experts = local_experts * groups
    block = w_query.shape[0]
    own = width // groups
    slab = max(own, HEAD_DIM)
    copies = slab // own
    heads = slab // HEAD_DIM
    share = 1.0 / copies
    offset = (me % copies) * own

    x_low = tokens.reshape(rows, width)
    g_low = grad_output.reshape(rows, width)

    my_dp = lax.axis_index("dp")
    small_size = block * (all_experts + 4)
    small_rows = -(-small_size // (16 * 128)) * 16
    small = jnp.concatenate(
        [w_router.reshape(-1), gain_attn, gain_query, gain_key, gain_ffn,
         jnp.zeros((small_rows * 128 - small_size,), BF16)]
    )
    x_all, small_all, w_qkv, w_o, _, _, gate0_x, gate0_y, gate1_x, gate1_y, g_low = opening(
        x_low, small.reshape(small_rows, 128), w_out, w_query, w_key, w_value, w_gate, copies, slab,
        g_low, 1,
    )
    small_all = small_all.reshape(seqs * groups, small_rows * 128)
    split = block * all_experts
    w_r = small_all[:, :split].reshape(width, all_experts)
    gains = [
        small_all[:, split + i * block : split + (i + 1) * block].reshape(width).astype(F32)
        for i in range(4)
    ]
    g_attn, g_ffn = gains[0], gains[3]
    slab_start = (me // copies) * slab
    g_query = lax.dynamic_slice(gains[1], (slab_start,), (slab,))
    g_key = lax.dynamic_slice(gains[2], (slab_start,), (slab,))

    total = seqs * groups
    moves = [(b, (b % seqs) * groups + b // seqs) for b in range(total)]

    x_in = x_low.astype(F32)
    inv_attn = inv_rms(x_in)
    x_wide = x_all.astype(F32)
    normed_all = (x_wide * inv_rms(x_wide) * g_attn).astype(BF16)
    if copies > 1:
        sets = [[c * copies + i for i in range(copies)] for c in range(groups // copies)]
        w_o = lax.all_gather(w_o, "expert", axis_index_groups=sets, axis=0, tiled=True)

    near_up = tie(w_up, x_all)
    up_x, up_y = swap_dp(near_up, 1), swap_dp(near_up, 2)
    g_all = lax.all_gather(g_low, "expert", axis=0, tiled=True)

    raw = dot(normed_all, w_qkv)
    q_raw, k_raw, v_raw = raw[:, :slab], raw[:, slab : 2 * slab], raw[:, 2 * slab :]
    squares = jnp.stack([jnp.sum(q_raw * q_raw, axis=1), jnp.sum(k_raw * k_raw, axis=1)], axis=0)
    squares = exchange(
        (squares * share).reshape(1, 2 * length // 128, 128), 4, same=True, reduce=True
    ).reshape(2, length)
    inv_qk = lax.rsqrt(squares / width + EPS)
    inv_q, inv_k = inv_qk[0][:, None], inv_qk[1][:, None]
    tables = rope_tables(length)

    def to_heads(values):
        return values.reshape(length, heads, HEAD_DIM)

    queries = rotary(to_heads(q_raw * inv_q * g_query), tables).astype(BF16).transpose(1, 0, 2)
    keys = rotary(to_heads(k_raw * inv_k * g_key), tables).astype(BF16).transpose(1, 0, 2)
    values = to_heads(v_raw).astype(BF16).transpose(1, 0, 2)
    positions = jnp.arange(length, dtype=jnp.int32)
    scale = HEAD_DIM ** (-0.5)

    def head_probs(q, k):
        scores = dot_nt(q, k) * scale
        scores = jnp.where(positions[None, :] <= positions[:, None], scores, NEG)
        exp_terms = jnp.exp(scores - jnp.max(scores, axis=-1, keepdims=True))
        return exp_terms / jnp.sum(exp_terms, axis=-1, keepdims=True)

    mixes = []
    for h in range(heads):
        mixes.append(dot(head_probs(queries[h], keys[h]).astype(BF16), values[h]).astype(BF16))
    mix = jnp.concatenate(mixes, axis=1)
    o_sum, gate0_f, gate1_f, up0_f, up1_f = line_reduce(
        dot(mix, w_o) * share, 5,
        sends=[(gate0_y, 0, 1, 1), (gate1_x, 0, 1, 2), (up_y, 0, 1, 1), (up_x, 1, 1, 2)],
    )
    after_attn = x_in + o_sum

    inv_ffn = inv_rms(after_attn)
    ffn_low = (after_attn * inv_ffn * g_ffn).astype(BF16)
    router_prob = jax.nn.softmax(dot(ffn_low, w_r), axis=-1)
    chosen = routes.reshape(rows, routes.shape[2])
    chosen_mask = jnp.sum(
        (chosen[:, :, None] == jnp.arange(all_experts, dtype=jnp.int32)[None, None, :]).astype(F32),
        axis=1,
    )
    route_dense = router_prob * chosen_mask
    gate_near = [(gate0_x, 0), (gate1_x, 0), (gate0_y, 0), (gate1_y, 0), (gate0_f, 0), (gate1_f, 0)]
    up_near = [(up_x, 0), (up_x, 1), (up_y, 0), (up_y, 1), (up0_f, 0), (up1_f, 0)]
    ff = w_gate.shape[2]
    if copies == 1 and length * width <= 1 << 21:
        high = lax.reduce_precision(route_dense, 8, 7)
        space = jnp.zeros((rows, LANES // 2 - all_experts), F32)
        extra = jnp.concatenate([high, space, route_dense - high, space], axis=1).astype(BF16)
        ffn_all, hidden_w, d_gate, d_up, tail, wd, d_down = expert_first(
            jnp.concatenate([ffn_low, extra], axis=1), g_all, w_gate, w_up, w_down,
            gate_near + up_near, 9,
        )
        d_gate_w, own_down, d_rows = expert_second(
            d_gate, d_up, tail, ffn_all, d_down, w_gate, w_up, gate_near + up_near, 13
        )
        d_weight = d_rows[:, width : width + LANES]
        d_weight = d_weight[:, :all_experts] + d_weight[:, LANES // 2 : LANES // 2 + all_experts]
        d_rows = d_rows[:, :width]
    else:
        ffn_all = line_gather(ffn_low, 3)
        pad = -local_experts % 8
        route_send = route_dense.T.reshape(groups, local_experts, rows)
        route_send = jnp.pad(route_send, ((0, 0), (0, pad), (0, 0)))
        route_mine = exchange(route_send, 6)[:, :local_experts].transpose(0, 2, 1)
        route_mine = route_mine.reshape(length, local_experts)
        near_down = near_dp(tie(w_down, ffn_all))
        wd = in_order(far_dp(near_down), my_dp, 1)
        hidden_w, d_gate, d_up, d_weights = [], [], [], []
        y_part, dx_part = 0.0, 0.0
        for i in range(local_experts):
            wg, wu = (
                in_order([own[i]] + [near[2 * q + i][0][near[2 * q + i][1]] for q in range(3)], my_dp, 0)
                for own, near in ((w_gate, gate_near), (w_up, up_near))
            )
            weight = route_mine[:, i : i + 1]
            gate, up = dot(ffn_all, wg), dot(ffn_all, wu)
            d_hid = dot_nt(g_all, wd[i])
            sig = jax.nn.sigmoid(gate)
            silu = gate * sig
            d_weights.append(jnp.sum(silu * up * d_hid, axis=1))
            hidden_w.append((silu * up * weight).astype(BF16))
            d_hid = d_hid * weight
            d_gate.append((d_hid * up * sig * (1.0 + gate * (1.0 - sig))).astype(BF16))
            d_up.append((d_hid * silu).astype(BF16))
            y_part = y_part + dot(hidden_w[i], wd[i])
            dx_part = dx_part + dot_nt(d_gate[i], wg) + dot_nt(d_up[i], wu)
            (ffn_all, y_part, dx_part) = lax.optimization_barrier((ffn_all, y_part, dx_part))
        hidden_w, d_gate, d_up = (jnp.concatenate(a, axis=1) for a in (hidden_w, d_gate, d_up))
        y_part = y_part.astype(BF16)
        d_down = dot_tn(hidden_w, g_all).astype(BF16).reshape(local_experts, ff, width)
        d_rows = line_reduce(dx_part, 10)
        d_weight = jnp.stack(d_weights, axis=0).reshape(local_experts, groups, rows)
        d_weight = jnp.pad(d_weight.transpose(1, 0, 2), ((0, 0), (0, pad), (0, 0)))
        d_weight = exchange(d_weight, 6)[:, :local_experts].reshape(all_experts, rows).T

    fused = copies == 1 and length * width <= 1 << 21

    def scatter_in(product):
        return lax.psum_scatter(product, "dp", scatter_dimension=0, tiled=True)

    def to_experts(own_grad):
        return jnp.stack([own_grad[:, i * ff : (i + 1) * ff] for i in range(local_experts)]).astype(F32)

    if not fused:
        own_down = lax.psum_scatter(d_down, "dp", scatter_dimension=1, tiled=True)
        d_gate_w = dot_tn(ffn_all, d_gate).astype(BF16)
    own_gate = scatter_in(d_gate_w)
    d_router_prob = d_weight * chosen_mask

    d_logits = (
        router_prob * (d_router_prob - jnp.sum(d_router_prob * router_prob, axis=-1, keepdims=True))
    ).astype(BF16)
    d_router_w = dot_tn(ffn_low, d_logits)
    d_normed_ffn = d_rows + dot_nt(d_logits, w_r)
    d_after_norm, d_gain_ffn = norm_back(after_attn, inv_ffn, g_ffn, d_normed_ffn)
    d_after = g_low.astype(F32) + d_after_norm
    if fused:
        d_after_all, d_up_w, y_part = gather_fill(
            d_after.astype(BF16), ffn_all, d_up, hidden_w, wd.reshape(local_experts * ff, width), 11
        )
    else:
        d_after_all = line_gather(d_after.astype(BF16), 16)
        d_up_w = dot_tn(ffn_all, d_up).astype(BF16)
    own_up = scatter_in(d_up_w)
    d_out_w = dot_tn(mix, d_after_all)
    d_mix = dot_nt(d_after_all, w_o).astype(BF16)
    dqs, dks, dvs = [], [], []
    for h in range(heads):
        prob = head_probs(queries[h], keys[h])
        d_m = d_mix[:, h * HEAD_DIM : (h + 1) * HEAD_DIM]
        d_prob = dot_nt(d_m, values[h])
        row_delta = jnp.sum(d_prob * prob, axis=-1, keepdims=True)
        d_score = (prob * (d_prob - row_delta) * scale).astype(BF16)
        dqs.append(dot(d_score, keys[h]))
        dks.append(dot_tn(d_score, queries[h]))
        dvs.append(dot_tn(prob.astype(BF16), d_m))
    dq_n = rotary_back(jnp.stack(dqs, axis=1), tables).reshape(length, slab)
    dk_n = rotary_back(jnp.stack(dks, axis=1), tables).reshape(length, slab)
    dv_low = jnp.concatenate(dvs, axis=1).astype(BF16)
    dots = jnp.stack(
        [jnp.sum(dq_n * g_query * q_raw, axis=1), jnp.sum(dk_n * g_key * k_raw, axis=1)], axis=0
    )
    dots = exchange(
        (dots * share).reshape(1, 2 * length // 128, 128), 4, same=True, reduce=True
    ).reshape(2, length) / width
    d_gain_query = jnp.sum(dq_n * q_raw * inv_q, axis=0)
    d_gain_key = jnp.sum(dk_n * k_raw * inv_k, axis=0)
    dq_low = (inv_q * dq_n * g_query - q_raw * (inv_q**3 * dots[0][:, None])).astype(BF16)
    dk_low = (inv_k * dk_n * g_key - k_raw * (inv_k**3 * dots[1][:, None])).astype(BF16)
    d_raw = jnp.concatenate([dq_low, dk_low, dv_low], axis=1)
    d_qkv_w = dot_tn(normed_all, d_raw).astype(BF16)
    d_qkv_w = d_qkv_w.reshape(width, 3, slab)
    d_qkv_w = lax.dynamic_slice(d_qkv_w, (0, 0, offset), (width, 3, own))
    d_qkv_w = d_qkv_w.reshape(width, 3 * own)
    d_out_w = lax.dynamic_slice(d_out_w.astype(BF16), (offset, 0), (own, width))
    dx_in = (dot_nt(d_raw, w_qkv) * share).astype(BF16)
    if length * width <= 1 << 21:
        d_normed_in, y_sum, own_qkv, own_out = joint_reduce(
            [dx_in, y_part], [d_qkv_w, d_out_w], [own_gate], 12
        )
    else:
        d_normed_in, own_qkv, own_out = joint_reduce(
            [dx_in], [d_qkv_w, d_out_w], [own_gate], 12
        )
        y_sum = line_reduce(y_part, 15)
    output = after_attn + y_sum
    d_in_norm, d_gain_attn = norm_back(x_in, inv_attn, g_attn, d_normed_in)
    input_grad = d_after + d_in_norm

    spread = jnp.zeros((2, width), F32)
    spread = lax.dynamic_update_slice(
        spread, jnp.stack([d_gain_query, d_gain_key]) * share, (0, slab_start)
    )
    total = seqs * groups
    small_grad = jnp.concatenate(
        [d_router_w.reshape(total, split)]
        + [v.reshape(total, block) for v in (d_gain_attn, spread[0], spread[1], d_gain_ffn)]
        + [jnp.zeros((total, small_rows * 128 - small_size), F32)],
        axis=1,
    )
    small_grad = small_grad.reshape(total, small_rows, 128)
    if own % 128 == 0:
        small_grad, *matrices = last_exchange(small_grad, own_qkv, own_out, 8)
    else:
        small_grad = exchange(small_grad, 8, spread=True, reduce=True)
        own_qkv = exchange(own_qkv.reshape(groups, block, 3 * own), 7)
        own_qkv = own_qkv.reshape(groups, block, 3, own).transpose(2, 1, 0, 3)
        own_out = lax.ppermute(own_out, ("dp", "expert"), [(b, a) for a, b in moves])
        matrices = [*own_qkv.reshape(3, block, width).astype(F32), own_out.astype(F32)]
    small_grad = small_grad.reshape(-1)
    expert_owned = [to_experts(own_gate), to_experts(own_up), own_down.astype(F32)]
    return (
        output.reshape(1, rows, width),
        input_grad.reshape(1, rows, width),
        *matrices,
        small_grad[:split].reshape(block, all_experts),
        small_grad[split : split + block],
        small_grad[split + block : split + 2 * block],
        small_grad[split + 2 * block : split + 3 * block],
        small_grad[split + 3 * block : split + 4 * block],
        *expert_owned,
    )


def solution(mesh):
    tok = P("dp", "expert", None)
    mat = P(("dp", "expert"), None)
    vec = P(("dp", "expert"))
    exp = P("expert", "dp", None)
    return jax.shard_map(
        shards,
        mesh=mesh,
        in_specs=(tok, tok, tok, mat, mat, mat, mat, mat, vec, vec, vec, vec, exp, exp, exp),
        out_specs=(tok, tok, mat, mat, mat, mat, mat, vec, vec, vec, vec, exp, exp, exp),
        check_vma=False,
    )
```

```python
import functools
import math

import jax
import jax.numpy as jnp
from jax import lax
from jax.experimental import pallas as pl
from jax.experimental.pallas import tpu as pltpu
from jax.sharding import PartitionSpec as P

HEADS = 16
HEAD_DIM = 128

EPS = 1e-05
THETA = 10000.0
NEG = -1e30

F32 = jnp.float32
BF16 = jnp.bfloat16


def dot(left, right):
    return jnp.dot(left, right, preferred_element_type=F32)


def dot_tn(left, right):
    return lax.dot_general(left, right, (((0,), (0,)), ((), ())), preferred_element_type=F32)


def dot_nt(left, right):
    return lax.dot_general(left, right, (((1,), (1,)), ((), ())), preferred_element_type=F32)


def inv_rms(values):
    return lax.rsqrt(jnp.mean(values * values, axis=-1, keepdims=True) + EPS)


def norm_back(values, inv, gain_vec, grad):
    scaled = grad * gain_vec
    mean_dot = jnp.mean(scaled * values, axis=-1, keepdims=True)
    d_values = inv * scaled - values * (inv * inv * inv * mean_dot)
    d_gain = jnp.sum(grad * values * inv, axis=0)
    return d_values, d_gain


def rope_tables(length):
    half_dim = HEAD_DIM // 2
    inv_freq = jnp.exp(
        jnp.arange(half_dim, dtype=F32) * (-2.0 * math.log(THETA) / HEAD_DIM)
    )
    angles = jnp.arange(length, dtype=jnp.int32).astype(F32)[:, None] * inv_freq[None, :]
    cosine, sine = jnp.cos(angles), jnp.sin(angles)
    return (
        jnp.concatenate([cosine, cosine], axis=1)[:, None, :],
        jnp.concatenate([-sine, sine], axis=1)[:, None, :],
    )


def swap_halves(values):
    half_dim = HEAD_DIM // 2
    return jnp.concatenate([values[..., half_dim:], values[..., :half_dim]], axis=-1)


def rotary(values, tables):
    return values * tables[0] + swap_halves(values) * tables[1]


def rotary_back(grad, tables):
    return grad * tables[0] - swap_halves(grad) * tables[1]


MESH = pl.DeviceIdType.MESH
VMEM_LIMIT = 56 * 1024 * 1024


def cost_of(micros):
    return pl.CostEstimate(flops=0, bytes_accessed=int(micros * 3.0e6), transcendentals=0)


def flipped(dp, flip):
    return dp + flip - 2 * flip * ((dp // flip) % 2)


class Whole:
    def __init__(self, source, target, own_sem, send, recv):
        self.me, self.dp = lax.axis_index("expert"), lax.axis_index("dp")
        self.source, self.target = source, target
        self.own_sem, self.send, self.recv = own_sem, send, recv
        self.rows = source.shape[0]
        half = self.rows // 2
        self.split = (half, half) if half % 16 == 0 else (self.rows, 0)

    def place(self, owner, start, size):
        return self.target.at[pl.ds(pl.multiple_of(owner * self.rows, self.rows) + start, size)]

    def keep(self):
        return pltpu.make_async_copy(self.source, self.place(self.dp, 0, self.rows), self.own_sem)

    def copy(self, i):
        flip = i % 2 + 1
        if i < 2:
            src, dst = self.source, self.place(self.dp, 0, self.rows)
        else:
            start = 0 if i == 2 else self.split[0]
            src = dst = self.place(flipped(self.dp, 3 - flip), start, self.split[i - 2])
        return pltpu.make_async_remote_copy(
            src_ref=src, dst_ref=dst, send_sem=self.send.at[i], recv_sem=self.recv.at[i],
            device_id=(flipped(self.dp, flip), self.me), device_id_type=MESH,
        )

    def start(self):
        self.copy(0).start()
        self.copy(1).start()
        self.keep().start()

    def start_later(self):
        self.copy(1).wait_recv()
        self.copy(2).start()
        self.copy(0).wait_recv()
        if self.split[1]:
            self.copy(3).start()

    def finish(self):
        self.keep().wait()
        for i in range(4 if self.split[1] else 3):
            self.copy(i).wait_send()
            if i >= 2:
                self.copy(i).wait_recv()


class Plane:
    def __init__(self, sends, later, sources, targets, send, recv, wholes=()):
        self.me, self.dp = lax.axis_index("expert"), lax.axis_index("dp")
        self.sends, self.later, self.wholes = sends, later, wholes
        self.sources, self.targets, self.send, self.recv = sources, targets, send, recv

    def busy(self):
        return len(self.sends) + len(self.wholes) > 0

    def greet(self, barrier):
        if self.busy():
            for flip in (1, 2):
                pl.semaphore_signal(
                    barrier, inc=1, device_id=(flipped(self.dp, flip), self.me), device_id_type=MESH
                )

    def copy(self, i):
        first = len(self.sends)
        if i < first:
            source, start, size, flip = self.sends[i]
            ref = self.sources[source]
        else:
            source, start, size, flip = self.later[i - first]
            ref = self.targets[source]
        return pltpu.make_async_remote_copy(
            src_ref=ref.at[pl.ds(start, size)],
            dst_ref=self.targets[i],
            send_sem=self.send.at[i],
            recv_sem=self.recv.at[i],
            device_id=(flipped(self.dp, flip), self.me),
            device_id_type=MESH,
        )

    def start(self):
        for whole in self.wholes:
            whole.start()
        for i in range(len(self.sends)):
            self.copy(i).start()

    def start_later(self):
        first = len(self.sends)
        for source in sorted({l[0] for l in self.later}):
            self.copy(source).wait_recv()
        for i in range(len(self.later)):
            self.copy(first + i).start()
        for whole in self.wholes:
            whole.start_later()

    def finish(self):
        for whole in self.wholes:
            whole.finish()
        waited = {l[0] for l in self.later}
        for i in range(len(self.sends) + len(self.later)):
            self.copy(i).wait_send()
            if i not in waited:
                self.copy(i).wait_recv()


def line_greet(me, dp, chip, chips, plane):
    barrier = pltpu.get_barrier_semaphore()
    sibling = chip * 2 + 1 - me % 2
    extra = 2 if plane.busy() else 0
    pl.semaphore_signal(barrier, inc=1, device_id=(dp, sibling), device_id_type=MESH)
    plane.greet(barrier)

    @pl.when(chip > 0)
    def _():
        pl.semaphore_signal(barrier, inc=1, device_id=(dp, me - 2), device_id_type=MESH)

    @pl.when(chip < chips - 1)
    def _():
        pl.semaphore_signal(barrier, inc=1, device_id=(dp, me + 2), device_id_type=MESH)

    @pl.when((chip > 0) & (chip < chips - 1))
    def _():
        pl.semaphore_wait(barrier, 3 + extra)

    @pl.when((chip == 0) | (chip == chips - 1))
    def _():
        pl.semaphore_wait(barrier, 2 + extra)


def gather_body(
    groups, rows, parts, plane, x_ref, o_ref, own_sem, send, recv, pair_send, pair_recv,
    greet=True, work=None,
):
    chips = groups // 2
    me, dp = lax.axis_index("expert"), lax.axis_index("dp")
    chip = me // 2
    sibling = chip * 2 + 1 - me % 2
    part = rows // parts
    if greet:
        line_greet(me, dp, chip, chips, plane)
    keep = pltpu.make_async_copy(x_ref, o_ref.at[pl.ds(pl.multiple_of(me * rows, rows), rows)], own_sem)

    def copy(origin, u, target, send_sem, recv_sem, first):
        place = pl.ds(pl.multiple_of(origin * rows + u * part, part), part)
        return pltpu.make_async_remote_copy(
            src_ref=x_ref.at[pl.ds(u * part, part)] if first else o_ref.at[place],
            dst_ref=o_ref.at[place],
            send_sem=send_sem,
            recv_sem=recv_sem,
            device_id=(dp, target),
            device_id_type=MESH,
        )

    def right(k, u):
        return copy(me - 2 * k, u, me + 2, send.at[0, k, u], recv.at[0, k, u], k == 0)

    def left(k, u):
        return copy(me + 2 * k, u, me - 2, send.at[1, k, u], recv.at[1, k, u], k == 0)

    def pair(side, k, u):
        origin = me - 2 * k if side == 0 else me + 2 * k
        return copy(origin, u, sibling, pair_send.at[side, k, u], pair_recv.at[side, k, u], k == 0)

    sides = lambda k: (
        (0, chip - k >= 0, chip < chips - 1),
        (1, chip + k <= chips - 1, chip > 0),
    )
    for k in range(chips):
        if k == 1 and not greet:
            plane.start_mid()
        if k == chips - 1:
            plane.start_later()
        for u in range(parts):
            for side, has, send_on in sides(k):
                step = right if side == 0 else left

                @pl.when(has)
                def _(k=k, u=u, side=side, send_on=send_on, step=step):
                    if k > 0:
                        step(k - 1, u).wait_recv()
                    if k < chips - 1:

                        @pl.when(send_on)
                        def _():
                            step(k, u).start()

                    if k > 0:
                        pair(side, k, u).start()

            if k == 0:
                pair(0, 0, u).start()
        if k == 0:
            plane.start()
            keep.start()
        if work is not None:
            work(k)

    keep.wait()
    for k in range(chips):
        for u in range(parts):
            if k == 0:
                pair(0, 0, u).wait()
            for side, has, send_on in sides(k):
                step = right if side == 0 else left

                @pl.when(has)
                def _(k=k, u=u, side=side, send_on=send_on, step=step):
                    if k < chips - 1:

                        @pl.when(send_on)
                        def _():
                            step(k, u).wait_send()

                    if k > 0:
                        pair(side, k, u).wait()

    plane.finish()


def reduce_body(
    groups, rows, parts, plane, p_ref, o_ref, own, pair, inbox, load_sem, pair_send, pair_recv, send, recv
):
    chips = groups // 2
    me, dp = lax.axis_index("expert"), lax.axis_index("dp")
    chip, core = me // 2, me % 2
    sibling = chip * 2 + 1 - core
    part = rows // parts
    step_rows = 16
    line_greet(me, dp, chip, chips, plane)

    def pair_copy(d):
        place = pl.ds(pl.multiple_of((2 * d + 1 - core) * rows, rows), rows)
        return pltpu.make_async_remote_copy(
            src_ref=p_ref.at[place],
            dst_ref=pair.at[d],
            send_sem=pair_send.at[d],
            recv_sem=pair_recv.at[d],
            device_id=(dp, sibling),
            device_id_type=MESH,
        )

    def own_copy(d):
        place = pl.ds(pl.multiple_of((2 * d + core) * rows, rows), rows)
        return pltpu.make_async_copy(p_ref.at[place], own.at[d], load_sem.at[d])

    order = []
    for j in range((chips + 1) // 2):
        order += [chips - 1 - j] + ([j] if j != chips - 1 - j else [])
    for d in order:
        pair_copy(d).start()
        own_copy(d).start()
    plane.start()

    def hop(d, u, side):
        place = pl.ds(u * part, part)
        target = me + 2 if side == 0 else me - 2
        slot = d if side == 0 else chips + d
        return pltpu.make_async_remote_copy(
            src_ref=own.at[d, place],
            dst_ref=inbox.at[slot, place],
            send_sem=send.at[d, u],
            recv_sem=recv.at[slot, u],
            device_id=(dp, target),
            device_id_type=MESH,
        )

    def add(d, u, slots, store):
        def body(i, carry):
            at = pl.ds(pl.multiple_of(u * part + i * step_rows, step_rows), step_rows)
            value = own[d, at].astype(F32) + pair[d, at].astype(F32)
            for slot in slots:
                value = value + inbox[slot, at].astype(F32)
            store(at, value)
            return carry

        lax.fori_loop(0, part // step_rows, body, 0)

    def forward(d, side):
        pair_copy(d).wait_recv()
        own_copy(d).wait()

        def store(at, value):
            own[d, at] = value.astype(BF16)

        end = chip == (0 if side == 0 else chips - 1)
        for u in range(parts):

            @pl.when(end)
            def _(u=u):
                add(d, u, (), store)

            @pl.when(jnp.logical_not(end))
            def _(u=u):
                hop(d, u, side).wait_recv()
                add(d, u, (d if side == 0 else chips + d,), store)

            hop(d, u, side).start()

    for j in range(chips - 1):
        far, near = chips - 1 - j, j

        @pl.when(far > chip)
        def _(far=far):
            forward(far, 0)

        @pl.when(near < chip)
        def _(near=near):
            forward(near, 1)

        if j == chips - 2:
            plane.start_later()

    pair_copy(chip).wait_recv()
    own_copy(chip).wait()

    def finish(at, value):
        o_ref[at] = value

    for u in range(parts):

        @pl.when(chip == 0)
        def _(u=u):
            hop(chip, u, 1).wait_recv()
            add(chip, u, (chips + chip,), finish)

        @pl.when(chip == chips - 1)
        def _(u=u):
            hop(chip, u, 0).wait_recv()
            add(chip, u, (chip,), finish)

        @pl.when((chip > 0) & (chip < chips - 1))
        def _(u=u):
            hop(chip, u, 0).wait_recv()
            hop(chip, u, 1).wait_recv()
            add(chip, u, (chip, chips + chip), finish)

    for d in range(chips):
        pair_copy(d).wait_send()
        for u in range(parts):

            @pl.when(d > chip)
            def _(d=d, u=u):
                hop(d, u, 0).wait_send()

            @pl.when(d < chip)
            def _(d=d, u=u):
                hop(d, u, 1).wait_send()

    plane.finish()


def joint_body(
    groups, rows, parts, plane, p_refs, o_refs, own, pair, inbox, load_sem, pair_send, pair_recv, send, recv
):
    kinds = range(len(p_refs))
    chips = groups // 2
    me, dp = lax.axis_index("expert"), lax.axis_index("dp")
    chip, core = me // 2, me % 2
    sibling = chip * 2 + 1 - core
    part = rows // parts
    step_rows = 16
    line_greet(me, dp, chip, chips, plane)

    def pair_copy(a, d):
        place = pl.ds(pl.multiple_of((2 * d + 1 - core) * rows, rows), rows)
        return pltpu.make_async_remote_copy(
            src_ref=p_refs[a].at[place],
            dst_ref=pair.at[a, d],
            send_sem=pair_send.at[a, d],
            recv_sem=pair_recv.at[a, d],
            device_id=(dp, sibling),
            device_id_type=MESH,
        )

    def own_copy(a, d):
        place = pl.ds(pl.multiple_of((2 * d + core) * rows, rows), rows)
        return pltpu.make_async_copy(p_refs[a].at[place], own.at[a, d], load_sem.at[a, d])

    order = []
    for j in range((chips + 1) // 2):
        order += [chips - 1 - j] + ([j] if j != chips - 1 - j else [])
    for a in kinds:
        for d in order:
            pair_copy(a, d).start()
            own_copy(a, d).start()
    plane.start()

    def hop(a, d, u, side):
        place = pl.ds(u * part, part)
        target = me + 2 if side == 0 else me - 2
        slot = d if side == 0 else chips + d
        return pltpu.make_async_remote_copy(
            src_ref=own.at[a, d, place],
            dst_ref=inbox.at[a, slot, place],
            send_sem=send.at[a, d, u],
            recv_sem=recv.at[a, slot, u],
            device_id=(dp, target),
            device_id_type=MESH,
        )

    def add(a, d, u, slots, store):
        def body(i, carry):
            at = pl.ds(pl.multiple_of(u * part + i * step_rows, step_rows), step_rows)
            value = own[a, d, at].astype(F32) + pair[a, d, at].astype(F32)
            for slot in slots:
                value = value + inbox[a, slot, at].astype(F32)
            store(at, value)
            return carry

        lax.fori_loop(0, part // step_rows, body, 0)

    def forward(a, d, side):
        pair_copy(a, d).wait_recv()
        own_copy(a, d).wait()

        def store(at, value):
            own[a, d, at] = value.astype(BF16)

        end = chip == (0 if side == 0 else chips - 1)
        for u in range(parts):

            @pl.when(end)
            def _(u=u):
                add(a, d, u, (), store)

            @pl.when(jnp.logical_not(end))
            def _(u=u):
                hop(a, d, u, side).wait_recv()
                add(a, d, u, (d if side == 0 else chips + d,), store)

            hop(a, d, u, side).start()

    def finish(a):
        pair_copy(a, chip).wait_recv()
        own_copy(a, chip).wait()

        def store(at, value):
            o_refs[a][at] = value

        for u in range(parts):

            @pl.when(chip == 0)
            def _(u=u):
                hop(a, chip, u, 1).wait_recv()
                add(a, chip, u, (chips + chip,), store)

            @pl.when(chip == chips - 1)
            def _(u=u):
                hop(a, chip, u, 0).wait_recv()
                add(a, chip, u, (chip,), store)

            @pl.when((chip > 0) & (chip < chips - 1))
            def _(u=u):
                hop(a, chip, u, 0).wait_recv()
                hop(a, chip, u, 1).wait_recv()
                add(a, chip, u, (chip, chips + chip), store)

    for a in kinds:
        for j in range(chips - 1):
            far, near = chips - 1 - j, j

            @pl.when(far > chip)
            def _(a=a, far=far):
                forward(a, far, 0)

            @pl.when(near < chip)
            def _(a=a, near=near):
                forward(a, near, 1)

        if a == 0 and len(p_refs) > 1:

            @pl.when((chip > 0) & (chip < chips - 1))
            def _():
                plane.start_later()

    if len(p_refs) > 1:

        @pl.when((chip == 0) | (chip == chips - 1))
        def _():
            plane.start_later()

    else:
        plane.start_later()
    for a in kinds:
        finish(a)

    for a in kinds:
        for d in range(chips):
            pair_copy(a, d).wait_send()
            for u in range(parts):

                @pl.when(d > chip)
                def _(a=a, d=d, u=u):
                    hop(a, d, u, 0).wait_send()

                @pl.when(d < chip)
                def _(a=a, d=d, u=u):
                    hop(a, d, u, 1).wait_send()

    plane.finish()


class PlaneSum:
    def __init__(self, parts):
        self.me, self.dp = lax.axis_index("expert"), lax.axis_index("dp")
        self.parts = parts
        self.owners = (
            self.dp, flipped(self.dp, 1), flipped(self.dp, 2), flipped(flipped(self.dp, 1), 2)
        )

    def busy(self):
        return True

    greet = Plane.greet

    def remote(self, src, dst, send, recv, flip):
        return pltpu.make_async_remote_copy(
            src_ref=src, dst_ref=dst, send_sem=send, recv_sem=recv,
            device_id=(flipped(self.dp, flip), self.me), device_id_type=MESH,
        )

    def sizes(self, p):
        rows = p["out"].shape[0]
        half = rows // 2
        return rows, ((half, half) if half % 16 == 0 else (rows, 0))

    def rows_of(self, p, q, start, size):
        rows, _ = self.sizes(p)
        return pl.ds(pl.multiple_of(self.owners[q] * rows, rows) + start, size)

    def load(self, p):
        return pltpu.make_async_copy(p["ref"], p["buf"], p["load"])

    def early(self, p, i):
        _, split = self.sizes(p)
        start = 0 if i == 0 else split[0]
        return self.remote(
            p["ref"].at[self.rows_of(p, 3, start, split[i])], p["first"].at[pl.ds(start, split[i])],
            p["send"].at[i], p["recv"].at[i], i + 1,
        )

    def late(self, p, i):
        rows, _ = self.sizes(p)
        return self.remote(
            p["buf"].at[self.rows_of(p, i + 1, 0, rows)], p["second"].at[i],
            p["send"].at[2 + i], p["recv"].at[2 + i], i + 1,
        )

    def counts(self, p):
        return 2 if self.sizes(p)[1][1] else 1

    def start(self):
        for p in self.parts:
            for i in range(self.counts(p)):
                self.early(p, i).start()
            self.load(p).start()

    def start_later(self):
        for p in self.parts:
            rows, split = self.sizes(p)
            self.load(p).wait()
            for i in range(self.counts(p)):
                self.early(p, i).wait_recv()
                start = 0 if i == 0 else split[0]
                step = 16
                base = pl.multiple_of(self.owners[2 - i] * rows, rows) + start

                def body(t, carry, p=p, start=start, base=base, step=step):
                    here = pl.ds(pl.multiple_of(base + t * step, step), step)
                    there = pl.ds(pl.multiple_of(start + t * step, step), step)
                    value = p["buf"][here].astype(F32) + p["first"][there].astype(F32)
                    p["buf"][here] = value.astype(BF16)
                    return carry

                lax.fori_loop(0, split[i] // step, body, 0)
            for i in range(2):
                self.late(p, i).start()

    def finish(self):
        for p in self.parts:
            rows, _ = self.sizes(p)
            for i in range(2):
                self.late(p, i).wait()
            for i in range(self.counts(p)):
                self.early(p, i).wait_send()
            step = 16
            base = pl.multiple_of(self.dp * rows, rows)

            def body(t, carry, p=p, base=base, step=step):
                here = pl.ds(pl.multiple_of(base + t * step, step), step)
                there = pl.ds(pl.multiple_of(t * step, step), step)
                value = p["buf"][here].astype(F32) + p["second"][0, there].astype(F32)
                value = value + p["second"][1, there].astype(F32)
                p["out"][there] = value.astype(BF16)
                return carry

            lax.fori_loop(0, rows // step, body, 0)


def joint_reduce(partials, sums, after, collective_id, parts=4):
    groups, seqs = lax.axis_size("expert"), lax.axis_size("dp")
    chips = groups // 2
    rows, width = partials[0].shape[0] // groups, partials[0].shape[1]
    n, m, extra = len(partials), len(sums), len(after)

    def kernel(*refs):
        p_refs, s_refs = refs[:n], refs[n : n + m]
        refs = refs[n + m + extra :]
        o_refs, outs, rest = refs[:n], refs[n : n + m], refs[n + m :]
        names = ("buf", "first", "second", "load", "send", "recv")
        made = [
            dict(zip(names, rest[len(names) * i : len(names) * (i + 1)]), ref=s_refs[i], out=outs[i])
            for i in range(m)
        ]
        joint_body(groups, rows, parts, PlaneSum(made), p_refs, o_refs, *rest[len(names) * m :])

    anywhere, vmem = pl.BlockSpec(memory_space=pl.ANY), pl.BlockSpec(memory_space=pltpu.VMEM)
    dma = pltpu.SemaphoreType.DMA
    scratch = []
    for s in sums:
        own_rows = s.shape[0] // seqs
        scratch += [
            pltpu.VMEM(s.shape, BF16), pltpu.VMEM((own_rows,) + s.shape[1:], BF16),
            pltpu.VMEM((2, own_rows) + s.shape[1:], BF16), dma, dma((4,)), dma((4,)),
        ]
    return pl.pallas_call(
        kernel,
        out_shape=[jax.ShapeDtypeStruct((rows, width), F32)] * n
        + [jax.ShapeDtypeStruct((s.shape[0] // seqs,) + s.shape[1:], BF16) for s in sums],
        in_specs=[anywhere] * (n + m + extra),
        out_specs=[vmem] * (n + m),
        scratch_shapes=scratch + [
            pltpu.VMEM((n, chips, rows, width), BF16),
            pltpu.VMEM((n, chips, rows, width), BF16),
            pltpu.VMEM((n, 2 * chips, rows, width), BF16),
            dma((n, chips)), dma((n, chips)), dma((n, chips)),
            dma((n, chips, parts)), dma((n, 2 * chips, parts)),
        ],
        compiler_params=pltpu.CompilerParams(
            collective_id=collective_id, has_side_effects=True, vmem_limit_bytes=VMEM_LIMIT
        ),
        cost_estimate=cost_of(70),
        name="joint_reduce",
    )(*partials, *sums, *after)


def last_body(
    groups, seqs, small_ref, qkv_ref, out_ref, small_to, q_to, k_to, v_to, o_to,
    box, qkv_box, out_box, send, recv, qkv_send, qkv_recv, out_sem,
):
    me, dp = lax.axis_index("expert"), lax.axis_index("dp")
    total = groups * seqs
    mine = dp * groups + me
    block, width = o_to.shape
    own = width // groups
    barrier = pltpu.get_barrier_semaphore()

    def device(index):
        return (index // groups, index % groups)

    def hello(s, carry):
        pl.semaphore_signal(
            barrier, inc=1, device_id=device((mine + s) % total), device_id_type=MESH
        )
        return carry

    lax.fori_loop(1, total, hello, 0)
    pl.semaphore_wait(barrier, total - 1)

    def qkv_copy(s):
        peer = (me + s) % groups
        return pltpu.make_async_remote_copy(
            src_ref=qkv_ref.at[pl.ds(pl.multiple_of(peer * block, block), block)],
            dst_ref=qkv_box.at[me],
            send_sem=qkv_send.at[s], recv_sem=qkv_recv.at[s],
            device_id=(dp, peer), device_id_type=MESH,
        )

    def small_copy(s):
        target = (mine + s) % total
        return pltpu.make_async_remote_copy(
            src_ref=small_ref.at[target], dst_ref=box.at[mine],
            send_sem=send.at[s], recv_sem=recv.at[s],
            device_id=device(target), device_id_type=MESH,
        )

    owner = me * seqs + dp
    out_copy = pltpu.make_async_remote_copy(
        src_ref=out_ref, dst_ref=out_box, send_sem=out_sem.at[0], recv_sem=out_sem.at[1],
        device_id=device(owner), device_id_type=MESH,
    )

    def start(s, carry):
        small_copy(s).start()
        return carry

    def wait(s, carry):
        small_copy(s).wait()
        return carry

    lax.fori_loop(1, total, start, 0)
    for s in range(1, groups):
        qkv_copy(s).start()

    @pl.when(owner != mine)
    def _():
        out_copy.start()

    box[mine] = small_ref[mine]
    qkv_box[me] = qkv_ref[pl.ds(pl.multiple_of(me * block, block), block)]
    lax.fori_loop(1, total, wait, 0)

    def add(s, value):
        return value + box[s]

    small_to[...] = lax.fori_loop(1, total, add, box[0])

    @pl.when(owner != mine)
    def _():
        out_copy.wait()
        o_to[...] = out_box[...].astype(F32)

    @pl.when(owner == mine)
    def _():
        o_to[...] = out_ref[...].astype(F32)

    for s in range(1, groups):
        qkv_copy(s).wait()
    for e in range(groups):
        for m, to in enumerate((q_to, k_to, v_to)):
            to[:, e * own : (e + 1) * own] = qkv_box[e, :, m * own : (m + 1) * own].astype(F32)


def last_exchange(small, qkv, out, after, collective_id):
    groups, seqs = lax.axis_size("expert"), lax.axis_size("dp")
    total = groups * seqs
    block, width = out.shape
    vmem = pl.BlockSpec(memory_space=pltpu.VMEM)
    dma = pltpu.SemaphoreType.DMA
    matrix = jax.ShapeDtypeStruct((block, width), F32)
    held = len(after)

    def kernel(*refs):
        last_body(groups, seqs, *refs[:3], *refs[3 + held :])

    return pl.pallas_call(
        kernel,
        out_shape=[jax.ShapeDtypeStruct(small.shape[1:], F32)] + [matrix] * 4,
        in_specs=[vmem] * 3 + [pl.BlockSpec(memory_space=pl.ANY)] * held,
        out_specs=[vmem] * 5,
        scratch_shapes=[
            pltpu.VMEM(small.shape, F32),
            pltpu.VMEM((groups, block, qkv.shape[1]), BF16),
            pltpu.VMEM((block, width), BF16),
            dma((total,)), dma((total,)), dma((groups,)), dma((groups,)), dma((2,)),
        ],
        compiler_params=pltpu.CompilerParams(
            collective_id=collective_id, has_side_effects=True, vmem_limit_bytes=VMEM_LIMIT
        ),
        cost_estimate=cost_of(25),
        name="last_exchange",
    )(small, qkv, out, *after)


def exchange_body(count, spread, same, reduce, plane, x_ref, o_ref, box, send, recv):
    me, dp = lax.axis_index("expert"), lax.axis_index("dp")
    groups = lax.axis_size("expert")
    mine = dp * groups + me if spread else me

    def device(index):
        return (index // groups, index % groups) if spread else (dp, index)

    barrier = pltpu.get_barrier_semaphore()

    def hello(s, carry):
        pl.semaphore_signal(
            barrier, inc=1, device_id=device((mine + s) % count), device_id_type=MESH
        )
        return carry

    lax.fori_loop(1, count, hello, 0)
    plane.greet(barrier)
    pl.semaphore_wait(barrier, count - 1 + (2 if plane.busy() else 0))

    def copy(s):
        target = (mine + s) % count
        return pltpu.make_async_remote_copy(
            src_ref=x_ref.at[0] if same else x_ref.at[target],
            dst_ref=box.at[mine],
            send_sem=send.at[s],
            recv_sem=recv.at[s],
            device_id=device(target),
            device_id_type=MESH,
        )

    def start(s, carry):
        copy(s).start()
        return carry

    def wait(s, carry):
        copy(s).wait()
        return carry

    lax.fori_loop(1, count, start, 0)
    plane.start()
    box[mine] = x_ref[0] if same else x_ref[mine]
    lax.fori_loop(1, count, wait, 0)
    if reduce:

        def add(s, total):
            return total + box[s]

        o_ref[...] = lax.fori_loop(1, count, add, box[0])
    else:
        o_ref[...] = box[...]
    plane.start_later()
    plane.finish()


def run(
    body, name, micros, collective_id, x, x_space, out, out_space, scratch, sends, later,
    carry=(), after=(), wholes=(),
):
    arrays, specs = [], []
    for array, start, size, flip in sends:
        found = [i for i, a in enumerate(arrays) if a is array]
        if not found:
            arrays.append(array)
            found = [len(arrays) - 1]
        specs.append((found[0], start, size, flip))
    targets = [jax.ShapeDtypeStruct((s[2],) + s[0].shape[1:], s[0].dtype) for s in sends]
    for source, start, size, flip in later:
        targets.append(jax.ShapeDtypeStruct((size,) + targets[source].shape[1:], targets[source].dtype))
    seqs = lax.axis_size("dp")
    whole_out = [jax.ShapeDtypeStruct((seqs * w.shape[0],) + w.shape[1:], w.dtype) for w in wholes]
    n_in, n_out, held, n_whole = len(arrays), len(targets), len(carry), len(wholes)

    def kernel(*refs):
        x_ref, sources, whole_in = refs[0], refs[1 : 1 + n_in], refs[1 + n_in : 1 + n_in + n_whole]
        refs = refs[1 + n_in + n_whole + held + len(after) :]
        o_ref, dests, whole_to = refs[0], refs[1 : 1 + n_out], refs[1 + n_out : 1 + n_out + n_whole]
        rest = refs[1 + n_out + n_whole + held :]
        made = [
            Whole(a, b, rest[2].at[i], rest[3].at[i], rest[4].at[i])
            for i, (a, b) in enumerate(zip(whole_in, whole_to))
        ]
        plane = Plane(specs, later, sources, dests, *rest[:2], made)
        body(plane, x_ref, o_ref, *rest[5 if n_whole else 2 :])

    anywhere = pl.BlockSpec(memory_space=pl.ANY)
    dma = pltpu.SemaphoreType.DMA
    first, second = 1 + n_in + n_whole, 1 + n_out + n_whole
    got = pl.pallas_call(
        kernel,
        out_shape=[out] + targets + whole_out + [jax.ShapeDtypeStruct(c.shape, c.dtype) for c in carry],
        in_specs=[pl.BlockSpec(memory_space=x_space)] + [anywhere] * (n_in + n_whole + held + len(after)),
        out_specs=[pl.BlockSpec(memory_space=out_space)] + [anywhere] * (n_out + n_whole + held),
        input_output_aliases={first + i: second + i for i in range(held)},
        scratch_shapes=[dma((max(n_out, 1),))] * 2
        + ([dma((n_whole,)), dma((n_whole, 4)), dma((n_whole, 4))] if n_whole else [])
        + scratch,
        compiler_params=pltpu.CompilerParams(
            collective_id=collective_id, has_side_effects=True, vmem_limit_bytes=VMEM_LIMIT
        ),
        cost_estimate=cost_of(micros),
        name=name,
    )(x, *arrays, *wholes, *carry, *after)
    return got if n_out + n_whole + held else got[0]


def line_gather(x, collective_id, sends=(), later=(), carry=(), after=(), wholes=(), parts=4):
    rows, width = x.shape
    groups = lax.axis_size("expert")
    shape = (2, groups // 2, parts)
    return run(
        functools.partial(gather_body, groups, rows, parts), "line_gather", 40, collective_id,
        x, pl.ANY, jax.ShapeDtypeStruct((groups * rows, width), x.dtype), pl.ANY,
        [pltpu.SemaphoreType.DMA] + [pltpu.SemaphoreType.DMA(shape)] * 4,
        sends, later, carry, after, wholes,
    )


def line_reduce(partial, collective_id, sends=(), later=(), after=(), parts=4):
    groups = lax.axis_size("expert")
    chips = groups // 2
    rows, width = partial.shape[0] // groups, partial.shape[1]
    return run(
        functools.partial(reduce_body, groups, rows, parts), "line_reduce", 40, collective_id,
        partial.astype(BF16), pl.ANY, jax.ShapeDtypeStruct((rows, width), F32), pltpu.VMEM,
        [
            pltpu.VMEM((chips, rows, width), BF16),
            pltpu.VMEM((chips, rows, width), BF16),
            pltpu.VMEM((2 * chips, rows, width), BF16),
            pltpu.SemaphoreType.DMA((chips,)),
            pltpu.SemaphoreType.DMA((chips,)),
            pltpu.SemaphoreType.DMA((chips,)),
            pltpu.SemaphoreType.DMA((chips, parts)),
            pltpu.SemaphoreType.DMA((2 * chips, parts)),
        ],
        sends, later, (), after,
    )


def exchange(
    x, collective_id, spread=False, same=False, reduce=False, sends=(), later=(), carry=()
):
    count = lax.axis_size("expert") * (lax.axis_size("dp") if spread else 1)
    block = x.shape[1:]
    return run(
        functools.partial(exchange_body, count, spread, same, reduce), "exchange", 8, collective_id,
        x, pltpu.VMEM, jax.ShapeDtypeStruct(block if reduce else (count,) + block, x.dtype), pltpu.VMEM,
        [
            pltpu.VMEM((count,) + block, x.dtype),
            pltpu.SemaphoreType.DMA((count,)),
            pltpu.SemaphoreType.DMA((count,)),
        ],
        sends, later, carry,
    )


LANES = 128
TILE = 512


def expert_first_body(
    groups, seqs, rows, width, ff, experts, parts,
    x_ref, g_ref, gate_ref, up_ref, down_ref, near_refs,
    f_out, hid_out, sg_out, su_out, tail_out, down_out, grad_out,
    f_buf, g_buf, wg, wu, wd, hid, sg, su, tail_buf, tail_sum, stage,
    line_send, line_recv, side_send, side_recv, own_sem, f_sem, w_sem, d_sem, g_sem, out_sem, tail_sem,
    plane_send, plane_recv, stage_sem,
):
    chips = groups // 2
    me, dp = lax.axis_index("expert"), lax.axis_index("dp")
    chip, core = me // 2, me % 2
    sibling = chip * 2 + 1 - core
    chunk = 2 * rows
    part = rows // parts
    depth, wide_ff = width // seqs, ff // seqs

    def remote(src, dst, send_sem, recv_sem, device):
        return pltpu.make_async_remote_copy(
            src_ref=src, dst_ref=dst, send_sem=send_sem, recv_sem=recv_sem,
            device_id=device, device_id_type=MESH,
        )

    def at(index, size):
        return pl.ds(pl.multiple_of(index * size, size), size)

    def neighbour(flip):
        return (flipped(dp, flip), me)

    barrier = pltpu.get_barrier_semaphore()
    pl.semaphore_signal(barrier, inc=1, device_id=(dp, sibling), device_id_type=MESH)
    for flip in (1, 2):
        pl.semaphore_signal(barrier, inc=1, device_id=neighbour(flip), device_id_type=MESH)

    @pl.when(chip > 0)
    def _():
        pl.semaphore_signal(barrier, inc=1, device_id=(dp, me - 2), device_id_type=MESH)

    @pl.when(chip < chips - 1)
    def _():
        pl.semaphore_signal(barrier, inc=1, device_id=(dp, me + 2), device_id_type=MESH)

    @pl.when((chip > 0) & (chip < chips - 1))
    def _():
        pl.semaphore_wait(barrier, 5)

    @pl.when((chip == 0) | (chip == chips - 1))
    def _():
        pl.semaphore_wait(barrier, 4)

    def row_copy(origin, u, target, send_sem, recv_sem, first):
        place = pl.ds(pl.multiple_of(origin * rows + u * part, part), part)
        return remote(
            x_ref.at[pl.ds(u * part, part)] if first else f_buf.at[place], f_buf.at[place],
            send_sem, recv_sem, (dp, target),
        )

    def step(side, k, u):
        origin, target = (me - 2 * k, me + 2) if side == 0 else (me + 2 * k, me - 2)
        return row_copy(origin, u, target, line_send.at[side, k, u], line_recv.at[side, k, u], k == 0)

    def aside(side, k, u):
        origin = me - 2 * k if side == 0 else me + 2 * k
        return row_copy(origin, u, sibling, side_send.at[side, k, u], side_recv.at[side, k, u], k == 0)

    def sides(k):
        return (
            (0, chip - k >= 0, chip < chips - 1),
            (1, chip + k <= chips - 1, chip > 0),
        )

    keep = pltpu.make_async_copy(x_ref, f_buf.at[at(me, rows)], own_sem)

    def rows_out(c):
        return pltpu.make_async_copy(
            f_buf.at[at(c, chunk), pl.ds(0, width)], f_out.at[at(c, chunk)], f_sem.at[c]
        )

    def plane_copy(i):
        e, flip = (i // 2, i % 2 + 1) if i < 4 else (i - 4, i - 3)
        if i < 4:
            src, dst = down_ref.at[e], wd.at[e, at(dp, wide_ff)]
        else:
            src = wd.at[e, at(flipped(dp, 3 - flip), wide_ff)]
            dst = src
        return remote(src, dst, plane_send.at[i], plane_recv.at[i], neighbour(flip))

    owners = (dp, flipped(dp, 1), flipped(dp, 2), flipped(flipped(dp, 1), 2))

    def weight_copies():
        copies = []
        for m, (own, buf) in enumerate(((gate_ref, wg), (up_ref, wu))):
            for e in range(experts):
                near = [near_refs[6 * m + 2 * q + e] for q in range(3)]
                pieces = [own.at[e]] + [ref.at[index] for ref, index in near]
                for q, piece in enumerate(pieces):
                    copies.append(
                        pltpu.make_async_copy(
                            piece, buf.at[at(owners[q], depth), pl.ds(e * ff, ff)],
                            w_sem.at[m, e, q],
                        )
                    )
        return copies

    def down_copies():
        return [
            pltpu.make_async_copy(down_ref.at[e], wd.at[e, at(dp, wide_ff)], d_sem.at[e])
            for e in range(experts)
        ]

    grad_rows = [
        pltpu.make_async_copy(
            g_ref.at[pl.ds(r * chunk, chunk)], g_buf.at[pl.ds(r * chunk, chunk)], g_sem.at[r]
        )
        for r in range(chips)
    ]

    def first_layer(c):
        place = at(c, chunk)

        def tile(t, carry):
            cols = at(t, TILE)
            gate = dot(f_buf[place, pl.ds(0, width)], wg[:, cols])
            up = dot(f_buf[place, pl.ds(0, width)], wu[:, cols])
            sig = 1.0 / (1.0 + jnp.exp(-gate))
            silu = gate * sig
            hid[place, cols] = (silu * up).astype(BF16)
            sg[place, cols] = (up * sig * (1.0 + gate * (1.0 - sig))).astype(BF16)
            su[place, cols] = silu.astype(BF16)
            return carry

        lax.fori_loop(0, experts * ff // TILE, tile, 0)

    def ready(k):
        for u in range(parts):
            if k == 0:
                aside(0, 0, u).wait_recv()
            else:
                for side, has, _ in sides(k):

                    @pl.when(has)
                    def _(side=side, u=u):
                        aside(side, k, u).wait_recv()

        if k == 0:
            rows_out(chip).start()
            first_layer(chip)
        else:
            for side, has, _ in sides(k):
                c = chip - k if side == 0 else chip + k

                @pl.when(has)
                def _(c=c):
                    rows_out(c).start()
                    first_layer(c)

    for k in range(chips):
        for u in range(parts):
            for side, has, send_on in sides(k):

                @pl.when(has)
                def _(k=k, u=u, side=side, send_on=send_on):
                    if k > 0:
                        step(side, k - 1, u).wait_recv()
                    if k < chips - 1:

                        @pl.when(send_on)
                        def _():
                            step(side, k, u).start()

                    if k > 0:
                        aside(side, k, u).start()

            if k == 0:
                aside(0, 0, u).start()
        if k == 0:
            for i in range(4):
                plane_copy(i).start()
            keep.start()
            for copy in weight_copies():
                copy.start()
            for copy in down_copies():
                copy.start()
            for copy in grad_rows:
                copy.start()
            keep.wait()
            for copy in weight_copies():
                copy.wait()
        if k > 0:
            ready(k - 1)
    plane_copy(1).wait_recv()
    plane_copy(4).start()
    plane_copy(2).wait_recv()
    plane_copy(5).start()
    ready(chips - 1)

    for copy in down_copies():
        copy.wait()
    for i in (0, 3):
        plane_copy(i).wait_recv()

    def outs(r):
        place = pl.ds(r * chunk, chunk)
        return [
            pltpu.make_async_copy(buf.at[place], out.at[place], out_sem.at[i, r])
            for i, (buf, out) in enumerate(((hid, hid_out), (sg, sg_out), (su, su_out)))
        ]

    lane = lax.broadcasted_iota(jnp.int32, (chunk, LANES), 1)

    def back(r, first, last):
        place = pl.ds(r * chunk, chunk)
        extra = f_buf[place, pl.ds(width, LANES)].astype(F32)
        tail = jnp.zeros((chunk, LANES), F32) if first == 0 else tail_sum[place, :]
        for e in range(experts):
            which = me * experts + e
            low = which + LANES // 2
            weight = jnp.sum(
                jnp.where((lane == which) | (lane == low), extra, 0.0), axis=1, keepdims=True
            )
            for owner in owners[first:last]:
                d_hid = dot_nt(g_buf[place, :], wd[e, at(owner, wide_ff), :])
                cols = pl.ds(pl.multiple_of(e * ff + owner * wide_ff, wide_ff), wide_ff)
                hidden = hid[place, cols].astype(F32)
                d_weight = jnp.sum(hidden * d_hid, axis=1, keepdims=True)
                tail = tail + jnp.where(lane == which, d_weight, 0.0)
                d_hid = d_hid * weight
                hid[place, cols] = (hidden * weight).astype(BF16)
                sg[place, cols] = (d_hid * sg[place, cols].astype(F32)).astype(BF16)
                su[place, cols] = (d_hid * su[place, cols].astype(F32)).astype(BF16)
        if last < len(owners):
            tail_sum[place, :] = tail
        else:
            high = tail.astype(BF16).astype(F32)
            tail_buf[place, :] = (high + pltpu.roll(tail - high, LANES // 2, 1)).astype(BF16)

    tiles = [(e, q) for q in range(len(owners)) for e in range(experts)]

    def grad_place(t):
        e, q = tiles[t]
        return pl.ds(pl.multiple_of(e * ff + owners[q] * wide_ff, wide_ff), wide_ff)

    def grad_copy(t):
        return pltpu.make_async_copy(stage.at[t % 2], grad_out.at[grad_place(t)], stage_sem.at[t % 2])

    def grad_tile(t):
        if t >= 2:
            grad_copy(t - 2).wait()
        for n in range(width // (2 * TILE)):
            cols = pl.ds(n * 2 * TILE, 2 * TILE)
            stage[t % 2, :, cols] = dot_tn(hid[:, grad_place(t)], g_buf[:, cols]).astype(BF16)
        grad_copy(t).start()

    for copy in grad_rows:
        copy.wait()
    for r in range(chips):
        back(r, 0, 3)
    for t in range(3 * experts):
        grad_tile(t)
    for i in (4, 5):
        plane_copy(i).wait_recv()
    keep_down = pltpu.make_async_copy(wd, down_out, d_sem.at[experts])
    keep_down.start()
    for r in range(chips):
        back(r, 3, 4)
        for copy in outs(r):
            copy.start()
    for t in range(3 * experts, 4 * experts):
        grad_tile(t)
    for t in range(4 * experts - 2, 4 * experts):
        grad_copy(t).wait()
    keep_tail = pltpu.make_async_copy(tail_buf, tail_out, tail_sem)
    keep_tail.start()
    keep_tail.wait()
    keep_down.wait()
    for k in range(chips):
        for u in range(parts):
            if k == 0:
                aside(0, 0, u).wait_send()
            for side, has, send_on in sides(k):

                @pl.when(has)
                def _(k=k, u=u, side=side, send_on=send_on):
                    if k < chips - 1:

                        @pl.when(send_on)
                        def _():
                            step(side, k, u).wait_send()

                    if k > 0:
                        aside(side, k, u).wait_send()

    for i in range(6):
        plane_copy(i).wait_send()
    for d in range(chips):
        rows_out(d).wait()
        for copy in outs(d):
            copy.wait()


def expert_first(x, g_all, w_gate, w_up, w_down, near, collective_id, parts=4):
    groups, seqs = lax.axis_size("expert"), lax.axis_size("dp")
    chips = groups // 2
    rows, wide = x.shape
    length, width = g_all.shape
    experts, _, ff = w_gate.shape
    where = [index for _, index in near]
    near = [array for array, _ in near]
    n = len(near)

    def kernel(*refs):
        expert_first_body(
            groups, seqs, rows, width, ff, experts, parts, *refs[:5],
            list(zip(refs[5 : 5 + n], where)), *refs[5 + n :],
        )

    anywhere = pl.BlockSpec(memory_space=pl.ANY)
    dma = pltpu.SemaphoreType.DMA
    flat = jax.ShapeDtypeStruct((length, experts * ff), BF16)
    return pl.pallas_call(
        kernel,
        out_shape=[
            jax.ShapeDtypeStruct((length, width), BF16), flat, flat, flat,
            jax.ShapeDtypeStruct((length, LANES), BF16),
            jax.ShapeDtypeStruct((experts, ff, width), BF16),
            jax.ShapeDtypeStruct((experts * ff, width), BF16),
        ],
        in_specs=[anywhere] * (5 + n),
        out_specs=[anywhere] * 7,
        scratch_shapes=[
            pltpu.VMEM((length, wide), BF16),
            pltpu.VMEM((length, width), BF16),
            pltpu.VMEM((width, experts * ff), BF16),
            pltpu.VMEM((width, experts * ff), BF16),
            pltpu.VMEM((experts, ff, width), BF16),
            pltpu.VMEM((length, experts * ff), BF16),
            pltpu.VMEM((length, experts * ff), BF16),
            pltpu.VMEM((length, experts * ff), BF16),
            pltpu.VMEM((length, LANES), BF16),
            pltpu.VMEM((length, LANES), F32),
            pltpu.VMEM((2, ff // seqs, width), BF16),
            dma((2, chips, parts)), dma((2, chips, parts)), dma((2, chips, parts)), dma((2, chips, parts)),
            dma, dma((chips,)), dma((2, experts, 4)), dma((experts + 1,)), dma((chips,)), dma((3, chips)), dma,
            dma((6,)), dma((6,)), dma((2,)),
        ],
        compiler_params=pltpu.CompilerParams(
            collective_id=collective_id, has_side_effects=True, vmem_limit_bytes=VMEM_LIMIT
        ),
        cost_estimate=cost_of(70),
        name="expert_first",
    )(x, g_all, w_gate, w_up, w_down, *near)


class Blocks:
    def __init__(self, ref, size, half_stride, owner_stride):
        self.me, self.dp = lax.axis_index("expert"), lax.axis_index("dp")
        self.ref, self.size = ref, size
        self.half_stride, self.owner_stride = half_stride, owner_stride
        x, y = flipped(self.dp, 1), flipped(self.dp, 2)
        self.owners = (self.dp, x, y, flipped(x, 2))

    def piece(self, half, q):
        start = half * self.half_stride + self.owners[q] * self.owner_stride
        return self.ref.at[pl.ds(pl.multiple_of(start, self.size), self.size)]

    def remote(self, src, dst, send, recv, flip):
        return pltpu.make_async_remote_copy(
            src_ref=src, dst_ref=dst, send_sem=send, recv_sem=recv,
            device_id=(flipped(self.dp, flip), self.me), device_id_type=MESH,
        )


class SumEarly:
    def __init__(self, blocks, first, mid, near_out, mid_out, load, send, recv):
        self.me, self.dp = blocks.me, blocks.dp
        self.blocks, self.first, self.mid = blocks, first, mid
        self.near_out, self.mid_out = near_out, mid_out
        self.load_sem, self.send, self.recv = load, send, recv

    def busy(self):
        return True

    greet = Plane.greet

    def copy(self, i):
        b = self.blocks
        src, dst = (
            (b.piece(0, 3), self.first.at[0]),
            (b.piece(1, 3), self.first.at[1]),
            (b.piece(0, 1), self.near_out.at[0]),
            (b.piece(1, 2), self.near_out.at[1]),
        )[i]
        return b.remote(src, dst, self.send.at[i], self.recv.at[i], i % 2 + 1)

    def loads(self):
        b = self.blocks
        return [
            pltpu.make_async_copy(b.piece(0, 2), self.mid.at[0], self.load_sem.at[0]),
            pltpu.make_async_copy(b.piece(1, 1), self.mid.at[1], self.load_sem.at[1]),
        ]

    def keep(self):
        return pltpu.make_async_copy(self.mid, self.mid_out, self.load_sem.at[2])

    def start(self):
        for i in range(4):
            self.copy(i).start()
        for copy in self.loads():
            copy.start()

    def start_later(self):
        for copy in self.loads():
            copy.wait()
        for i in range(2):
            self.copy(i).wait_recv()

            def body(t, carry, i=i):
                here = pl.ds(pl.multiple_of(t * 16, 16), 16)
                value = self.mid[i, here].astype(F32) + self.first[i, here].astype(F32)
                self.mid[i, here] = value.astype(BF16)
                return carry

            lax.fori_loop(0, self.blocks.size // 16, body, 0)
        self.keep().start()

    def finish(self):
        for i in range(4):
            if i >= 2:
                self.copy(i).wait_recv()
            self.copy(i).wait_send()
        self.keep().wait()


class SumLate:
    def __init__(self, blocks, mid_ref, near_ref, late, near, own, out, load, send, recv):
        self.blocks, self.mid_ref, self.near_ref = blocks, mid_ref, near_ref
        self.late, self.near, self.own, self.out = late, near, own, out
        self.load_sem, self.send, self.recv = load, send, recv

    def copy(self, i):
        return self.blocks.remote(
            self.mid_ref.at[1 - i], self.late.at[1 - i], self.send.at[i], self.recv.at[i], i + 1
        )

    def loads(self):
        b = self.blocks
        return [
            pltpu.make_async_copy(b.piece(0, 0), self.own.at[0], self.load_sem.at[0]),
            pltpu.make_async_copy(b.piece(1, 0), self.own.at[1], self.load_sem.at[1]),
            pltpu.make_async_copy(self.near_ref, self.near, self.load_sem.at[2]),
        ]

    def start(self):
        for i in range(2):
            self.copy(i).start()
        for copy in self.loads():
            copy.start()

    def start_later(self):
        pass

    def finish(self):
        for copy in self.loads():
            copy.wait()
        for i in range(2):
            self.copy(i).wait()
        for half in range(2):

            def body(t, carry, half=half):
                here = pl.ds(pl.multiple_of(t * 16, 16), 16)
                value = self.own[half, here].astype(F32) + self.near[half, here].astype(F32)
                value = value + self.late[half, here].astype(F32)
                self.out[half, here] = value.astype(BF16)
                return carry

            lax.fori_loop(0, self.blocks.size // 16, body, 0)


class Several:
    def __init__(self, parts):
        self.me, self.dp = lax.axis_index("expert"), lax.axis_index("dp")
        self.parts = parts

    def busy(self):
        return True

    greet = Plane.greet

    def start(self):
        for part in self.parts:
            part.start()

    def start_later(self):
        for part in self.parts:
            part.start_later()

    def finish(self):
        for part in self.parts:
            part.finish()


def expert_second_body(
    groups, seqs, rows, width, ff, experts, parts,
    sg_ref, su_ref, tail_ref, f_ref, gate_ref, up_ref, down_ref, near_refs, grad_out, near_out, mid_out, o_ref,
    wg, wu, sg, su, tail_buf, f_buf, stage, acc, pair_in, inbox, last,
    first, mid,
    in_sem, w_sem, stage_sem, pair_send, pair_recv, hop_send, hop_recv, last_recv,
    sum_load, sum_send, sum_recv,
):
    chips = groups // 2
    me, dp = lax.axis_index("expert"), lax.axis_index("dp")
    chip, core = me // 2, me % 2
    sibling = chip * 2 + 1 - core
    chunk = 2 * rows
    part = rows // parts
    depth = width // seqs

    def remote(src, dst, send_sem, recv_sem, device):
        return pltpu.make_async_remote_copy(
            src_ref=src, dst_ref=dst, send_sem=send_sem, recv_sem=recv_sem,
            device_id=device, device_id_type=MESH,
        )

    def at(index, size):
        return pl.ds(pl.multiple_of(index * size, size), size)

    owners = (dp, flipped(dp, 1), flipped(dp, 2), flipped(flipped(dp, 1), 2))
    loads = [
        pltpu.make_async_copy(src, dst, in_sem.at[i])
        for i, (src, dst) in enumerate(
            ((sg_ref, sg), (su_ref, su), (tail_ref, tail_buf), (f_ref, f_buf))
        )
    ]
    weights = []
    for m, (own, buf) in enumerate(((gate_ref, wg), (up_ref, wu))):
        for e in range(experts):
            near = [near_refs[6 * m + 2 * q + e] for q in range(3)]
            pieces = [own.at[e]] + [ref.at[index] for ref, index in near]
            for q, piece in enumerate(pieces):
                weights.append(
                    pltpu.make_async_copy(
                        piece, buf.at[at(owners[q], depth), pl.ds(e * ff, ff)], w_sem.at[m, e, q]
                    )
                )
    for copy in loads[:3] + weights + loads[3:]:
        copy.start()
    blocks = Blocks(down_ref, ff // seqs, ff, ff // seqs)
    total = SumEarly(blocks, first, mid, near_out, mid_out, sum_load, sum_send, sum_recv)
    line_greet(me, dp, chip, chips, total)
    total.start()
    for copy in loads[:3]:
        copy.wait()
    for r in range(chips):
        for half in range(2):
            acc[r, half, :, pl.ds(width, LANES)] = tail_buf[pl.ds(r * chunk + half * rows, rows), :]

    out_tile = 256

    def row_grads(d, first=False):
        place = at(d, chunk)
        per = depth // out_tile

        def tile(t, carry):
            cols = at(t, out_tile)
            value = dot_nt(sg[place, :], wg[cols, :]) + dot_nt(su[place, :], wu[cols, :])
            value = value.astype(BF16)
            acc[d, 0, :, cols] = value[:rows]
            acc[d, 1, :, cols] = value[rows:]
            return carry

        if not first:
            lax.fori_loop(0, width // out_tile, tile, 0)
            return
        for q, owner in enumerate(owners):
            for copy in weights[q :: len(owners)]:
                copy.wait()
            lax.fori_loop(owner * per, owner * per + per, tile, 0)

    def pair_copy(d):
        return remote(acc.at[d, 1 - core], pair_in.at[d], pair_send.at[d], pair_recv.at[d], (dp, sibling))

    def hop(d, u, kind):
        place = pl.ds(u * part, part)
        if kind == 0:
            return remote(
                acc.at[d, core, place], inbox.at[d, place], hop_send.at[d, u], hop_recv.at[d, u],
                (dp, me + 2),
            )
        if kind == 1:
            return remote(
                acc.at[d, core, place], inbox.at[d, place], hop_send.at[d, u], hop_recv.at[d, u],
                (dp, me - 2),
            )
        return remote(
            acc.at[d, core, place], last.at[place], hop_send.at[d, u], last_recv.at[u], (dp, me - 2)
        )

    step_rows = 16

    def add(d, u, more, store):
        def body(i, carry):
            here = pl.ds(pl.multiple_of(u * part + i * step_rows, step_rows), step_rows)
            value = acc[d, core, here].astype(F32) + pair_in[d, here].astype(F32)
            for ref in more:
                value = value + ref[here].astype(F32)
            store(here, value)
            return carry

        lax.fori_loop(0, part // step_rows, body, 0)

    def forward(d):
        pair_copy(d).wait_recv()

        def store(here, value):
            acc[d, core, here] = value.astype(BF16)

        source = ((d > chip) & (chip == 0)) | ((d < chip) & (chip == chips - 1))
        for u in range(parts):

            @pl.when(source)
            def _(u=u):
                add(d, u, (), store)

            @pl.when(jnp.logical_not(source))
            def _(u=u):
                hop(d, u, 0).wait_recv()
                add(d, u, (inbox.at[d],), store)

            @pl.when(d > chip)
            def _(u=u):
                hop(d, u, 0).start()

            @pl.when((d < chip) & (d != chip - 1))
            def _(u=u):
                hop(d, u, 1).start()

            @pl.when((d < chip) & (d == chip - 1))
            def _(u=u):
                hop(d, u, 2).start()

    upper = chip // (chips // 2)
    mirrored = chip + upper * (chips - 1 - 2 * chip)

    def goal(j):
        turn = (j + mirrored) // (chips - 1)
        d = (1 - turn) * (chips - 1 - j) + turn * (j + mirrored - (chips - 1))
        return d + upper * (chips - 1 - 2 * d)

    edge = (chip == 0) | (chip == chips - 1)

    def grad_copy(t):
        return pltpu.make_async_copy(
            stage.at[t % 2], grad_out.at[pl.ds(t * out_tile, out_tile)], stage_sem.at[t % 2]
        )

    def grad_tile(t):
        if t >= 2:
            grad_copy(t - 2).wait()
        for n in range(experts * ff // (2 * TILE)):
            cols = pl.ds(n * 2 * TILE, 2 * TILE)
            stage[t % 2, :, cols] = dot_tn(
                f_buf[:, pl.ds(t * out_tile, out_tile)], sg[:, cols]
            ).astype(BF16)
        grad_copy(t).start()

    tiles = width // out_tile
    for j in range(chips):
        row_grads(goal(j), j == 0)
        pair_copy(goal(j)).start()
        if j > 0:

            @pl.when(edge)
            def _(j=j):
                forward(goal(j - 1))

    for copy in loads[3:]:
        copy.wait()
    for j in range(chips):
        if j < chips - 1:

            @pl.when(jnp.logical_not(edge))
            def _(j=j):
                forward(goal(j))

        if j == min(1, chips - 1):
            total.start_later()
        for t in range(j * tiles // chips, (j + 1) * tiles // chips):
            grad_tile(t)

    pair_copy(chip).wait_recv()

    def finish(here, value):
        o_ref[here] = value

    for u in range(parts):

        @pl.when(chip == 0)
        def _(u=u):
            hop(chip, u, 2).wait_recv()
            add(chip, u, (last,), finish)

        @pl.when(chip == chips - 1)
        def _(u=u):
            hop(chip, u, 0).wait_recv()
            add(chip, u, (inbox.at[chip],), finish)

        @pl.when((chip > 0) & (chip < chips - 1))
        def _(u=u):
            hop(chip, u, 0).wait_recv()
            hop(chip, u, 2).wait_recv()
            add(chip, u, (inbox.at[chip], last), finish)

    for d in range(chips):
        pair_copy(d).wait_send()
        for u in range(parts):

            @pl.when(d != chip)
            def _(d=d, u=u):
                hop(d, u, 0).wait_send()

    for t in range(tiles - 2, tiles):
        grad_copy(t).wait()
    total.finish()


def expert_second(sg, su, tail, ffn_all, d_down, w_gate, w_up, near, collective_id, parts=4):
    groups, seqs = lax.axis_size("expert"), lax.axis_size("dp")
    chips = groups // 2
    length, width = ffn_all.shape
    rows = length // groups
    experts, _, ff = w_gate.shape
    wide = width + LANES
    size = ff // seqs
    where = [index for _, index in near]
    near = [array for array, _ in near]
    n = len(near)

    def kernel(*refs):
        expert_second_body(
            groups, seqs, rows, width, ff, experts, parts, *refs[:7], list(zip(refs[7 : 7 + n], where)),
            *refs[7 + n :],
        )

    anywhere = pl.BlockSpec(memory_space=pl.ANY)
    dma = pltpu.SemaphoreType.DMA
    flat = pltpu.VMEM((length, experts * ff), BF16)
    block = pltpu.VMEM((2, size, width), BF16)
    return pl.pallas_call(
        kernel,
        out_shape=[
            jax.ShapeDtypeStruct((width, experts * ff), BF16),
            jax.ShapeDtypeStruct((2, size, width), BF16),
            jax.ShapeDtypeStruct((2, size, width), BF16),
            jax.ShapeDtypeStruct((rows, wide), F32),
        ],
        in_specs=[anywhere] * (7 + n),
        out_specs=[anywhere] * 3 + [pl.BlockSpec(memory_space=pltpu.VMEM)],
        scratch_shapes=[
            pltpu.VMEM((width, experts * ff), BF16),
            pltpu.VMEM((width, experts * ff), BF16),
            flat, flat,
            pltpu.VMEM((length, LANES), BF16),
            pltpu.VMEM((length, width), BF16),
            pltpu.VMEM((2, 256, experts * ff), BF16),
            pltpu.VMEM((chips, 2, rows, wide), BF16),
            pltpu.VMEM((chips, rows, wide), BF16),
            pltpu.VMEM((chips, rows, wide), BF16),
            pltpu.VMEM((rows, wide), BF16),
            block, block,
            dma((4,)), dma((2, experts, 4)), dma((2,)), dma((chips,)), dma((chips,)),
            dma((chips, parts)), dma((chips, parts)), dma((parts,)),
            dma((3,)), dma((4,)), dma((4,)),
        ],
        compiler_params=pltpu.CompilerParams(
            collective_id=collective_id, has_side_effects=True, vmem_limit_bytes=60 * 1024 * 1024
        ),
        cost_estimate=cost_of(65),
        name="expert_second",
    )(sg, su, tail, ffn_all, w_gate, w_up, d_down, *near)


def gather_fill_body(
    groups, seqs, ff, rows, parts, x_ref, f_ref, su_ref, hid_ref, wd_ref, down_ref, mid_ref, near_ref,
    o_ref, grad_out, y_out, down_out,
    f_buf, su, hid, wd, stage, late, near, own_block, in_sem, stage_sem, sum_load, sum_send, sum_recv,
    own_sem, send, recv, pair_send, pair_recv,
):
    chips = groups // 2
    length, width = f_buf.shape
    hidden = su.shape[1]
    size = stage.shape[1]
    loads = [
        pltpu.make_async_copy(src, dst, in_sem.at[i])
        for i, (src, dst) in enumerate(((f_ref, f_buf), (su_ref, su), (hid_ref, hid), (wd_ref, wd)))
    ]
    for copy in loads:
        copy.start()
    grads, mixes = width // size, length // size
    total = grads + mixes

    def place(t):
        return pl.ds((t if t < grads else t - grads) * size, size)

    def out_copy(t):
        to = grad_out if t < grads else y_out
        return pltpu.make_async_copy(stage.at[t % 2], to.at[place(t)], stage_sem.at[t % 2])

    def tile(t):
        if t == 0:
            loads[0].wait()
            loads[1].wait()
        if t == grads:
            loads[2].wait()
            loads[3].wait()
        if t >= 2:
            out_copy(t - 2).wait()
        for n in range(hidden // (2 * TILE)):
            cols = pl.ds(n * 2 * TILE, 2 * TILE)
            if t < grads:
                value = dot_tn(f_buf[:, place(t)], su[:, cols])
            else:
                value = dot(hid[place(t), :], wd[:, cols])
            stage[t % 2, :, cols] = value.astype(BF16)
        out_copy(t).start()

    turns = max(chips - 1, 1)
    rest = SumLate(
        Blocks(down_ref, ff // seqs, ff, ff // seqs), mid_ref, near_ref, late, near, own_block, down_out,
        sum_load, sum_send, sum_recv,
    )

    def work(k):
        if k < turns:
            for t in range(k * total // turns, (k + 1) * total // turns):
                tile(t)

    gather_body(
        groups, rows, parts, Several([rest]), x_ref, o_ref,
        own_sem, send, recv, pair_send, pair_recv, work=work,
    )
    for t in range(total - 2, total):
        out_copy(t).wait()


def gather_fill(x, ffn_all, su, hid, wd, d_down, mid, near, ff, collective_id, parts=4):
    groups, seqs = lax.axis_size("expert"), lax.axis_size("dp")
    rows, width = x.shape
    length, hidden = su.shape
    anywhere, vmem = pl.BlockSpec(memory_space=pl.ANY), pl.BlockSpec(memory_space=pltpu.VMEM)
    dma = pltpu.SemaphoreType.DMA
    line = dma((2, groups // 2, parts))
    tokens = jax.ShapeDtypeStruct((length, width), BF16)
    return pl.pallas_call(
        functools.partial(gather_fill_body, groups, seqs, ff, rows, parts),
        out_shape=[
            tokens, jax.ShapeDtypeStruct((width, hidden), BF16), tokens,
            jax.ShapeDtypeStruct(mid.shape, BF16),
        ],
        in_specs=[anywhere] * 8,
        out_specs=[anywhere] * 3 + [vmem],
        scratch_shapes=[
            pltpu.VMEM((length, width), BF16),
            pltpu.VMEM((length, hidden), BF16),
            pltpu.VMEM((length, hidden), BF16),
            pltpu.VMEM((hidden, width), BF16),
            pltpu.VMEM((2, 256, max(hidden, width)), BF16),
            pltpu.VMEM(mid.shape, BF16),
            pltpu.VMEM(mid.shape, BF16),
            pltpu.VMEM(mid.shape, BF16),
            dma((4,)), dma((2,)), dma((3,)), dma((2,)), dma((2,)),
            dma, line, line, line, line,
        ],
        compiler_params=pltpu.CompilerParams(
            collective_id=collective_id, has_side_effects=True, vmem_limit_bytes=VMEM_LIMIT
        ),
        cost_estimate=cost_of(45),
        name="gather_fill",
    )(x, ffn_all, su, hid, wd, d_down, mid, near)


class Opening:
    def __init__(self, sends, arrived, wholes):
        self.sends, self.arrived, self.wholes = sends, arrived, wholes

    def start(self):
        pass

    def start_mid(self):
        self.arrived()
        for whole in self.wholes:
            whole.start()

    def start_later(self):
        for whole in self.wholes:
            whole.start_later()

    def finish(self):
        for whole in self.wholes:
            whole.finish()
        self.sends.finish()


def opening_body(
    groups, seqs, copies, slab, rows, parts, gate_refs, x_ref, small_ref, out_ref, q_ref, k_ref, v_ref, gate_ref,
    x_to, small_to, qkv_to, wo_to, out_to, spread_to,
    box, send, recv, out_sem, own_sem, qkv_send, qkv_recv, small_sem, plane_send, plane_recv,
    whole_own, whole_send, whole_recv, keep_sem, line_send, line_recv, pair_send, pair_recv,
):
    me, dp = lax.axis_index("expert"), lax.axis_index("dp")
    total = groups * seqs
    mine = dp * groups + me
    block = q_ref.shape[0]
    barrier = pltpu.get_barrier_semaphore()

    def device(index):
        return (index // groups, index % groups)

    def hello(s, carry):
        pl.semaphore_signal(
            barrier, inc=1, device_id=device((mine + s) % total), device_id_type=MESH
        )
        return carry

    lax.fori_loop(1, total, hello, 0)
    pl.semaphore_wait(barrier, total - 1)

    def small_copy(s):
        return pltpu.make_async_remote_copy(
            src_ref=small_ref, dst_ref=box.at[mine], send_sem=send.at[s], recv_sem=recv.at[s],
            device_id=device((mine + s) % total), device_id_type=MESH,
        )

    def start(s, carry):
        small_copy(s).start()
        return carry

    def wait(s, carry):
        small_copy(s).wait()
        return carry

    lax.fori_loop(1, total, start, 0)
    place = pl.ds(pl.multiple_of(me * block, block), block)
    spread, own = [], []
    for m, ref in enumerate((q_ref, k_ref, v_ref)):
        cols = pl.ds(pl.multiple_of((me // copies) * slab, slab), slab)
        dst = spread_to.at[place, pl.ds(m * slab, slab)]
        own.append(pltpu.make_async_copy(ref.at[:, cols], dst, own_sem.at[m]))
        for s in range(1, groups):
            peer = (me + s) % groups
            cols = pl.ds(pl.multiple_of((peer // copies) * slab, slab), slab)
            spread.append(
                pltpu.make_async_remote_copy(
                    src_ref=ref.at[:, cols], dst_ref=dst,
                    send_sem=qkv_send.at[s, m], recv_sem=qkv_recv.at[s, m],
                    device_id=(dp, peer), device_id_type=MESH,
                )
            )
    moved = (mine % seqs) * groups + mine // seqs
    away = pltpu.make_async_remote_copy(
        src_ref=out_ref, dst_ref=out_to, send_sem=out_sem.at[0], recv_sem=out_sem.at[1],
        device_id=device(moved), device_id_type=MESH,
    )
    stay = pltpu.make_async_copy(out_ref, out_to, out_sem.at[0])
    @pl.when(moved != mine)
    def _():
        away.start()

    @pl.when(moved == mine)
    def _():
        stay.start()

    sends = Plane(
        [(0, 0, 1, 1), (0, 0, 1, 2), (0, 1, 1, 1), (0, 1, 1, 2)], (), [gate_ref], gate_refs,
        plane_send, plane_recv,
    )
    sends.start()
    for copy in spread:
        copy.start()
    for copy in own:
        copy.start()
    box[mine] = small_ref[...]
    out_small = pltpu.make_async_copy(box, small_to, small_sem)

    def arrived():
        for copy in own + spread:
            copy.wait()

        @pl.when(moved != mine)
        def _():
            away.wait()

        @pl.when(moved == mine)
        def _():
            stay.wait()

    wholes = [
        Whole(a, b, whole_own.at[i], whole_send.at[i], whole_recv.at[i])
        for i, (a, b) in enumerate(((spread_to, qkv_to), (out_to, wo_to)))
    ]
    gather_body(
        groups, rows, parts, Opening(sends, arrived, wholes), x_ref, x_to,
        keep_sem, line_send, line_recv, pair_send, pair_recv, greet=False,
    )
    lax.fori_loop(1, total, wait, 0)
    out_small.start()
    out_small.wait()


def opening(x, small, w_out, w_query, w_key, w_value, w_gate, copies, slab, carry, collective_id, parts=4):
    groups, seqs = lax.axis_size("expert"), lax.axis_size("dp")
    total = groups * seqs
    block, width = w_query.shape
    rows = x.shape[0]
    gate = jax.ShapeDtypeStruct((1,) + w_gate.shape[1:], BF16)

    def kernel(*refs):
        ins, refs = refs[:7], refs[8:]
        outs, gates, rest = refs[:6], refs[6:10], refs[11:]
        opening_body(groups, seqs, copies, slab, rows, parts, gates, *ins, *outs, *rest)

    vmem, anywhere = pl.BlockSpec(memory_space=pltpu.VMEM), pl.BlockSpec(memory_space=pl.ANY)
    dma = pltpu.SemaphoreType.DMA
    line = dma((2, groups // 2, parts))
    return pl.pallas_call(
        kernel,
        out_shape=[
            jax.ShapeDtypeStruct((groups * rows, width), x.dtype),
            jax.ShapeDtypeStruct((total,) + small.shape, small.dtype),
            jax.ShapeDtypeStruct((seqs * groups * block, 3 * slab), BF16),
            jax.ShapeDtypeStruct((seqs * block, width), BF16),
            jax.ShapeDtypeStruct((block, width), BF16),
            jax.ShapeDtypeStruct((groups * block, 3 * slab), BF16),
        ]
        + [gate] * 4
        + [jax.ShapeDtypeStruct(carry.shape, carry.dtype)],
        in_specs=[anywhere, vmem] + [anywhere] * 6,
        out_specs=[anywhere] * 11,
        input_output_aliases={7: 10},
        scratch_shapes=[pltpu.VMEM((total,) + small.shape, small.dtype)]
        + [dma((total,)), dma((total,)), dma((2,)), dma((3,)), dma((groups, 3)), dma((groups, 3)), dma]
        + [dma((4,)), dma((4,)), dma((2,)), dma((2, 4)), dma((2, 4))]
        + [dma] + [line] * 4,
        compiler_params=pltpu.CompilerParams(collective_id=collective_id, has_side_effects=True),
        cost_estimate=cost_of(80),
        name="opening",
    )(x, small, w_out, w_query, w_key, w_value, w_gate, carry)


def both(array, start=0, size=None):
    size = array.shape[0] if size is None else size
    return [(array, start, size, 1), (array, start, size, 2)]


def swap_dp(block, flip):
    seqs = lax.axis_size("dp")
    return lax.ppermute(block, "dp", [(i, i ^ flip) for i in range(seqs)])


def tie(value, *deps):
    return lax.optimization_barrier((value,) + deps)[0]


def near_dp(block):
    return block, swap_dp(block, 1), swap_dp(block, 2)


def far_dp(near, *deps):
    block, near_x, near_y = near
    half = block.shape[0] // 2
    via_x, via_y = lax.optimization_barrier((near_y[:half], near_x[half:]) + deps)[:2]
    far = jnp.concatenate([swap_dp(via_x, 1), swap_dp(via_y, 2)], axis=0)
    return [block, near_x, near_y, far]


def halves(block):
    half = block.shape[0] // 2
    return [(block, 0, half, 1), (block, half, half, 2)]


def relay(blocks, from_x, from_y):
    _, to_x, to_y, _ = blocks
    half = to_x.shape[0] // 2
    to_x = jnp.concatenate(
        [to_x[:half], (to_x[half:].astype(F32) + from_y.astype(F32)).astype(BF16)], axis=0
    )
    to_y = jnp.concatenate(
        [(to_y[:half].astype(F32) + from_x.astype(F32)).astype(BF16), to_y[half:]], axis=0
    )
    return to_x, to_y


def settle(blocks, from_x, from_y):
    return blocks[0].astype(F32) + from_x.astype(F32) + from_y.astype(F32)


def send_halves(blocks):
    half = blocks[3].shape[0] // 2
    return swap_dp(blocks[3][:half], 1), swap_dp(blocks[3][half:], 2)


def in_order(pieces, index, axis):
    low = (index % 2) == 1
    high = (index // 2) == 1
    a, b, c, d = pieces
    a, b, c, d = (
        jnp.where(low, b, a), jnp.where(low, a, b), jnp.where(low, d, c), jnp.where(low, c, d)
    )
    return jnp.concatenate(
        [jnp.where(high, c, a), jnp.where(high, d, b), jnp.where(high, a, c), jnp.where(high, b, d)],
        axis=axis,
    )


def own_order(array, index, axis):
    return in_order(jnp.split(array, 4, axis=axis), index, axis)


def shards(
    tokens, routes, grad_output, w_query, w_key, w_value, w_out, w_router,
    gain_attn, gain_query, gain_key, gain_ffn, w_gate, w_up, w_down,
):
    rows = tokens.shape[1]
    width = tokens.shape[2]
    groups = lax.axis_size("expert")
    seqs = lax.axis_size("dp")
    me = lax.axis_index("expert")
    length = rows * groups
    local_experts = w_gate.shape[0]
    all_experts = local_experts * groups
    block = w_query.shape[0]
    own = width // groups
    slab = max(own, HEAD_DIM)
    copies = slab // own
    heads = slab // HEAD_DIM
    share = 1.0 / copies
    offset = (me % copies) * own

    x_low = tokens.reshape(rows, width)
    g_low = grad_output.reshape(rows, width)

    my_dp = lax.axis_index("dp")
    small_size = block * (all_experts + 4)
    small_rows = -(-small_size // (16 * 128)) * 16
    small = jnp.concatenate(
        [w_router.reshape(-1), gain_attn, gain_query, gain_key, gain_ffn,
         jnp.zeros((small_rows * 128 - small_size,), BF16)]
    )
    x_all, small_all, w_qkv, w_o, _, _, gate0_x, gate0_y, gate1_x, gate1_y, g_low = opening(
        x_low, small.reshape(small_rows, 128), w_out, w_query, w_key, w_value, w_gate, copies, slab,
        g_low, 1,
    )
    small_all = small_all.reshape(seqs * groups, small_rows * 128)
    split = block * all_experts
    w_r = small_all[:, :split].reshape(width, all_experts)
    gains = [
        small_all[:, split + i * block : split + (i + 1) * block].reshape(width).astype(F32)
        for i in range(4)
    ]
    g_attn, g_ffn = gains[0], gains[3]
    slab_start = (me // copies) * slab
    g_query = lax.dynamic_slice(gains[1], (slab_start,), (slab,))
    g_key = lax.dynamic_slice(gains[2], (slab_start,), (slab,))

    total = seqs * groups
    moves = [(b, (b % seqs) * groups + b // seqs) for b in range(total)]

    x_in = x_low.astype(F32)
    inv_attn = inv_rms(x_in)
    x_wide = x_all.astype(F32)
    normed_all = (x_wide * inv_rms(x_wide) * g_attn).astype(BF16)
    if copies > 1:
        sets = [[c * copies + i for i in range(copies)] for c in range(groups // copies)]
        w_o = lax.all_gather(w_o, "expert", axis_index_groups=sets, axis=0, tiled=True)

    near_up = tie(w_up, x_all)
    up_x, up_y = swap_dp(near_up, 1), swap_dp(near_up, 2)
    g_all = lax.all_gather(g_low, "expert", axis=0, tiled=True)

    raw = dot(normed_all, w_qkv)
    q_raw, k_raw, v_raw = raw[:, :slab], raw[:, slab : 2 * slab], raw[:, 2 * slab :]
    squares = jnp.stack([jnp.sum(q_raw * q_raw, axis=1), jnp.sum(k_raw * k_raw, axis=1)], axis=0)
    squares = exchange(
        (squares * share).reshape(1, 2 * length // 128, 128), 4, same=True, reduce=True
    ).reshape(2, length)
    inv_qk = lax.rsqrt(squares / width + EPS)
    inv_q, inv_k = inv_qk[0][:, None], inv_qk[1][:, None]
    tables = rope_tables(length)

    def to_heads(values):
        return values.reshape(length, heads, HEAD_DIM)

    queries = rotary(to_heads(q_raw * inv_q * g_query), tables).astype(BF16).transpose(1, 0, 2)
    keys = rotary(to_heads(k_raw * inv_k * g_key), tables).astype(BF16).transpose(1, 0, 2)
    values = to_heads(v_raw).astype(BF16).transpose(1, 0, 2)
    positions = jnp.arange(length, dtype=jnp.int32)
    scale = HEAD_DIM ** (-0.5)

    def head_probs(q, k):
        scores = dot_nt(q, k) * scale
        scores = jnp.where(positions[None, :] <= positions[:, None], scores, NEG)
        exp_terms = jnp.exp(scores - jnp.max(scores, axis=-1, keepdims=True))
        return exp_terms / jnp.sum(exp_terms, axis=-1, keepdims=True)

    mixes = []
    for h in range(heads):
        mixes.append(dot(head_probs(queries[h], keys[h]).astype(BF16), values[h]).astype(BF16))
    mix = jnp.concatenate(mixes, axis=1)
    o_sum, gate0_f, gate1_f, up0_f, up1_f = line_reduce(
        dot(mix, w_o) * share, 5,
        sends=[(gate0_y, 0, 1, 1), (gate1_x, 0, 1, 2), (up_y, 0, 1, 1), (up_x, 1, 1, 2)],
    )
    after_attn = x_in + o_sum

    inv_ffn = inv_rms(after_attn)
    ffn_low = (after_attn * inv_ffn * g_ffn).astype(BF16)
    router_prob = jax.nn.softmax(dot(ffn_low, w_r), axis=-1)
    chosen = routes.reshape(rows, routes.shape[2])
    chosen_mask = jnp.sum(
        (chosen[:, :, None] == jnp.arange(all_experts, dtype=jnp.int32)[None, None, :]).astype(F32),
        axis=1,
    )
    route_dense = router_prob * chosen_mask
    gate_near = [(gate0_x, 0), (gate1_x, 0), (gate0_y, 0), (gate1_y, 0), (gate0_f, 0), (gate1_f, 0)]
    up_near = [(up_x, 0), (up_x, 1), (up_y, 0), (up_y, 1), (up0_f, 0), (up1_f, 0)]
    ff = w_gate.shape[2]
    if copies == 1 and length * width <= 1 << 21:
        high = lax.reduce_precision(route_dense, 8, 7)
        space = jnp.zeros((rows, LANES // 2 - all_experts), F32)
        extra = jnp.concatenate([high, space, route_dense - high, space], axis=1).astype(BF16)
        ffn_all, hidden_w, d_gate, d_up, tail, wd, d_down = expert_first(
            jnp.concatenate([ffn_low, extra], axis=1), g_all, w_gate, w_up, w_down,
            gate_near + up_near, 9,
        )
        d_gate_w, down_near, down_mid, d_rows = expert_second(
            d_gate, d_up, tail, ffn_all, d_down, w_gate, w_up, gate_near + up_near, 13
        )
        d_weight = d_rows[:, width : width + LANES]
        d_weight = d_weight[:, :all_experts] + d_weight[:, LANES // 2 : LANES // 2 + all_experts]
        d_rows = d_rows[:, :width]
    else:
        ffn_all = line_gather(ffn_low, 3)
        pad = -local_experts % 8
        route_send = route_dense.T.reshape(groups, local_experts, rows)
        route_send = jnp.pad(route_send, ((0, 0), (0, pad), (0, 0)))
        route_mine = exchange(route_send, 6)[:, :local_experts].transpose(0, 2, 1)
        route_mine = route_mine.reshape(length, local_experts)
        near_down = near_dp(tie(w_down, ffn_all))
        wd = in_order(far_dp(near_down), my_dp, 1)
        hidden_w, d_gate, d_up, d_weights = [], [], [], []
        y_part, dx_part = 0.0, 0.0
        for i in range(local_experts):
            wg, wu = (
                in_order([own[i]] + [near[2 * q + i][0][near[2 * q + i][1]] for q in range(3)], my_dp, 0)
                for own, near in ((w_gate, gate_near), (w_up, up_near))
            )
            weight = route_mine[:, i : i + 1]
            gate, up = dot(ffn_all, wg), dot(ffn_all, wu)
            d_hid = dot_nt(g_all, wd[i])
            sig = jax.nn.sigmoid(gate)
            silu = gate * sig
            d_weights.append(jnp.sum(silu * up * d_hid, axis=1))
            hidden_w.append((silu * up * weight).astype(BF16))
            d_hid = d_hid * weight
            d_gate.append((d_hid * up * sig * (1.0 + gate * (1.0 - sig))).astype(BF16))
            d_up.append((d_hid * silu).astype(BF16))
            y_part = y_part + dot(hidden_w[i], wd[i])
            dx_part = dx_part + dot_nt(d_gate[i], wg) + dot_nt(d_up[i], wu)
            (ffn_all, y_part, dx_part) = lax.optimization_barrier((ffn_all, y_part, dx_part))
        hidden_w, d_gate, d_up = (jnp.concatenate(a, axis=1) for a in (hidden_w, d_gate, d_up))
        y_part = y_part.astype(BF16)
        d_down = dot_tn(hidden_w, g_all).astype(BF16).reshape(local_experts, ff, width)
        d_rows = line_reduce(dx_part, 10)
        d_weight = jnp.stack(d_weights, axis=0).reshape(local_experts, groups, rows)
        d_weight = jnp.pad(d_weight.transpose(1, 0, 2), ((0, 0), (0, pad), (0, 0)))
        d_weight = exchange(d_weight, 6)[:, :local_experts].reshape(all_experts, rows).T

    fused = copies == 1 and length * width <= 1 << 21

    def scatter_in(product):
        return lax.psum_scatter(product, "dp", scatter_dimension=0, tiled=True)

    def to_experts(own_grad):
        return jnp.stack([own_grad[:, i * ff : (i + 1) * ff] for i in range(local_experts)]).astype(F32)

    if not fused:
        own_down = lax.psum_scatter(d_down, "dp", scatter_dimension=1, tiled=True)
        d_gate_w = dot_tn(ffn_all, d_gate).astype(BF16)
    own_gate = to_experts(scatter_in(d_gate_w))
    d_router_prob = d_weight * chosen_mask

    d_logits = (
        router_prob * (d_router_prob - jnp.sum(d_router_prob * router_prob, axis=-1, keepdims=True))
    ).astype(BF16)
    d_router_w = dot_tn(ffn_low, d_logits)
    d_normed_ffn = d_rows + dot_nt(d_logits, w_r)
    d_after_norm, d_gain_ffn = norm_back(after_attn, inv_ffn, g_ffn, d_normed_ffn)
    d_after = g_low.astype(F32) + d_after_norm
    if fused:
        d_after_all, d_up_w, y_part, own_down = gather_fill(
            d_after.astype(BF16), ffn_all, d_up, hidden_w, wd.reshape(local_experts * ff, width),
            d_down, down_mid, down_near, ff, 11,
        )
    else:
        d_after_all = line_gather(d_after.astype(BF16), 16)
        d_up_w = dot_tn(ffn_all, d_up).astype(BF16)
    own_up = scatter_in(d_up_w)
    d_out_w = dot_tn(mix, d_after_all)
    d_mix = dot_nt(d_after_all, w_o).astype(BF16)
    dqs, dks, dvs = [], [], []
    for h in range(heads):
        prob = head_probs(queries[h], keys[h])
        d_m = d_mix[:, h * HEAD_DIM : (h + 1) * HEAD_DIM]
        d_prob = dot_nt(d_m, values[h])
        row_delta = jnp.sum(d_prob * prob, axis=-1, keepdims=True)
        d_score = (prob * (d_prob - row_delta) * scale).astype(BF16)
        dqs.append(dot(d_score, keys[h]))
        dks.append(dot_tn(d_score, queries[h]))
        dvs.append(dot_tn(prob.astype(BF16), d_m))
    dq_n = rotary_back(jnp.stack(dqs, axis=1), tables).reshape(length, slab)
    dk_n = rotary_back(jnp.stack(dks, axis=1), tables).reshape(length, slab)
    dv_low = jnp.concatenate(dvs, axis=1).astype(BF16)
    dots = jnp.stack(
        [jnp.sum(dq_n * g_query * q_raw, axis=1), jnp.sum(dk_n * g_key * k_raw, axis=1)], axis=0
    )
    dots = exchange(
        (dots * share).reshape(1, 2 * length // 128, 128), 4, same=True, reduce=True
    ).reshape(2, length) / width
    d_gain_query = jnp.sum(dq_n * q_raw * inv_q, axis=0)
    d_gain_key = jnp.sum(dk_n * k_raw * inv_k, axis=0)
    dq_low = (inv_q * dq_n * g_query - q_raw * (inv_q**3 * dots[0][:, None])).astype(BF16)
    dk_low = (inv_k * dk_n * g_key - k_raw * (inv_k**3 * dots[1][:, None])).astype(BF16)
    d_raw = jnp.concatenate([dq_low, dk_low, dv_low], axis=1)
    d_qkv_w = dot_tn(normed_all, d_raw).astype(BF16)
    d_qkv_w = d_qkv_w.reshape(width, 3, slab)
    d_qkv_w = lax.dynamic_slice(d_qkv_w, (0, 0, offset), (width, 3, own))
    d_qkv_w = d_qkv_w.reshape(width, 3 * own)
    d_out_w = lax.dynamic_slice(d_out_w.astype(BF16), (offset, 0), (own, width))
    dx_in = (dot_nt(d_raw, w_qkv) * share).astype(BF16)
    if length * width <= 1 << 21:
        d_normed_in, y_sum, own_qkv, own_out = joint_reduce(
            [dx_in, y_part], [d_qkv_w, d_out_w], [own_gate], 12
        )
    else:
        d_normed_in, own_qkv, own_out = joint_reduce(
            [dx_in], [d_qkv_w, d_out_w], [own_gate], 12
        )
        y_sum = line_reduce(y_part, 15)
    output = after_attn + y_sum
    d_in_norm, d_gain_attn = norm_back(x_in, inv_attn, g_attn, d_normed_in)
    input_grad = d_after + d_in_norm

    spread = jnp.zeros((2, width), F32)
    spread = lax.dynamic_update_slice(
        spread, jnp.stack([d_gain_query, d_gain_key]) * share, (0, slab_start)
    )
    total = seqs * groups
    small_grad = jnp.concatenate(
        [d_router_w.reshape(total, split)]
        + [v.reshape(total, block) for v in (d_gain_attn, spread[0], spread[1], d_gain_ffn)]
        + [jnp.zeros((total, small_rows * 128 - small_size), F32)],
        axis=1,
    )
    small_grad = small_grad.reshape(total, small_rows, 128)
    if own % 128 == 0:
        output, input_grad = (a.reshape(1, rows, width) for a in (output, input_grad))
        small_grad, *matrices = last_exchange(
            small_grad, own_qkv, own_out, [output, input_grad], 8
        )
    else:
        small_grad = exchange(small_grad, 8, spread=True, reduce=True)
        own_qkv = exchange(own_qkv.reshape(groups, block, 3 * own), 7)
        own_qkv = own_qkv.reshape(groups, block, 3, own).transpose(2, 1, 0, 3)
        own_out = lax.ppermute(own_out, ("dp", "expert"), [(b, a) for a, b in moves])
        matrices = [*own_qkv.reshape(3, block, width).astype(F32), own_out.astype(F32)]
    small_grad = small_grad.reshape(-1)
    expert_owned = [own_gate, to_experts(own_up), own_down.astype(F32)]
    return (
        output.reshape(1, rows, width),
        input_grad.reshape(1, rows, width),
        *matrices,
        small_grad[:split].reshape(block, all_experts),
        small_grad[split : split + block],
        small_grad[split + block : split + 2 * block],
        small_grad[split + 2 * block : split + 3 * block],
        small_grad[split + 3 * block : split + 4 * block],
        *expert_owned,
    )


def solution(mesh):
    tok = P("dp", "expert", None)
    mat = P(("dp", "expert"), None)
    vec = P(("dp", "expert"))
    exp = P("expert", "dp", None)
    return jax.shard_map(
        shards,
        mesh=mesh,
        in_specs=(tok, tok, tok, mat, mat, mat, mat, mat, vec, vec, vec, vec, exp, exp, exp),
        out_specs=(tok, tok, mat, mat, mat, mat, mat, vec, vec, vec, vec, exp, exp, exp),
        check_vma=False,
    )
```

```python
import functools
import math

import jax
import jax.numpy as jnp
from jax import lax
from jax.experimental import pallas as pl
from jax.experimental.pallas import tpu as pltpu
from jax.sharding import PartitionSpec as P

HEADS = 16
HEAD_DIM = 128

EPS = 1e-05
THETA = 10000.0
NEG = -1e30

F32 = jnp.float32
BF16 = jnp.bfloat16


def dot(left, right):
    return jnp.dot(left, right, preferred_element_type=F32)


def dot_tn(left, right):
    return lax.dot_general(left, right, (((0,), (0,)), ((), ())), preferred_element_type=F32)


def dot_nt(left, right):
    return lax.dot_general(left, right, (((1,), (1,)), ((), ())), preferred_element_type=F32)


def inv_rms(values):
    return lax.rsqrt(jnp.mean(values * values, axis=-1, keepdims=True) + EPS)


def norm_back(values, inv, gain_vec, grad):
    scaled = grad * gain_vec
    mean_dot = jnp.mean(scaled * values, axis=-1, keepdims=True)
    d_values = inv * scaled - values * (inv * inv * inv * mean_dot)
    d_gain = jnp.sum(grad * values * inv, axis=0)
    return d_values, d_gain


def rope_tables(length):
    half_dim = HEAD_DIM // 2
    inv_freq = jnp.exp(
        jnp.arange(half_dim, dtype=F32) * (-2.0 * math.log(THETA) / HEAD_DIM)
    )
    angles = jnp.arange(length, dtype=jnp.int32).astype(F32)[:, None] * inv_freq[None, :]
    cosine, sine = jnp.cos(angles), jnp.sin(angles)
    return (
        jnp.concatenate([cosine, cosine], axis=1)[:, None, :],
        jnp.concatenate([-sine, sine], axis=1)[:, None, :],
    )


def swap_halves(values):
    half_dim = HEAD_DIM // 2
    return jnp.concatenate([values[..., half_dim:], values[..., :half_dim]], axis=-1)


def rotary(values, tables):
    return values * tables[0] + swap_halves(values) * tables[1]


def rotary_back(grad, tables):
    return grad * tables[0] - swap_halves(grad) * tables[1]


MESH = pl.DeviceIdType.MESH
VMEM_LIMIT = 56 * 1024 * 1024


def cost_of(micros):
    return pl.CostEstimate(flops=0, bytes_accessed=int(micros * 3.0e6), transcendentals=0)


def flipped(dp, flip):
    return dp + flip - 2 * flip * ((dp // flip) % 2)


class Whole:
    def __init__(self, source, target, own_sem, send, recv):
        self.me, self.dp = lax.axis_index("expert"), lax.axis_index("dp")
        self.source, self.target = source, target
        self.own_sem, self.send, self.recv = own_sem, send, recv
        self.rows = source.shape[0]
        half = self.rows // 2
        self.split = (half, half) if half % 16 == 0 else (self.rows, 0)

    def place(self, owner, start, size):
        return self.target.at[pl.ds(pl.multiple_of(owner * self.rows, self.rows) + start, size)]

    def keep(self):
        return pltpu.make_async_copy(self.source, self.place(self.dp, 0, self.rows), self.own_sem)

    def copy(self, i):
        flip = i % 2 + 1
        if i < 2:
            src, dst = self.source, self.place(self.dp, 0, self.rows)
        else:
            start = 0 if i == 2 else self.split[0]
            src = dst = self.place(flipped(self.dp, 3 - flip), start, self.split[i - 2])
        return pltpu.make_async_remote_copy(
            src_ref=src, dst_ref=dst, send_sem=self.send.at[i], recv_sem=self.recv.at[i],
            device_id=(flipped(self.dp, flip), self.me), device_id_type=MESH,
        )

    def start(self):
        self.copy(0).start()
        self.copy(1).start()
        self.keep().start()

    def start_later(self):
        self.copy(1).wait_recv()
        self.copy(2).start()
        self.copy(0).wait_recv()
        if self.split[1]:
            self.copy(3).start()

    def finish(self):
        self.keep().wait()
        for i in range(4 if self.split[1] else 3):
            self.copy(i).wait_send()
            if i >= 2:
                self.copy(i).wait_recv()


class Plane:
    def __init__(self, sends, later, sources, targets, send, recv, wholes=()):
        self.me, self.dp = lax.axis_index("expert"), lax.axis_index("dp")
        self.sends, self.later, self.wholes = sends, later, wholes
        self.sources, self.targets, self.send, self.recv = sources, targets, send, recv

    def busy(self):
        return len(self.sends) + len(self.wholes) > 0

    def greet(self, barrier):
        if self.busy():
            for flip in (1, 2):
                pl.semaphore_signal(
                    barrier, inc=1, device_id=(flipped(self.dp, flip), self.me), device_id_type=MESH
                )

    def copy(self, i):
        first = len(self.sends)
        if i < first:
            source, start, size, flip = self.sends[i]
            ref = self.sources[source]
        else:
            source, start, size, flip = self.later[i - first]
            ref = self.targets[source]
        return pltpu.make_async_remote_copy(
            src_ref=ref.at[pl.ds(start, size)],
            dst_ref=self.targets[i],
            send_sem=self.send.at[i],
            recv_sem=self.recv.at[i],
            device_id=(flipped(self.dp, flip), self.me),
            device_id_type=MESH,
        )

    def start(self):
        for whole in self.wholes:
            whole.start()
        for i in range(len(self.sends)):
            self.copy(i).start()

    def start_later(self):
        first = len(self.sends)
        for source in sorted({l[0] for l in self.later}):
            self.copy(source).wait_recv()
        for i in range(len(self.later)):
            self.copy(first + i).start()
        for whole in self.wholes:
            whole.start_later()

    def finish(self):
        for whole in self.wholes:
            whole.finish()
        waited = {l[0] for l in self.later}
        for i in range(len(self.sends) + len(self.later)):
            self.copy(i).wait_send()
            if i not in waited:
                self.copy(i).wait_recv()


def line_greet(me, dp, chip, chips, plane):
    barrier = pltpu.get_barrier_semaphore()
    sibling = chip * 2 + 1 - me % 2
    extra = 2 if plane.busy() else 0
    pl.semaphore_signal(barrier, inc=1, device_id=(dp, sibling), device_id_type=MESH)
    plane.greet(barrier)

    @pl.when(chip > 0)
    def _():
        pl.semaphore_signal(barrier, inc=1, device_id=(dp, me - 2), device_id_type=MESH)

    @pl.when(chip < chips - 1)
    def _():
        pl.semaphore_signal(barrier, inc=1, device_id=(dp, me + 2), device_id_type=MESH)

    @pl.when((chip > 0) & (chip < chips - 1))
    def _():
        pl.semaphore_wait(barrier, 3 + extra)

    @pl.when((chip == 0) | (chip == chips - 1))
    def _():
        pl.semaphore_wait(barrier, 2 + extra)


def gather_body(
    groups, rows, parts, plane, x_ref, o_ref, own_sem, send, recv, pair_send, pair_recv,
    greet=True, work=None,
):
    chips = groups // 2
    me, dp = lax.axis_index("expert"), lax.axis_index("dp")
    chip = me // 2
    sibling = chip * 2 + 1 - me % 2
    part = rows // parts
    if greet:
        line_greet(me, dp, chip, chips, plane)
    keep = pltpu.make_async_copy(x_ref, o_ref.at[pl.ds(pl.multiple_of(me * rows, rows), rows)], own_sem)

    def copy(origin, u, target, send_sem, recv_sem, first):
        place = pl.ds(pl.multiple_of(origin * rows + u * part, part), part)
        return pltpu.make_async_remote_copy(
            src_ref=x_ref.at[pl.ds(u * part, part)] if first else o_ref.at[place],
            dst_ref=o_ref.at[place],
            send_sem=send_sem,
            recv_sem=recv_sem,
            device_id=(dp, target),
            device_id_type=MESH,
        )

    def right(k, u):
        return copy(me - 2 * k, u, me + 2, send.at[0, k, u], recv.at[0, k, u], k == 0)

    def left(k, u):
        return copy(me + 2 * k, u, me - 2, send.at[1, k, u], recv.at[1, k, u], k == 0)

    def pair(side, k, u):
        origin = me - 2 * k if side == 0 else me + 2 * k
        return copy(origin, u, sibling, pair_send.at[side, k, u], pair_recv.at[side, k, u], k == 0)

    sides = lambda k: (
        (0, chip - k >= 0, chip < chips - 1),
        (1, chip + k <= chips - 1, chip > 0),
    )
    for k in range(chips):
        if k == 1 and not greet:
            plane.start_mid()
        if k == chips - 1:
            plane.start_later()
        for u in range(parts):
            for side, has, send_on in sides(k):
                step = right if side == 0 else left

                @pl.when(has)
                def _(k=k, u=u, side=side, send_on=send_on, step=step):
                    if k > 0:
                        step(k - 1, u).wait_recv()
                    if k < chips - 1:

                        @pl.when(send_on)
                        def _():
                            step(k, u).start()

                    if k > 0:
                        pair(side, k, u).start()

            if k == 0:
                pair(0, 0, u).start()
        if k == 0:
            plane.start()
            keep.start()
        if work is not None:
            work(k)

    keep.wait()
    for k in range(chips):
        for u in range(parts):
            if k == 0:
                pair(0, 0, u).wait()
            for side, has, send_on in sides(k):
                step = right if side == 0 else left

                @pl.when(has)
                def _(k=k, u=u, side=side, send_on=send_on, step=step):
                    if k < chips - 1:

                        @pl.when(send_on)
                        def _():
                            step(k, u).wait_send()

                    if k > 0:
                        pair(side, k, u).wait()

    plane.finish()


def reduce_body(
    groups, rows, parts, plane, p_ref, o_ref, own, pair, inbox, load_sem, pair_send, pair_recv, send, recv
):
    chips = groups // 2
    me, dp = lax.axis_index("expert"), lax.axis_index("dp")
    chip, core = me // 2, me % 2
    sibling = chip * 2 + 1 - core
    part = rows // parts
    step_rows = 16
    line_greet(me, dp, chip, chips, plane)

    def pair_copy(d):
        place = pl.ds(pl.multiple_of((2 * d + 1 - core) * rows, rows), rows)
        return pltpu.make_async_remote_copy(
            src_ref=p_ref.at[place],
            dst_ref=pair.at[d],
            send_sem=pair_send.at[d],
            recv_sem=pair_recv.at[d],
            device_id=(dp, sibling),
            device_id_type=MESH,
        )

    def own_copy(d):
        place = pl.ds(pl.multiple_of((2 * d + core) * rows, rows), rows)
        return pltpu.make_async_copy(p_ref.at[place], own.at[d], load_sem.at[d])

    order = []
    for j in range((chips + 1) // 2):
        order += [chips - 1 - j] + ([j] if j != chips - 1 - j else [])
    for d in order:
        pair_copy(d).start()
        own_copy(d).start()
    plane.start()

    def hop(d, u, side):
        place = pl.ds(u * part, part)
        target = me + 2 if side == 0 else me - 2
        slot = d if side == 0 else chips + d
        return pltpu.make_async_remote_copy(
            src_ref=own.at[d, place],
            dst_ref=inbox.at[slot, place],
            send_sem=send.at[d, u],
            recv_sem=recv.at[slot, u],
            device_id=(dp, target),
            device_id_type=MESH,
        )

    def add(d, u, slots, store):
        def body(i, carry):
            at = pl.ds(pl.multiple_of(u * part + i * step_rows, step_rows), step_rows)
            value = own[d, at].astype(F32) + pair[d, at].astype(F32)
            for slot in slots:
                value = value + inbox[slot, at].astype(F32)
            store(at, value)
            return carry

        lax.fori_loop(0, part // step_rows, body, 0)

    def forward(d, side):
        pair_copy(d).wait_recv()
        own_copy(d).wait()

        def store(at, value):
            own[d, at] = value.astype(BF16)

        end = chip == (0 if side == 0 else chips - 1)
        for u in range(parts):

            @pl.when(end)
            def _(u=u):
                add(d, u, (), store)

            @pl.when(jnp.logical_not(end))
            def _(u=u):
                hop(d, u, side).wait_recv()
                add(d, u, (d if side == 0 else chips + d,), store)

            hop(d, u, side).start()

    for j in range(chips - 1):
        far, near = chips - 1 - j, j

        @pl.when(far > chip)
        def _(far=far):
            forward(far, 0)

        @pl.when(near < chip)
        def _(near=near):
            forward(near, 1)

        if j == chips - 2:
            plane.start_later()

    pair_copy(chip).wait_recv()
    own_copy(chip).wait()

    def finish(at, value):
        o_ref[at] = value

    for u in range(parts):

        @pl.when(chip == 0)
        def _(u=u):
            hop(chip, u, 1).wait_recv()
            add(chip, u, (chips + chip,), finish)

        @pl.when(chip == chips - 1)
        def _(u=u):
            hop(chip, u, 0).wait_recv()
            add(chip, u, (chip,), finish)

        @pl.when((chip > 0) & (chip < chips - 1))
        def _(u=u):
            hop(chip, u, 0).wait_recv()
            hop(chip, u, 1).wait_recv()
            add(chip, u, (chip, chips + chip), finish)

    for d in range(chips):
        pair_copy(d).wait_send()
        for u in range(parts):

            @pl.when(d > chip)
            def _(d=d, u=u):
                hop(d, u, 0).wait_send()

            @pl.when(d < chip)
            def _(d=d, u=u):
                hop(d, u, 1).wait_send()

    plane.finish()


def joint_body(
    groups, rows, parts, plane, p_refs, o_refs, own, pair, inbox, load_sem, pair_send, pair_recv, send, recv
):
    kinds = range(len(p_refs))
    chips = groups // 2
    me, dp = lax.axis_index("expert"), lax.axis_index("dp")
    chip, core = me // 2, me % 2
    sibling = chip * 2 + 1 - core
    part = rows // parts
    step_rows = 16
    line_greet(me, dp, chip, chips, plane)

    def pair_copy(a, d):
        place = pl.ds(pl.multiple_of((2 * d + 1 - core) * rows, rows), rows)
        return pltpu.make_async_remote_copy(
            src_ref=p_refs[a].at[place],
            dst_ref=pair.at[a, d],
            send_sem=pair_send.at[a, d],
            recv_sem=pair_recv.at[a, d],
            device_id=(dp, sibling),
            device_id_type=MESH,
        )

    def own_copy(a, d):
        place = pl.ds(pl.multiple_of((2 * d + core) * rows, rows), rows)
        return pltpu.make_async_copy(p_refs[a].at[place], own.at[a, d], load_sem.at[a, d])

    order = []
    for j in range((chips + 1) // 2):
        order += [chips - 1 - j] + ([j] if j != chips - 1 - j else [])
    for a in kinds:
        for d in order:
            pair_copy(a, d).start()
            own_copy(a, d).start()
    plane.start()

    def hop(a, d, u, side):
        place = pl.ds(u * part, part)
        target = me + 2 if side == 0 else me - 2
        slot = d if side == 0 else chips + d
        return pltpu.make_async_remote_copy(
            src_ref=own.at[a, d, place],
            dst_ref=inbox.at[a, slot, place],
            send_sem=send.at[a, d, u],
            recv_sem=recv.at[a, slot, u],
            device_id=(dp, target),
            device_id_type=MESH,
        )

    def add(a, d, u, slots, store):
        def body(i, carry):
            at = pl.ds(pl.multiple_of(u * part + i * step_rows, step_rows), step_rows)
            value = own[a, d, at].astype(F32) + pair[a, d, at].astype(F32)
            for slot in slots:
                value = value + inbox[a, slot, at].astype(F32)
            store(at, value)
            return carry

        lax.fori_loop(0, part // step_rows, body, 0)

    def forward(a, d, side):
        pair_copy(a, d).wait_recv()
        own_copy(a, d).wait()

        def store(at, value):
            own[a, d, at] = value.astype(BF16)

        end = chip == (0 if side == 0 else chips - 1)
        for u in range(parts):

            @pl.when(end)
            def _(u=u):
                add(a, d, u, (), store)

            @pl.when(jnp.logical_not(end))
            def _(u=u):
                hop(a, d, u, side).wait_recv()
                add(a, d, u, (d if side == 0 else chips + d,), store)

            hop(a, d, u, side).start()

    def finish(a):
        pair_copy(a, chip).wait_recv()
        own_copy(a, chip).wait()

        def store(at, value):
            o_refs[a][at] = value

        for u in range(parts):

            @pl.when(chip == 0)
            def _(u=u):
                hop(a, chip, u, 1).wait_recv()
                add(a, chip, u, (chips + chip,), store)

            @pl.when(chip == chips - 1)
            def _(u=u):
                hop(a, chip, u, 0).wait_recv()
                add(a, chip, u, (chip,), store)

            @pl.when((chip > 0) & (chip < chips - 1))
            def _(u=u):
                hop(a, chip, u, 0).wait_recv()
                hop(a, chip, u, 1).wait_recv()
                add(a, chip, u, (chip, chips + chip), store)

    for a in kinds:
        for j in range(chips - 1):
            far, near = chips - 1 - j, j

            @pl.when(far > chip)
            def _(a=a, far=far):
                forward(a, far, 0)

            @pl.when(near < chip)
            def _(a=a, near=near):
                forward(a, near, 1)

            if a == 0 and j == (chips - 1) // 2:

                @pl.when((chip > 0) & (chip < chips - 1))
                def _():
                    plane.start_later()

    if len(p_refs) > 1:

        @pl.when((chip == 0) | (chip == chips - 1))
        def _():
            plane.start_later()

    else:
        plane.start_later()
    for a in kinds:
        finish(a)

    for a in kinds:
        for d in range(chips):
            pair_copy(a, d).wait_send()
            for u in range(parts):

                @pl.when(d > chip)
                def _(a=a, d=d, u=u):
                    hop(a, d, u, 0).wait_send()

                @pl.when(d < chip)
                def _(a=a, d=d, u=u):
                    hop(a, d, u, 1).wait_send()

    plane.finish()


class PlaneSum:
    def __init__(self, parts):
        self.me, self.dp = lax.axis_index("expert"), lax.axis_index("dp")
        self.parts = parts
        self.owners = (
            self.dp, flipped(self.dp, 1), flipped(self.dp, 2), flipped(flipped(self.dp, 1), 2)
        )

    def busy(self):
        return True

    greet = Plane.greet

    def remote(self, src, dst, send, recv, flip):
        return pltpu.make_async_remote_copy(
            src_ref=src, dst_ref=dst, send_sem=send, recv_sem=recv,
            device_id=(flipped(self.dp, flip), self.me), device_id_type=MESH,
        )

    def sizes(self, p):
        rows = p["out"].shape[0]
        half = rows // 2
        return rows, ((half, half) if half % 16 == 0 else (rows, 0))

    def rows_of(self, p, q, start, size):
        rows, _ = self.sizes(p)
        return pl.ds(pl.multiple_of(self.owners[q] * rows, rows) + start, size)

    def load(self, p):
        return pltpu.make_async_copy(p["ref"], p["buf"], p["load"])

    def early(self, p, i):
        _, split = self.sizes(p)
        start = 0 if i == 0 else split[0]
        return self.remote(
            p["ref"].at[self.rows_of(p, 3, start, split[i])], p["first"].at[pl.ds(start, split[i])],
            p["send"].at[i], p["recv"].at[i], i + 1,
        )

    def late(self, p, i):
        rows, _ = self.sizes(p)
        return self.remote(
            p["buf"].at[self.rows_of(p, i + 1, 0, rows)], p["second"].at[i],
            p["send"].at[2 + i], p["recv"].at[2 + i], i + 1,
        )

    def counts(self, p):
        return 2 if self.sizes(p)[1][1] else 1

    def start(self):
        for p in self.parts:
            for i in range(self.counts(p)):
                self.early(p, i).start()
            self.load(p).start()

    def start_later(self):
        for p in self.parts:
            rows, split = self.sizes(p)
            self.load(p).wait()
            for i in range(self.counts(p)):
                self.early(p, i).wait_recv()
                start = 0 if i == 0 else split[0]
                step = 16
                base = pl.multiple_of(self.owners[2 - i] * rows, rows) + start

                def body(t, carry, p=p, start=start, base=base, step=step):
                    here = pl.ds(pl.multiple_of(base + t * step, step), step)
                    there = pl.ds(pl.multiple_of(start + t * step, step), step)
                    value = p["buf"][here].astype(F32) + p["first"][there].astype(F32)
                    p["buf"][here] = value.astype(BF16)
                    return carry

                lax.fori_loop(0, split[i] // step, body, 0)
            for i in range(2):
                self.late(p, i).start()

    def finish(self):
        for p in self.parts:
            rows, _ = self.sizes(p)
            for i in range(2):
                self.late(p, i).wait()
            for i in range(self.counts(p)):
                self.early(p, i).wait_send()
            step = 16
            base = pl.multiple_of(self.dp * rows, rows)

            def body(t, carry, p=p, base=base, step=step):
                here = pl.ds(pl.multiple_of(base + t * step, step), step)
                there = pl.ds(pl.multiple_of(t * step, step), step)
                value = p["buf"][here].astype(F32) + p["second"][0, there].astype(F32)
                value = value + p["second"][1, there].astype(F32)
                p["out"][there] = value.astype(BF16)
                return carry

            lax.fori_loop(0, rows // step, body, 0)


def joint_reduce(partials, sums, after, collective_id, parts=4):
    groups, seqs = lax.axis_size("expert"), lax.axis_size("dp")
    chips = groups // 2
    rows, width = partials[0].shape[0] // groups, partials[0].shape[1]
    n, m, extra = len(partials), len(sums), len(after)

    def kernel(*refs):
        p_refs, s_refs = refs[:n], refs[n : n + m]
        refs = refs[n + m + extra :]
        o_refs, outs, rest = refs[:n], refs[n : n + m], refs[n + m :]
        names = ("buf", "first", "second", "load", "send", "recv")
        made = [
            dict(zip(names, rest[len(names) * i : len(names) * (i + 1)]), ref=s_refs[i], out=outs[i])
            for i in range(m)
        ]
        joint_body(groups, rows, parts, PlaneSum(made), p_refs, o_refs, *rest[len(names) * m :])

    anywhere, vmem = pl.BlockSpec(memory_space=pl.ANY), pl.BlockSpec(memory_space=pltpu.VMEM)
    dma = pltpu.SemaphoreType.DMA
    scratch = []
    for s in sums:
        own_rows = s.shape[0] // seqs
        scratch += [
            pltpu.VMEM(s.shape, BF16), pltpu.VMEM((own_rows,) + s.shape[1:], BF16),
            pltpu.VMEM((2, own_rows) + s.shape[1:], BF16), dma, dma((4,)), dma((4,)),
        ]
    return pl.pallas_call(
        kernel,
        out_shape=[jax.ShapeDtypeStruct((rows, width), F32)] * n
        + [jax.ShapeDtypeStruct((s.shape[0] // seqs,) + s.shape[1:], BF16) for s in sums],
        in_specs=[anywhere] * (n + m + extra),
        out_specs=[vmem] * (n + m),
        scratch_shapes=scratch + [
            pltpu.VMEM((n, chips, rows, width), BF16),
            pltpu.VMEM((n, chips, rows, width), BF16),
            pltpu.VMEM((n, 2 * chips, rows, width), BF16),
            dma((n, chips)), dma((n, chips)), dma((n, chips)),
            dma((n, chips, parts)), dma((n, 2 * chips, parts)),
        ],
        compiler_params=pltpu.CompilerParams(
            collective_id=collective_id, has_side_effects=True, vmem_limit_bytes=VMEM_LIMIT
        ),
        cost_estimate=cost_of(70),
        name="joint_reduce",
    )(*partials, *sums, *after)


def last_body(
    groups, seqs, small_ref, qkv_ref, out_ref, small_to, q_to, k_to, v_to, o_to,
    box, qkv_box, out_box, send, recv, qkv_send, qkv_recv, out_sem,
):
    me, dp = lax.axis_index("expert"), lax.axis_index("dp")
    total = groups * seqs
    mine = dp * groups + me
    block, width = o_to.shape
    own = width // groups
    barrier = pltpu.get_barrier_semaphore()

    def device(index):
        return (index // groups, index % groups)

    def hello(s, carry):
        pl.semaphore_signal(
            barrier, inc=1, device_id=device((mine + s) % total), device_id_type=MESH
        )
        return carry

    lax.fori_loop(1, total, hello, 0)
    pl.semaphore_wait(barrier, total - 1)

    def qkv_copy(s):
        peer = (me + s) % groups
        return pltpu.make_async_remote_copy(
            src_ref=qkv_ref.at[pl.ds(pl.multiple_of(peer * block, block), block)],
            dst_ref=qkv_box.at[me],
            send_sem=qkv_send.at[s], recv_sem=qkv_recv.at[s],
            device_id=(dp, peer), device_id_type=MESH,
        )

    def small_copy(s):
        target = (mine + s) % total
        return pltpu.make_async_remote_copy(
            src_ref=small_ref.at[target], dst_ref=box.at[mine],
            send_sem=send.at[s], recv_sem=recv.at[s],
            device_id=device(target), device_id_type=MESH,
        )

    owner = me * seqs + dp
    out_copy = pltpu.make_async_remote_copy(
        src_ref=out_ref, dst_ref=out_box, send_sem=out_sem.at[0], recv_sem=out_sem.at[1],
        device_id=device(owner), device_id_type=MESH,
    )

    def start(s, carry):
        small_copy(s).start()
        return carry

    def wait(s, carry):
        small_copy(s).wait()
        return carry

    lax.fori_loop(1, total, start, 0)
    for s in range(1, groups):
        qkv_copy(s).start()

    @pl.when(owner != mine)
    def _():
        out_copy.start()

    box[mine] = small_ref[mine]
    qkv_box[me] = qkv_ref[pl.ds(pl.multiple_of(me * block, block), block)]
    lax.fori_loop(1, total, wait, 0)

    def add(s, value):
        return value + box[s]

    small_to[...] = lax.fori_loop(1, total, add, box[0])

    @pl.when(owner != mine)
    def _():
        out_copy.wait()
        o_to[...] = out_box[...].astype(F32)

    @pl.when(owner == mine)
    def _():
        o_to[...] = out_ref[...].astype(F32)

    for s in range(1, groups):
        qkv_copy(s).wait()
    for e in range(groups):
        for m, to in enumerate((q_to, k_to, v_to)):
            to[:, e * own : (e + 1) * own] = qkv_box[e, :, m * own : (m + 1) * own].astype(F32)


def last_exchange(small, qkv, out, after, collective_id):
    groups, seqs = lax.axis_size("expert"), lax.axis_size("dp")
    total = groups * seqs
    block, width = out.shape
    vmem = pl.BlockSpec(memory_space=pltpu.VMEM)
    dma = pltpu.SemaphoreType.DMA
    matrix = jax.ShapeDtypeStruct((block, width), F32)
    held = len(after)

    def kernel(*refs):
        last_body(groups, seqs, *refs[:3], *refs[3 + held :])

    return pl.pallas_call(
        kernel,
        out_shape=[jax.ShapeDtypeStruct(small.shape[1:], F32)] + [matrix] * 4,
        in_specs=[vmem] * 3 + [pl.BlockSpec(memory_space=pl.ANY)] * held,
        out_specs=[vmem] * 5,
        scratch_shapes=[
            pltpu.VMEM(small.shape, F32),
            pltpu.VMEM((groups, block, qkv.shape[1]), BF16),
            pltpu.VMEM((block, width), BF16),
            dma((total,)), dma((total,)), dma((groups,)), dma((groups,)), dma((2,)),
        ],
        compiler_params=pltpu.CompilerParams(
            collective_id=collective_id, has_side_effects=True, vmem_limit_bytes=VMEM_LIMIT
        ),
        cost_estimate=cost_of(25),
        name="last_exchange",
    )(small, qkv, out, *after)


def exchange_body(count, spread, same, reduce, plane, x_ref, o_ref, box, send, recv):
    me, dp = lax.axis_index("expert"), lax.axis_index("dp")
    groups = lax.axis_size("expert")
    mine = dp * groups + me if spread else me

    def device(index):
        return (index // groups, index % groups) if spread else (dp, index)

    barrier = pltpu.get_barrier_semaphore()

    def hello(s, carry):
        pl.semaphore_signal(
            barrier, inc=1, device_id=device((mine + s) % count), device_id_type=MESH
        )
        return carry

    lax.fori_loop(1, count, hello, 0)
    plane.greet(barrier)
    pl.semaphore_wait(barrier, count - 1 + (2 if plane.busy() else 0))

    def copy(s):
        target = (mine + s) % count
        return pltpu.make_async_remote_copy(
            src_ref=x_ref.at[0] if same else x_ref.at[target],
            dst_ref=box.at[mine],
            send_sem=send.at[s],
            recv_sem=recv.at[s],
            device_id=device(target),
            device_id_type=MESH,
        )

    def start(s, carry):
        copy(s).start()
        return carry

    def wait(s, carry):
        copy(s).wait()
        return carry

    lax.fori_loop(1, count, start, 0)
    plane.start()
    box[mine] = x_ref[0] if same else x_ref[mine]
    lax.fori_loop(1, count, wait, 0)
    if reduce:

        def add(s, total):
            return total + box[s]

        o_ref[...] = lax.fori_loop(1, count, add, box[0])
    else:
        o_ref[...] = box[...]
    plane.start_later()
    plane.finish()


def run(
    body, name, micros, collective_id, x, x_space, out, out_space, scratch, sends, later,
    carry=(), after=(), wholes=(),
):
    arrays, specs = [], []
    for array, start, size, flip in sends:
        found = [i for i, a in enumerate(arrays) if a is array]
        if not found:
            arrays.append(array)
            found = [len(arrays) - 1]
        specs.append((found[0], start, size, flip))
    targets = [jax.ShapeDtypeStruct((s[2],) + s[0].shape[1:], s[0].dtype) for s in sends]
    for source, start, size, flip in later:
        targets.append(jax.ShapeDtypeStruct((size,) + targets[source].shape[1:], targets[source].dtype))
    seqs = lax.axis_size("dp")
    whole_out = [jax.ShapeDtypeStruct((seqs * w.shape[0],) + w.shape[1:], w.dtype) for w in wholes]
    n_in, n_out, held, n_whole = len(arrays), len(targets), len(carry), len(wholes)

    def kernel(*refs):
        x_ref, sources, whole_in = refs[0], refs[1 : 1 + n_in], refs[1 + n_in : 1 + n_in + n_whole]
        refs = refs[1 + n_in + n_whole + held + len(after) :]
        o_ref, dests, whole_to = refs[0], refs[1 : 1 + n_out], refs[1 + n_out : 1 + n_out + n_whole]
        rest = refs[1 + n_out + n_whole + held :]
        made = [
            Whole(a, b, rest[2].at[i], rest[3].at[i], rest[4].at[i])
            for i, (a, b) in enumerate(zip(whole_in, whole_to))
        ]
        plane = Plane(specs, later, sources, dests, *rest[:2], made)
        body(plane, x_ref, o_ref, *rest[5 if n_whole else 2 :])

    anywhere = pl.BlockSpec(memory_space=pl.ANY)
    dma = pltpu.SemaphoreType.DMA
    first, second = 1 + n_in + n_whole, 1 + n_out + n_whole
    got = pl.pallas_call(
        kernel,
        out_shape=[out] + targets + whole_out + [jax.ShapeDtypeStruct(c.shape, c.dtype) for c in carry],
        in_specs=[pl.BlockSpec(memory_space=x_space)] + [anywhere] * (n_in + n_whole + held + len(after)),
        out_specs=[pl.BlockSpec(memory_space=out_space)] + [anywhere] * (n_out + n_whole + held),
        input_output_aliases={first + i: second + i for i in range(held)},
        scratch_shapes=[dma((max(n_out, 1),))] * 2
        + ([dma((n_whole,)), dma((n_whole, 4)), dma((n_whole, 4))] if n_whole else [])
        + scratch,
        compiler_params=pltpu.CompilerParams(
            collective_id=collective_id, has_side_effects=True, vmem_limit_bytes=VMEM_LIMIT
        ),
        cost_estimate=cost_of(micros),
        name=name,
    )(x, *arrays, *wholes, *carry, *after)
    return got if n_out + n_whole + held else got[0]


def line_gather(x, collective_id, sends=(), later=(), carry=(), after=(), wholes=(), parts=4):
    rows, width = x.shape
    groups = lax.axis_size("expert")
    shape = (2, groups // 2, parts)
    return run(
        functools.partial(gather_body, groups, rows, parts), "line_gather", 40, collective_id,
        x, pl.ANY, jax.ShapeDtypeStruct((groups * rows, width), x.dtype), pl.ANY,
        [pltpu.SemaphoreType.DMA] + [pltpu.SemaphoreType.DMA(shape)] * 4,
        sends, later, carry, after, wholes,
    )


def line_reduce(partial, collective_id, sends=(), later=(), after=(), parts=4):
    groups = lax.axis_size("expert")
    chips = groups // 2
    rows, width = partial.shape[0] // groups, partial.shape[1]
    return run(
        functools.partial(reduce_body, groups, rows, parts), "line_reduce", 40, collective_id,
        partial.astype(BF16), pl.ANY, jax.ShapeDtypeStruct((rows, width), F32), pltpu.VMEM,
        [
            pltpu.VMEM((chips, rows, width), BF16),
            pltpu.VMEM((chips, rows, width), BF16),
            pltpu.VMEM((2 * chips, rows, width), BF16),
            pltpu.SemaphoreType.DMA((chips,)),
            pltpu.SemaphoreType.DMA((chips,)),
            pltpu.SemaphoreType.DMA((chips,)),
            pltpu.SemaphoreType.DMA((chips, parts)),
            pltpu.SemaphoreType.DMA((2 * chips, parts)),
        ],
        sends, later, (), after,
    )


def exchange(
    x, collective_id, spread=False, same=False, reduce=False, sends=(), later=(), carry=()
):
    count = lax.axis_size("expert") * (lax.axis_size("dp") if spread else 1)
    block = x.shape[1:]
    return run(
        functools.partial(exchange_body, count, spread, same, reduce), "exchange", 8, collective_id,
        x, pltpu.VMEM, jax.ShapeDtypeStruct(block if reduce else (count,) + block, x.dtype), pltpu.VMEM,
        [
            pltpu.VMEM((count,) + block, x.dtype),
            pltpu.SemaphoreType.DMA((count,)),
            pltpu.SemaphoreType.DMA((count,)),
        ],
        sends, later, carry,
    )


LANES = 128
TILE = 512


def expert_first_body(
    groups, seqs, rows, width, ff, experts, parts,
    x_ref, g_ref, gate_ref, up_ref, down_ref, near_refs,
    f_out, hid_out, sg_out, su_out, tail_out, down_out, grad_out,
    f_buf, g_buf, wg, wu, wd, hid, sg, su, tail_buf, tail_sum, stage,
    line_send, line_recv, side_send, side_recv, own_sem, f_sem, w_sem, d_sem, g_sem, out_sem, tail_sem,
    plane_send, plane_recv, stage_sem,
):
    chips = groups // 2
    me, dp = lax.axis_index("expert"), lax.axis_index("dp")
    chip, core = me // 2, me % 2
    sibling = chip * 2 + 1 - core
    chunk = 2 * rows
    part = rows // parts
    depth, wide_ff = width // seqs, ff // seqs

    def remote(src, dst, send_sem, recv_sem, device):
        return pltpu.make_async_remote_copy(
            src_ref=src, dst_ref=dst, send_sem=send_sem, recv_sem=recv_sem,
            device_id=device, device_id_type=MESH,
        )

    def at(index, size):
        return pl.ds(pl.multiple_of(index * size, size), size)

    def neighbour(flip):
        return (flipped(dp, flip), me)

    barrier = pltpu.get_barrier_semaphore()
    pl.semaphore_signal(barrier, inc=1, device_id=(dp, sibling), device_id_type=MESH)
    for flip in (1, 2):
        pl.semaphore_signal(barrier, inc=1, device_id=neighbour(flip), device_id_type=MESH)

    @pl.when(chip > 0)
    def _():
        pl.semaphore_signal(barrier, inc=1, device_id=(dp, me - 2), device_id_type=MESH)

    @pl.when(chip < chips - 1)
    def _():
        pl.semaphore_signal(barrier, inc=1, device_id=(dp, me + 2), device_id_type=MESH)

    @pl.when((chip > 0) & (chip < chips - 1))
    def _():
        pl.semaphore_wait(barrier, 5)

    @pl.when((chip == 0) | (chip == chips - 1))
    def _():
        pl.semaphore_wait(barrier, 4)

    def row_copy(origin, u, target, send_sem, recv_sem, first):
        place = pl.ds(pl.multiple_of(origin * rows + u * part, part), part)
        return remote(
            x_ref.at[pl.ds(u * part, part)] if first else f_buf.at[place], f_buf.at[place],
            send_sem, recv_sem, (dp, target),
        )

    def step(side, k, u):
        origin, target = (me - 2 * k, me + 2) if side == 0 else (me + 2 * k, me - 2)
        return row_copy(origin, u, target, line_send.at[side, k, u], line_recv.at[side, k, u], k == 0)

    def aside(side, k, u):
        origin = me - 2 * k if side == 0 else me + 2 * k
        return row_copy(origin, u, sibling, side_send.at[side, k, u], side_recv.at[side, k, u], k == 0)

    def sides(k):
        return (
            (0, chip - k >= 0, chip < chips - 1),
            (1, chip + k <= chips - 1, chip > 0),
        )

    keep = pltpu.make_async_copy(x_ref, f_buf.at[at(me, rows)], own_sem)

    def rows_out(c):
        return pltpu.make_async_copy(
            f_buf.at[at(c, chunk), pl.ds(0, width)], f_out.at[at(c, chunk)], f_sem.at[c]
        )

    def plane_copy(i):
        e, flip = (i // 2, i % 2 + 1) if i < 4 else (i - 4, i - 3)
        if i < 4:
            src, dst = down_ref.at[e], wd.at[e, at(dp, wide_ff)]
        else:
            src = wd.at[e, at(flipped(dp, 3 - flip), wide_ff)]
            dst = src
        return remote(src, dst, plane_send.at[i], plane_recv.at[i], neighbour(flip))

    owners = (dp, flipped(dp, 1), flipped(dp, 2), flipped(flipped(dp, 1), 2))

    def weight_copies():
        copies = []
        for m, (own, buf) in enumerate(((gate_ref, wg), (up_ref, wu))):
            for e in range(experts):
                near = [near_refs[6 * m + 2 * q + e] for q in range(3)]
                pieces = [own.at[e]] + [ref.at[index] for ref, index in near]
                for q, piece in enumerate(pieces):
                    copies.append(
                        pltpu.make_async_copy(
                            piece, buf.at[at(owners[q], depth), pl.ds(e * ff, ff)],
                            w_sem.at[m, e, q],
                        )
                    )
        return copies

    def down_copies():
        return [
            pltpu.make_async_copy(down_ref.at[e], wd.at[e, at(dp, wide_ff)], d_sem.at[e])
            for e in range(experts)
        ]

    grad_rows = [
        pltpu.make_async_copy(
            g_ref.at[pl.ds(r * chunk, chunk)], g_buf.at[pl.ds(r * chunk, chunk)], g_sem.at[r]
        )
        for r in range(chips)
    ]

    def first_layer(c):
        place = at(c, chunk)

        def tile(t, carry):
            cols = at(t, TILE)
            gate = dot(f_buf[place, pl.ds(0, width)], wg[:, cols])
            up = dot(f_buf[place, pl.ds(0, width)], wu[:, cols])
            sig = 1.0 / (1.0 + jnp.exp(-gate))
            silu = gate * sig
            hid[place, cols] = (silu * up).astype(BF16)
            sg[place, cols] = (up * sig * (1.0 + gate * (1.0 - sig))).astype(BF16)
            su[place, cols] = silu.astype(BF16)
            return carry

        lax.fori_loop(0, experts * ff // TILE, tile, 0)

    def ready(k):
        for u in range(parts):
            if k == 0:
                aside(0, 0, u).wait_recv()
            else:
                for side, has, _ in sides(k):

                    @pl.when(has)
                    def _(side=side, u=u):
                        aside(side, k, u).wait_recv()

        if k == 0:
            rows_out(chip).start()
            first_layer(chip)
        else:
            for side, has, _ in sides(k):
                c = chip - k if side == 0 else chip + k

                @pl.when(has)
                def _(c=c):
                    rows_out(c).start()
                    first_layer(c)

    for k in range(chips):
        for u in range(parts):
            for side, has, send_on in sides(k):

                @pl.when(has)
                def _(k=k, u=u, side=side, send_on=send_on):
                    if k > 0:
                        step(side, k - 1, u).wait_recv()
                    if k < chips - 1:

                        @pl.when(send_on)
                        def _():
                            step(side, k, u).start()

                    if k > 0:
                        aside(side, k, u).start()

            if k == 0:
                aside(0, 0, u).start()
        if k == 0:
            for i in range(4):
                plane_copy(i).start()
            keep.start()
            for copy in weight_copies():
                copy.start()
            for copy in down_copies():
                copy.start()
            for copy in grad_rows:
                copy.start()
            keep.wait()
            for copy in weight_copies():
                copy.wait()
        if k > 0:
            ready(k - 1)
    plane_copy(1).wait_recv()
    plane_copy(4).start()
    plane_copy(2).wait_recv()
    plane_copy(5).start()
    ready(chips - 1)

    for copy in down_copies():
        copy.wait()
    for i in (0, 3):
        plane_copy(i).wait_recv()

    def outs(r):
        place = pl.ds(r * chunk, chunk)
        return [
            pltpu.make_async_copy(buf.at[place], out.at[place], out_sem.at[i, r])
            for i, (buf, out) in enumerate(((hid, hid_out), (sg, sg_out), (su, su_out)))
        ]

    lane = lax.broadcasted_iota(jnp.int32, (chunk, LANES), 1)

    def back(r, first, last):
        place = pl.ds(r * chunk, chunk)
        extra = f_buf[place, pl.ds(width, LANES)].astype(F32)
        tail = jnp.zeros((chunk, LANES), F32) if first == 0 else tail_sum[place, :]
        for e in range(experts):
            which = me * experts + e
            low = which + LANES // 2
            weight = jnp.sum(
                jnp.where((lane == which) | (lane == low), extra, 0.0), axis=1, keepdims=True
            )
            for owner in owners[first:last]:
                d_hid = dot_nt(g_buf[place, :], wd[e, at(owner, wide_ff), :])
                cols = pl.ds(pl.multiple_of(e * ff + owner * wide_ff, wide_ff), wide_ff)
                hidden = hid[place, cols].astype(F32)
                d_weight = jnp.sum(hidden * d_hid, axis=1, keepdims=True)
                tail = tail + jnp.where(lane == which, d_weight, 0.0)
                d_hid = d_hid * weight
                hid[place, cols] = (hidden * weight).astype(BF16)
                sg[place, cols] = (d_hid * sg[place, cols].astype(F32)).astype(BF16)
                su[place, cols] = (d_hid * su[place, cols].astype(F32)).astype(BF16)
        if last < len(owners):
            tail_sum[place, :] = tail
        else:
            high = tail.astype(BF16).astype(F32)
            tail_buf[place, :] = (high + pltpu.roll(tail - high, LANES // 2, 1)).astype(BF16)

    tiles = [(e, q) for q in range(len(owners)) for e in range(experts)]

    def grad_place(t):
        e, q = tiles[t]
        return pl.ds(pl.multiple_of(e * ff + owners[q] * wide_ff, wide_ff), wide_ff)

    def grad_copy(t):
        return pltpu.make_async_copy(stage.at[t % 2], grad_out.at[grad_place(t)], stage_sem.at[t % 2])

    def grad_tile(t):
        if t >= 2:
            grad_copy(t - 2).wait()
        for n in range(width // (2 * TILE)):
            cols = pl.ds(n * 2 * TILE, 2 * TILE)
            stage[t % 2, :, cols] = dot_tn(hid[:, grad_place(t)], g_buf[:, cols]).astype(BF16)
        grad_copy(t).start()

    for copy in grad_rows:
        copy.wait()
    for r in range(chips):
        back(r, 0, 3)
    for t in range(3 * experts):
        grad_tile(t)
    for i in (4, 5):
        plane_copy(i).wait_recv()
    keep_down = pltpu.make_async_copy(wd, down_out, d_sem.at[experts])
    keep_down.start()
    for r in range(chips):
        back(r, 3, 4)
        for copy in outs(r):
            copy.start()
    for t in range(3 * experts, 4 * experts):
        grad_tile(t)
    for t in range(4 * experts - 2, 4 * experts):
        grad_copy(t).wait()
    keep_tail = pltpu.make_async_copy(tail_buf, tail_out, tail_sem)
    keep_tail.start()
    keep_tail.wait()
    keep_down.wait()
    for k in range(chips):
        for u in range(parts):
            if k == 0:
                aside(0, 0, u).wait_send()
            for side, has, send_on in sides(k):

                @pl.when(has)
                def _(k=k, u=u, side=side, send_on=send_on):
                    if k < chips - 1:

                        @pl.when(send_on)
                        def _():
                            step(side, k, u).wait_send()

                    if k > 0:
                        aside(side, k, u).wait_send()

    for i in range(6):
        plane_copy(i).wait_send()
    for d in range(chips):
        rows_out(d).wait()
        for copy in outs(d):
            copy.wait()


def expert_first(x, g_all, w_gate, w_up, w_down, near, collective_id, parts=4):
    groups, seqs = lax.axis_size("expert"), lax.axis_size("dp")
    chips = groups // 2
    rows, wide = x.shape
    length, width = g_all.shape
    experts, _, ff = w_gate.shape
    where = [index for _, index in near]
    near = [array for array, _ in near]
    n = len(near)

    def kernel(*refs):
        expert_first_body(
            groups, seqs, rows, width, ff, experts, parts, *refs[:5],
            list(zip(refs[5 : 5 + n], where)), *refs[5 + n :],
        )

    anywhere = pl.BlockSpec(memory_space=pl.ANY)
    dma = pltpu.SemaphoreType.DMA
    flat = jax.ShapeDtypeStruct((length, experts * ff), BF16)
    return pl.pallas_call(
        kernel,
        out_shape=[
            jax.ShapeDtypeStruct((length, width), BF16), flat, flat, flat,
            jax.ShapeDtypeStruct((length, LANES), BF16),
            jax.ShapeDtypeStruct((experts, ff, width), BF16),
            jax.ShapeDtypeStruct((experts * ff, width), BF16),
        ],
        in_specs=[anywhere] * (5 + n),
        out_specs=[anywhere] * 7,
        scratch_shapes=[
            pltpu.VMEM((length, wide), BF16),
            pltpu.VMEM((length, width), BF16),
            pltpu.VMEM((width, experts * ff), BF16),
            pltpu.VMEM((width, experts * ff), BF16),
            pltpu.VMEM((experts, ff, width), BF16),
            pltpu.VMEM((length, experts * ff), BF16),
            pltpu.VMEM((length, experts * ff), BF16),
            pltpu.VMEM((length, experts * ff), BF16),
            pltpu.VMEM((length, LANES), BF16),
            pltpu.VMEM((length, LANES), F32),
            pltpu.VMEM((2, ff // seqs, width), BF16),
            dma((2, chips, parts)), dma((2, chips, parts)), dma((2, chips, parts)), dma((2, chips, parts)),
            dma, dma((chips,)), dma((2, experts, 4)), dma((experts + 1,)), dma((chips,)), dma((3, chips)), dma,
            dma((6,)), dma((6,)), dma((2,)),
        ],
        compiler_params=pltpu.CompilerParams(
            collective_id=collective_id, has_side_effects=True, vmem_limit_bytes=VMEM_LIMIT
        ),
        cost_estimate=cost_of(70),
        name="expert_first",
    )(x, g_all, w_gate, w_up, w_down, *near)


class Blocks:
    def __init__(self, ref, size, half_stride, owner_stride):
        self.me, self.dp = lax.axis_index("expert"), lax.axis_index("dp")
        self.ref, self.size = ref, size
        self.half_stride, self.owner_stride = half_stride, owner_stride
        x, y = flipped(self.dp, 1), flipped(self.dp, 2)
        self.owners = (self.dp, x, y, flipped(x, 2))

    def piece(self, half, q):
        start = half * self.half_stride + self.owners[q] * self.owner_stride
        return self.ref.at[pl.ds(pl.multiple_of(start, self.size), self.size)]

    def remote(self, src, dst, send, recv, flip):
        return pltpu.make_async_remote_copy(
            src_ref=src, dst_ref=dst, send_sem=send, recv_sem=recv,
            device_id=(flipped(self.dp, flip), self.me), device_id_type=MESH,
        )


class SumEarly:
    def __init__(self, blocks, first, mid, near_out, mid_out, load, send, recv):
        self.me, self.dp = blocks.me, blocks.dp
        self.blocks, self.first, self.mid = blocks, first, mid
        self.near_out, self.mid_out = near_out, mid_out
        self.load_sem, self.send, self.recv = load, send, recv

    def busy(self):
        return True

    greet = Plane.greet

    def copy(self, i):
        b = self.blocks
        src, dst = (
            (b.piece(0, 3), self.first.at[0]),
            (b.piece(1, 3), self.first.at[1]),
            (b.piece(0, 1), self.near_out.at[0]),
            (b.piece(1, 2), self.near_out.at[1]),
        )[i]
        return b.remote(src, dst, self.send.at[i], self.recv.at[i], i % 2 + 1)

    def loads(self):
        b = self.blocks
        return [
            pltpu.make_async_copy(b.piece(0, 2), self.mid.at[0], self.load_sem.at[0]),
            pltpu.make_async_copy(b.piece(1, 1), self.mid.at[1], self.load_sem.at[1]),
        ]

    def keep(self):
        return pltpu.make_async_copy(self.mid, self.mid_out, self.load_sem.at[2])

    def start(self):
        for i in range(4):
            self.copy(i).start()
        for copy in self.loads():
            copy.start()

    def start_later(self):
        for copy in self.loads():
            copy.wait()
        for i in range(2):
            self.copy(i).wait_recv()

            def body(t, carry, i=i):
                here = pl.ds(pl.multiple_of(t * 16, 16), 16)
                value = self.mid[i, here].astype(F32) + self.first[i, here].astype(F32)
                self.mid[i, here] = value.astype(BF16)
                return carry

            lax.fori_loop(0, self.blocks.size // 16, body, 0)
        self.keep().start()

    def finish(self):
        for i in range(4):
            if i >= 2:
                self.copy(i).wait_recv()
            self.copy(i).wait_send()
        self.keep().wait()


class SumLate:
    def __init__(self, blocks, mid_ref, near_ref, late, near, own, out, load, send, recv):
        self.blocks, self.mid_ref, self.near_ref = blocks, mid_ref, near_ref
        self.late, self.near, self.own, self.out = late, near, own, out
        self.load_sem, self.send, self.recv = load, send, recv

    def copy(self, i):
        return self.blocks.remote(
            self.mid_ref.at[1 - i], self.late.at[1 - i], self.send.at[i], self.recv.at[i], i + 1
        )

    def loads(self):
        b = self.blocks
        return [
            pltpu.make_async_copy(b.piece(0, 0), self.own.at[0], self.load_sem.at[0]),
            pltpu.make_async_copy(b.piece(1, 0), self.own.at[1], self.load_sem.at[1]),
            pltpu.make_async_copy(self.near_ref, self.near, self.load_sem.at[2]),
        ]

    def start(self):
        for i in range(2):
            self.copy(i).start()
        for copy in self.loads():
            copy.start()

    def start_later(self):
        pass

    def finish(self):
        for copy in self.loads():
            copy.wait()
        for i in range(2):
            self.copy(i).wait()
        for half in range(2):

            def body(t, carry, half=half):
                here = pl.ds(pl.multiple_of(t * 16, 16), 16)
                value = self.own[half, here].astype(F32) + self.near[half, here].astype(F32)
                value = value + self.late[half, here].astype(F32)
                self.out[half, here] = value.astype(BF16)
                return carry

            lax.fori_loop(0, self.blocks.size // 16, body, 0)


class Several:
    def __init__(self, parts):
        self.me, self.dp = lax.axis_index("expert"), lax.axis_index("dp")
        self.parts = parts

    def busy(self):
        return True

    greet = Plane.greet

    def start(self):
        for part in self.parts:
            part.start()

    def start_later(self):
        for part in self.parts:
            part.start_later()

    def finish(self):
        for part in self.parts:
            part.finish()


def expert_second_body(
    groups, seqs, rows, width, ff, experts, parts,
    sg_ref, su_ref, tail_ref, f_ref, gate_ref, up_ref, down_ref, near_refs, grad_out, near_out, mid_out, o_ref,
    wg, wu, sg, su, tail_buf, f_buf, stage, acc, pair_in, inbox, last,
    first, mid,
    in_sem, w_sem, stage_sem, pair_send, pair_recv, hop_send, hop_recv, last_recv,
    sum_load, sum_send, sum_recv,
):
    chips = groups // 2
    me, dp = lax.axis_index("expert"), lax.axis_index("dp")
    chip, core = me // 2, me % 2
    sibling = chip * 2 + 1 - core
    chunk = 2 * rows
    part = rows // parts
    depth = width // seqs

    def remote(src, dst, send_sem, recv_sem, device):
        return pltpu.make_async_remote_copy(
            src_ref=src, dst_ref=dst, send_sem=send_sem, recv_sem=recv_sem,
            device_id=device, device_id_type=MESH,
        )

    def at(index, size):
        return pl.ds(pl.multiple_of(index * size, size), size)

    owners = (dp, flipped(dp, 1), flipped(dp, 2), flipped(flipped(dp, 1), 2))
    loads = [
        pltpu.make_async_copy(src, dst, in_sem.at[i])
        for i, (src, dst) in enumerate(
            ((sg_ref, sg), (su_ref, su), (tail_ref, tail_buf), (f_ref, f_buf))
        )
    ]
    weights = []
    for m, (own, buf) in enumerate(((gate_ref, wg), (up_ref, wu))):
        for e in range(experts):
            near = [near_refs[6 * m + 2 * q + e] for q in range(3)]
            pieces = [own.at[e]] + [ref.at[index] for ref, index in near]
            for q, piece in enumerate(pieces):
                weights.append(
                    pltpu.make_async_copy(
                        piece, buf.at[at(owners[q], depth), pl.ds(e * ff, ff)], w_sem.at[m, e, q]
                    )
                )
    for copy in loads[:3] + weights + loads[3:]:
        copy.start()
    blocks = Blocks(down_ref, ff // seqs, ff, ff // seqs)
    total = SumEarly(blocks, first, mid, near_out, mid_out, sum_load, sum_send, sum_recv)
    line_greet(me, dp, chip, chips, total)
    total.start()
    for copy in loads[:3]:
        copy.wait()
    for r in range(chips):
        for half in range(2):
            acc[r, half, :, pl.ds(width, LANES)] = tail_buf[pl.ds(r * chunk + half * rows, rows), :]

    out_tile = 256

    def row_grads(d, first=False):
        place = at(d, chunk)
        per = depth // out_tile

        def tile(t, carry):
            cols = at(t, out_tile)
            value = dot_nt(sg[place, :], wg[cols, :]) + dot_nt(su[place, :], wu[cols, :])
            value = value.astype(BF16)
            acc[d, 0, :, cols] = value[:rows]
            acc[d, 1, :, cols] = value[rows:]
            return carry

        if not first:
            lax.fori_loop(0, width // out_tile, tile, 0)
            return
        for q, owner in enumerate(owners):
            for copy in weights[q :: len(owners)]:
                copy.wait()
            lax.fori_loop(owner * per, owner * per + per, tile, 0)

    def pair_copy(d):
        return remote(acc.at[d, 1 - core], pair_in.at[d], pair_send.at[d], pair_recv.at[d], (dp, sibling))

    def hop(d, u, kind):
        place = pl.ds(u * part, part)
        if kind == 0:
            return remote(
                acc.at[d, core, place], inbox.at[d, place], hop_send.at[d, u], hop_recv.at[d, u],
                (dp, me + 2),
            )
        if kind == 1:
            return remote(
                acc.at[d, core, place], inbox.at[d, place], hop_send.at[d, u], hop_recv.at[d, u],
                (dp, me - 2),
            )
        return remote(
            acc.at[d, core, place], last.at[place], hop_send.at[d, u], last_recv.at[u], (dp, me - 2)
        )

    step_rows = 16

    def add(d, u, more, store):
        def body(i, carry):
            here = pl.ds(pl.multiple_of(u * part + i * step_rows, step_rows), step_rows)
            value = acc[d, core, here].astype(F32) + pair_in[d, here].astype(F32)
            for ref in more:
                value = value + ref[here].astype(F32)
            store(here, value)
            return carry

        lax.fori_loop(0, part // step_rows, body, 0)

    def forward(d):
        pair_copy(d).wait_recv()

        def store(here, value):
            acc[d, core, here] = value.astype(BF16)

        source = ((d > chip) & (chip == 0)) | ((d < chip) & (chip == chips - 1))
        for u in range(parts):

            @pl.when(source)
            def _(u=u):
                add(d, u, (), store)

            @pl.when(jnp.logical_not(source))
            def _(u=u):
                hop(d, u, 0).wait_recv()
                add(d, u, (inbox.at[d],), store)

            @pl.when(d > chip)
            def _(u=u):
                hop(d, u, 0).start()

            @pl.when((d < chip) & (d != chip - 1))
            def _(u=u):
                hop(d, u, 1).start()

            @pl.when((d < chip) & (d == chip - 1))
            def _(u=u):
                hop(d, u, 2).start()

    upper = chip // (chips // 2)
    mirrored = chip + upper * (chips - 1 - 2 * chip)

    def goal(j):
        turn = (j + mirrored) // (chips - 1)
        d = (1 - turn) * (chips - 1 - j) + turn * (j + mirrored - (chips - 1))
        return d + upper * (chips - 1 - 2 * d)

    edge = (chip == 0) | (chip == chips - 1)

    def grad_copy(t):
        return pltpu.make_async_copy(
            stage.at[t % 2], grad_out.at[pl.ds(t * out_tile, out_tile)], stage_sem.at[t % 2]
        )

    def grad_tile(t):
        if t >= 2:
            grad_copy(t - 2).wait()
        for n in range(experts * ff // (2 * TILE)):
            cols = pl.ds(n * 2 * TILE, 2 * TILE)
            stage[t % 2, :, cols] = dot_tn(
                f_buf[:, pl.ds(t * out_tile, out_tile)], sg[:, cols]
            ).astype(BF16)
        grad_copy(t).start()

    tiles = width // out_tile
    for j in range(chips):
        row_grads(goal(j), j == 0)
        pair_copy(goal(j)).start()
        if j > 0:

            @pl.when(edge)
            def _(j=j):
                forward(goal(j - 1))

    for copy in loads[3:]:
        copy.wait()
    for j in range(chips):
        if j < chips - 1:

            @pl.when(jnp.logical_not(edge))
            def _(j=j):
                forward(goal(j))

        if j == min(1, chips - 1):
            total.start_later()
        for t in range(j * tiles // chips, (j + 1) * tiles // chips):
            grad_tile(t)

    pair_copy(chip).wait_recv()

    def finish(here, value):
        o_ref[here] = value

    for u in range(parts):

        @pl.when(chip == 0)
        def _(u=u):
            hop(chip, u, 2).wait_recv()
            add(chip, u, (last,), finish)

        @pl.when(chip == chips - 1)
        def _(u=u):
            hop(chip, u, 0).wait_recv()
            add(chip, u, (inbox.at[chip],), finish)

        @pl.when((chip > 0) & (chip < chips - 1))
        def _(u=u):
            hop(chip, u, 0).wait_recv()
            hop(chip, u, 2).wait_recv()
            add(chip, u, (inbox.at[chip], last), finish)

    for d in range(chips):
        pair_copy(d).wait_send()
        for u in range(parts):

            @pl.when(d != chip)
            def _(d=d, u=u):
                hop(d, u, 0).wait_send()

    for t in range(tiles - 2, tiles):
        grad_copy(t).wait()
    total.finish()


def expert_second(sg, su, tail, ffn_all, d_down, w_gate, w_up, near, collective_id, parts=4):
    groups, seqs = lax.axis_size("expert"), lax.axis_size("dp")
    chips = groups // 2
    length, width = ffn_all.shape
    rows = length // groups
    experts, _, ff = w_gate.shape
    wide = width + LANES
    size = ff // seqs
    where = [index for _, index in near]
    near = [array for array, _ in near]
    n = len(near)

    def kernel(*refs):
        expert_second_body(
            groups, seqs, rows, width, ff, experts, parts, *refs[:7], list(zip(refs[7 : 7 + n], where)),
            *refs[7 + n :],
        )

    anywhere = pl.BlockSpec(memory_space=pl.ANY)
    dma = pltpu.SemaphoreType.DMA
    flat = pltpu.VMEM((length, experts * ff), BF16)
    block = pltpu.VMEM((2, size, width), BF16)
    return pl.pallas_call(
        kernel,
        out_shape=[
            jax.ShapeDtypeStruct((width, experts * ff), BF16),
            jax.ShapeDtypeStruct((2, size, width), BF16),
            jax.ShapeDtypeStruct((2, size, width), BF16),
            jax.ShapeDtypeStruct((rows, wide), F32),
        ],
        in_specs=[anywhere] * (7 + n),
        out_specs=[anywhere] * 3 + [pl.BlockSpec(memory_space=pltpu.VMEM)],
        scratch_shapes=[
            pltpu.VMEM((width, experts * ff), BF16),
            pltpu.VMEM((width, experts * ff), BF16),
            flat, flat,
            pltpu.VMEM((length, LANES), BF16),
            pltpu.VMEM((length, width), BF16),
            pltpu.VMEM((2, 256, experts * ff), BF16),
            pltpu.VMEM((chips, 2, rows, wide), BF16),
            pltpu.VMEM((chips, rows, wide), BF16),
            pltpu.VMEM((chips, rows, wide), BF16),
            pltpu.VMEM((rows, wide), BF16),
            block, block,
            dma((4,)), dma((2, experts, 4)), dma((2,)), dma((chips,)), dma((chips,)),
            dma((chips, parts)), dma((chips, parts)), dma((parts,)),
            dma((3,)), dma((4,)), dma((4,)),
        ],
        compiler_params=pltpu.CompilerParams(
            collective_id=collective_id, has_side_effects=True, vmem_limit_bytes=60 * 1024 * 1024
        ),
        cost_estimate=cost_of(65),
        name="expert_second",
    )(sg, su, tail, ffn_all, w_gate, w_up, d_down, *near)


def gather_fill_body(
    groups, seqs, ff, rows, parts, x_ref, f_ref, su_ref, hid_ref, wd_ref, down_ref, mid_ref, near_ref,
    o_ref, grad_out, y_out, down_out,
    f_buf, su, hid, wd, stage, late, near, own_block, in_sem, stage_sem, sum_load, sum_send, sum_recv,
    own_sem, send, recv, pair_send, pair_recv,
):
    chips = groups // 2
    length, width = f_buf.shape
    hidden = su.shape[1]
    size = stage.shape[1]
    loads = [
        pltpu.make_async_copy(src, dst, in_sem.at[i])
        for i, (src, dst) in enumerate(((f_ref, f_buf), (su_ref, su), (hid_ref, hid), (wd_ref, wd)))
    ]
    for copy in loads:
        copy.start()
    grads, mixes = width // size, length // size
    total = grads + mixes

    def place(t):
        return pl.ds((t if t < grads else t - grads) * size, size)

    def out_copy(t):
        to = grad_out if t < grads else y_out
        return pltpu.make_async_copy(stage.at[t % 2], to.at[place(t)], stage_sem.at[t % 2])

    def tile(t):
        if t == 0:
            loads[0].wait()
            loads[1].wait()
        if t == grads:
            loads[2].wait()
            loads[3].wait()
        if t >= 2:
            out_copy(t - 2).wait()
        for n in range(hidden // (2 * TILE)):
            cols = pl.ds(n * 2 * TILE, 2 * TILE)
            if t < grads:
                value = dot_tn(f_buf[:, place(t)], su[:, cols])
            else:
                value = dot(hid[place(t), :], wd[:, cols])
            stage[t % 2, :, cols] = value.astype(BF16)
        out_copy(t).start()

    turns = max(chips - 1, 1)
    rest = SumLate(
        Blocks(down_ref, ff // seqs, ff, ff // seqs), mid_ref, near_ref, late, near, own_block, down_out,
        sum_load, sum_send, sum_recv,
    )

    def work(k):
        if k < turns:
            for t in range(k * total // turns, (k + 1) * total // turns):
                tile(t)

    gather_body(
        groups, rows, parts, Several([rest]), x_ref, o_ref,
        own_sem, send, recv, pair_send, pair_recv, work=work,
    )
    for t in range(total - 2, total):
        out_copy(t).wait()


def gather_fill(x, ffn_all, su, hid, wd, d_down, mid, near, ff, collective_id, parts=4):
    groups, seqs = lax.axis_size("expert"), lax.axis_size("dp")
    rows, width = x.shape
    length, hidden = su.shape
    anywhere, vmem = pl.BlockSpec(memory_space=pl.ANY), pl.BlockSpec(memory_space=pltpu.VMEM)
    dma = pltpu.SemaphoreType.DMA
    line = dma((2, groups // 2, parts))
    tokens = jax.ShapeDtypeStruct((length, width), BF16)
    return pl.pallas_call(
        functools.partial(gather_fill_body, groups, seqs, ff, rows, parts),
        out_shape=[
            tokens, jax.ShapeDtypeStruct((width, hidden), BF16), tokens,
            jax.ShapeDtypeStruct(mid.shape, BF16),
        ],
        in_specs=[anywhere] * 8,
        out_specs=[anywhere] * 3 + [vmem],
        scratch_shapes=[
            pltpu.VMEM((length, width), BF16),
            pltpu.VMEM((length, hidden), BF16),
            pltpu.VMEM((length, hidden), BF16),
            pltpu.VMEM((hidden, width), BF16),
            pltpu.VMEM((2, 256, max(hidden, width)), BF16),
            pltpu.VMEM(mid.shape, BF16),
            pltpu.VMEM(mid.shape, BF16),
            pltpu.VMEM(mid.shape, BF16),
            dma((4,)), dma((2,)), dma((3,)), dma((2,)), dma((2,)),
            dma, line, line, line, line,
        ],
        compiler_params=pltpu.CompilerParams(
            collective_id=collective_id, has_side_effects=True, vmem_limit_bytes=VMEM_LIMIT
        ),
        cost_estimate=cost_of(45),
        name="gather_fill",
    )(x, ffn_all, su, hid, wd, d_down, mid, near)


class Opening:
    def __init__(self, sends, arrived, wholes):
        self.sends, self.arrived, self.wholes = sends, arrived, wholes

    def start(self):
        pass

    def start_mid(self):
        self.arrived()
        for whole in self.wholes:
            whole.start()

    def start_later(self):
        for whole in self.wholes:
            whole.start_later()

    def finish(self):
        for whole in self.wholes:
            whole.finish()
        self.sends.finish()


def opening_body(
    groups, seqs, copies, slab, rows, parts, gate_refs, x_ref, small_ref, out_ref, q_ref, k_ref, v_ref, gate_ref,
    x_to, small_to, qkv_to, wo_to, out_to, spread_to,
    box, send, recv, out_sem, own_sem, qkv_send, qkv_recv, small_sem, plane_send, plane_recv,
    whole_own, whole_send, whole_recv, keep_sem, line_send, line_recv, pair_send, pair_recv,
):
    me, dp = lax.axis_index("expert"), lax.axis_index("dp")
    total = groups * seqs
    mine = dp * groups + me
    block = q_ref.shape[0]
    barrier = pltpu.get_barrier_semaphore()

    def device(index):
        return (index // groups, index % groups)

    def hello(s, carry):
        pl.semaphore_signal(
            barrier, inc=1, device_id=device((mine + s) % total), device_id_type=MESH
        )
        return carry

    lax.fori_loop(1, total, hello, 0)
    pl.semaphore_wait(barrier, total - 1)

    def small_copy(s):
        return pltpu.make_async_remote_copy(
            src_ref=small_ref, dst_ref=box.at[mine], send_sem=send.at[s], recv_sem=recv.at[s],
            device_id=device((mine + s) % total), device_id_type=MESH,
        )

    def start(s, carry):
        small_copy(s).start()
        return carry

    def wait(s, carry):
        small_copy(s).wait()
        return carry

    lax.fori_loop(1, total, start, 0)
    place = pl.ds(pl.multiple_of(me * block, block), block)
    spread, own = [], []
    for m, ref in enumerate((q_ref, k_ref, v_ref)):
        cols = pl.ds(pl.multiple_of((me // copies) * slab, slab), slab)
        dst = spread_to.at[place, pl.ds(m * slab, slab)]
        own.append(pltpu.make_async_copy(ref.at[:, cols], dst, own_sem.at[m]))
        for s in range(1, groups):
            peer = (me + s) % groups
            cols = pl.ds(pl.multiple_of((peer // copies) * slab, slab), slab)
            spread.append(
                pltpu.make_async_remote_copy(
                    src_ref=ref.at[:, cols], dst_ref=dst,
                    send_sem=qkv_send.at[s, m], recv_sem=qkv_recv.at[s, m],
                    device_id=(dp, peer), device_id_type=MESH,
                )
            )
    moved = (mine % seqs) * groups + mine // seqs
    away = pltpu.make_async_remote_copy(
        src_ref=out_ref, dst_ref=out_to, send_sem=out_sem.at[0], recv_sem=out_sem.at[1],
        device_id=device(moved), device_id_type=MESH,
    )
    stay = pltpu.make_async_copy(out_ref, out_to, out_sem.at[0])
    @pl.when(moved != mine)
    def _():
        away.start()

    @pl.when(moved == mine)
    def _():
        stay.start()

    sends = Plane(
        [(0, 0, 1, 1), (0, 0, 1, 2), (0, 1, 1, 1), (0, 1, 1, 2)], (), [gate_ref], gate_refs,
        plane_send, plane_recv,
    )
    sends.start()
    for copy in spread:
        copy.start()
    for copy in own:
        copy.start()
    box[mine] = small_ref[...]
    out_small = pltpu.make_async_copy(box, small_to, small_sem)

    def arrived():
        for copy in own + spread:
            copy.wait()

        @pl.when(moved != mine)
        def _():
            away.wait()

        @pl.when(moved == mine)
        def _():
            stay.wait()

    wholes = [
        Whole(a, b, whole_own.at[i], whole_send.at[i], whole_recv.at[i])
        for i, (a, b) in enumerate(((spread_to, qkv_to), (out_to, wo_to)))
    ]
    gather_body(
        groups, rows, parts, Opening(sends, arrived, wholes), x_ref, x_to,
        keep_sem, line_send, line_recv, pair_send, pair_recv, greet=False,
    )
    lax.fori_loop(1, total, wait, 0)
    out_small.start()
    out_small.wait()


def opening(x, small, w_out, w_query, w_key, w_value, w_gate, copies, slab, collective_id, parts=4):
    groups, seqs = lax.axis_size("expert"), lax.axis_size("dp")
    total = groups * seqs
    block, width = w_query.shape
    rows = x.shape[0]
    gate = jax.ShapeDtypeStruct((1,) + w_gate.shape[1:], BF16)

    def kernel(*refs):
        ins, refs = refs[:7], refs[7:]
        outs, gates, rest = refs[:6], refs[6:10], refs[10:]
        opening_body(groups, seqs, copies, slab, rows, parts, gates, *ins, *outs, *rest)

    vmem, anywhere = pl.BlockSpec(memory_space=pltpu.VMEM), pl.BlockSpec(memory_space=pl.ANY)
    dma = pltpu.SemaphoreType.DMA
    line = dma((2, groups // 2, parts))
    return pl.pallas_call(
        kernel,
        out_shape=[
            jax.ShapeDtypeStruct((groups * rows, width), x.dtype),
            jax.ShapeDtypeStruct((total,) + small.shape, small.dtype),
            jax.ShapeDtypeStruct((seqs * groups * block, 3 * slab), BF16),
            jax.ShapeDtypeStruct((seqs * block, width), BF16),
            jax.ShapeDtypeStruct((block, width), BF16),
            jax.ShapeDtypeStruct((groups * block, 3 * slab), BF16),
        ]
        + [gate] * 4,
        in_specs=[anywhere, vmem] + [anywhere] * 5,
        out_specs=[anywhere] * 10,
        scratch_shapes=[pltpu.VMEM((total,) + small.shape, small.dtype)]
        + [dma((total,)), dma((total,)), dma((2,)), dma((3,)), dma((groups, 3)), dma((groups, 3)), dma]
        + [dma((4,)), dma((4,)), dma((2,)), dma((2, 4)), dma((2, 4))]
        + [dma] + [line] * 4,
        compiler_params=pltpu.CompilerParams(collective_id=collective_id, has_side_effects=True),
        cost_estimate=cost_of(80),
        name="opening",
    )(x, small, w_out, w_query, w_key, w_value, w_gate)


def both(array, start=0, size=None):
    size = array.shape[0] if size is None else size
    return [(array, start, size, 1), (array, start, size, 2)]


def swap_dp(block, flip):
    seqs = lax.axis_size("dp")
    return lax.ppermute(block, "dp", [(i, i ^ flip) for i in range(seqs)])


def tie(value, *deps):
    return lax.optimization_barrier((value,) + deps)[0]


def near_dp(block):
    return block, swap_dp(block, 1), swap_dp(block, 2)


def far_dp(near, *deps):
    block, near_x, near_y = near
    half = block.shape[0] // 2
    via_x, via_y = lax.optimization_barrier((near_y[:half], near_x[half:]) + deps)[:2]
    far = jnp.concatenate([swap_dp(via_x, 1), swap_dp(via_y, 2)], axis=0)
    return [block, near_x, near_y, far]


def halves(block):
    half = block.shape[0] // 2
    return [(block, 0, half, 1), (block, half, half, 2)]


def relay(blocks, from_x, from_y):
    _, to_x, to_y, _ = blocks
    half = to_x.shape[0] // 2
    to_x = jnp.concatenate(
        [to_x[:half], (to_x[half:].astype(F32) + from_y.astype(F32)).astype(BF16)], axis=0
    )
    to_y = jnp.concatenate(
        [(to_y[:half].astype(F32) + from_x.astype(F32)).astype(BF16), to_y[half:]], axis=0
    )
    return to_x, to_y


def settle(blocks, from_x, from_y):
    return blocks[0].astype(F32) + from_x.astype(F32) + from_y.astype(F32)


def send_halves(blocks):
    half = blocks[3].shape[0] // 2
    return swap_dp(blocks[3][:half], 1), swap_dp(blocks[3][half:], 2)


def in_order(pieces, index, axis):
    low = (index % 2) == 1
    high = (index // 2) == 1
    a, b, c, d = pieces
    a, b, c, d = (
        jnp.where(low, b, a), jnp.where(low, a, b), jnp.where(low, d, c), jnp.where(low, c, d)
    )
    return jnp.concatenate(
        [jnp.where(high, c, a), jnp.where(high, d, b), jnp.where(high, a, c), jnp.where(high, b, d)],
        axis=axis,
    )


def own_order(array, index, axis):
    return in_order(jnp.split(array, 4, axis=axis), index, axis)


def shards(
    tokens, routes, grad_output, w_query, w_key, w_value, w_out, w_router,
    gain_attn, gain_query, gain_key, gain_ffn, w_gate, w_up, w_down,
):
    rows = tokens.shape[1]
    width = tokens.shape[2]
    groups = lax.axis_size("expert")
    seqs = lax.axis_size("dp")
    me = lax.axis_index("expert")
    length = rows * groups
    local_experts = w_gate.shape[0]
    all_experts = local_experts * groups
    block = w_query.shape[0]
    own = width // groups
    slab = max(own, HEAD_DIM)
    copies = slab // own
    heads = slab // HEAD_DIM
    share = 1.0 / copies
    offset = (me % copies) * own

    x_low = tokens.reshape(rows, width)
    g_low = grad_output.reshape(rows, width)

    my_dp = lax.axis_index("dp")
    small_size = block * (all_experts + 4)
    small_rows = -(-small_size // (16 * 128)) * 16
    small = jnp.concatenate(
        [w_router.reshape(-1), gain_attn, gain_query, gain_key, gain_ffn,
         jnp.zeros((small_rows * 128 - small_size,), BF16)]
    )
    x_all, small_all, w_qkv, w_o, _, _, gate0_x, gate0_y, gate1_x, gate1_y = opening(
        x_low, small.reshape(small_rows, 128), w_out, w_query, w_key, w_value, w_gate, copies, slab,
        1,
    )
    small_all = small_all.reshape(seqs * groups, small_rows * 128)
    split = block * all_experts
    w_r = small_all[:, :split].reshape(width, all_experts)
    gains = [
        small_all[:, split + i * block : split + (i + 1) * block].reshape(width).astype(F32)
        for i in range(4)
    ]
    g_attn, g_ffn = gains[0], gains[3]
    slab_start = (me // copies) * slab
    g_query = lax.dynamic_slice(gains[1], (slab_start,), (slab,))
    g_key = lax.dynamic_slice(gains[2], (slab_start,), (slab,))

    total = seqs * groups
    moves = [(b, (b % seqs) * groups + b // seqs) for b in range(total)]

    x_in = x_low.astype(F32)
    inv_attn = inv_rms(x_in)
    x_wide = x_all.astype(F32)
    normed_all = (x_wide * inv_rms(x_wide) * g_attn).astype(BF16)
    if copies > 1:
        sets = [[c * copies + i for i in range(copies)] for c in range(groups // copies)]
        w_o = lax.all_gather(w_o, "expert", axis_index_groups=sets, axis=0, tiled=True)

    near_up = tie(w_up, x_all)
    up_x, up_y = swap_dp(near_up, 1), swap_dp(near_up, 2)
    g_all = lax.all_gather(g_low, "expert", axis=0, tiled=True)

    raw = dot(normed_all, w_qkv)
    q_raw, k_raw, v_raw = raw[:, :slab], raw[:, slab : 2 * slab], raw[:, 2 * slab :]
    squares = jnp.stack([jnp.sum(q_raw * q_raw, axis=1), jnp.sum(k_raw * k_raw, axis=1)], axis=0)
    squares = exchange(
        (squares * share).reshape(1, 2 * length // 128, 128), 4, same=True, reduce=True
    ).reshape(2, length)
    inv_qk = lax.rsqrt(squares / width + EPS)
    inv_q, inv_k = inv_qk[0][:, None], inv_qk[1][:, None]
    tables = rope_tables(length)

    def to_heads(values):
        return values.reshape(length, heads, HEAD_DIM)

    queries = rotary(to_heads(q_raw * inv_q * g_query), tables).astype(BF16).transpose(1, 0, 2)
    keys = rotary(to_heads(k_raw * inv_k * g_key), tables).astype(BF16).transpose(1, 0, 2)
    values = to_heads(v_raw).astype(BF16).transpose(1, 0, 2)
    positions = jnp.arange(length, dtype=jnp.int32)
    scale = HEAD_DIM ** (-0.5)

    def head_probs(q, k):
        scores = dot_nt(q, k) * scale
        scores = jnp.where(positions[None, :] <= positions[:, None], scores, NEG)
        exp_terms = jnp.exp(scores - jnp.max(scores, axis=-1, keepdims=True))
        return exp_terms / jnp.sum(exp_terms, axis=-1, keepdims=True)

    mixes = []
    for h in range(heads):
        mixes.append(dot(head_probs(queries[h], keys[h]).astype(BF16), values[h]).astype(BF16))
    mix = jnp.concatenate(mixes, axis=1)
    o_sum, gate0_f, gate1_f, up0_f, up1_f = line_reduce(
        dot(mix, w_o) * share, 5,
        sends=[(gate0_y, 0, 1, 1), (gate1_x, 0, 1, 2), (up_y, 0, 1, 1), (up_x, 1, 1, 2)],
    )
    after_attn = x_in + o_sum

    inv_ffn = inv_rms(after_attn)
    ffn_low = (after_attn * inv_ffn * g_ffn).astype(BF16)
    router_prob = jax.nn.softmax(dot(ffn_low, w_r), axis=-1)
    chosen = routes.reshape(rows, routes.shape[2])
    chosen_mask = jnp.sum(
        (chosen[:, :, None] == jnp.arange(all_experts, dtype=jnp.int32)[None, None, :]).astype(F32),
        axis=1,
    )
    route_dense = router_prob * chosen_mask
    gate_near = [(gate0_x, 0), (gate1_x, 0), (gate0_y, 0), (gate1_y, 0), (gate0_f, 0), (gate1_f, 0)]
    up_near = [(up_x, 0), (up_x, 1), (up_y, 0), (up_y, 1), (up0_f, 0), (up1_f, 0)]
    ff = w_gate.shape[2]
    if copies == 1 and length * width <= 1 << 21:
        high = lax.reduce_precision(route_dense, 8, 7)
        space = jnp.zeros((rows, LANES // 2 - all_experts), F32)
        extra = jnp.concatenate([high, space, route_dense - high, space], axis=1).astype(BF16)
        ffn_all, hidden_w, d_gate, d_up, tail, wd, d_down = expert_first(
            jnp.concatenate([ffn_low, extra], axis=1), g_all, w_gate, w_up, w_down,
            gate_near + up_near, 9,
        )
        d_gate_w, down_near, down_mid, d_rows = expert_second(
            d_gate, d_up, tail, ffn_all, d_down, w_gate, w_up, gate_near + up_near, 13
        )
        d_weight = d_rows[:, width : width + LANES]
        d_weight = d_weight[:, :all_experts] + d_weight[:, LANES // 2 : LANES // 2 + all_experts]
        d_rows = d_rows[:, :width]
    else:
        ffn_all = line_gather(ffn_low, 3)
        pad = -local_experts % 8
        route_send = route_dense.T.reshape(groups, local_experts, rows)
        route_send = jnp.pad(route_send, ((0, 0), (0, pad), (0, 0)))
        route_mine = exchange(route_send, 6)[:, :local_experts].transpose(0, 2, 1)
        route_mine = route_mine.reshape(length, local_experts)
        near_down = near_dp(tie(w_down, ffn_all))
        wd = in_order(far_dp(near_down), my_dp, 1)
        hidden_w, d_gate, d_up, d_weights = [], [], [], []
        y_part, dx_part = 0.0, 0.0
        for i in range(local_experts):
            wg, wu = (
                in_order([own[i]] + [near[2 * q + i][0][near[2 * q + i][1]] for q in range(3)], my_dp, 0)
                for own, near in ((w_gate, gate_near), (w_up, up_near))
            )
            weight = route_mine[:, i : i + 1]
            gate, up = dot(ffn_all, wg), dot(ffn_all, wu)
            d_hid = dot_nt(g_all, wd[i])
            sig = jax.nn.sigmoid(gate)
            silu = gate * sig
            d_weights.append(jnp.sum(silu * up * d_hid, axis=1))
            hidden_w.append((silu * up * weight).astype(BF16))
            d_hid = d_hid * weight
            d_gate.append((d_hid * up * sig * (1.0 + gate * (1.0 - sig))).astype(BF16))
            d_up.append((d_hid * silu).astype(BF16))
            y_part = y_part + dot(hidden_w[i], wd[i])
            dx_part = dx_part + dot_nt(d_gate[i], wg) + dot_nt(d_up[i], wu)
            (ffn_all, y_part, dx_part) = lax.optimization_barrier((ffn_all, y_part, dx_part))
        hidden_w, d_gate, d_up = (jnp.concatenate(a, axis=1) for a in (hidden_w, d_gate, d_up))
        y_part = y_part.astype(BF16)
        d_down = dot_tn(hidden_w, g_all).astype(BF16).reshape(local_experts, ff, width)
        d_rows = line_reduce(dx_part, 10)
        d_weight = jnp.stack(d_weights, axis=0).reshape(local_experts, groups, rows)
        d_weight = jnp.pad(d_weight.transpose(1, 0, 2), ((0, 0), (0, pad), (0, 0)))
        d_weight = exchange(d_weight, 6)[:, :local_experts].reshape(all_experts, rows).T

    fused = copies == 1 and length * width <= 1 << 21

    def scatter_in(product):
        return lax.psum_scatter(product, "dp", scatter_dimension=0, tiled=True)

    def to_experts(own_grad):
        return jnp.stack([own_grad[:, i * ff : (i + 1) * ff] for i in range(local_experts)]).astype(F32)

    if not fused:
        own_down = lax.psum_scatter(d_down, "dp", scatter_dimension=1, tiled=True)
        d_gate_w = dot_tn(ffn_all, d_gate).astype(BF16)
    own_gate = to_experts(scatter_in(d_gate_w))
    d_router_prob = d_weight * chosen_mask

    d_logits = (
        router_prob * (d_router_prob - jnp.sum(d_router_prob * router_prob, axis=-1, keepdims=True))
    ).astype(BF16)
    d_router_w = dot_tn(ffn_low, d_logits)
    d_normed_ffn = d_rows + dot_nt(d_logits, w_r)
    d_after_norm, d_gain_ffn = norm_back(after_attn, inv_ffn, g_ffn, d_normed_ffn)
    d_after = g_low.astype(F32) + d_after_norm
    if fused:
        d_after_all, d_up_w, y_part, own_down = gather_fill(
            d_after.astype(BF16), ffn_all, d_up, hidden_w, wd.reshape(local_experts * ff, width),
            d_down, down_mid, down_near, ff, 11,
        )
    else:
        d_after_all = line_gather(d_after.astype(BF16), 16)
        d_up_w = dot_tn(ffn_all, d_up).astype(BF16)
    own_up = scatter_in(d_up_w)
    d_out_w = dot_tn(mix, d_after_all)
    d_mix = dot_nt(d_after_all, w_o).astype(BF16)
    dqs, dks, dvs = [], [], []
    for h in range(heads):
        prob = head_probs(queries[h], keys[h])
        d_m = d_mix[:, h * HEAD_DIM : (h + 1) * HEAD_DIM]
        d_prob = dot_nt(d_m, values[h])
        row_delta = jnp.sum(d_prob * prob, axis=-1, keepdims=True)
        d_score = (prob * (d_prob - row_delta) * scale).astype(BF16)
        dqs.append(dot(d_score, keys[h]))
        dks.append(dot_tn(d_score, queries[h]))
        dvs.append(dot_tn(prob.astype(BF16), d_m))
    dq_n = rotary_back(jnp.stack(dqs, axis=1), tables).reshape(length, slab)
    dk_n = rotary_back(jnp.stack(dks, axis=1), tables).reshape(length, slab)
    dv_low = jnp.concatenate(dvs, axis=1).astype(BF16)
    dots = jnp.stack(
        [jnp.sum(dq_n * g_query * q_raw, axis=1), jnp.sum(dk_n * g_key * k_raw, axis=1)], axis=0
    )
    dots = exchange(
        (dots * share).reshape(1, 2 * length // 128, 128), 4, same=True, reduce=True
    ).reshape(2, length) / width
    d_gain_query = jnp.sum(dq_n * q_raw * inv_q, axis=0)
    d_gain_key = jnp.sum(dk_n * k_raw * inv_k, axis=0)
    dq_low = (inv_q * dq_n * g_query - q_raw * (inv_q**3 * dots[0][:, None])).astype(BF16)
    dk_low = (inv_k * dk_n * g_key - k_raw * (inv_k**3 * dots[1][:, None])).astype(BF16)
    d_raw = jnp.concatenate([dq_low, dk_low, dv_low], axis=1)
    d_qkv_w = dot_tn(normed_all, d_raw).astype(BF16)
    d_qkv_w = d_qkv_w.reshape(width, 3, slab)
    d_qkv_w = lax.dynamic_slice(d_qkv_w, (0, 0, offset), (width, 3, own))
    d_qkv_w = d_qkv_w.reshape(width, 3 * own)
    d_out_w = lax.dynamic_slice(d_out_w.astype(BF16), (offset, 0), (own, width))
    dx_in = (dot_nt(d_raw, w_qkv) * share).astype(BF16)
    if length * width <= 1 << 21:
        d_normed_in, y_sum, own_qkv, own_out = joint_reduce(
            [dx_in, y_part], [d_qkv_w, d_out_w], [own_gate], 12
        )
    else:
        d_normed_in, own_qkv, own_out = joint_reduce(
            [dx_in], [d_qkv_w, d_out_w], [own_gate], 12
        )
        y_sum = line_reduce(y_part, 15)
    output = after_attn + y_sum
    d_in_norm, d_gain_attn = norm_back(x_in, inv_attn, g_attn, d_normed_in)
    input_grad = d_after + d_in_norm

    spread = jnp.zeros((2, width), F32)
    spread = lax.dynamic_update_slice(
        spread, jnp.stack([d_gain_query, d_gain_key]) * share, (0, slab_start)
    )
    total = seqs * groups
    small_grad = jnp.concatenate(
        [d_router_w.reshape(total, split)]
        + [v.reshape(total, block) for v in (d_gain_attn, spread[0], spread[1], d_gain_ffn)]
        + [jnp.zeros((total, small_rows * 128 - small_size), F32)],
        axis=1,
    )
    small_grad = small_grad.reshape(total, small_rows, 128)
    if own % 128 == 0:
        output, input_grad = (a.reshape(1, rows, width) for a in (output, input_grad))
        small_grad, *matrices = last_exchange(
            small_grad, own_qkv, own_out, [output, input_grad], 8
        )
    else:
        small_grad = exchange(small_grad, 8, spread=True, reduce=True)
        own_qkv = exchange(own_qkv.reshape(groups, block, 3 * own), 7)
        own_qkv = own_qkv.reshape(groups, block, 3, own).transpose(2, 1, 0, 3)
        own_out = lax.ppermute(own_out, ("dp", "expert"), [(b, a) for a, b in moves])
        matrices = [*own_qkv.reshape(3, block, width).astype(F32), own_out.astype(F32)]
    small_grad = small_grad.reshape(-1)
    expert_owned = [own_gate, to_experts(own_up), own_down.astype(F32)]
    return (
        output.reshape(1, rows, width),
        input_grad.reshape(1, rows, width),
        *matrices,
        small_grad[:split].reshape(block, all_experts),
        small_grad[split : split + block],
        small_grad[split + block : split + 2 * block],
        small_grad[split + 2 * block : split + 3 * block],
        small_grad[split + 3 * block : split + 4 * block],
        *expert_owned,
    )


def solution(mesh):
    tok = P("dp", "expert", None)
    mat = P(("dp", "expert"), None)
    vec = P(("dp", "expert"))
    exp = P("expert", "dp", None)
    return jax.shard_map(
        shards,
        mesh=mesh,
        in_specs=(tok, tok, tok, mat, mat, mat, mat, mat, vec, vec, vec, vec, exp, exp, exp),
        out_specs=(tok, tok, mat, mat, mat, mat, mat, vec, vec, vec, vec, exp, exp, exp),
        check_vma=False,
    )
```

```python
import functools
import math

import jax
import jax.numpy as jnp
from jax import lax
from jax.experimental import pallas as pl
from jax.experimental.pallas import tpu as pltpu
from jax.sharding import PartitionSpec as P

HEADS = 16
HEAD_DIM = 128

EPS = 1e-05
THETA = 10000.0
NEG = -1e30

F32 = jnp.float32
BF16 = jnp.bfloat16


def dot(left, right):
    return jnp.dot(left, right, preferred_element_type=F32)


def dot_tn(left, right):
    return lax.dot_general(left, right, (((0,), (0,)), ((), ())), preferred_element_type=F32)


def dot_nt(left, right):
    return lax.dot_general(left, right, (((1,), (1,)), ((), ())), preferred_element_type=F32)


def inv_rms(values):
    return lax.rsqrt(jnp.mean(values * values, axis=-1, keepdims=True) + EPS)


def norm_back(values, inv, gain_vec, grad):
    scaled = grad * gain_vec
    mean_dot = jnp.mean(scaled * values, axis=-1, keepdims=True)
    d_values = inv * scaled - values * (inv * inv * inv * mean_dot)
    d_gain = jnp.sum(grad * values * inv, axis=0)
    return d_values, d_gain


def rope_tables(length):
    half_dim = HEAD_DIM // 2
    inv_freq = jnp.exp(
        jnp.arange(half_dim, dtype=F32) * (-2.0 * math.log(THETA) / HEAD_DIM)
    )
    angles = jnp.arange(length, dtype=jnp.int32).astype(F32)[:, None] * inv_freq[None, :]
    cosine, sine = jnp.cos(angles), jnp.sin(angles)
    return (
        jnp.concatenate([cosine, cosine], axis=1)[:, None, :],
        jnp.concatenate([-sine, sine], axis=1)[:, None, :],
    )


def swap_halves(values):
    half_dim = HEAD_DIM // 2
    return jnp.concatenate([values[..., half_dim:], values[..., :half_dim]], axis=-1)


def rotary(values, tables):
    return values * tables[0] + swap_halves(values) * tables[1]


def rotary_back(grad, tables):
    return grad * tables[0] - swap_halves(grad) * tables[1]


MESH = pl.DeviceIdType.MESH
VMEM_LIMIT = 56 * 1024 * 1024


def cost_of(micros):
    return pl.CostEstimate(flops=0, bytes_accessed=int(micros * 3.0e6), transcendentals=0)


def flipped(dp, flip):
    return dp + flip - 2 * flip * ((dp // flip) % 2)


class Whole:
    def __init__(self, source, target, own_sem, send, recv):
        self.me, self.dp = lax.axis_index("expert"), lax.axis_index("dp")
        self.source, self.target = source, target
        self.own_sem, self.send, self.recv = own_sem, send, recv
        self.rows = source.shape[0]
        half = self.rows // 2
        self.split = (half, half) if half % 16 == 0 else (self.rows, 0)

    def place(self, owner, start, size):
        return self.target.at[pl.ds(pl.multiple_of(owner * self.rows, self.rows) + start, size)]

    def keep(self):
        return pltpu.make_async_copy(self.source, self.place(self.dp, 0, self.rows), self.own_sem)

    def copy(self, i):
        flip = i % 2 + 1
        if i < 2:
            src, dst = self.source, self.place(self.dp, 0, self.rows)
        else:
            start = 0 if i == 2 else self.split[0]
            src = dst = self.place(flipped(self.dp, 3 - flip), start, self.split[i - 2])
        return pltpu.make_async_remote_copy(
            src_ref=src, dst_ref=dst, send_sem=self.send.at[i], recv_sem=self.recv.at[i],
            device_id=(flipped(self.dp, flip), self.me), device_id_type=MESH,
        )

    def start(self):
        self.copy(0).start()
        self.copy(1).start()
        self.keep().start()

    def start_later(self):
        self.copy(1).wait_recv()
        self.copy(2).start()
        self.copy(0).wait_recv()
        if self.split[1]:
            self.copy(3).start()

    def finish(self):
        self.keep().wait()
        for i in range(4 if self.split[1] else 3):
            self.copy(i).wait_send()
            if i >= 2:
                self.copy(i).wait_recv()


class Plane:
    def __init__(self, sends, later, sources, targets, send, recv, wholes=()):
        self.me, self.dp = lax.axis_index("expert"), lax.axis_index("dp")
        self.sends, self.later, self.wholes = sends, later, wholes
        self.sources, self.targets, self.send, self.recv = sources, targets, send, recv

    def busy(self):
        return len(self.sends) + len(self.wholes) > 0

    def greet(self, barrier):
        if self.busy():
            for flip in (1, 2):
                pl.semaphore_signal(
                    barrier, inc=1, device_id=(flipped(self.dp, flip), self.me), device_id_type=MESH
                )

    def copy(self, i):
        first = len(self.sends)
        if i < first:
            source, start, size, flip = self.sends[i]
            ref = self.sources[source]
        else:
            source, start, size, flip = self.later[i - first]
            ref = self.targets[source]
        return pltpu.make_async_remote_copy(
            src_ref=ref.at[pl.ds(start, size)],
            dst_ref=self.targets[i],
            send_sem=self.send.at[i],
            recv_sem=self.recv.at[i],
            device_id=(flipped(self.dp, flip), self.me),
            device_id_type=MESH,
        )

    def start(self):
        for whole in self.wholes:
            whole.start()
        for i in range(len(self.sends)):
            self.copy(i).start()

    def start_later(self):
        first = len(self.sends)
        for source in sorted({l[0] for l in self.later}):
            self.copy(source).wait_recv()
        for i in range(len(self.later)):
            self.copy(first + i).start()
        for whole in self.wholes:
            whole.start_later()

    def finish(self):
        for whole in self.wholes:
            whole.finish()
        waited = {l[0] for l in self.later}
        for i in range(len(self.sends) + len(self.later)):
            self.copy(i).wait_send()
            if i not in waited:
                self.copy(i).wait_recv()


def line_greet(me, dp, chip, chips, plane):
    barrier = pltpu.get_barrier_semaphore()
    sibling = chip * 2 + 1 - me % 2
    extra = 2 if plane.busy() else 0
    pl.semaphore_signal(barrier, inc=1, device_id=(dp, sibling), device_id_type=MESH)
    plane.greet(barrier)

    @pl.when(chip > 0)
    def _():
        pl.semaphore_signal(barrier, inc=1, device_id=(dp, me - 2), device_id_type=MESH)

    @pl.when(chip < chips - 1)
    def _():
        pl.semaphore_signal(barrier, inc=1, device_id=(dp, me + 2), device_id_type=MESH)

    @pl.when((chip > 0) & (chip < chips - 1))
    def _():
        pl.semaphore_wait(barrier, 3 + extra)

    @pl.when((chip == 0) | (chip == chips - 1))
    def _():
        pl.semaphore_wait(barrier, 2 + extra)


def gather_body(
    groups, rows, parts, plane, x_ref, o_ref, own_sem, send, recv, pair_send, pair_recv,
    greet=True, work=None,
):
    chips = groups // 2
    me, dp = lax.axis_index("expert"), lax.axis_index("dp")
    chip = me // 2
    sibling = chip * 2 + 1 - me % 2
    part = rows // parts
    if greet:
        line_greet(me, dp, chip, chips, plane)
    keep = pltpu.make_async_copy(x_ref, o_ref.at[pl.ds(pl.multiple_of(me * rows, rows), rows)], own_sem)

    def copy(origin, u, target, send_sem, recv_sem, first):
        place = pl.ds(pl.multiple_of(origin * rows + u * part, part), part)
        return pltpu.make_async_remote_copy(
            src_ref=x_ref.at[pl.ds(u * part, part)] if first else o_ref.at[place],
            dst_ref=o_ref.at[place],
            send_sem=send_sem,
            recv_sem=recv_sem,
            device_id=(dp, target),
            device_id_type=MESH,
        )

    def right(k, u):
        return copy(me - 2 * k, u, me + 2, send.at[0, k, u], recv.at[0, k, u], k == 0)

    def left(k, u):
        return copy(me + 2 * k, u, me - 2, send.at[1, k, u], recv.at[1, k, u], k == 0)

    def pair(side, k, u):
        origin = me - 2 * k if side == 0 else me + 2 * k
        return copy(origin, u, sibling, pair_send.at[side, k, u], pair_recv.at[side, k, u], k == 0)

    sides = lambda k: (
        (0, chip - k >= 0, chip < chips - 1),
        (1, chip + k <= chips - 1, chip > 0),
    )
    for k in range(chips):
        if k == 1 and not greet:
            plane.start_mid()
        if k == chips - 1:
            plane.start_later()
        for u in range(parts):
            for side, has, send_on in sides(k):
                step = right if side == 0 else left

                @pl.when(has)
                def _(k=k, u=u, side=side, send_on=send_on, step=step):
                    if k > 0:
                        step(k - 1, u).wait_recv()
                    if k < chips - 1:

                        @pl.when(send_on)
                        def _():
                            step(k, u).start()

                    if k > 0:
                        pair(side, k, u).start()

            if k == 0:
                pair(0, 0, u).start()
        if k == 0:
            plane.start()
            keep.start()
        if work is not None:
            work(k)

    keep.wait()
    for k in range(chips):
        for u in range(parts):
            if k == 0:
                pair(0, 0, u).wait()
            for side, has, send_on in sides(k):
                step = right if side == 0 else left

                @pl.when(has)
                def _(k=k, u=u, side=side, send_on=send_on, step=step):
                    if k < chips - 1:

                        @pl.when(send_on)
                        def _():
                            step(k, u).wait_send()

                    if k > 0:
                        pair(side, k, u).wait()

    plane.finish()


def reduce_body(
    groups, rows, parts, plane, p_ref, o_ref, own, pair, inbox, load_sem, pair_send, pair_recv, send, recv
):
    chips = groups // 2
    me, dp = lax.axis_index("expert"), lax.axis_index("dp")
    chip, core = me // 2, me % 2
    sibling = chip * 2 + 1 - core
    part = rows // parts
    step_rows = 16
    line_greet(me, dp, chip, chips, plane)

    def pair_copy(d):
        place = pl.ds(pl.multiple_of((2 * d + 1 - core) * rows, rows), rows)
        return pltpu.make_async_remote_copy(
            src_ref=p_ref.at[place],
            dst_ref=pair.at[d],
            send_sem=pair_send.at[d],
            recv_sem=pair_recv.at[d],
            device_id=(dp, sibling),
            device_id_type=MESH,
        )

    def own_copy(d):
        place = pl.ds(pl.multiple_of((2 * d + core) * rows, rows), rows)
        return pltpu.make_async_copy(p_ref.at[place], own.at[d], load_sem.at[d])

    order = []
    for j in range((chips + 1) // 2):
        order += [chips - 1 - j] + ([j] if j != chips - 1 - j else [])
    for d in order:
        pair_copy(d).start()
        own_copy(d).start()
    plane.start()

    def hop(d, u, side):
        place = pl.ds(u * part, part)
        target = me + 2 if side == 0 else me - 2
        slot = d if side == 0 else chips + d
        return pltpu.make_async_remote_copy(
            src_ref=own.at[d, place],
            dst_ref=inbox.at[slot, place],
            send_sem=send.at[d, u],
            recv_sem=recv.at[slot, u],
            device_id=(dp, target),
            device_id_type=MESH,
        )

    def add(d, u, slots, store):
        def body(i, carry):
            at = pl.ds(pl.multiple_of(u * part + i * step_rows, step_rows), step_rows)
            value = own[d, at].astype(F32) + pair[d, at].astype(F32)
            for slot in slots:
                value = value + inbox[slot, at].astype(F32)
            store(at, value)
            return carry

        lax.fori_loop(0, part // step_rows, body, 0)

    def forward(d, side):
        pair_copy(d).wait_recv()
        own_copy(d).wait()

        def store(at, value):
            own[d, at] = value.astype(BF16)

        end = chip == (0 if side == 0 else chips - 1)
        for u in range(parts):

            @pl.when(end)
            def _(u=u):
                add(d, u, (), store)

            @pl.when(jnp.logical_not(end))
            def _(u=u):
                hop(d, u, side).wait_recv()
                add(d, u, (d if side == 0 else chips + d,), store)

            hop(d, u, side).start()

    for j in range(chips - 1):
        far, near = chips - 1 - j, j

        @pl.when(far > chip)
        def _(far=far):
            forward(far, 0)

        @pl.when(near < chip)
        def _(near=near):
            forward(near, 1)

        if j == chips - 2:
            plane.start_later()

    pair_copy(chip).wait_recv()
    own_copy(chip).wait()

    def finish(at, value):
        o_ref[at] = value

    for u in range(parts):

        @pl.when(chip == 0)
        def _(u=u):
            hop(chip, u, 1).wait_recv()
            add(chip, u, (chips + chip,), finish)

        @pl.when(chip == chips - 1)
        def _(u=u):
            hop(chip, u, 0).wait_recv()
            add(chip, u, (chip,), finish)

        @pl.when((chip > 0) & (chip < chips - 1))
        def _(u=u):
            hop(chip, u, 0).wait_recv()
            hop(chip, u, 1).wait_recv()
            add(chip, u, (chip, chips + chip), finish)

    for d in range(chips):
        pair_copy(d).wait_send()
        for u in range(parts):

            @pl.when(d > chip)
            def _(d=d, u=u):
                hop(d, u, 0).wait_send()

            @pl.when(d < chip)
            def _(d=d, u=u):
                hop(d, u, 1).wait_send()

    plane.finish()


def joint_body(
    groups, rows, parts, plane, p_refs, o_refs, own, pair, inbox, load_sem, pair_send, pair_recv, send, recv
):
    kinds = range(len(p_refs))
    chips = groups // 2
    me, dp = lax.axis_index("expert"), lax.axis_index("dp")
    chip, core = me // 2, me % 2
    sibling = chip * 2 + 1 - core
    part = rows // parts
    step_rows = 16
    line_greet(me, dp, chip, chips, plane)

    def pair_copy(a, d):
        place = pl.ds(pl.multiple_of((2 * d + 1 - core) * rows, rows), rows)
        return pltpu.make_async_remote_copy(
            src_ref=p_refs[a].at[place],
            dst_ref=pair.at[a, d],
            send_sem=pair_send.at[a, d],
            recv_sem=pair_recv.at[a, d],
            device_id=(dp, sibling),
            device_id_type=MESH,
        )

    def own_copy(a, d):
        place = pl.ds(pl.multiple_of((2 * d + core) * rows, rows), rows)
        return pltpu.make_async_copy(p_refs[a].at[place], own.at[a, d], load_sem.at[a, d])

    order = []
    for j in range((chips + 1) // 2):
        order += [chips - 1 - j] + ([j] if j != chips - 1 - j else [])
    for a in kinds:
        for d in order:
            pair_copy(a, d).start()
            own_copy(a, d).start()
    plane.start()

    def hop(a, d, u, side):
        place = pl.ds(u * part, part)
        target = me + 2 if side == 0 else me - 2
        slot = d if side == 0 else chips + d
        return pltpu.make_async_remote_copy(
            src_ref=own.at[a, d, place],
            dst_ref=inbox.at[a, slot, place],
            send_sem=send.at[a, d, u],
            recv_sem=recv.at[a, slot, u],
            device_id=(dp, target),
            device_id_type=MESH,
        )

    def add(a, d, u, slots, store):
        def body(i, carry):
            at = pl.ds(pl.multiple_of(u * part + i * step_rows, step_rows), step_rows)
            value = own[a, d, at].astype(F32) + pair[a, d, at].astype(F32)
            for slot in slots:
                value = value + inbox[a, slot, at].astype(F32)
            store(at, value)
            return carry

        lax.fori_loop(0, part // step_rows, body, 0)

    def forward(a, d, side):
        pair_copy(a, d).wait_recv()
        own_copy(a, d).wait()

        def store(at, value):
            own[a, d, at] = value.astype(BF16)

        end = chip == (0 if side == 0 else chips - 1)
        for u in range(parts):

            @pl.when(end)
            def _(u=u):
                add(a, d, u, (), store)

            @pl.when(jnp.logical_not(end))
            def _(u=u):
                hop(a, d, u, side).wait_recv()
                add(a, d, u, (d if side == 0 else chips + d,), store)

            hop(a, d, u, side).start()

    def finish(a):
        pair_copy(a, chip).wait_recv()
        own_copy(a, chip).wait()

        def store(at, value):
            o_refs[a][at] = value

        for u in range(parts):

            @pl.when(chip == 0)
            def _(u=u):
                hop(a, chip, u, 1).wait_recv()
                add(a, chip, u, (chips + chip,), store)

            @pl.when(chip == chips - 1)
            def _(u=u):
                hop(a, chip, u, 0).wait_recv()
                add(a, chip, u, (chip,), store)

            @pl.when((chip > 0) & (chip < chips - 1))
            def _(u=u):
                hop(a, chip, u, 0).wait_recv()
                hop(a, chip, u, 1).wait_recv()
                add(a, chip, u, (chip, chips + chip), store)

    for a in kinds:
        for j in range(chips - 1):
            far, near = chips - 1 - j, j

            @pl.when(far > chip)
            def _(a=a, far=far):
                forward(a, far, 0)

            @pl.when(near < chip)
            def _(a=a, near=near):
                forward(a, near, 1)

            if a == 0 and j == (chips - 1) // 2:

                @pl.when((chip > 0) & (chip < chips - 1))
                def _():
                    plane.start_later()

    if len(p_refs) > 1:

        @pl.when((chip == 0) | (chip == chips - 1))
        def _():
            plane.start_later()

    else:
        plane.start_later()
    for a in kinds:
        finish(a)

    for a in kinds:
        for d in range(chips):
            pair_copy(a, d).wait_send()
            for u in range(parts):

                @pl.when(d > chip)
                def _(a=a, d=d, u=u):
                    hop(a, d, u, 0).wait_send()

                @pl.when(d < chip)
                def _(a=a, d=d, u=u):
                    hop(a, d, u, 1).wait_send()

    plane.finish()


class PlaneSum:
    def __init__(self, parts):
        self.me, self.dp = lax.axis_index("expert"), lax.axis_index("dp")
        self.parts = parts
        self.owners = (
            self.dp, flipped(self.dp, 1), flipped(self.dp, 2), flipped(flipped(self.dp, 1), 2)
        )

    def busy(self):
        return True

    greet = Plane.greet

    def remote(self, src, dst, send, recv, flip):
        return pltpu.make_async_remote_copy(
            src_ref=src, dst_ref=dst, send_sem=send, recv_sem=recv,
            device_id=(flipped(self.dp, flip), self.me), device_id_type=MESH,
        )

    def sizes(self, p):
        rows = p["out"].shape[0]
        half = rows // 2
        return rows, ((half, half) if half % 16 == 0 else (rows, 0))

    def rows_of(self, p, q, start, size):
        rows, _ = self.sizes(p)
        return pl.ds(pl.multiple_of(self.owners[q] * rows, rows) + start, size)

    def load(self, p):
        return pltpu.make_async_copy(p["ref"], p["buf"], p["load"])

    def early(self, p, i):
        _, split = self.sizes(p)
        start = 0 if i == 0 else split[0]
        return self.remote(
            p["ref"].at[self.rows_of(p, 3, start, split[i])], p["first"].at[pl.ds(start, split[i])],
            p["send"].at[i], p["recv"].at[i], i + 1,
        )

    def late(self, p, i):
        rows, _ = self.sizes(p)
        return self.remote(
            p["buf"].at[self.rows_of(p, i + 1, 0, rows)], p["second"].at[i],
            p["send"].at[2 + i], p["recv"].at[2 + i], i + 1,
        )

    def counts(self, p):
        return 2 if self.sizes(p)[1][1] else 1

    def start(self):
        for p in self.parts:
            for i in range(self.counts(p)):
                self.early(p, i).start()
            self.load(p).start()

    def start_later(self):
        for p in self.parts:
            rows, split = self.sizes(p)
            self.load(p).wait()
            for i in range(self.counts(p)):
                self.early(p, i).wait_recv()
                start = 0 if i == 0 else split[0]
                step = 16
                base = pl.multiple_of(self.owners[2 - i] * rows, rows) + start

                def body(t, carry, p=p, start=start, base=base, step=step):
                    here = pl.ds(pl.multiple_of(base + t * step, step), step)
                    there = pl.ds(pl.multiple_of(start + t * step, step), step)
                    value = p["buf"][here].astype(F32) + p["first"][there].astype(F32)
                    p["buf"][here] = value.astype(BF16)
                    return carry

                lax.fori_loop(0, split[i] // step, body, 0)
            for i in range(2):
                self.late(p, i).start()

    def finish(self):
        for p in self.parts:
            rows, _ = self.sizes(p)
            for i in range(2):
                self.late(p, i).wait()
            for i in range(self.counts(p)):
                self.early(p, i).wait_send()
            step = 16
            base = pl.multiple_of(self.dp * rows, rows)

            def body(t, carry, p=p, base=base, step=step):
                here = pl.ds(pl.multiple_of(base + t * step, step), step)
                there = pl.ds(pl.multiple_of(t * step, step), step)
                value = p["buf"][here].astype(F32) + p["second"][0, there].astype(F32)
                value = value + p["second"][1, there].astype(F32)
                p["out"][there] = value.astype(BF16)
                return carry

            lax.fori_loop(0, rows // step, body, 0)


def joint_reduce(partials, sums, after, collective_id, parts=4):
    groups, seqs = lax.axis_size("expert"), lax.axis_size("dp")
    chips = groups // 2
    rows, width = partials[0].shape[0] // groups, partials[0].shape[1]
    n, m, extra = len(partials), len(sums), len(after)

    def kernel(*refs):
        p_refs, s_refs = refs[:n], refs[n : n + m]
        refs = refs[n + m + extra :]
        o_refs, outs, rest = refs[:n], refs[n : n + m], refs[n + m :]
        names = ("buf", "first", "second", "load", "send", "recv")
        made = [
            dict(zip(names, rest[len(names) * i : len(names) * (i + 1)]), ref=s_refs[i], out=outs[i])
            for i in range(m)
        ]
        joint_body(groups, rows, parts, PlaneSum(made), p_refs, o_refs, *rest[len(names) * m :])

    anywhere, vmem = pl.BlockSpec(memory_space=pl.ANY), pl.BlockSpec(memory_space=pltpu.VMEM)
    dma = pltpu.SemaphoreType.DMA
    scratch = []
    for s in sums:
        own_rows = s.shape[0] // seqs
        scratch += [
            pltpu.VMEM(s.shape, BF16), pltpu.VMEM((own_rows,) + s.shape[1:], BF16),
            pltpu.VMEM((2, own_rows) + s.shape[1:], BF16), dma, dma((4,)), dma((4,)),
        ]
    return pl.pallas_call(
        kernel,
        out_shape=[jax.ShapeDtypeStruct((rows, width), F32)] * n
        + [jax.ShapeDtypeStruct((s.shape[0] // seqs,) + s.shape[1:], BF16) for s in sums],
        in_specs=[anywhere] * (n + m + extra),
        out_specs=[vmem] * (n + m),
        scratch_shapes=scratch + [
            pltpu.VMEM((n, chips, rows, width), BF16),
            pltpu.VMEM((n, chips, rows, width), BF16),
            pltpu.VMEM((n, 2 * chips, rows, width), BF16),
            dma((n, chips)), dma((n, chips)), dma((n, chips)),
            dma((n, chips, parts)), dma((n, 2 * chips, parts)),
        ],
        compiler_params=pltpu.CompilerParams(
            collective_id=collective_id, has_side_effects=True, vmem_limit_bytes=VMEM_LIMIT
        ),
        cost_estimate=cost_of(70),
        name="joint_reduce",
    )(*partials, *sums, *after)


def last_body(
    groups, seqs, small_ref, qkv_ref, out_ref, small_to, q_to, k_to, v_to, o_to,
    box, qkv_box, out_box, send, recv, qkv_send, qkv_recv, out_sem,
):
    me, dp = lax.axis_index("expert"), lax.axis_index("dp")
    total = groups * seqs
    mine = dp * groups + me
    block, width = o_to.shape
    own = width // groups
    barrier = pltpu.get_barrier_semaphore()

    def device(index):
        return (index // groups, index % groups)

    def hello(s, carry):
        pl.semaphore_signal(
            barrier, inc=1, device_id=device((mine + s) % total), device_id_type=MESH
        )
        return carry

    lax.fori_loop(1, total, hello, 0)
    pl.semaphore_wait(barrier, total - 1)

    def qkv_copy(s):
        peer = (me + s) % groups
        return pltpu.make_async_remote_copy(
            src_ref=qkv_ref.at[pl.ds(pl.multiple_of(peer * block, block), block)],
            dst_ref=qkv_box.at[me],
            send_sem=qkv_send.at[s], recv_sem=qkv_recv.at[s],
            device_id=(dp, peer), device_id_type=MESH,
        )

    def small_copy(s):
        target = (mine + s) % total
        return pltpu.make_async_remote_copy(
            src_ref=small_ref.at[target], dst_ref=box.at[mine],
            send_sem=send.at[s], recv_sem=recv.at[s],
            device_id=device(target), device_id_type=MESH,
        )

    owner = me * seqs + dp
    out_copy = pltpu.make_async_remote_copy(
        src_ref=out_ref, dst_ref=out_box, send_sem=out_sem.at[0], recv_sem=out_sem.at[1],
        device_id=device(owner), device_id_type=MESH,
    )

    def start(s, carry):
        small_copy(s).start()
        return carry

    def wait(s, carry):
        small_copy(s).wait()
        return carry

    lax.fori_loop(1, total, start, 0)
    for s in range(1, groups):
        qkv_copy(s).start()

    @pl.when(owner != mine)
    def _():
        out_copy.start()

    box[mine] = small_ref[mine]
    qkv_box[me] = qkv_ref[pl.ds(pl.multiple_of(me * block, block), block)]
    lax.fori_loop(1, total, wait, 0)

    def add(s, value):
        return value + box[s]

    small_to[...] = lax.fori_loop(1, total, add, box[0])

    @pl.when(owner != mine)
    def _():
        out_copy.wait()
        o_to[...] = out_box[...].astype(F32)

    @pl.when(owner == mine)
    def _():
        o_to[...] = out_ref[...].astype(F32)

    for s in range(1, groups):
        qkv_copy(s).wait()
    for e in range(groups):
        for m, to in enumerate((q_to, k_to, v_to)):
            to[:, e * own : (e + 1) * own] = qkv_box[e, :, m * own : (m + 1) * own].astype(F32)


def last_exchange(small, qkv, out, after, collective_id):
    groups, seqs = lax.axis_size("expert"), lax.axis_size("dp")
    total = groups * seqs
    block, width = out.shape
    vmem = pl.BlockSpec(memory_space=pltpu.VMEM)
    dma = pltpu.SemaphoreType.DMA
    matrix = jax.ShapeDtypeStruct((block, width), F32)
    held = len(after)

    def kernel(*refs):
        last_body(groups, seqs, *refs[:3], *refs[3 + held :])

    return pl.pallas_call(
        kernel,
        out_shape=[jax.ShapeDtypeStruct(small.shape[1:], F32)] + [matrix] * 4,
        in_specs=[vmem] * 3 + [pl.BlockSpec(memory_space=pl.ANY)] * held,
        out_specs=[vmem] * 5,
        scratch_shapes=[
            pltpu.VMEM(small.shape, F32),
            pltpu.VMEM((groups, block, qkv.shape[1]), BF16),
            pltpu.VMEM((block, width), BF16),
            dma((total,)), dma((total,)), dma((groups,)), dma((groups,)), dma((2,)),
        ],
        compiler_params=pltpu.CompilerParams(
            collective_id=collective_id, has_side_effects=True, vmem_limit_bytes=VMEM_LIMIT
        ),
        cost_estimate=cost_of(25),
        name="last_exchange",
    )(small, qkv, out, *after)


def exchange_body(count, spread, same, reduce, plane, x_ref, o_ref, box, send, recv):
    me, dp = lax.axis_index("expert"), lax.axis_index("dp")
    groups = lax.axis_size("expert")
    mine = dp * groups + me if spread else me

    def device(index):
        return (index // groups, index % groups) if spread else (dp, index)

    barrier = pltpu.get_barrier_semaphore()

    def hello(s, carry):
        pl.semaphore_signal(
            barrier, inc=1, device_id=device((mine + s) % count), device_id_type=MESH
        )
        return carry

    lax.fori_loop(1, count, hello, 0)
    plane.greet(barrier)
    pl.semaphore_wait(barrier, count - 1 + (2 if plane.busy() else 0))

    def copy(s):
        target = (mine + s) % count
        return pltpu.make_async_remote_copy(
            src_ref=x_ref.at[0] if same else x_ref.at[target],
            dst_ref=box.at[mine],
            send_sem=send.at[s],
            recv_sem=recv.at[s],
            device_id=device(target),
            device_id_type=MESH,
        )

    def start(s, carry):
        copy(s).start()
        return carry

    def wait(s, carry):
        copy(s).wait()
        return carry

    lax.fori_loop(1, count, start, 0)
    plane.start()
    box[mine] = x_ref[0] if same else x_ref[mine]
    lax.fori_loop(1, count, wait, 0)
    if reduce:

        def add(s, total):
            return total + box[s]

        o_ref[...] = lax.fori_loop(1, count, add, box[0])
    else:
        o_ref[...] = box[...]
    plane.start_later()
    plane.finish()


def run(
    body, name, micros, collective_id, x, x_space, out, out_space, scratch, sends, later,
    carry=(), after=(), wholes=(),
):
    arrays, specs = [], []
    for array, start, size, flip in sends:
        found = [i for i, a in enumerate(arrays) if a is array]
        if not found:
            arrays.append(array)
            found = [len(arrays) - 1]
        specs.append((found[0], start, size, flip))
    targets = [jax.ShapeDtypeStruct((s[2],) + s[0].shape[1:], s[0].dtype) for s in sends]
    for source, start, size, flip in later:
        targets.append(jax.ShapeDtypeStruct((size,) + targets[source].shape[1:], targets[source].dtype))
    seqs = lax.axis_size("dp")
    whole_out = [jax.ShapeDtypeStruct((seqs * w.shape[0],) + w.shape[1:], w.dtype) for w in wholes]
    n_in, n_out, held, n_whole = len(arrays), len(targets), len(carry), len(wholes)

    def kernel(*refs):
        x_ref, sources, whole_in = refs[0], refs[1 : 1 + n_in], refs[1 + n_in : 1 + n_in + n_whole]
        refs = refs[1 + n_in + n_whole + held + len(after) :]
        o_ref, dests, whole_to = refs[0], refs[1 : 1 + n_out], refs[1 + n_out : 1 + n_out + n_whole]
        rest = refs[1 + n_out + n_whole + held :]
        made = [
            Whole(a, b, rest[2].at[i], rest[3].at[i], rest[4].at[i])
            for i, (a, b) in enumerate(zip(whole_in, whole_to))
        ]
        plane = Plane(specs, later, sources, dests, *rest[:2], made)
        body(plane, x_ref, o_ref, *rest[5 if n_whole else 2 :])

    anywhere = pl.BlockSpec(memory_space=pl.ANY)
    dma = pltpu.SemaphoreType.DMA
    first, second = 1 + n_in + n_whole, 1 + n_out + n_whole
    got = pl.pallas_call(
        kernel,
        out_shape=[out] + targets + whole_out + [jax.ShapeDtypeStruct(c.shape, c.dtype) for c in carry],
        in_specs=[pl.BlockSpec(memory_space=x_space)] + [anywhere] * (n_in + n_whole + held + len(after)),
        out_specs=[pl.BlockSpec(memory_space=out_space)] + [anywhere] * (n_out + n_whole + held),
        input_output_aliases={first + i: second + i for i in range(held)},
        scratch_shapes=[dma((max(n_out, 1),))] * 2
        + ([dma((n_whole,)), dma((n_whole, 4)), dma((n_whole, 4))] if n_whole else [])
        + scratch,
        compiler_params=pltpu.CompilerParams(
            collective_id=collective_id, has_side_effects=True, vmem_limit_bytes=VMEM_LIMIT
        ),
        cost_estimate=cost_of(micros),
        name=name,
    )(x, *arrays, *wholes, *carry, *after)
    return got if n_out + n_whole + held else got[0]


def line_gather(x, collective_id, sends=(), later=(), carry=(), after=(), wholes=(), parts=4):
    rows, width = x.shape
    groups = lax.axis_size("expert")
    shape = (2, groups // 2, parts)
    return run(
        functools.partial(gather_body, groups, rows, parts), "line_gather", 40, collective_id,
        x, pl.ANY, jax.ShapeDtypeStruct((groups * rows, width), x.dtype), pl.ANY,
        [pltpu.SemaphoreType.DMA] + [pltpu.SemaphoreType.DMA(shape)] * 4,
        sends, later, carry, after, wholes,
    )


def line_reduce(partial, collective_id, sends=(), later=(), after=(), parts=4):
    groups = lax.axis_size("expert")
    chips = groups // 2
    rows, width = partial.shape[0] // groups, partial.shape[1]
    return run(
        functools.partial(reduce_body, groups, rows, parts), "line_reduce", 40, collective_id,
        partial.astype(BF16), pl.ANY, jax.ShapeDtypeStruct((rows, width), F32), pltpu.VMEM,
        [
            pltpu.VMEM((chips, rows, width), BF16),
            pltpu.VMEM((chips, rows, width), BF16),
            pltpu.VMEM((2 * chips, rows, width), BF16),
            pltpu.SemaphoreType.DMA((chips,)),
            pltpu.SemaphoreType.DMA((chips,)),
            pltpu.SemaphoreType.DMA((chips,)),
            pltpu.SemaphoreType.DMA((chips, parts)),
            pltpu.SemaphoreType.DMA((2 * chips, parts)),
        ],
        sends, later, (), after,
    )


def exchange(
    x, collective_id, spread=False, same=False, reduce=False, sends=(), later=(), carry=()
):
    count = lax.axis_size("expert") * (lax.axis_size("dp") if spread else 1)
    block = x.shape[1:]
    return run(
        functools.partial(exchange_body, count, spread, same, reduce), "exchange", 8, collective_id,
        x, pltpu.VMEM, jax.ShapeDtypeStruct(block if reduce else (count,) + block, x.dtype), pltpu.VMEM,
        [
            pltpu.VMEM((count,) + block, x.dtype),
            pltpu.SemaphoreType.DMA((count,)),
            pltpu.SemaphoreType.DMA((count,)),
        ],
        sends, later, carry,
    )


LANES = 128
TILE = 512


def expert_first_body(
    groups, seqs, rows, width, ff, experts, parts,
    x_ref, g_ref, gate_ref, up_ref, down_ref, near_refs,
    f_out, hid_out, sg_out, su_out, tail_out, down_out, grad_out,
    f_buf, g_buf, wg, wu, wd, hid, sg, su, tail_buf, tail_sum, stage,
    line_send, line_recv, side_send, side_recv, own_sem, f_sem, w_sem, d_sem, g_sem, out_sem, tail_sem,
    plane_send, plane_recv, stage_sem,
):
    chips = groups // 2
    me, dp = lax.axis_index("expert"), lax.axis_index("dp")
    chip, core = me // 2, me % 2
    sibling = chip * 2 + 1 - core
    chunk = 2 * rows
    part = rows // parts
    depth, wide_ff = width // seqs, ff // seqs

    def remote(src, dst, send_sem, recv_sem, device):
        return pltpu.make_async_remote_copy(
            src_ref=src, dst_ref=dst, send_sem=send_sem, recv_sem=recv_sem,
            device_id=device, device_id_type=MESH,
        )

    def at(index, size):
        return pl.ds(pl.multiple_of(index * size, size), size)

    def neighbour(flip):
        return (flipped(dp, flip), me)

    barrier = pltpu.get_barrier_semaphore()
    pl.semaphore_signal(barrier, inc=1, device_id=(dp, sibling), device_id_type=MESH)
    for flip in (1, 2):
        pl.semaphore_signal(barrier, inc=1, device_id=neighbour(flip), device_id_type=MESH)

    @pl.when(chip > 0)
    def _():
        pl.semaphore_signal(barrier, inc=1, device_id=(dp, me - 2), device_id_type=MESH)

    @pl.when(chip < chips - 1)
    def _():
        pl.semaphore_signal(barrier, inc=1, device_id=(dp, me + 2), device_id_type=MESH)

    @pl.when((chip > 0) & (chip < chips - 1))
    def _():
        pl.semaphore_wait(barrier, 5)

    @pl.when((chip == 0) | (chip == chips - 1))
    def _():
        pl.semaphore_wait(barrier, 4)

    def row_copy(origin, u, target, send_sem, recv_sem, first):
        place = pl.ds(pl.multiple_of(origin * rows + u * part, part), part)
        return remote(
            x_ref.at[pl.ds(u * part, part)] if first else f_buf.at[place], f_buf.at[place],
            send_sem, recv_sem, (dp, target),
        )

    def step(side, k, u):
        origin, target = (me - 2 * k, me + 2) if side == 0 else (me + 2 * k, me - 2)
        return row_copy(origin, u, target, line_send.at[side, k, u], line_recv.at[side, k, u], k == 0)

    def aside(side, k, u):
        origin = me - 2 * k if side == 0 else me + 2 * k
        return row_copy(origin, u, sibling, side_send.at[side, k, u], side_recv.at[side, k, u], k == 0)

    def sides(k):
        return (
            (0, chip - k >= 0, chip < chips - 1),
            (1, chip + k <= chips - 1, chip > 0),
        )

    keep = pltpu.make_async_copy(x_ref, f_buf.at[at(me, rows)], own_sem)

    def rows_out(c):
        return pltpu.make_async_copy(
            f_buf.at[at(c, chunk), pl.ds(0, width)], f_out.at[at(c, chunk)], f_sem.at[c]
        )

    def plane_copy(i):
        e, flip = (i // 2, i % 2 + 1) if i < 4 else (i - 4, i - 3)
        if i < 4:
            src, dst = down_ref.at[e], wd.at[e, at(dp, wide_ff)]
        else:
            src = wd.at[e, at(flipped(dp, 3 - flip), wide_ff)]
            dst = src
        return remote(src, dst, plane_send.at[i], plane_recv.at[i], neighbour(flip))

    owners = (dp, flipped(dp, 1), flipped(dp, 2), flipped(flipped(dp, 1), 2))

    def weight_copies():
        copies = []
        for m, (own, buf) in enumerate(((gate_ref, wg), (up_ref, wu))):
            for e in range(experts):
                near = [near_refs[6 * m + 2 * q + e] for q in range(3)]
                pieces = [own.at[e]] + [ref.at[index] for ref, index in near]
                for q, piece in enumerate(pieces):
                    copies.append(
                        pltpu.make_async_copy(
                            piece, buf.at[at(owners[q], depth), pl.ds(e * ff, ff)],
                            w_sem.at[m, e, q],
                        )
                    )
        return copies

    def down_copies():
        return [
            pltpu.make_async_copy(down_ref.at[e], wd.at[e, at(dp, wide_ff)], d_sem.at[e])
            for e in range(experts)
        ]

    grad_rows = [
        pltpu.make_async_copy(
            g_ref.at[pl.ds(r * chunk, chunk)], g_buf.at[pl.ds(r * chunk, chunk)], g_sem.at[r]
        )
        for r in range(chips)
    ]

    def first_layer(c):
        place = at(c, chunk)

        def tile(t, carry):
            cols = at(t, TILE)
            gate = dot(f_buf[place, pl.ds(0, width)], wg[:, cols])
            up = dot(f_buf[place, pl.ds(0, width)], wu[:, cols])
            sig = 1.0 / (1.0 + jnp.exp(-gate))
            silu = gate * sig
            hid[place, cols] = (silu * up).astype(BF16)
            sg[place, cols] = (up * sig * (1.0 + gate * (1.0 - sig))).astype(BF16)
            su[place, cols] = silu.astype(BF16)
            return carry

        lax.fori_loop(0, experts * ff // TILE, tile, 0)

    def ready(k):
        for u in range(parts):
            if k == 0:
                aside(0, 0, u).wait_recv()
            else:
                for side, has, _ in sides(k):

                    @pl.when(has)
                    def _(side=side, u=u):
                        aside(side, k, u).wait_recv()

        if k == 0:
            rows_out(chip).start()
            first_layer(chip)
        else:
            for side, has, _ in sides(k):
                c = chip - k if side == 0 else chip + k

                @pl.when(has)
                def _(c=c):
                    rows_out(c).start()
                    first_layer(c)

    for k in range(chips):
        for u in range(parts):
            for side, has, send_on in sides(k):

                @pl.when(has)
                def _(k=k, u=u, side=side, send_on=send_on):
                    if k > 0:
                        step(side, k - 1, u).wait_recv()
                    if k < chips - 1:

                        @pl.when(send_on)
                        def _():
                            step(side, k, u).start()

                    if k > 0:
                        aside(side, k, u).start()

            if k == 0:
                aside(0, 0, u).start()
        if k == 0:
            for i in range(4):
                plane_copy(i).start()
            keep.start()
            for copy in weight_copies():
                copy.start()
            for copy in down_copies():
                copy.start()
            for copy in grad_rows:
                copy.start()
            keep.wait()
            for copy in weight_copies():
                copy.wait()
        if k > 0:
            ready(k - 1)
    plane_copy(1).wait_recv()
    plane_copy(4).start()
    plane_copy(2).wait_recv()
    plane_copy(5).start()
    ready(chips - 1)

    for copy in down_copies():
        copy.wait()
    for i in (0, 3):
        plane_copy(i).wait_recv()

    def outs(r):
        place = pl.ds(r * chunk, chunk)
        return [
            pltpu.make_async_copy(buf.at[place], out.at[place], out_sem.at[i, r])
            for i, (buf, out) in enumerate(((hid, hid_out), (sg, sg_out), (su, su_out)))
        ]

    lane = lax.broadcasted_iota(jnp.int32, (chunk, LANES), 1)

    def back(r, first, last):
        place = pl.ds(r * chunk, chunk)
        extra = f_buf[place, pl.ds(width, LANES)].astype(F32)
        tail = jnp.zeros((chunk, LANES), F32) if first == 0 else tail_sum[place, :]
        for e in range(experts):
            which = me * experts + e
            low = which + LANES // 2
            weight = jnp.sum(
                jnp.where((lane == which) | (lane == low), extra, 0.0), axis=1, keepdims=True
            )
            for owner in owners[first:last]:
                d_hid = dot_nt(g_buf[place, :], wd[e, at(owner, wide_ff), :])
                cols = pl.ds(pl.multiple_of(e * ff + owner * wide_ff, wide_ff), wide_ff)
                hidden = hid[place, cols].astype(F32)
                d_weight = jnp.sum(hidden * d_hid, axis=1, keepdims=True)
                tail = tail + jnp.where(lane == which, d_weight, 0.0)
                d_hid = d_hid * weight
                hid[place, cols] = (hidden * weight).astype(BF16)
                sg[place, cols] = (d_hid * sg[place, cols].astype(F32)).astype(BF16)
                su[place, cols] = (d_hid * su[place, cols].astype(F32)).astype(BF16)
        if last < len(owners):
            tail_sum[place, :] = tail
        else:
            high = tail.astype(BF16).astype(F32)
            tail_buf[place, :] = (high + pltpu.roll(tail - high, LANES // 2, 1)).astype(BF16)

    tiles = [(e, q) for q in range(len(owners)) for e in range(experts)]

    def grad_place(t):
        e, q = tiles[t]
        return pl.ds(pl.multiple_of(e * ff + owners[q] * wide_ff, wide_ff), wide_ff)

    def grad_copy(t):
        return pltpu.make_async_copy(stage.at[t % 2], grad_out.at[grad_place(t)], stage_sem.at[t % 2])

    def grad_tile(t):
        if t >= 2:
            grad_copy(t - 2).wait()
        for n in range(width // (2 * TILE)):
            cols = pl.ds(n * 2 * TILE, 2 * TILE)
            stage[t % 2, :, cols] = dot_tn(hid[:, grad_place(t)], g_buf[:, cols]).astype(BF16)
        grad_copy(t).start()

    for copy in grad_rows:
        copy.wait()
    for r in range(chips):
        back(r, 0, 3)
    for t in range(3 * experts):
        grad_tile(t)
    for i in (4, 5):
        plane_copy(i).wait_recv()
    keep_down = pltpu.make_async_copy(wd, down_out, d_sem.at[experts])
    keep_down.start()
    for r in range(chips):
        back(r, 3, 4)
        for copy in outs(r):
            copy.start()
    for t in range(3 * experts, 4 * experts):
        grad_tile(t)
    for t in range(4 * experts - 2, 4 * experts):
        grad_copy(t).wait()
    keep_tail = pltpu.make_async_copy(tail_buf, tail_out, tail_sem)
    keep_tail.start()
    keep_tail.wait()
    keep_down.wait()
    for k in range(chips):
        for u in range(parts):
            if k == 0:
                aside(0, 0, u).wait_send()
            for side, has, send_on in sides(k):

                @pl.when(has)
                def _(k=k, u=u, side=side, send_on=send_on):
                    if k < chips - 1:

                        @pl.when(send_on)
                        def _():
                            step(side, k, u).wait_send()

                    if k > 0:
                        aside(side, k, u).wait_send()

    for i in range(6):
        plane_copy(i).wait_send()
    for d in range(chips):
        rows_out(d).wait()
        for copy in outs(d):
            copy.wait()


def expert_first(x, g_all, w_gate, w_up, w_down, near, collective_id, parts=4):
    groups, seqs = lax.axis_size("expert"), lax.axis_size("dp")
    chips = groups // 2
    rows, wide = x.shape
    length, width = g_all.shape
    experts, _, ff = w_gate.shape
    where = [index for _, index in near]
    near = [array for array, _ in near]
    n = len(near)

    def kernel(*refs):
        expert_first_body(
            groups, seqs, rows, width, ff, experts, parts, *refs[:5],
            list(zip(refs[5 : 5 + n], where)), *refs[5 + n :],
        )

    anywhere = pl.BlockSpec(memory_space=pl.ANY)
    dma = pltpu.SemaphoreType.DMA
    flat = jax.ShapeDtypeStruct((length, experts * ff), BF16)
    return pl.pallas_call(
        kernel,
        out_shape=[
            jax.ShapeDtypeStruct((length, width), BF16), flat, flat, flat,
            jax.ShapeDtypeStruct((length, LANES), BF16),
            jax.ShapeDtypeStruct((experts, ff, width), BF16),
            jax.ShapeDtypeStruct((experts * ff, width), BF16),
        ],
        in_specs=[anywhere] * (5 + n),
        out_specs=[anywhere] * 7,
        scratch_shapes=[
            pltpu.VMEM((length, wide), BF16),
            pltpu.VMEM((length, width), BF16),
            pltpu.VMEM((width, experts * ff), BF16),
            pltpu.VMEM((width, experts * ff), BF16),
            pltpu.VMEM((experts, ff, width), BF16),
            pltpu.VMEM((length, experts * ff), BF16),
            pltpu.VMEM((length, experts * ff), BF16),
            pltpu.VMEM((length, experts * ff), BF16),
            pltpu.VMEM((length, LANES), BF16),
            pltpu.VMEM((length, LANES), F32),
            pltpu.VMEM((2, ff // seqs, width), BF16),
            dma((2, chips, parts)), dma((2, chips, parts)), dma((2, chips, parts)), dma((2, chips, parts)),
            dma, dma((chips,)), dma((2, experts, 4)), dma((experts + 1,)), dma((chips,)), dma((3, chips)), dma,
            dma((6,)), dma((6,)), dma((2,)),
        ],
        compiler_params=pltpu.CompilerParams(
            collective_id=collective_id, has_side_effects=True, vmem_limit_bytes=VMEM_LIMIT
        ),
        cost_estimate=cost_of(70),
        name="expert_first",
    )(x, g_all, w_gate, w_up, w_down, *near)


class Blocks:
    def __init__(self, ref, size, half_stride, owner_stride):
        self.me, self.dp = lax.axis_index("expert"), lax.axis_index("dp")
        self.ref, self.size = ref, size
        self.half_stride, self.owner_stride = half_stride, owner_stride
        x, y = flipped(self.dp, 1), flipped(self.dp, 2)
        self.owners = (self.dp, x, y, flipped(x, 2))

    def piece(self, half, q):
        start = half * self.half_stride + self.owners[q] * self.owner_stride
        return self.ref.at[pl.ds(pl.multiple_of(start, self.size), self.size)]

    def remote(self, src, dst, send, recv, flip):
        return pltpu.make_async_remote_copy(
            src_ref=src, dst_ref=dst, send_sem=send, recv_sem=recv,
            device_id=(flipped(self.dp, flip), self.me), device_id_type=MESH,
        )


class SumEarly:
    def __init__(self, blocks, first, mid, near_out, mid_out, load, send, recv):
        self.me, self.dp = blocks.me, blocks.dp
        self.blocks, self.first, self.mid = blocks, first, mid
        self.near_out, self.mid_out = near_out, mid_out
        self.load_sem, self.send, self.recv = load, send, recv

    def busy(self):
        return True

    greet = Plane.greet

    def copy(self, i):
        b = self.blocks
        src, dst = (
            (b.piece(0, 3), self.first.at[0]),
            (b.piece(1, 3), self.first.at[1]),
            (b.piece(0, 1), self.near_out.at[0]),
            (b.piece(1, 2), self.near_out.at[1]),
        )[i]
        return b.remote(src, dst, self.send.at[i], self.recv.at[i], i % 2 + 1)

    def loads(self):
        b = self.blocks
        return [
            pltpu.make_async_copy(b.piece(0, 2), self.mid.at[0], self.load_sem.at[0]),
            pltpu.make_async_copy(b.piece(1, 1), self.mid.at[1], self.load_sem.at[1]),
        ]

    def keep(self):
        return pltpu.make_async_copy(self.mid, self.mid_out, self.load_sem.at[2])

    def start(self):
        for i in range(4):
            self.copy(i).start()
        for copy in self.loads():
            copy.start()

    def start_later(self):
        for copy in self.loads():
            copy.wait()
        for i in range(2):
            self.copy(i).wait_recv()

            def body(t, carry, i=i):
                here = pl.ds(pl.multiple_of(t * 16, 16), 16)
                value = self.mid[i, here].astype(F32) + self.first[i, here].astype(F32)
                self.mid[i, here] = value.astype(BF16)
                return carry

            lax.fori_loop(0, self.blocks.size // 16, body, 0)
        self.keep().start()

    def finish(self):
        for i in range(4):
            if i >= 2:
                self.copy(i).wait_recv()
            self.copy(i).wait_send()
        self.keep().wait()


class SumLate:
    def __init__(self, blocks, mid_ref, near_ref, late, near, own, out, load, send, recv):
        self.blocks, self.mid_ref, self.near_ref = blocks, mid_ref, near_ref
        self.late, self.near, self.own, self.out = late, near, own, out
        self.load_sem, self.send, self.recv = load, send, recv

    def copy(self, i):
        return self.blocks.remote(
            self.mid_ref.at[1 - i], self.late.at[1 - i], self.send.at[i], self.recv.at[i], i + 1
        )

    def loads(self):
        b = self.blocks
        return [
            pltpu.make_async_copy(b.piece(0, 0), self.own.at[0], self.load_sem.at[0]),
            pltpu.make_async_copy(b.piece(1, 0), self.own.at[1], self.load_sem.at[1]),
            pltpu.make_async_copy(self.near_ref, self.near, self.load_sem.at[2]),
        ]

    def start(self):
        for i in range(2):
            self.copy(i).start()
        for copy in self.loads():
            copy.start()

    def start_later(self):
        pass

    def finish(self):
        for copy in self.loads():
            copy.wait()
        for i in range(2):
            self.copy(i).wait()
        for half in range(2):

            def body(t, carry, half=half):
                here = pl.ds(pl.multiple_of(t * 16, 16), 16)
                value = self.own[half, here].astype(F32) + self.near[half, here].astype(F32)
                value = value + self.late[half, here].astype(F32)
                self.out[half, here] = value.astype(BF16)
                return carry

            lax.fori_loop(0, self.blocks.size // 16, body, 0)


class Several:
    def __init__(self, parts):
        self.me, self.dp = lax.axis_index("expert"), lax.axis_index("dp")
        self.parts = parts

    def busy(self):
        return True

    greet = Plane.greet

    def start(self):
        for part in self.parts:
            part.start()

    def start_later(self):
        for part in self.parts:
            part.start_later()

    def finish(self):
        for part in self.parts:
            part.finish()


def expert_second_body(
    groups, seqs, rows, width, ff, experts, parts,
    sg_ref, su_ref, tail_ref, f_ref, gate_ref, up_ref, down_ref, near_refs, grad_out, near_out, mid_out, o_ref,
    wg, wu, sg, su, tail_buf, f_buf, stage, acc, pair_in, inbox, last,
    first, mid,
    in_sem, w_sem, stage_sem, pair_send, pair_recv, hop_send, hop_recv, last_recv,
    sum_load, sum_send, sum_recv,
):
    chips = groups // 2
    me, dp = lax.axis_index("expert"), lax.axis_index("dp")
    chip, core = me // 2, me % 2
    sibling = chip * 2 + 1 - core
    chunk = 2 * rows
    part = rows // parts
    depth = width // seqs

    def remote(src, dst, send_sem, recv_sem, device):
        return pltpu.make_async_remote_copy(
            src_ref=src, dst_ref=dst, send_sem=send_sem, recv_sem=recv_sem,
            device_id=device, device_id_type=MESH,
        )

    def at(index, size):
        return pl.ds(pl.multiple_of(index * size, size), size)

    owners = (dp, flipped(dp, 1), flipped(dp, 2), flipped(flipped(dp, 1), 2))
    loads = [
        pltpu.make_async_copy(src, dst, in_sem.at[i])
        for i, (src, dst) in enumerate(
            ((sg_ref, sg), (su_ref, su), (tail_ref, tail_buf), (f_ref, f_buf))
        )
    ]
    weights = []
    for m, (own, buf) in enumerate(((gate_ref, wg), (up_ref, wu))):
        for e in range(experts):
            near = [near_refs[6 * m + 2 * q + e] for q in range(3)]
            pieces = [own.at[e]] + [ref.at[index] for ref, index in near]
            for q, piece in enumerate(pieces):
                weights.append(
                    pltpu.make_async_copy(
                        piece, buf.at[at(owners[q], depth), pl.ds(e * ff, ff)], w_sem.at[m, e, q]
                    )
                )
    for copy in loads[:3] + weights + loads[3:]:
        copy.start()
    blocks = Blocks(down_ref, ff // seqs, ff, ff // seqs)
    total = SumEarly(blocks, first, mid, near_out, mid_out, sum_load, sum_send, sum_recv)
    line_greet(me, dp, chip, chips, total)
    total.start()
    for copy in loads[:3]:
        copy.wait()
    for r in range(chips):
        for half in range(2):
            acc[r, half, :, pl.ds(width, LANES)] = tail_buf[pl.ds(r * chunk + half * rows, rows), :]

    out_tile = 256

    def row_grads(d, first=False):
        place = at(d, chunk)
        per = depth // out_tile

        def tile(t, carry):
            cols = at(t, out_tile)
            value = dot_nt(sg[place, :], wg[cols, :]) + dot_nt(su[place, :], wu[cols, :])
            value = value.astype(BF16)
            acc[d, 0, :, cols] = value[:rows]
            acc[d, 1, :, cols] = value[rows:]
            return carry

        if not first:
            lax.fori_loop(0, width // out_tile, tile, 0)
            return
        for q, owner in enumerate(owners):
            for copy in weights[q :: len(owners)]:
                copy.wait()
            lax.fori_loop(owner * per, owner * per + per, tile, 0)

    def pair_copy(d):
        return remote(acc.at[d, 1 - core], pair_in.at[d], pair_send.at[d], pair_recv.at[d], (dp, sibling))

    def hop(d, u, kind):
        place = pl.ds(u * part, part)
        if kind == 0:
            return remote(
                acc.at[d, core, place], inbox.at[d, place], hop_send.at[d, u], hop_recv.at[d, u],
                (dp, me + 2),
            )
        if kind == 1:
            return remote(
                acc.at[d, core, place], inbox.at[d, place], hop_send.at[d, u], hop_recv.at[d, u],
                (dp, me - 2),
            )
        return remote(
            acc.at[d, core, place], last.at[place], hop_send.at[d, u], last_recv.at[u], (dp, me - 2)
        )

    step_rows = 16

    def add(d, u, more, store):
        def body(i, carry):
            here = pl.ds(pl.multiple_of(u * part + i * step_rows, step_rows), step_rows)
            value = acc[d, core, here].astype(F32) + pair_in[d, here].astype(F32)
            for ref in more:
                value = value + ref[here].astype(F32)
            store(here, value)
            return carry

        lax.fori_loop(0, part // step_rows, body, 0)

    def forward(d):
        pair_copy(d).wait_recv()

        def store(here, value):
            acc[d, core, here] = value.astype(BF16)

        source = ((d > chip) & (chip == 0)) | ((d < chip) & (chip == chips - 1))
        for u in range(parts):

            @pl.when(source)
            def _(u=u):
                add(d, u, (), store)

            @pl.when(jnp.logical_not(source))
            def _(u=u):
                hop(d, u, 0).wait_recv()
                add(d, u, (inbox.at[d],), store)

            @pl.when(d > chip)
            def _(u=u):
                hop(d, u, 0).start()

            @pl.when((d < chip) & (d != chip - 1))
            def _(u=u):
                hop(d, u, 1).start()

            @pl.when((d < chip) & (d == chip - 1))
            def _(u=u):
                hop(d, u, 2).start()

    upper = chip // (chips // 2)
    mirrored = chip + upper * (chips - 1 - 2 * chip)

    def goal(j):
        turn = (j + mirrored) // (chips - 1)
        d = (1 - turn) * (chips - 1 - j) + turn * (j + mirrored - (chips - 1))
        return d + upper * (chips - 1 - 2 * d)

    edge = (chip == 0) | (chip == chips - 1)

    def grad_copy(t):
        return pltpu.make_async_copy(
            stage.at[t % 2], grad_out.at[pl.ds(t * out_tile, out_tile)], stage_sem.at[t % 2]
        )

    def grad_tile(t):
        if t >= 2:
            grad_copy(t - 2).wait()
        for n in range(experts * ff // (2 * TILE)):
            cols = pl.ds(n * 2 * TILE, 2 * TILE)
            stage[t % 2, :, cols] = dot_tn(
                f_buf[:, pl.ds(t * out_tile, out_tile)], sg[:, cols]
            ).astype(BF16)
        grad_copy(t).start()

    tiles = width // out_tile
    for j in range(chips):
        row_grads(goal(j), j == 0)
        pair_copy(goal(j)).start()
        if j > 0:

            @pl.when(edge)
            def _(j=j):
                forward(goal(j - 1))

    for copy in loads[3:]:
        copy.wait()
    for j in range(chips):
        if j < chips - 1:

            @pl.when(jnp.logical_not(edge))
            def _(j=j):
                forward(goal(j))

        if j == min(1, chips - 1):
            total.start_later()
        for t in range(j * tiles // chips, (j + 1) * tiles // chips):
            grad_tile(t)

    pair_copy(chip).wait_recv()

    def finish(here, value):
        o_ref[here] = value

    for u in range(parts):

        @pl.when(chip == 0)
        def _(u=u):
            hop(chip, u, 2).wait_recv()
            add(chip, u, (last,), finish)

        @pl.when(chip == chips - 1)
        def _(u=u):
            hop(chip, u, 0).wait_recv()
            add(chip, u, (inbox.at[chip],), finish)

        @pl.when((chip > 0) & (chip < chips - 1))
        def _(u=u):
            hop(chip, u, 0).wait_recv()
            hop(chip, u, 2).wait_recv()
            add(chip, u, (inbox.at[chip], last), finish)

    for d in range(chips):
        pair_copy(d).wait_send()
        for u in range(parts):

            @pl.when(d != chip)
            def _(d=d, u=u):
                hop(d, u, 0).wait_send()

    for t in range(tiles - 2, tiles):
        grad_copy(t).wait()
    total.finish()


def expert_second(sg, su, tail, ffn_all, d_down, w_gate, w_up, near, collective_id, parts=4):
    groups, seqs = lax.axis_size("expert"), lax.axis_size("dp")
    chips = groups // 2
    length, width = ffn_all.shape
    rows = length // groups
    experts, _, ff = w_gate.shape
    wide = width + LANES
    size = ff // seqs
    where = [index for _, index in near]
    near = [array for array, _ in near]
    n = len(near)

    def kernel(*refs):
        expert_second_body(
            groups, seqs, rows, width, ff, experts, parts, *refs[:7], list(zip(refs[7 : 7 + n], where)),
            *refs[7 + n :],
        )

    anywhere = pl.BlockSpec(memory_space=pl.ANY)
    dma = pltpu.SemaphoreType.DMA
    flat = pltpu.VMEM((length, experts * ff), BF16)
    block = pltpu.VMEM((2, size, width), BF16)
    return pl.pallas_call(
        kernel,
        out_shape=[
            jax.ShapeDtypeStruct((width, experts * ff), BF16),
            jax.ShapeDtypeStruct((2, size, width), BF16),
            jax.ShapeDtypeStruct((2, size, width), BF16),
            jax.ShapeDtypeStruct((rows, wide), F32),
        ],
        in_specs=[anywhere] * (7 + n),
        out_specs=[anywhere] * 3 + [pl.BlockSpec(memory_space=pltpu.VMEM)],
        scratch_shapes=[
            pltpu.VMEM((width, experts * ff), BF16),
            pltpu.VMEM((width, experts * ff), BF16),
            flat, flat,
            pltpu.VMEM((length, LANES), BF16),
            pltpu.VMEM((length, width), BF16),
            pltpu.VMEM((2, 256, experts * ff), BF16),
            pltpu.VMEM((chips, 2, rows, wide), BF16),
            pltpu.VMEM((chips, rows, wide), BF16),
            pltpu.VMEM((chips, rows, wide), BF16),
            pltpu.VMEM((rows, wide), BF16),
            block, block,
            dma((4,)), dma((2, experts, 4)), dma((2,)), dma((chips,)), dma((chips,)),
            dma((chips, parts)), dma((chips, parts)), dma((parts,)),
            dma((3,)), dma((4,)), dma((4,)),
        ],
        compiler_params=pltpu.CompilerParams(
            collective_id=collective_id, has_side_effects=True, vmem_limit_bytes=60 * 1024 * 1024
        ),
        cost_estimate=cost_of(65),
        name="expert_second",
    )(sg, su, tail, ffn_all, w_gate, w_up, d_down, *near)


def gather_fill_body(
    groups, seqs, ff, rows, parts, x_ref, f_ref, su_ref, hid_ref, wd_ref, down_ref, mid_ref, near_ref,
    o_ref, grad_out, y_out, down_out,
    f_buf, su, hid, wd, stage, late, near, own_block, in_sem, stage_sem, sum_load, sum_send, sum_recv,
    own_sem, send, recv, pair_send, pair_recv,
):
    chips = groups // 2
    length, width = f_buf.shape
    hidden = su.shape[1]
    size = stage.shape[1]
    loads = [
        pltpu.make_async_copy(src, dst, in_sem.at[i])
        for i, (src, dst) in enumerate(((f_ref, f_buf), (su_ref, su), (hid_ref, hid), (wd_ref, wd)))
    ]
    for copy in loads:
        copy.start()
    grads, mixes = width // size, length // size
    total = grads + mixes

    def place(t):
        return pl.ds((t if t < grads else t - grads) * size, size)

    experts, per = hidden // ff, width // seqs // size

    def out_copies(t):
        if t >= grads:
            return [pltpu.make_async_copy(stage.at[t % 2], y_out.at[place(t)], stage_sem.at[t % 2, 0])]
        return [
            pltpu.make_async_copy(
                stage.at[t % 2, :, pl.ds(e * ff, ff)],
                grad_out.at[t // per, e, pl.ds(t % per * size, size)],
                stage_sem.at[t % 2, e],
            )
            for e in range(experts)
        ]

    def tile(t):
        if t == 0:
            loads[0].wait()
            loads[1].wait()
        if t == grads:
            loads[2].wait()
            loads[3].wait()
        if t >= 2:
            for copy in out_copies(t - 2):
                copy.wait()
        for n in range(hidden // (2 * TILE)):
            cols = pl.ds(n * 2 * TILE, 2 * TILE)
            if t < grads:
                value = dot_tn(f_buf[:, place(t)], su[:, cols])
            else:
                value = dot(hid[place(t), :], wd[:, cols])
            stage[t % 2, :, cols] = value.astype(BF16)
        for copy in out_copies(t):
            copy.start()

    turns = max(chips - 1, 1)
    rest = SumLate(
        Blocks(down_ref, ff // seqs, ff, ff // seqs), mid_ref, near_ref, late, near, own_block, down_out,
        sum_load, sum_send, sum_recv,
    )

    def work(k):
        if k < turns:
            for t in range(k * total // turns, (k + 1) * total // turns):
                tile(t)

    gather_body(
        groups, rows, parts, Several([rest]), x_ref, o_ref,
        own_sem, send, recv, pair_send, pair_recv, work=work,
    )
    for t in range(total - 2, total):
        for copy in out_copies(t):
            copy.wait()


def gather_fill(x, ffn_all, su, hid, wd, d_down, mid, near, ff, collective_id, parts=4):
    groups, seqs = lax.axis_size("expert"), lax.axis_size("dp")
    rows, width = x.shape
    length, hidden = su.shape
    anywhere, vmem = pl.BlockSpec(memory_space=pl.ANY), pl.BlockSpec(memory_space=pltpu.VMEM)
    dma = pltpu.SemaphoreType.DMA
    line = dma((2, groups // 2, parts))
    tokens = jax.ShapeDtypeStruct((length, width), BF16)
    return pl.pallas_call(
        functools.partial(gather_fill_body, groups, seqs, ff, rows, parts),
        out_shape=[
            tokens, jax.ShapeDtypeStruct((seqs, hidden // ff, width // seqs, ff), BF16), tokens,
            jax.ShapeDtypeStruct(mid.shape, BF16),
        ],
        in_specs=[anywhere] * 8,
        out_specs=[anywhere] * 3 + [vmem],
        scratch_shapes=[
            pltpu.VMEM((length, width), BF16),
            pltpu.VMEM((length, hidden), BF16),
            pltpu.VMEM((length, hidden), BF16),
            pltpu.VMEM((hidden, width), BF16),
            pltpu.VMEM((2, 256, max(hidden, width)), BF16),
            pltpu.VMEM(mid.shape, BF16),
            pltpu.VMEM(mid.shape, BF16),
            pltpu.VMEM(mid.shape, BF16),
            dma((4,)), dma((2, hidden // ff)), dma((3,)), dma((2,)), dma((2,)),
            dma, line, line, line, line,
        ],
        compiler_params=pltpu.CompilerParams(
            collective_id=collective_id, has_side_effects=True, vmem_limit_bytes=VMEM_LIMIT
        ),
        cost_estimate=cost_of(45),
        name="gather_fill",
    )(x, ffn_all, su, hid, wd, d_down, mid, near)


class Opening:
    def __init__(self, sends, arrived, wholes):
        self.sends, self.arrived, self.wholes = sends, arrived, wholes

    def start(self):
        pass

    def start_mid(self):
        self.arrived()
        for whole in self.wholes:
            whole.start()

    def start_later(self):
        for whole in self.wholes:
            whole.start_later()

    def finish(self):
        for whole in self.wholes:
            whole.finish()
        self.sends.finish()


def opening_body(
    groups, seqs, copies, slab, rows, parts, gate_refs, x_ref, small_ref, out_ref, q_ref, k_ref, v_ref, gate_ref,
    x_to, small_to, qkv_to, wo_to, out_to, spread_to,
    box, send, recv, out_sem, own_sem, qkv_send, qkv_recv, small_sem, plane_send, plane_recv,
    whole_own, whole_send, whole_recv, keep_sem, line_send, line_recv, pair_send, pair_recv,
):
    me, dp = lax.axis_index("expert"), lax.axis_index("dp")
    total = groups * seqs
    mine = dp * groups + me
    block = q_ref.shape[0]
    barrier = pltpu.get_barrier_semaphore()

    def device(index):
        return (index // groups, index % groups)

    def hello(s, carry):
        pl.semaphore_signal(
            barrier, inc=1, device_id=device((mine + s) % total), device_id_type=MESH
        )
        return carry

    lax.fori_loop(1, total, hello, 0)
    pl.semaphore_wait(barrier, total - 1)

    def small_copy(s):
        return pltpu.make_async_remote_copy(
            src_ref=small_ref, dst_ref=box.at[mine], send_sem=send.at[s], recv_sem=recv.at[s],
            device_id=device((mine + s) % total), device_id_type=MESH,
        )

    def start(s, carry):
        small_copy(s).start()
        return carry

    def wait(s, carry):
        small_copy(s).wait()
        return carry

    lax.fori_loop(1, total, start, 0)
    place = pl.ds(pl.multiple_of(me * block, block), block)
    spread, own = [], []
    for m, ref in enumerate((q_ref, k_ref, v_ref)):
        cols = pl.ds(pl.multiple_of((me // copies) * slab, slab), slab)
        dst = spread_to.at[place, pl.ds(m * slab, slab)]
        own.append(pltpu.make_async_copy(ref.at[:, cols], dst, own_sem.at[m]))
        for s in range(1, groups):
            peer = (me + s) % groups
            cols = pl.ds(pl.multiple_of((peer // copies) * slab, slab), slab)
            spread.append(
                pltpu.make_async_remote_copy(
                    src_ref=ref.at[:, cols], dst_ref=dst,
                    send_sem=qkv_send.at[s, m], recv_sem=qkv_recv.at[s, m],
                    device_id=(dp, peer), device_id_type=MESH,
                )
            )
    moved = (mine % seqs) * groups + mine // seqs
    away = pltpu.make_async_remote_copy(
        src_ref=out_ref, dst_ref=out_to, send_sem=out_sem.at[0], recv_sem=out_sem.at[1],
        device_id=device(moved), device_id_type=MESH,
    )
    stay = pltpu.make_async_copy(out_ref, out_to, out_sem.at[0])
    @pl.when(moved != mine)
    def _():
        away.start()

    @pl.when(moved == mine)
    def _():
        stay.start()

    sends = Plane(
        [(0, 0, 1, 1), (0, 0, 1, 2), (0, 1, 1, 1), (0, 1, 1, 2)], (), [gate_ref], gate_refs,
        plane_send, plane_recv,
    )
    sends.start()
    for copy in spread:
        copy.start()
    for copy in own:
        copy.start()
    box[mine] = small_ref[...]
    out_small = pltpu.make_async_copy(box, small_to, small_sem)

    def arrived():
        for copy in own + spread:
            copy.wait()

        @pl.when(moved != mine)
        def _():
            away.wait()

        @pl.when(moved == mine)
        def _():
            stay.wait()

    wholes = [
        Whole(a, b, whole_own.at[i], whole_send.at[i], whole_recv.at[i])
        for i, (a, b) in enumerate(((spread_to, qkv_to), (out_to, wo_to)))
    ]
    gather_body(
        groups, rows, parts, Opening(sends, arrived, wholes), x_ref, x_to,
        keep_sem, line_send, line_recv, pair_send, pair_recv, greet=False,
    )
    lax.fori_loop(1, total, wait, 0)
    out_small.start()
    out_small.wait()


def opening(x, small, w_out, w_query, w_key, w_value, w_gate, copies, slab, collective_id, parts=4):
    groups, seqs = lax.axis_size("expert"), lax.axis_size("dp")
    total = groups * seqs
    block, width = w_query.shape
    rows = x.shape[0]
    gate = jax.ShapeDtypeStruct((1,) + w_gate.shape[1:], BF16)

    def kernel(*refs):
        ins, refs = refs[:7], refs[7:]
        outs, gates, rest = refs[:6], refs[6:10], refs[10:]
        opening_body(groups, seqs, copies, slab, rows, parts, gates, *ins, *outs, *rest)

    vmem, anywhere = pl.BlockSpec(memory_space=pltpu.VMEM), pl.BlockSpec(memory_space=pl.ANY)
    dma = pltpu.SemaphoreType.DMA
    line = dma((2, groups // 2, parts))
    return pl.pallas_call(
        kernel,
        out_shape=[
            jax.ShapeDtypeStruct((groups * rows, width), x.dtype),
            jax.ShapeDtypeStruct((total,) + small.shape, small.dtype),
            jax.ShapeDtypeStruct((seqs * groups * block, 3 * slab), BF16),
            jax.ShapeDtypeStruct((seqs * block, width), BF16),
            jax.ShapeDtypeStruct((block, width), BF16),
            jax.ShapeDtypeStruct((groups * block, 3 * slab), BF16),
        ]
        + [gate] * 4,
        in_specs=[anywhere, vmem] + [anywhere] * 5,
        out_specs=[anywhere] * 10,
        scratch_shapes=[pltpu.VMEM((total,) + small.shape, small.dtype)]
        + [dma((total,)), dma((total,)), dma((2,)), dma((3,)), dma((groups, 3)), dma((groups, 3)), dma]
        + [dma((4,)), dma((4,)), dma((2,)), dma((2, 4)), dma((2, 4))]
        + [dma] + [line] * 4,
        compiler_params=pltpu.CompilerParams(collective_id=collective_id, has_side_effects=True),
        cost_estimate=cost_of(80),
        name="opening",
    )(x, small, w_out, w_query, w_key, w_value, w_gate)


def both(array, start=0, size=None):
    size = array.shape[0] if size is None else size
    return [(array, start, size, 1), (array, start, size, 2)]


def swap_dp(block, flip):
    seqs = lax.axis_size("dp")
    return lax.ppermute(block, "dp", [(i, i ^ flip) for i in range(seqs)])


def tie(value, *deps):
    return lax.optimization_barrier((value,) + deps)[0]


def near_dp(block):
    return block, swap_dp(block, 1), swap_dp(block, 2)


def far_dp(near, *deps):
    block, near_x, near_y = near
    half = block.shape[0] // 2
    via_x, via_y = lax.optimization_barrier((near_y[:half], near_x[half:]) + deps)[:2]
    far = jnp.concatenate([swap_dp(via_x, 1), swap_dp(via_y, 2)], axis=0)
    return [block, near_x, near_y, far]


def halves(block):
    half = block.shape[0] // 2
    return [(block, 0, half, 1), (block, half, half, 2)]


def relay(blocks, from_x, from_y):
    _, to_x, to_y, _ = blocks
    half = to_x.shape[0] // 2
    to_x = jnp.concatenate(
        [to_x[:half], (to_x[half:].astype(F32) + from_y.astype(F32)).astype(BF16)], axis=0
    )
    to_y = jnp.concatenate(
        [(to_y[:half].astype(F32) + from_x.astype(F32)).astype(BF16), to_y[half:]], axis=0
    )
    return to_x, to_y


def settle(blocks, from_x, from_y):
    return blocks[0].astype(F32) + from_x.astype(F32) + from_y.astype(F32)


def send_halves(blocks):
    half = blocks[3].shape[0] // 2
    return swap_dp(blocks[3][:half], 1), swap_dp(blocks[3][half:], 2)


def in_order(pieces, index, axis):
    low = (index % 2) == 1
    high = (index // 2) == 1
    a, b, c, d = pieces
    a, b, c, d = (
        jnp.where(low, b, a), jnp.where(low, a, b), jnp.where(low, d, c), jnp.where(low, c, d)
    )
    return jnp.concatenate(
        [jnp.where(high, c, a), jnp.where(high, d, b), jnp.where(high, a, c), jnp.where(high, b, d)],
        axis=axis,
    )


def own_order(array, index, axis):
    return in_order(jnp.split(array, 4, axis=axis), index, axis)


def shards(
    tokens, routes, grad_output, w_query, w_key, w_value, w_out, w_router,
    gain_attn, gain_query, gain_key, gain_ffn, w_gate, w_up, w_down,
):
    rows = tokens.shape[1]
    width = tokens.shape[2]
    groups = lax.axis_size("expert")
    seqs = lax.axis_size("dp")
    me = lax.axis_index("expert")
    length = rows * groups
    local_experts = w_gate.shape[0]
    all_experts = local_experts * groups
    block = w_query.shape[0]
    own = width // groups
    slab = max(own, HEAD_DIM)
    copies = slab // own
    heads = slab // HEAD_DIM
    share = 1.0 / copies
    offset = (me % copies) * own

    x_low = tokens.reshape(rows, width)
    g_low = grad_output.reshape(rows, width)

    my_dp = lax.axis_index("dp")
    small_size = block * (all_experts + 4)
    small_rows = -(-small_size // (16 * 128)) * 16
    small = jnp.concatenate(
        [w_router.reshape(-1), gain_attn, gain_query, gain_key, gain_ffn,
         jnp.zeros((small_rows * 128 - small_size,), BF16)]
    )
    x_all, small_all, w_qkv, w_o, _, _, gate0_x, gate0_y, gate1_x, gate1_y = opening(
        x_low, small.reshape(small_rows, 128), w_out, w_query, w_key, w_value, w_gate, copies, slab,
        1,
    )
    small_all = small_all.reshape(seqs * groups, small_rows * 128)
    split = block * all_experts
    w_r = small_all[:, :split].reshape(width, all_experts)
    gains = [
        small_all[:, split + i * block : split + (i + 1) * block].reshape(width).astype(F32)
        for i in range(4)
    ]
    g_attn, g_ffn = gains[0], gains[3]
    slab_start = (me // copies) * slab
    g_query = lax.dynamic_slice(gains[1], (slab_start,), (slab,))
    g_key = lax.dynamic_slice(gains[2], (slab_start,), (slab,))

    total = seqs * groups
    moves = [(b, (b % seqs) * groups + b // seqs) for b in range(total)]

    x_in = x_low.astype(F32)
    inv_attn = inv_rms(x_in)
    x_wide = x_all.astype(F32)
    normed_all = (x_wide * inv_rms(x_wide) * g_attn).astype(BF16)
    if copies > 1:
        sets = [[c * copies + i for i in range(copies)] for c in range(groups // copies)]
        w_o = lax.all_gather(w_o, "expert", axis_index_groups=sets, axis=0, tiled=True)

    near_up = tie(w_up, x_all)
    up_x, up_y = swap_dp(near_up, 1), swap_dp(near_up, 2)
    g_all = lax.all_gather(g_low, "expert", axis=0, tiled=True)

    raw = dot(normed_all, w_qkv)
    q_raw, k_raw, v_raw = raw[:, :slab], raw[:, slab : 2 * slab], raw[:, 2 * slab :]
    squares = jnp.stack([jnp.sum(q_raw * q_raw, axis=1), jnp.sum(k_raw * k_raw, axis=1)], axis=0)
    squares = exchange(
        (squares * share).reshape(1, 2 * length // 128, 128), 4, same=True, reduce=True
    ).reshape(2, length)
    inv_qk = lax.rsqrt(squares / width + EPS)
    inv_q, inv_k = inv_qk[0][:, None], inv_qk[1][:, None]
    tables = rope_tables(length)

    def to_heads(values):
        return values.reshape(length, heads, HEAD_DIM)

    queries = rotary(to_heads(q_raw * inv_q * g_query), tables).astype(BF16).transpose(1, 0, 2)
    keys = rotary(to_heads(k_raw * inv_k * g_key), tables).astype(BF16).transpose(1, 0, 2)
    values = to_heads(v_raw).astype(BF16).transpose(1, 0, 2)
    positions = jnp.arange(length, dtype=jnp.int32)
    scale = HEAD_DIM ** (-0.5)

    def head_probs(q, k):
        scores = dot_nt(q, k) * scale
        scores = jnp.where(positions[None, :] <= positions[:, None], scores, NEG)
        exp_terms = jnp.exp(scores - jnp.max(scores, axis=-1, keepdims=True))
        return exp_terms / jnp.sum(exp_terms, axis=-1, keepdims=True)

    mixes = []
    for h in range(heads):
        mixes.append(dot(head_probs(queries[h], keys[h]).astype(BF16), values[h]).astype(BF16))
    mix = jnp.concatenate(mixes, axis=1)
    o_sum, gate0_f, gate1_f, up0_f, up1_f = line_reduce(
        dot(mix, w_o) * share, 5,
        sends=[(gate0_y, 0, 1, 1), (gate1_x, 0, 1, 2), (up_y, 0, 1, 1), (up_x, 1, 1, 2)],
    )
    after_attn = x_in + o_sum

    inv_ffn = inv_rms(after_attn)
    ffn_low = (after_attn * inv_ffn * g_ffn).astype(BF16)
    router_prob = jax.nn.softmax(dot(ffn_low, w_r), axis=-1)
    chosen = routes.reshape(rows, routes.shape[2])
    chosen_mask = jnp.sum(
        (chosen[:, :, None] == jnp.arange(all_experts, dtype=jnp.int32)[None, None, :]).astype(F32),
        axis=1,
    )
    route_dense = router_prob * chosen_mask
    gate_near = [(gate0_x, 0), (gate1_x, 0), (gate0_y, 0), (gate1_y, 0), (gate0_f, 0), (gate1_f, 0)]
    up_near = [(up_x, 0), (up_x, 1), (up_y, 0), (up_y, 1), (up0_f, 0), (up1_f, 0)]
    ff = w_gate.shape[2]
    if copies == 1 and length * width <= 1 << 21:
        high = lax.reduce_precision(route_dense, 8, 7)
        space = jnp.zeros((rows, LANES // 2 - all_experts), F32)
        extra = jnp.concatenate([high, space, route_dense - high, space], axis=1).astype(BF16)
        ffn_all, hidden_w, d_gate, d_up, tail, wd, d_down = expert_first(
            jnp.concatenate([ffn_low, extra], axis=1), g_all, w_gate, w_up, w_down,
            gate_near + up_near, 9,
        )
        d_gate_w, down_near, down_mid, d_rows = expert_second(
            d_gate, d_up, tail, ffn_all, d_down, w_gate, w_up, gate_near + up_near, 13
        )
        d_weight = d_rows[:, width : width + LANES]
        d_weight = d_weight[:, :all_experts] + d_weight[:, LANES // 2 : LANES // 2 + all_experts]
        d_rows = d_rows[:, :width]
    else:
        ffn_all = line_gather(ffn_low, 3)
        pad = -local_experts % 8
        route_send = route_dense.T.reshape(groups, local_experts, rows)
        route_send = jnp.pad(route_send, ((0, 0), (0, pad), (0, 0)))
        route_mine = exchange(route_send, 6)[:, :local_experts].transpose(0, 2, 1)
        route_mine = route_mine.reshape(length, local_experts)
        near_down = near_dp(tie(w_down, ffn_all))
        wd = in_order(far_dp(near_down), my_dp, 1)
        hidden_w, d_gate, d_up, d_weights = [], [], [], []
        y_part, dx_part = 0.0, 0.0
        for i in range(local_experts):
            wg, wu = (
                in_order([own[i]] + [near[2 * q + i][0][near[2 * q + i][1]] for q in range(3)], my_dp, 0)
                for own, near in ((w_gate, gate_near), (w_up, up_near))
            )
            weight = route_mine[:, i : i + 1]
            gate, up = dot(ffn_all, wg), dot(ffn_all, wu)
            d_hid = dot_nt(g_all, wd[i])
            sig = jax.nn.sigmoid(gate)
            silu = gate * sig
            d_weights.append(jnp.sum(silu * up * d_hid, axis=1))
            hidden_w.append((silu * up * weight).astype(BF16))
            d_hid = d_hid * weight
            d_gate.append((d_hid * up * sig * (1.0 + gate * (1.0 - sig))).astype(BF16))
            d_up.append((d_hid * silu).astype(BF16))
            y_part = y_part + dot(hidden_w[i], wd[i])
            dx_part = dx_part + dot_nt(d_gate[i], wg) + dot_nt(d_up[i], wu)
            (ffn_all, y_part, dx_part) = lax.optimization_barrier((ffn_all, y_part, dx_part))
        hidden_w, d_gate, d_up = (jnp.concatenate(a, axis=1) for a in (hidden_w, d_gate, d_up))
        y_part = y_part.astype(BF16)
        d_down = dot_tn(hidden_w, g_all).astype(BF16).reshape(local_experts, ff, width)
        d_rows = line_reduce(dx_part, 10)
        d_weight = jnp.stack(d_weights, axis=0).reshape(local_experts, groups, rows)
        d_weight = jnp.pad(d_weight.transpose(1, 0, 2), ((0, 0), (0, pad), (0, 0)))
        d_weight = exchange(d_weight, 6)[:, :local_experts].reshape(all_experts, rows).T

    fused = copies == 1 and length * width <= 1 << 21

    def scatter_in(product):
        return lax.psum_scatter(product, "dp", scatter_dimension=0, tiled=True)

    def to_experts(own_grad):
        return jnp.stack([own_grad[:, i * ff : (i + 1) * ff] for i in range(local_experts)]).astype(F32)

    if not fused:
        own_down = lax.psum_scatter(d_down, "dp", scatter_dimension=1, tiled=True)
        d_gate_w = dot_tn(ffn_all, d_gate).astype(BF16)
    own_gate = to_experts(scatter_in(d_gate_w))
    d_router_prob = d_weight * chosen_mask

    d_logits = (
        router_prob * (d_router_prob - jnp.sum(d_router_prob * router_prob, axis=-1, keepdims=True))
    ).astype(BF16)
    d_router_w = dot_tn(ffn_low, d_logits)
    d_normed_ffn = d_rows + dot_nt(d_logits, w_r)
    d_after_norm, d_gain_ffn = norm_back(after_attn, inv_ffn, g_ffn, d_normed_ffn)
    d_after = g_low.astype(F32) + d_after_norm
    if fused:
        d_after_all, d_up_w, y_part, own_down = gather_fill(
            d_after.astype(BF16), ffn_all, d_up, hidden_w, wd.reshape(local_experts * ff, width),
            d_down, down_mid, down_near, ff, 11,
        )
    else:
        d_after_all = line_gather(d_after.astype(BF16), 16)
        d_up_w = dot_tn(ffn_all, d_up).astype(BF16)
    own_up = scatter_in(d_up_w)
    own_up = own_up[0].astype(F32) if fused else to_experts(own_up)
    d_out_w = dot_tn(mix, d_after_all)
    d_mix = dot_nt(d_after_all, w_o).astype(BF16)
    dqs, dks, dvs = [], [], []
    for h in range(heads):
        prob = head_probs(queries[h], keys[h])
        d_m = d_mix[:, h * HEAD_DIM : (h + 1) * HEAD_DIM]
        d_prob = dot_nt(d_m, values[h])
        row_delta = jnp.sum(d_prob * prob, axis=-1, keepdims=True)
        d_score = (prob * (d_prob - row_delta) * scale).astype(BF16)
        dqs.append(dot(d_score, keys[h]))
        dks.append(dot_tn(d_score, queries[h]))
        dvs.append(dot_tn(prob.astype(BF16), d_m))
    dq_n = rotary_back(jnp.stack(dqs, axis=1), tables).reshape(length, slab)
    dk_n = rotary_back(jnp.stack(dks, axis=1), tables).reshape(length, slab)
    dv_low = jnp.concatenate(dvs, axis=1).astype(BF16)
    dots = jnp.stack(
        [jnp.sum(dq_n * g_query * q_raw, axis=1), jnp.sum(dk_n * g_key * k_raw, axis=1)], axis=0
    )
    dots = exchange(
        (dots * share).reshape(1, 2 * length // 128, 128), 4, same=True, reduce=True
    ).reshape(2, length) / width
    d_gain_query = jnp.sum(dq_n * q_raw * inv_q, axis=0)
    d_gain_key = jnp.sum(dk_n * k_raw * inv_k, axis=0)
    dq_low = (inv_q * dq_n * g_query - q_raw * (inv_q**3 * dots[0][:, None])).astype(BF16)
    dk_low = (inv_k * dk_n * g_key - k_raw * (inv_k**3 * dots[1][:, None])).astype(BF16)
    d_raw = jnp.concatenate([dq_low, dk_low, dv_low], axis=1)
    d_qkv_w = dot_tn(normed_all, d_raw).astype(BF16)
    d_qkv_w = d_qkv_w.reshape(width, 3, slab)
    d_qkv_w = lax.dynamic_slice(d_qkv_w, (0, 0, offset), (width, 3, own))
    d_qkv_w = d_qkv_w.reshape(width, 3 * own)
    d_out_w = lax.dynamic_slice(d_out_w.astype(BF16), (offset, 0), (own, width))
    dx_in = (dot_nt(d_raw, w_qkv) * share).astype(BF16)
    if length * width <= 1 << 21:
        d_normed_in, y_sum, own_qkv, own_out = joint_reduce(
            [dx_in, y_part], [d_qkv_w, d_out_w], [own_gate], 12
        )
    else:
        d_normed_in, own_qkv, own_out = joint_reduce(
            [dx_in], [d_qkv_w, d_out_w], [own_gate], 12
        )
        y_sum = line_reduce(y_part, 15)
    output = after_attn + y_sum
    d_in_norm, d_gain_attn = norm_back(x_in, inv_attn, g_attn, d_normed_in)
    input_grad = d_after + d_in_norm

    spread = jnp.zeros((2, width), F32)
    spread = lax.dynamic_update_slice(
        spread, jnp.stack([d_gain_query, d_gain_key]) * share, (0, slab_start)
    )
    total = seqs * groups
    small_grad = jnp.concatenate(
        [d_router_w.reshape(total, split)]
        + [v.reshape(total, block) for v in (d_gain_attn, spread[0], spread[1], d_gain_ffn)]
        + [jnp.zeros((total, small_rows * 128 - small_size), F32)],
        axis=1,
    )
    small_grad = small_grad.reshape(total, small_rows, 128)
    if own % 128 == 0:
        output, input_grad = (a.reshape(1, rows, width) for a in (output, input_grad))
        small_grad, *matrices = last_exchange(
            small_grad, own_qkv, own_out, [output, input_grad], 8
        )
    else:
        small_grad = exchange(small_grad, 8, spread=True, reduce=True)
        own_qkv = exchange(own_qkv.reshape(groups, block, 3 * own), 7)
        own_qkv = own_qkv.reshape(groups, block, 3, own).transpose(2, 1, 0, 3)
        own_out = lax.ppermute(own_out, ("dp", "expert"), [(b, a) for a, b in moves])
        matrices = [*own_qkv.reshape(3, block, width).astype(F32), own_out.astype(F32)]
    small_grad = small_grad.reshape(-1)
    expert_owned = [own_gate, own_up, own_down.astype(F32)]
    return (
        output.reshape(1, rows, width),
        input_grad.reshape(1, rows, width),
        *matrices,
        small_grad[:split].reshape(block, all_experts),
        small_grad[split : split + block],
        small_grad[split + block : split + 2 * block],
        small_grad[split + 2 * block : split + 3 * block],
        small_grad[split + 3 * block : split + 4 * block],
        *expert_owned,
    )


def solution(mesh):
    tok = P("dp", "expert", None)
    mat = P(("dp", "expert"), None)
    vec = P(("dp", "expert"))
    exp = P("expert", "dp", None)
    return jax.shard_map(
        shards,
        mesh=mesh,
        in_specs=(tok, tok, tok, mat, mat, mat, mat, mat, vec, vec, vec, vec, exp, exp, exp),
        out_specs=(tok, tok, mat, mat, mat, mat, mat, vec, vec, vec, vec, exp, exp, exp),
        check_vma=False,
    )
```
